32 devices in a mesh: dom: 2 (over x), vocab: 16 (over z, y, core).
Axes of the slice: x: 2, y: 2, z: 4, core: 2. Of those that a mesh axis runs over, the one named last changes fastest.
Arguments:
- hidden_states: bfloat16 [128, 5120], P('dom', 'vocab'), parts along dimension 0
- head: bfloat16 [19456, 5120], P('vocab'), may hold values from -0.078125 to 0.078125
- teacher_values: bfloat16 [128, 19456], P(('dom', 'vocab')), parts along dimension 0
- teacher_scales: float32 [128, 608], P(('dom', 'vocab')), parts along dimension 0, as said below
- token_ids: int32 [128], P('dom'), parts along dimension 0, may hold values from 0 to 19455
- lengths: int32 [4], P('dom'), parts along dimension 0, may hold values from 1 to 32, as said below
- row_map: int32 [128], P('dom'), parts along dimension 0, may hold values from -1 to 63, as said below
- loss_scale: float32 [1], replicated, may hold values from 65536 to 262144
Outputs:
- grad_hidden: bfloat16 [128, 5120], P('dom', 'vocab'), parts along dimension 0
- loss: float32 [2], P('dom'), parts along dimension 0
The draws below stay inside these ranges and needn't reach their ends.
There are 2 independent parts, one for each index of `dom`. The reference program is written for one: setup_inputs(seed, part) draws one part's arguments, and reference() takes and returns one part's arrays. A program takes and returns all parts, laid end to end along the dimension named above; an argument that names none is the same for every part. Nothing has to cross between parts.
Inputs may be any that keep to these rules, and one draw needn't show every extreme that they name: `lengths`: every response has at least one live position, and some response has all 32 positions live. `row_map`: each live position t (t % 32 < lengths[t // 32]) is named by exactly one slot; no other position is named; slots naming no position hold -1. How many live rows a device's slots hold varies. `teacher_scales`: every scale is a power of two.
All inputs are finite; a program needn't handle non-finite values.
Results may differ from the reference program's by a relative error of at most 0.0054.
Values may be sent and summed in bfloat16 or wider, within the bound.
No kernel may reach another device: no remote copies, remote signals or barrier semaphores. Data moves between devices by JAX's collectives and lax.ppermute only.
A program may use at most 64 MiB of HBM per device.

```python
import math
import jax
import jax.numpy as jnp
import numpy as np
from jax import lax

D = 5120
BLOCK = 32
SEQLEN = 32
V = 19456
TOK = 64
SEQS = 2


def response_lengths(key):
    longest = jax.random.randint(jax.random.fold_in(key, 11), (), 0, SEQS)
    drawn = jax.random.randint(jax.random.fold_in(key, 12), (SEQS,), 1, SEQLEN + 1)
    return jnp.where(jnp.arange(SEQS, dtype=jnp.int32) == longest, SEQLEN, drawn).astype(jnp.int32)


def draw_lengths(key, part):
    return response_lengths(key)


def draw_row_map(key, part):
    lengths = response_lengths(key)
    key = jax.random.fold_in(key, 3)
    positions = jnp.arange(TOK, dtype=jnp.int32)
    seq_ids = jnp.arange(SEQS, dtype=jnp.int32)
    own_length = jnp.sum(jnp.where((positions // SEQLEN)[:, None] == seq_ids[None, :], lengths[None, :], 0), axis=1)
    live = positions % SEQLEN < own_length
    ranks = jnp.maximum(jnp.cumsum(live.astype(jnp.int32)) - 1, 0)
    order = jax.random.permutation(key, TOK).astype(jnp.int32)
    target_slot = jnp.where(live, jnp.take(order, ranks), TOK)
    empty_map = jnp.full((TOK,), -1, jnp.int32)
    return empty_map.at[target_slot].set(positions, mode='drop')


def draw_hidden_states(key, part):
    key = jax.random.fold_in(key, 5)
    key_base = jax.random.fold_in(key, 1)
    return jnp.clip(jax.random.normal(key_base, (TOK, D), jnp.float32), -6.0, 6.0).astype(jnp.bfloat16)


def draw_teacher_values(key, part):
    key = jax.random.fold_in(key, 7)
    key_base = jax.random.fold_in(key, 1)
    return jnp.clip(2.0 * jax.random.normal(key_base, (TOK, V), jnp.float32), -12.0, 12.0).astype(jnp.bfloat16)


def draw_teacher_scales(key, part):
    key = jax.random.fold_in(key, 9)
    powers = jax.random.randint(key, (TOK, V // BLOCK), -2, 3)
    return jnp.exp2(powers.astype(jnp.float32))


def set_ends(entries, own_key, least, largest):
    shape = entries.shape
    index_at = [jax.random.randint(jax.random.fold_in(own_key, axis), (), 0, shape[axis]) for axis in range(len(shape))]
    entries = entries.at[tuple(index_at)].set(least)
    longest = shape.index(max(shape))
    index_at[longest] = (index_at[longest] + 1) % shape[longest]
    return entries.at[tuple(index_at)].set(largest)


def shard_levels(stream_key, shape, shards, least, top_value):
    def one(position, parts):
        heights = jax.random.uniform(jax.random.fold_in(jax.random.fold_in(stream_key, 6), position), (parts,), jnp.float32, least / len(shards), top_value / len(shards))
        return jnp.repeat(jnp.exp(heights), shape[position] // parts).reshape((-1,) + (1,) * (len(shape) - position - 1))

    level = one(*shards[0])
    for cut in shards[1:]:
        level = level * one(*cut)
    return level


def cumulative_ranks(count, lean):
    weights = [(1 << 20) // math.isqrt(standing ** lean) + 1 for standing in range(1, count + 1)]
    width = 1 + sum(weights) // (1 << 30)
    return np.cumsum(np.array([max(1, weight // width) for weight in weights]))


def ranked(rng, extent, amount, slope):
    grid = cumulative_ranks(amount, slope)
    ticket = jax.random.randint(jax.random.fold_in(rng, 1), extent, 0, int(grid[amount - 1]))
    grade = jnp.searchsorted(jnp.asarray(grid, jnp.int32), ticket, side="right")
    return jax.random.permutation(jax.random.fold_in(rng, 2), amount)[grade].astype(jnp.int32)


def centred(key, extent, width, bound, shards=(), kind=jnp.bfloat16):
    values = jax.random.normal(key, extent, jnp.float32) * width
    if len(shards) > 0:
        values = shard_levels(key, extent, shards, -0.22, 0.18) * values
    return jnp.clip(values, min=-bound, max=bound).astype(kind)


def setup_inputs(seed: int = 0, part: int = 0) -> dict:
    key_list = jax.random.split(jax.random.key(seed), 9)
    part_keys = jax.random.split(jax.random.fold_in(key_list[8], part), 9)
    hidden_states = draw_hidden_states(jax.random.fold_in(jax.random.fold_in(key_list[8], part), 71), part)
    head = centred(key_list[1], (V, D), D ** -0.5, 0.078125, ((0, 16),))
    teacher_values = draw_teacher_values(jax.random.fold_in(jax.random.fold_in(key_list[8], part), 71), part)
    teacher_scales = draw_teacher_scales(jax.random.fold_in(jax.random.fold_in(key_list[8], part), 71), part)
    token_ids = set_ends(ranked(part_keys[4], (TOK,), V, 2), jax.random.fold_in(part_keys[4], 3), 0, V - 1).astype(jnp.int32)
    lengths = draw_lengths(jax.random.fold_in(jax.random.fold_in(key_list[8], part), 71), part)
    row_map = draw_row_map(jax.random.fold_in(jax.random.fold_in(key_list[8], part), 71), part)
    loss_scale = jnp.clip(jnp.exp(jax.random.uniform(key_list[7], (1,), jnp.float32, math.log(65536.0), math.log(262144.0))), 65536.0, 262144.0)
    return {"hidden_states": hidden_states, "head": head, "teacher_values": teacher_values, "teacher_scales": teacher_scales, "token_ids": token_ids, "lengths": lengths, "row_map": row_map, "loss_scale": loss_scale}


sample_weight = 0.5


def reference(hidden_states, head, teacher_values, teacher_scales, token_ids, lengths, row_map, loss_scale):
    contract_last = (((1,), (1,)), ((), ()))
    logits = lax.dot_general(hidden_states, head, contract_last, preferred_element_type=jnp.float32)
    positions = jnp.arange(TOK, dtype=jnp.int32)
    owner = row_map[None, :] == positions[:, None]
    slot_of = jnp.sum(jnp.where(owner, positions[None, :], 0), axis=1).astype(jnp.int32)
    placed_values = jnp.take(teacher_values, slot_of, axis=0)
    placed_scales = jnp.take(teacher_scales, slot_of, axis=0)
    teacher_logits = (placed_values.astype(jnp.float32).reshape(TOK, V // BLOCK, BLOCK) * placed_scales[:, :, None]).reshape(TOK, V)
    seq_ids = jnp.arange(SEQS, dtype=jnp.int32)
    own_length = jnp.sum(jnp.where((positions // SEQLEN)[:, None] == seq_ids[None, :], lengths[None, :], 0), axis=1)
    live_mask = ((positions % SEQLEN) < own_length).astype(jnp.float32)
    live_count = jnp.sum(live_mask)
    student_max = jnp.max(logits, axis=1)
    student_lse = student_max + jnp.log(jnp.sum(jnp.exp(logits - student_max[:, None]), axis=1))
    teacher_max = jnp.max(teacher_logits, axis=1)
    teacher_lse = teacher_max + jnp.log(jnp.sum(jnp.exp(teacher_logits - teacher_max[:, None]), axis=1))
    log_student = logits - student_lse[:, None]
    log_teacher = teacher_logits - teacher_lse[:, None]
    student_prob = jnp.exp(log_student)
    divergence = jnp.sum(student_prob * (log_student - log_teacher), axis=1)
    target_hit = token_ids[:, None] == jnp.arange(V, dtype=jnp.int32)[None, :]
    target = jnp.sum(jnp.where(target_hit, logits, 0.0), axis=1)
    per_token = divergence + sample_weight * (student_lse - target)
    loss = jnp.reshape(jnp.sum(live_mask * per_token) / live_count, (1,))
    token_weight = live_mask * loss_scale[0] / live_count
    grad_logits = (token_weight[:, None] * (student_prob * (log_student - log_teacher - divergence[:, None]) + sample_weight * (student_prob - target_hit.astype(jnp.float32)))).astype(jnp.bfloat16)
    grad_hidden = jnp.dot(grad_logits, head, preferred_element_type=jnp.float32).astype(jnp.bfloat16)
    return grad_hidden, loss
```

```python
import jax
import jax.numpy as jnp
from jax import lax
from jax.sharding import PartitionSpec as P

BLOCK = 32


sample_weight = 0.5


def to_all(piece, count):
    copies = jnp.broadcast_to(piece[None], (count,) + piece.shape)
    return lax.all_to_all(copies, "vocab", split_axis=0, concat_axis=0, tiled=True)


def shards(
    hidden_states, head, teacher_values, teacher_scales, token_ids, lengths, row_map, loss_scale
):
    count = lax.axis_size("vocab")
    own_index = lax.axis_index("vocab")
    tokens = hidden_states.shape[0]
    own_features = hidden_states.shape[1]
    shard_rows = head.shape[0]
    seq_length = tokens // lengths.shape[0]
    slot_rows = teacher_values.shape[0]
    contract_last = (((1,), (1,)), ((), ()))

    scaled = (
        teacher_values.astype(jnp.float32).reshape(slot_rows, -1, BLOCK) * teacher_scales[:, :, None]
    ).astype(jnp.bfloat16)
    scaled = scaled.reshape(slot_rows, count, shard_rows).transpose(1, 0, 2)
    arrived = lax.all_to_all(scaled, "vocab", split_axis=0, concat_axis=0, tiled=True)
    arrived = arrived.reshape(tokens, shard_rows)

    gathered = to_all(hidden_states, count).transpose(1, 0, 2).reshape(tokens, -1)
    logits = lax.dot_general(gathered, head, contract_last, preferred_element_type=jnp.float32)

    positions = jnp.arange(tokens, dtype=jnp.int32)
    owner = row_map[None, :] == positions[:, None]
    slot_of = jnp.sum(jnp.where(owner, positions[None, :], 0), axis=1)
    teacher = jnp.take(arrived, slot_of, axis=0).astype(jnp.float32)

    seq_ids = jnp.arange(lengths.shape[0], dtype=jnp.int32)
    own_length = jnp.sum(
        jnp.where((positions // seq_length)[:, None] == seq_ids[None, :], lengths[None, :], 0),
        axis=1,
    )
    live_mask = (positions % seq_length < own_length).astype(jnp.float32)
    live_count = jnp.sum(live_mask)

    local_ids = token_ids - own_index * shard_rows
    target_hit = local_ids[:, None] == jnp.arange(shard_rows, dtype=jnp.int32)[None, :]
    target_part = jnp.sum(jnp.where(target_hit, logits, 0.0), axis=1)
    student_top = jnp.max(logits, axis=1)
    teacher_top = jnp.max(teacher, axis=1)
    student_off = logits - student_top[:, None]
    teacher_off = teacher - teacher_top[:, None]
    student_exp = jnp.exp(student_off)
    student_sum = jnp.sum(student_exp, axis=1)
    teacher_sum = jnp.sum(jnp.exp(teacher_off), axis=1)
    cross_sum = jnp.sum(student_exp * (student_off - teacher_off), axis=1)

    stats = to_all(
        jnp.stack(
            [student_top, student_sum, teacher_top, teacher_sum, cross_sum, target_part]
        ),
        count,
    )
    tops, sums, teacher_tops, teacher_sums, crosses, targets = [stats[:, i] for i in range(6)]
    student_max = jnp.max(tops, axis=0)
    teacher_max = jnp.max(teacher_tops, axis=0)
    student_shift = tops - student_max[None, :]
    teacher_shift = teacher_tops - teacher_max[None, :]
    weight = jnp.exp(student_shift)
    student_total = jnp.sum(sums * weight, axis=0)
    teacher_total = jnp.sum(teacher_sums * jnp.exp(teacher_shift), axis=0)
    cross_total = jnp.sum(weight * (crosses + sums * (student_shift - teacher_shift)), axis=0)
    student_log = jnp.log(student_total)
    teacher_log = jnp.log(teacher_total)
    student_lse = student_max + student_log
    teacher_lse = teacher_max + teacher_log
    divergence = cross_total / student_total - (student_log - teacher_log)
    target = jnp.sum(targets, axis=0)

    per_token = divergence + sample_weight * (student_lse - target)
    loss = jnp.reshape(jnp.sum(live_mask * per_token) / live_count, (1,))
    token_weight = live_mask * loss_scale[0] / live_count
    log_student = logits - student_lse[:, None]
    log_teacher = teacher - teacher_lse[:, None]
    student_prob = jnp.exp(log_student)
    grad_logits = (
        token_weight[:, None]
        * (
            student_prob * (log_student - log_teacher - divergence[:, None])
            + sample_weight * (student_prob - target_hit.astype(jnp.float32))
        )
    ).astype(jnp.bfloat16)
    terms = jnp.dot(grad_logits, head, preferred_element_type=jnp.float32).astype(jnp.bfloat16)
    terms = terms.reshape(tokens, count, own_features).transpose(1, 0, 2)
    shares = lax.all_to_all(terms, "vocab", split_axis=0, concat_axis=0, tiled=True)
    grad_hidden = jnp.sum(shares.astype(jnp.float32), axis=0)
    return (grad_hidden.astype(jnp.bfloat16), loss)


def solution(mesh):
    in_specs = (
        P("dom", "vocab"),
        P("vocab", None),
        P(("dom", "vocab"), None),
        P(("dom", "vocab"), None),
        P("dom"),
        P("dom"),
        P("dom"),
        P(),
    )
    out_specs = (P("dom", "vocab"), P("dom"))
    return jax.shard_map(shards, mesh=mesh, in_specs=in_specs, out_specs=out_specs, check_vma=False)
```

```python
import functools

import jax
import jax.numpy as jnp
from jax import lax
from jax.experimental import pallas as pl
from jax.experimental.pallas import tpu as pltpu
from jax.sharding import PartitionSpec as P

BLOCK = 32
LANES = 128
STATS = 8


sample_weight = 0.5


def to_all(piece, count):
    copies = jnp.broadcast_to(piece[None], (count,) + piece.shape)
    return lax.all_to_all(copies, "vocab", split_axis=0, concat_axis=0, tiled=True)


def scaled_teacher(teacher_values, teacher_scales, count, shard_rows):
    slot_rows = teacher_values.shape[0]
    scaled = (
        teacher_values.astype(jnp.float32).reshape(slot_rows, -1, BLOCK) * teacher_scales[:, :, None]
    ).astype(jnp.bfloat16)
    scaled = scaled.reshape(slot_rows, count, shard_rows).transpose(1, 0, 2)
    arrived = lax.all_to_all(scaled, "vocab", split_axis=0, concat_axis=0, tiled=True)
    return arrived.reshape(count * slot_rows, shard_rows)


def merge_stats(tops, sums, teacher_tops, teacher_sums, crosses):
    top = jnp.max(tops, axis=0)
    teacher_top = jnp.max(teacher_tops, axis=0)
    shift = tops - top[None]
    teacher_shift = teacher_tops - teacher_top[None]
    weight = jnp.exp(shift)
    total = jnp.sum(sums * weight, axis=0)
    teacher_total = jnp.sum(teacher_sums * jnp.exp(teacher_shift), axis=0)
    cross = jnp.sum(weight * (crosses + sums * (shift - teacher_shift)), axis=0)
    return top, total, teacher_top, teacher_total, cross


def swap_cores(count):
    return [(i, i ^ 1) for i in range(count)]


def next_chips(count, step):
    return [(i, (i + 2 * step) % count) for i in range(count)]


def gather_chips(piece, count):
    return [piece] + [
        lax.ppermute(piece, "vocab", next_chips(count, step)) for step in range(1, count // 2)
    ]


def all_stats(stats, count):
    own_index = lax.axis_index("vocab")
    reach = 1
    while reach < count:
        other = lax.ppermute(stats, "vocab", [(i, i ^ reach) for i in range(count)])
        upper = (own_index & reach) > 0
        low = jnp.where(upper, other, stats)
        high = jnp.where(upper, stats, other)
        pair = jnp.stack([low, high])
        top, total, teacher_top, teacher_total, cross = merge_stats(
            *[pair[:, i : i + 1] for i in range(5)]
        )
        target = low[5:6] + high[5:6]
        stats = jnp.concatenate(
            [top, total, teacher_top, teacher_total, cross, target, target, target]
        )
        reach *= 2
    return stats


def logits_kernel(
    place_ref,
    *refs,
    chips,
    width,
):
    near = refs[:chips]
    far = refs[chips : 2 * chips]
    head_ref, arrived_ref, map_ref, ids_ref, logits_ref, teacher_ref, stats_ref, hidden = refs[
        2 * chips :
    ]
    own_index = place_ref[0]
    chip, core = own_index // 2, own_index % 2
    tokens, shard_rows = logits_ref.shape
    for step in range(chips):
        mine, other = near[step][...], far[step][...]
        hidden[step] = jnp.where(
            core == 0,
            jnp.concatenate([mine, other], axis=1),
            jnp.concatenate([other, mine], axis=1),
        )

    def add(step, _):
        source = lax.rem(chip - step + chips, chips)
        columns = pl.ds(pl.multiple_of(source * width, LANES), width)
        logits_ref[...] += lax.dot_general(
            hidden[step],
            head_ref[:, columns],
            (((1,), (1,)), ((), ())),
            preferred_element_type=jnp.float32,
        )

    logits_ref[...] = jnp.zeros_like(logits_ref)
    lax.fori_loop(0, chips, add, None)

    token = lax.broadcasted_iota(jnp.int32, (tokens, tokens), 0)
    slot = lax.broadcasted_iota(jnp.int32, (tokens, tokens), 1)
    owner = (map_ref[...] == token).astype(jnp.float32)
    named = jnp.max(owner, axis=1, keepdims=True)
    owner = jnp.where((slot == 0) & (named == 0.0), 1.0, owner)
    teacher = jnp.dot(
        owner.astype(jnp.bfloat16), arrived_ref[...], preferred_element_type=jnp.float32
    )
    teacher_ref[...] = teacher

    logits = logits_ref[...]
    top = jnp.max(logits, axis=1, keepdims=True)
    teacher_top = jnp.max(teacher, axis=1, keepdims=True)
    off = logits - top
    teacher_off = teacher - teacher_top
    exps = jnp.exp(off)
    total = jnp.sum(exps, axis=1, keepdims=True)
    teacher_total = jnp.sum(jnp.exp(teacher_off), axis=1, keepdims=True)
    cross = jnp.sum(exps * (off - teacher_off), axis=1, keepdims=True)
    entry = lax.broadcasted_iota(jnp.int32, (tokens, shard_rows), 1)
    hit = entry == ids_ref[...] - own_index * shard_rows
    target = jnp.sum(jnp.where(hit, logits, 0.0), axis=1, keepdims=True)
    lane = lax.broadcasted_iota(jnp.int32, (tokens, LANES), 1)
    table = jnp.zeros((tokens, LANES), jnp.float32)
    for place, column in enumerate((top, total, teacher_top, teacher_total, cross, target)):
        table = jnp.where(lane == place, column, table)
    stats_ref[...] = table.T[:STATS]


def grads_kernel(
    place_ref,
    lengths_ref,
    scale_ref,
    logits_ref,
    teacher_ref,
    stats_ref,
    ids_ref,
    head_ref,
    keep_ref,
    give_ref,
    loss_ref,
    grads,
    *,
    chips,
    width,
):
    own_index = place_ref[0]
    chip, core = own_index // 2, own_index % 2
    tokens, shard_rows = logits_ref.shape
    half = width // 2
    seqs = lengths_ref.shape[0]
    seq_length = tokens // seqs
    stats = jnp.concatenate(
        [stats_ref[...], jnp.zeros((LANES - STATS, tokens), jnp.float32)], axis=0
    ).T
    top, total, teacher_top, teacher_total, cross, target = [stats[:, i : i + 1] for i in range(6)]
    student_log = jnp.log(total)
    teacher_log = jnp.log(teacher_total)
    student_lse = top + student_log
    teacher_lse = teacher_top + teacher_log
    divergence = cross / total - (student_log - teacher_log)

    position = lax.broadcasted_iota(jnp.int32, (tokens, 1), 0)
    own_length = jnp.zeros((tokens, 1), jnp.int32)
    for seq in range(seqs):
        inside = (position >= seq * seq_length) & (position < (seq + 1) * seq_length)
        own_length = jnp.where(inside, lengths_ref[seq] + seq * seq_length, own_length)
    live = (position < own_length).astype(jnp.float32)
    live_count = jnp.sum(live, axis=0, keepdims=True)
    per_token = divergence + sample_weight * (student_lse - target)
    loss_ref[...] = jnp.sum(live * per_token, axis=0, keepdims=True) / live_count
    token_weight = live * scale_ref[0] / live_count

    log_student = logits_ref[...] - student_lse
    log_teacher = teacher_ref[...] - teacher_lse
    prob = jnp.exp(log_student)
    entry = lax.broadcasted_iota(jnp.int32, (tokens, shard_rows), 1)
    hit = (entry == ids_ref[...] - own_index * shard_rows).astype(jnp.float32)
    grads[...] = (
        token_weight
        * (prob * (log_student - log_teacher - divergence) + sample_weight * (prob - hit))
    ).astype(jnp.bfloat16)

    def put(step, _):
        to = lax.rem(chip + step, chips)
        columns = pl.ds(pl.multiple_of(to * width, LANES), width)
        terms = jnp.dot(grads[...], head_ref[:, columns], preferred_element_type=jnp.float32)
        first, second = terms[:, :half], terms[:, half:]
        keep_ref[step] = jnp.where(core == 0, first, second)
        give_ref[step] = jnp.where(core == 0, second, first).astype(jnp.bfloat16)

    lax.fori_loop(0, chips, put, None)


def paired_shards(
    hidden_states, head, teacher_values, teacher_scales, token_ids, lengths, row_map, loss_scale
):
    count = lax.axis_size("vocab")
    own_index = lax.axis_index("vocab")
    chips = count // 2
    tokens, half = hidden_states.shape
    width = 2 * half
    shard_rows = head.shape[0]
    place = jnp.reshape(own_index, (1,))
    vmem = pl.BlockSpec(memory_space=pltpu.VMEM)
    smem = pl.BlockSpec(memory_space=pltpu.SMEM)

    near = gather_chips(hidden_states, count)
    far = [lax.ppermute(piece, "vocab", swap_cores(count)) for piece in near]
    arrived = scaled_teacher(teacher_values, teacher_scales, count, shard_rows)
    ids = token_ids[:, None]
    logits, teacher, stats = pl.pallas_call(
        functools.partial(logits_kernel, chips=chips, width=width),
        out_shape=(
            jax.ShapeDtypeStruct((tokens, shard_rows), jnp.float32),
            jax.ShapeDtypeStruct((tokens, shard_rows), jnp.float32),
            jax.ShapeDtypeStruct((STATS, tokens), jnp.float32),
        ),
        in_specs=[smem] + [vmem] * (2 * chips + 4),
        out_specs=[vmem] * 3,
        scratch_shapes=[pltpu.VMEM((chips, tokens, width), jnp.bfloat16)],
        compiler_params=pltpu.CompilerParams(vmem_limit_bytes=VMEM_LIMIT),
        name="logits",
    )(place, *near, *far, in_vmem(head), arrived, row_map[None, :], ids)

    stats = all_stats(stats, count)

    keep, give, loss = pl.pallas_call(
        functools.partial(grads_kernel, chips=chips, width=width),
        out_shape=(
            jax.ShapeDtypeStruct((chips, tokens, half), jnp.float32),
            jax.ShapeDtypeStruct((chips, tokens, half), jnp.bfloat16),
            jax.ShapeDtypeStruct((1, 1), jnp.float32),
        ),
        in_specs=[smem] * 3 + [vmem] * 5,
        out_specs=[vmem] * 3,
        scratch_shapes=[pltpu.VMEM((tokens, shard_rows), jnp.bfloat16)],
        compiler_params=pltpu.CompilerParams(vmem_limit_bytes=VMEM_LIMIT),
        name="grads",
    )(place, lengths, loss_scale, logits, teacher, stats, ids, in_vmem(head))

    taken = lax.ppermute(give, "vocab", swap_cores(count))
    sums = keep + taken.astype(jnp.float32)
    total = sums[0]
    for step in range(1, chips):
        share = lax.ppermute(
            sums[step].astype(jnp.bfloat16), "vocab", next_chips(count, step)
        )
        total = total + share.astype(jnp.float32)
    return total.astype(jnp.bfloat16), jnp.reshape(loss, (1,))


VMEM_LIMIT = 40 * 1024 * 1024


def in_vmem(array):
    return pltpu.with_memory_space_constraint(array, pltpu.VMEM)


def shards(
    hidden_states, head, teacher_values, teacher_scales, token_ids, lengths, row_map, loss_scale
):
    count = lax.axis_size("vocab")
    own_index = lax.axis_index("vocab")
    tokens = hidden_states.shape[0]
    own_features = hidden_states.shape[1]
    shard_rows = head.shape[0]
    seq_length = tokens // lengths.shape[0]
    contract_last = (((1,), (1,)), ((), ()))

    arrived = scaled_teacher(teacher_values, teacher_scales, count, shard_rows)
    gathered = to_all(hidden_states, count).transpose(1, 0, 2).reshape(tokens, -1)
    logits = lax.dot_general(gathered, head, contract_last, preferred_element_type=jnp.float32)

    positions = jnp.arange(tokens, dtype=jnp.int32)
    owner = row_map[None, :] == positions[:, None]
    slot_of = jnp.sum(jnp.where(owner, positions[None, :], 0), axis=1)
    teacher = jnp.take(arrived, slot_of, axis=0).astype(jnp.float32)

    seq_ids = jnp.arange(lengths.shape[0], dtype=jnp.int32)
    own_length = jnp.sum(
        jnp.where((positions // seq_length)[:, None] == seq_ids[None, :], lengths[None, :], 0),
        axis=1,
    )
    live_mask = (positions % seq_length < own_length).astype(jnp.float32)
    live_count = jnp.sum(live_mask)

    local_ids = token_ids - own_index * shard_rows
    target_hit = local_ids[:, None] == jnp.arange(shard_rows, dtype=jnp.int32)[None, :]
    target_part = jnp.sum(jnp.where(target_hit, logits, 0.0), axis=1)
    student_top = jnp.max(logits, axis=1)
    teacher_top = jnp.max(teacher, axis=1)
    student_off = logits - student_top[:, None]
    teacher_off = teacher - teacher_top[:, None]
    student_exp = jnp.exp(student_off)
    student_sum = jnp.sum(student_exp, axis=1)
    teacher_sum = jnp.sum(jnp.exp(teacher_off), axis=1)
    cross_sum = jnp.sum(student_exp * (student_off - teacher_off), axis=1)

    stats = to_all(
        jnp.stack(
            [student_top, student_sum, teacher_top, teacher_sum, cross_sum, target_part]
        ),
        count,
    )
    tops, sums, teacher_tops, teacher_sums, crosses, targets = [stats[:, i] for i in range(6)]
    student_max, student_total, teacher_max, teacher_total, cross_total = merge_stats(
        tops, sums, teacher_tops, teacher_sums, crosses
    )
    student_log = jnp.log(student_total)
    teacher_log = jnp.log(teacher_total)
    student_lse = student_max + student_log
    teacher_lse = teacher_max + teacher_log
    divergence = cross_total / student_total - (student_log - teacher_log)
    target = jnp.sum(targets, axis=0)

    per_token = divergence + sample_weight * (student_lse - target)
    loss = jnp.reshape(jnp.sum(live_mask * per_token) / live_count, (1,))
    token_weight = live_mask * loss_scale[0] / live_count
    log_student = logits - student_lse[:, None]
    log_teacher = teacher - teacher_lse[:, None]
    student_prob = jnp.exp(log_student)
    grad_logits = (
        token_weight[:, None]
        * (
            student_prob * (log_student - log_teacher - divergence[:, None])
            + sample_weight * (student_prob - target_hit.astype(jnp.float32))
        )
    ).astype(jnp.bfloat16)
    terms = jnp.dot(grad_logits, head, preferred_element_type=jnp.float32).astype(jnp.bfloat16)
    terms = terms.reshape(tokens, count, own_features).transpose(1, 0, 2)
    shares = lax.all_to_all(terms, "vocab", split_axis=0, concat_axis=0, tiled=True)
    grad_hidden = jnp.sum(shares.astype(jnp.float32), axis=0)
    return (grad_hidden.astype(jnp.bfloat16), loss)


def any_shards(*arrays):
    pair_width = 2 * arrays[0].shape[1]
    if lax.axis_size("vocab") > 2 and pair_width % LANES == 0:
        return paired_shards(*arrays)
    return shards(*arrays)


def solution(mesh):
    in_specs = (
        P("dom", "vocab"),
        P("vocab", None),
        P(("dom", "vocab"), None),
        P(("dom", "vocab"), None),
        P("dom"),
        P("dom"),
        P("dom"),
        P(),
    )
    out_specs = (P("dom", "vocab"), P("dom"))
    return jax.shard_map(
        any_shards, mesh=mesh, in_specs=in_specs, out_specs=out_specs, check_vma=False
    )
```

```python
import functools

import jax
import jax.numpy as jnp
from jax import lax
from jax.experimental import pallas as pl
from jax.experimental.pallas import tpu as pltpu
from jax.sharding import PartitionSpec as P

BLOCK = 32
LANES = 128
STATS = 8


sample_weight = 0.5


def to_all(piece, count):
    copies = jnp.broadcast_to(piece[None], (count,) + piece.shape)
    return lax.all_to_all(copies, "vocab", split_axis=0, concat_axis=0, tiled=True)


def scaled_teacher(teacher_values, teacher_scales, count, shard_rows):
    slot_rows = teacher_values.shape[0]
    scaled = (
        teacher_values.astype(jnp.float32).reshape(slot_rows, -1, BLOCK) * teacher_scales[:, :, None]
    ).astype(jnp.bfloat16)
    scaled = scaled.reshape(slot_rows, count, shard_rows).transpose(1, 0, 2)
    arrived = lax.all_to_all(scaled, "vocab", split_axis=0, concat_axis=0, tiled=True)
    return arrived.reshape(count * slot_rows, shard_rows)


def merge_stats(tops, sums, teacher_tops, teacher_sums, crosses):
    top = jnp.max(tops, axis=0)
    teacher_top = jnp.max(teacher_tops, axis=0)
    shift = tops - top[None]
    teacher_shift = teacher_tops - teacher_top[None]
    weight = jnp.exp(shift)
    total = jnp.sum(sums * weight, axis=0)
    teacher_total = jnp.sum(teacher_sums * jnp.exp(teacher_shift), axis=0)
    cross = jnp.sum(weight * (crosses + sums * (shift - teacher_shift)), axis=0)
    return top, total, teacher_top, teacher_total, cross


def swap_cores(array):
    count = lax.axis_size("vocab")
    return lax.ppermute(array, "vocab", [(i, i ^ 1) for i in range(count)])


def across_chips(blocks):
    count = lax.axis_size("vocab")
    groups = [list(range(core, count, 2)) for core in range(2)]
    return lax.all_to_all(
        blocks, "vocab", split_axis=0, concat_axis=0, axis_index_groups=groups, tiled=True
    )


def vmem_array(shape, dtype):
    return pltpu.VMEM(shape, dtype)


def in_vmem(array):
    return pltpu.with_memory_space_constraint(array, pltpu.VMEM)


def in_hbm(array):
    return pltpu.with_memory_space_constraint(array, pltpu.HBM)


def column_of(row):
    size = row.shape[1]
    down = lax.broadcasted_iota(jnp.int32, (size, size), 0)
    along = lax.broadcasted_iota(jnp.int32, (size, size), 1)
    return jnp.sum(jnp.where(down == along, row, jnp.zeros_like(row)), axis=1, keepdims=True)


def prepare_kernel(
    place_ref, lengths_ref, scale_ref, ids_ref, map_ref, head_ref, held_ref, owner_ref, tokens_ref, sem
):
    copy = pltpu.make_async_copy(head_ref, held_ref, sem)
    copy.start()
    tokens = map_ref.shape[1]
    shard_rows = head_ref.shape[0]
    token = lax.broadcasted_iota(jnp.int32, (tokens, tokens), 0)
    slot = lax.broadcasted_iota(jnp.int32, (tokens, tokens), 1)
    owner = (map_ref[...] == token).astype(jnp.float32)
    named = jnp.max(owner, axis=1, keepdims=True)
    owner = jnp.where((slot == 0) & (named == 0.0), 1.0, owner)
    owner_ref[...] = owner.astype(jnp.bfloat16)

    seqs = lengths_ref.shape[0]
    seq_length = tokens // seqs
    position = lax.broadcasted_iota(jnp.int32, (tokens, 1), 0)
    live_until = jnp.zeros((tokens, 1), jnp.int32)
    for seq in range(seqs):
        inside = (position >= seq * seq_length) & (position < (seq + 1) * seq_length)
        live_until = jnp.where(inside, lengths_ref[seq] + seq * seq_length, live_until)
    live = (position < live_until).astype(jnp.float32)
    share = live / jnp.sum(live, axis=0, keepdims=True)
    weight = live * scale_ref[0] / jnp.sum(live, axis=0, keepdims=True)
    entry = (column_of(ids_ref[...]) - place_ref[0] * shard_rows).astype(jnp.float32)
    lane = lax.broadcasted_iota(jnp.int32, (tokens, LANES), 1)
    table = jnp.where(lane == 0, entry, jnp.where(lane == 1, share, weight))
    tokens_ref[...] = table
    copy.wait()


def logits_kernel(
    place_ref,
    own_ref,
    other_ref,
    head_ref,
    arrived_ref,
    owner_ref,
    tokens_ref,
    rows_ref,
    stats_ref,
):
    core = place_ref[0] % 2
    chips, tokens, half = own_ref.shape
    shard_rows = head_ref.shape[0]
    logits = jnp.zeros((tokens, shard_rows), jnp.float32)
    for chip in range(chips):
        own, other = own_ref[chip], other_ref[chip]
        block = jnp.where(
            core == 0,
            jnp.concatenate([own, other], axis=1),
            jnp.concatenate([other, own], axis=1),
        )
        logits += lax.dot_general(
            block,
            head_ref[:, 2 * half * chip : 2 * half * (chip + 1)],
            (((1,), (1,)), ((), ())),
            preferred_element_type=jnp.float32,
        )
    teacher = jnp.dot(owner_ref[...], arrived_ref[...], preferred_element_type=jnp.float32)

    top = jnp.max(logits, axis=1, keepdims=True)
    teacher_top = jnp.max(teacher, axis=1, keepdims=True)
    off = logits - top
    teacher_off = teacher - teacher_top
    exps = jnp.exp(off)
    total = jnp.sum(exps, axis=1, keepdims=True)
    teacher_total = jnp.sum(jnp.exp(teacher_off), axis=1, keepdims=True)
    gap = off - teacher_off
    cross = jnp.sum(exps * gap, axis=1, keepdims=True)
    centre = cross / total
    entry = lax.broadcasted_iota(jnp.int32, (tokens, shard_rows), 1)
    hit = entry == tokens_ref[:, :1].astype(jnp.int32)
    target = jnp.sum(jnp.where(hit, logits, 0.0), axis=1, keepdims=True)
    rows_ref[:tokens] = (exps * (gap - centre)).astype(jnp.bfloat16)
    rows_ref[tokens : 2 * tokens] = exps.astype(jnp.bfloat16)
    rows_ref[2 * tokens :] = hit.astype(jnp.bfloat16)

    lane = lax.broadcasted_iota(jnp.int32, (tokens, LANES), 1)
    table = jnp.zeros((tokens, LANES), jnp.float32)
    for place, column in enumerate(
        (top, total, teacher_top, teacher_total, cross, target, centre)
    ):
        table = jnp.where(lane == place, column, table)
    stats = jnp.concatenate([table, jnp.zeros((stats_ref.shape[2] - tokens, LANES), jnp.float32)])
    stats_ref[...] = jnp.broadcast_to(stats.T[None, :STATS], stats_ref.shape)


def products_kernel(rows_ref, head_ref, terms_ref):
    chips, _, width = terms_ref.shape

    def multiply(chip, _):
        columns = pl.ds(pl.multiple_of(chip * width, LANES), width)
        terms_ref[chip] = jnp.dot(
            rows_ref[...], head_ref[:, columns], preferred_element_type=jnp.float32
        )

    lax.fori_loop(0, chips, multiply, None)


def combine_kernel(
    place_ref, stats_ref, own_ref, tokens_ref, terms_ref, keep_ref, give_ref, loss_ref
):
    core = place_ref[0] % 2
    chips, _, width = terms_ref.shape
    tokens = tokens_ref.shape[0]
    half = width // 2
    tops, sums, teacher_tops, teacher_sums, crosses, targets = [
        stats_ref[:, i, :tokens] for i in range(6)
    ]
    top, total, teacher_top, teacher_total, cross = [
        part[None] for part in merge_stats(tops, sums, teacher_tops, teacher_sums, crosses)
    ]
    target = jnp.sum(targets, axis=0, keepdims=True)
    student_log = jnp.log(total)
    teacher_log = jnp.log(teacher_total)
    divergence = cross / total - (student_log - teacher_log)
    student_lse = top + student_log
    per_token = divergence + sample_weight * (student_lse - target)
    student_shift = own_ref[0, 0:1, :tokens] - top - student_log
    teacher_shift = own_ref[0, 2:3, :tokens] - teacher_top - teacher_log
    factor = jnp.exp(student_shift)
    level = own_ref[0, 6:7, :tokens] + student_shift - teacher_shift - divergence + sample_weight
    zeros = jnp.zeros((LANES - 3, tokens), jnp.float32)
    columns = jnp.concatenate([factor, level, per_token, zeros], axis=0).T
    share, weight = tokens_ref[:, 1:2], tokens_ref[:, 2:3]
    loss_ref[...] = jnp.sum(share * columns[:, 2:3], axis=0, keepdims=True)
    factor = weight * columns[:, 0:1]
    level = columns[:, 1:2]
    weight = sample_weight * weight
    for chip in range(chips):
        block = (
            factor * (terms_ref[chip, :tokens] + level * terms_ref[chip, tokens : 2 * tokens])
            - weight * terms_ref[chip, 2 * tokens :]
        )
        first, second = block[:, :half], block[:, half:]
        keep_ref[chip] = jnp.where(core == 0, first, second)
        give_ref[chip] = jnp.where(core == 0, second, first).astype(jnp.bfloat16)


def sum_kernel(shares_ref, total_ref):
    total = shares_ref[0].astype(jnp.float32)
    for chip in range(1, shares_ref.shape[0]):
        total += shares_ref[chip].astype(jnp.float32)
    total_ref[...] = total.astype(total_ref.dtype)


def paired_shards(
    hidden_states, head, teacher_values, teacher_scales, token_ids, lengths, row_map, loss_scale
):
    count = lax.axis_size("vocab")
    own_index = lax.axis_index("vocab")
    chips = count // 2
    tokens, half = hidden_states.shape
    width = 2 * half
    shard_rows = head.shape[0]
    place = jnp.reshape(own_index, (1,))
    vmem = pl.BlockSpec(memory_space=pltpu.VMEM)
    smem = pl.BlockSpec(memory_space=pltpu.SMEM)
    params = pltpu.CompilerParams(vmem_limit_bytes=VMEM_LIMIT)

    gathered = across_chips(jnp.broadcast_to(hidden_states[None], (chips, tokens, half)))
    other = swap_cores(gathered)

    held, owner, table = pl.pallas_call(
        prepare_kernel,
        out_shape=(
            vmem_array(head.shape, head.dtype),
            vmem_array((tokens, tokens), jnp.bfloat16),
            vmem_array((tokens, LANES), jnp.float32),
        ),
        in_specs=[smem] * 3 + [vmem] * 2 + [pl.BlockSpec(memory_space=pl.ANY)],
        out_specs=[vmem] * 3,
        scratch_shapes=[pltpu.SemaphoreType.DMA],
        compiler_params=params,
        cost_estimate=pl.CostEstimate(
            flops=0, bytes_accessed=2 * head.size * 2, transcendentals=0
        ),
        name="prepare",
    )(place, lengths, loss_scale, token_ids[None, :], row_map[None, :], in_hbm(head))

    arrived = scaled_teacher(teacher_values, teacher_scales, count, shard_rows)
    rows, stats = pl.pallas_call(
        logits_kernel,
        out_shape=(
            vmem_array((3 * tokens, shard_rows), jnp.bfloat16),
            vmem_array((count, STATS, pl.cdiv(tokens, LANES) * LANES), jnp.float32),
        ),
        in_specs=[smem] + [vmem] * 6,
        out_specs=[vmem] * 2,
        compiler_params=params,
        cost_estimate=pl.CostEstimate(
            flops=2 * tokens * head.size, bytes_accessed=2 * head.size, transcendentals=0
        ),
        name="logits",
    )(place, in_vmem(gathered), in_vmem(other), in_vmem(held), in_vmem(arrived), in_vmem(owner), in_vmem(table))

    all_stats = lax.all_to_all(stats, "vocab", split_axis=0, concat_axis=0, tiled=True)

    terms = pl.pallas_call(
        products_kernel,
        out_shape=vmem_array((chips, 3 * tokens, width), jnp.float32),
        in_specs=[vmem] * 2,
        out_specs=vmem,
        compiler_params=params,
        cost_estimate=pl.CostEstimate(
            flops=6 * tokens * head.size, bytes_accessed=2 * head.size, transcendentals=0
        ),
        name="products",
    )(in_vmem(rows), in_vmem(held))

    keep, give, loss = pl.pallas_call(
        combine_kernel,
        out_shape=(
            vmem_array((chips, tokens, half), jnp.float32),
            vmem_array((chips, tokens, half), jnp.bfloat16),
            jax.ShapeDtypeStruct((1, 1), jnp.float32),
        ),
        in_specs=[smem] + [vmem] * 4,
        out_specs=[vmem] * 3,
        compiler_params=params,
        name="combine",
    )(place, in_vmem(all_stats), in_vmem(stats), in_vmem(table), in_vmem(terms))

    sums = keep + swap_cores(give).astype(jnp.float32)
    shares = across_chips(sums.astype(jnp.bfloat16))
    total = pl.pallas_call(
        sum_kernel,
        out_shape=jax.ShapeDtypeStruct((tokens, half), jnp.bfloat16),
        in_specs=[vmem],
        out_specs=vmem,
        compiler_params=params,
        name="total",
    )(in_vmem(shares))
    return total, jnp.reshape(loss, (1,))


VMEM_LIMIT = 12 * 1024 * 1024


def shards(
    hidden_states, head, teacher_values, teacher_scales, token_ids, lengths, row_map, loss_scale
):
    count = lax.axis_size("vocab")
    own_index = lax.axis_index("vocab")
    tokens = hidden_states.shape[0]
    own_features = hidden_states.shape[1]
    shard_rows = head.shape[0]
    seq_length = tokens // lengths.shape[0]
    contract_last = (((1,), (1,)), ((), ()))

    arrived = scaled_teacher(teacher_values, teacher_scales, count, shard_rows)
    gathered = to_all(hidden_states, count).transpose(1, 0, 2).reshape(tokens, -1)
    logits = lax.dot_general(gathered, head, contract_last, preferred_element_type=jnp.float32)

    positions = jnp.arange(tokens, dtype=jnp.int32)
    owner = row_map[None, :] == positions[:, None]
    slot_of = jnp.sum(jnp.where(owner, positions[None, :], 0), axis=1)
    teacher = jnp.take(arrived, slot_of, axis=0).astype(jnp.float32)

    seq_ids = jnp.arange(lengths.shape[0], dtype=jnp.int32)
    own_length = jnp.sum(
        jnp.where((positions // seq_length)[:, None] == seq_ids[None, :], lengths[None, :], 0),
        axis=1,
    )
    live_mask = (positions % seq_length < own_length).astype(jnp.float32)
    live_count = jnp.sum(live_mask)

    local_ids = token_ids - own_index * shard_rows
    target_hit = local_ids[:, None] == jnp.arange(shard_rows, dtype=jnp.int32)[None, :]
    target_part = jnp.sum(jnp.where(target_hit, logits, 0.0), axis=1)
    student_top = jnp.max(logits, axis=1)
    teacher_top = jnp.max(teacher, axis=1)
    student_off = logits - student_top[:, None]
    teacher_off = teacher - teacher_top[:, None]
    student_exp = jnp.exp(student_off)
    student_sum = jnp.sum(student_exp, axis=1)
    teacher_sum = jnp.sum(jnp.exp(teacher_off), axis=1)
    cross_sum = jnp.sum(student_exp * (student_off - teacher_off), axis=1)

    stats = to_all(
        jnp.stack(
            [student_top, student_sum, teacher_top, teacher_sum, cross_sum, target_part]
        ),
        count,
    )
    tops, sums, teacher_tops, teacher_sums, crosses, targets = [stats[:, i] for i in range(6)]
    student_max, student_total, teacher_max, teacher_total, cross_total = merge_stats(
        tops, sums, teacher_tops, teacher_sums, crosses
    )
    student_log = jnp.log(student_total)
    teacher_log = jnp.log(teacher_total)
    student_lse = student_max + student_log
    teacher_lse = teacher_max + teacher_log
    divergence = cross_total / student_total - (student_log - teacher_log)
    target = jnp.sum(targets, axis=0)

    per_token = divergence + sample_weight * (student_lse - target)
    loss = jnp.reshape(jnp.sum(live_mask * per_token) / live_count, (1,))
    token_weight = live_mask * loss_scale[0] / live_count
    log_student = logits - student_lse[:, None]
    log_teacher = teacher - teacher_lse[:, None]
    student_prob = jnp.exp(log_student)
    grad_logits = (
        token_weight[:, None]
        * (
            student_prob * (log_student - log_teacher - divergence[:, None])
            + sample_weight * (student_prob - target_hit.astype(jnp.float32))
        )
    ).astype(jnp.bfloat16)
    terms = jnp.dot(grad_logits, head, preferred_element_type=jnp.float32).astype(jnp.bfloat16)
    terms = terms.reshape(tokens, count, own_features).transpose(1, 0, 2)
    shares = lax.all_to_all(terms, "vocab", split_axis=0, concat_axis=0, tiled=True)
    grad_hidden = jnp.sum(shares.astype(jnp.float32), axis=0)
    return (grad_hidden.astype(jnp.bfloat16), loss)


def any_shards(*arrays):
    pair_width = 2 * arrays[0].shape[1]
    if lax.axis_size("vocab") > 2 and pair_width % LANES == 0:
        return paired_shards(*arrays)
    return shards(*arrays)


def solution(mesh):
    in_specs = (
        P("dom", "vocab"),
        P("vocab", None),
        P(("dom", "vocab"), None),
        P(("dom", "vocab"), None),
        P("dom"),
        P("dom"),
        P("dom"),
        P(),
    )
    out_specs = (P("dom", "vocab"), P("dom"))
    return jax.shard_map(
        any_shards, mesh=mesh, in_specs=in_specs, out_specs=out_specs, check_vma=False
    )
```

```python
import functools

import jax
import jax.numpy as jnp
from jax import lax
from jax.experimental import pallas as pl
from jax.experimental.pallas import tpu as pltpu
from jax.sharding import PartitionSpec as P

BLOCK = 32
LANES = 128
STATS = 8


sample_weight = 0.5


def to_all(piece, count):
    copies = jnp.broadcast_to(piece[None], (count,) + piece.shape)
    return lax.all_to_all(copies, "vocab", split_axis=0, concat_axis=0, tiled=True)


def scaled_teacher(teacher_values, teacher_scales, count, shard_rows):
    slot_rows = teacher_values.shape[0]
    scaled = (
        teacher_values.astype(jnp.float32).reshape(slot_rows, -1, BLOCK) * teacher_scales[:, :, None]
    ).astype(jnp.bfloat16)
    return scaled.reshape(slot_rows, count, shard_rows).transpose(1, 0, 2)


def merge_stats(tops, sums, teacher_tops, teacher_sums, crosses):
    top = jnp.max(tops, axis=0)
    teacher_top = jnp.max(teacher_tops, axis=0)
    shift = tops - top[None]
    teacher_shift = teacher_tops - teacher_top[None]
    weight = jnp.exp(shift)
    total = jnp.sum(sums * weight, axis=0)
    teacher_total = jnp.sum(teacher_sums * jnp.exp(teacher_shift), axis=0)
    cross = jnp.sum(weight * (crosses + sums * (shift - teacher_shift)), axis=0)
    return top, total, teacher_top, teacher_total, cross


def swap_cores(array):
    count = lax.axis_size("vocab")
    return lax.ppermute(array, "vocab", [(i, i ^ 1) for i in range(count)])


def across_chips(array, step):
    count = lax.axis_size("vocab")
    return lax.ppermute(array, "vocab", [(i, i ^ (2 * step)) for i in range(count)])


def vmem_array(shape, dtype):
    return pltpu.VMEM(shape, dtype)


def in_vmem(array):
    return pltpu.with_memory_space_constraint(array, pltpu.VMEM)


def in_hbm(array):
    return pltpu.with_memory_space_constraint(array, pltpu.HBM)


def column_of(row):
    size = row.shape[1]
    down = lax.broadcasted_iota(jnp.int32, (size, size), 0)
    along = lax.broadcasted_iota(jnp.int32, (size, size), 1)
    return jnp.sum(jnp.where(down == along, row, jnp.zeros_like(row)), axis=1, keepdims=True)


def prepare_kernel(
    place_ref, lengths_ref, scale_ref, ids_ref, map_ref, owner_ref, tokens_ref, *, shard_rows
):
    tokens = map_ref.shape[1]
    token = lax.broadcasted_iota(jnp.int32, (tokens, tokens), 0)
    slot = lax.broadcasted_iota(jnp.int32, (tokens, tokens), 1)
    owner = (map_ref[...] == token).astype(jnp.float32)
    named = jnp.max(owner, axis=1, keepdims=True)
    owner = jnp.where((slot == 0) & (named == 0.0), 1.0, owner)
    owner_ref[...] = owner.astype(jnp.bfloat16)

    seqs = lengths_ref.shape[0]
    seq_length = tokens // seqs
    position = lax.broadcasted_iota(jnp.int32, (tokens, 1), 0)
    live_until = jnp.zeros((tokens, 1), jnp.int32)
    for seq in range(seqs):
        inside = (position >= seq * seq_length) & (position < (seq + 1) * seq_length)
        live_until = jnp.where(inside, lengths_ref[seq] + seq * seq_length, live_until)
    live = (position < live_until).astype(jnp.float32)
    share = live / jnp.sum(live, axis=0, keepdims=True)
    weight = live * scale_ref[0] / jnp.sum(live, axis=0, keepdims=True)
    entry = (column_of(ids_ref[...]) - place_ref[0] * shard_rows).astype(jnp.float32)
    lane = lax.broadcasted_iota(jnp.int32, (tokens, LANES), 1)
    tokens_ref[...] = jnp.where(lane == 0, entry, jnp.where(lane == 1, share, weight))


def head_copies(place_ref, head_ref, held_ref, sems):
    chips, _, width = held_ref.shape
    chip = place_ref[0] // 2
    copies = []
    for step in range(chips):
        columns = pl.ds(pl.multiple_of(jnp.bitwise_xor(chip, step) * width, LANES), width)
        copies.append(
            pltpu.make_async_copy(head_ref.at[:, columns], held_ref.at[step], sems.at[step])
        )
    return copies


def logits_kernel(place_ref, *refs, chips):
    near, far = refs[:chips], refs[chips : 2 * chips]
    head_ref, logits_ref, held_ref, sems = refs[2 * chips :]
    copies = head_copies(place_ref, head_ref, held_ref, sems)
    for copy in copies:
        copy.start()
    core = place_ref[0] % 2
    logits = jnp.zeros(logits_ref.shape, jnp.float32)
    for step in range(chips):
        own, other = near[step][...], far[step][...]
        block = jnp.where(
            core == 0,
            jnp.concatenate([own, other], axis=1),
            jnp.concatenate([other, own], axis=1),
        )
        copies[step].wait()
        logits += lax.dot_general(
            block, held_ref[step], (((1,), (1,)), ((), ())), preferred_element_type=jnp.float32
        )
    logits_ref[...] = logits


def softmax_kernel(logits_ref, arrived_ref, owner_ref, tokens_ref, rows_ref, stats_ref):
    tokens, shard_rows = logits_ref.shape
    logits = logits_ref[...]
    teacher = jnp.dot(owner_ref[...], arrived_ref[...], preferred_element_type=jnp.float32)
    top = jnp.max(logits, axis=1, keepdims=True)
    teacher_top = jnp.max(teacher, axis=1, keepdims=True)
    off = logits - top
    teacher_off = teacher - teacher_top
    exps = jnp.exp(off)
    total = jnp.sum(exps, axis=1, keepdims=True)
    teacher_total = jnp.sum(jnp.exp(teacher_off), axis=1, keepdims=True)
    gap = off - teacher_off
    cross = jnp.sum(exps * gap, axis=1, keepdims=True)
    centre = cross / total
    entry = lax.broadcasted_iota(jnp.int32, (tokens, shard_rows), 1)
    hit = entry == tokens_ref[:, :1].astype(jnp.int32)
    target = jnp.sum(jnp.where(hit, logits, 0.0), axis=1, keepdims=True)
    rows_ref[:tokens] = (exps * (gap - centre)).astype(jnp.bfloat16)
    rows_ref[tokens : 2 * tokens] = exps.astype(jnp.bfloat16)
    rows_ref[2 * tokens :] = hit.astype(jnp.bfloat16)

    lane = lax.broadcasted_iota(jnp.int32, (tokens, LANES), 1)
    table = jnp.zeros((tokens, LANES), jnp.float32)
    for place, column in enumerate(
        (top, total, teacher_top, teacher_total, cross, target, centre)
    ):
        table = jnp.where(lane == place, column, table)
    stats = jnp.concatenate([table, jnp.zeros((stats_ref.shape[2] - tokens, LANES), jnp.float32)])
    stats_ref[...] = jnp.broadcast_to(stats.T[None, :STATS], stats_ref.shape)


def products_kernel(place_ref, rows_ref, head_ref, terms_ref, picks_ref, held_ref, sems):
    copies = head_copies(place_ref, head_ref, held_ref, sems)
    for copy in copies:
        copy.start()
    sums_rows = terms_ref.shape[1]
    for step, copy in enumerate(copies):
        copy.wait()
        products = jnp.dot(rows_ref[...], held_ref[step], preferred_element_type=jnp.float32)
        terms_ref[step] = products[:sums_rows]
        picks_ref[step] = products[sums_rows:].astype(jnp.bfloat16)


def combine_kernel(
    place_ref, stats_ref, own_ref, tokens_ref, terms_ref, picks_ref, keep_ref, give_ref, loss_ref
):
    core = place_ref[0] % 2
    chips, _, width = terms_ref.shape
    tokens = tokens_ref.shape[0]
    half = width // 2
    tops, sums, teacher_tops, teacher_sums, crosses, targets = [
        stats_ref[:, i, :tokens] for i in range(6)
    ]
    top, total, teacher_top, teacher_total, cross = [
        part[None] for part in merge_stats(tops, sums, teacher_tops, teacher_sums, crosses)
    ]
    target = jnp.sum(targets, axis=0, keepdims=True)
    student_log = jnp.log(total)
    teacher_log = jnp.log(teacher_total)
    divergence = cross / total - (student_log - teacher_log)
    student_lse = top + student_log
    per_token = divergence + sample_weight * (student_lse - target)
    student_shift = own_ref[0, 0:1, :tokens] - top - student_log
    teacher_shift = own_ref[0, 2:3, :tokens] - teacher_top - teacher_log
    factor = jnp.exp(student_shift)
    level = (
        own_ref[0, 6:7, :tokens] + student_shift - teacher_shift - divergence + sample_weight
    )
    zeros = jnp.zeros((LANES - 3, tokens), jnp.float32)
    columns = jnp.concatenate([factor, level, per_token, zeros], axis=0).T
    share, weight = tokens_ref[:, 1:2], tokens_ref[:, 2:3]
    loss_ref[...] = jnp.sum(share * columns[:, 2:3], axis=0, keepdims=True)
    factor = weight * columns[:, 0:1]
    level = columns[:, 1:2]
    weight = sample_weight * weight
    for step in range(chips):
        block = (
            factor * (terms_ref[step, :tokens] + level * terms_ref[step, tokens:])
            - weight * picks_ref[step].astype(jnp.float32)
        )
        first, second = block[:, :half], block[:, half:]
        keep_ref[step] = jnp.where(core == 0, first, second)
        give_ref[step] = jnp.where(core == 0, second, first).astype(jnp.bfloat16)


def sum_kernel(own_ref, *refs):
    total = own_ref[...]
    for share_ref in refs[:-1]:
        total += share_ref[...].astype(jnp.float32)
    refs[-1][...] = total.astype(refs[-1].dtype)


def paired_shards(
    hidden_states, head, teacher_values, teacher_scales, token_ids, lengths, row_map, loss_scale
):
    count = lax.axis_size("vocab")
    own_index = lax.axis_index("vocab")
    chips = count // 2
    tokens, half = hidden_states.shape
    width = 2 * half
    shard_rows = head.shape[0]
    place = jnp.reshape(own_index, (1,))
    vmem = pl.BlockSpec(memory_space=pltpu.VMEM)
    smem = pl.BlockSpec(memory_space=pltpu.SMEM)
    hbm = pl.BlockSpec(memory_space=pl.ANY)
    params = pltpu.CompilerParams(vmem_limit_bytes=VMEM_LIMIT)
    head = in_hbm(head)
    head_scratch = [
        pltpu.VMEM((chips, shard_rows, width), head.dtype),
        pltpu.SemaphoreType.DMA((chips,)),
    ]

    steps = list(range(chips - 1, 0, -1))
    near = [across_chips(hidden_states, step) for step in steps]
    scaled = scaled_teacher(teacher_values, teacher_scales, count, shard_rows)
    near, scaled = lax.optimization_barrier((near, scaled))
    near = [hidden_states] + near[::-1]
    far = [swap_cores(piece) for piece in near]
    arrived = lax.all_to_all(scaled, "vocab", split_axis=0, concat_axis=0, tiled=True)
    arrived = arrived.reshape(tokens, shard_rows)

    owner, table = pl.pallas_call(
        functools.partial(prepare_kernel, shard_rows=shard_rows),
        out_shape=(
            vmem_array((tokens, tokens), jnp.bfloat16),
            vmem_array((tokens, LANES), jnp.float32),
        ),
        in_specs=[smem] * 3 + [vmem] * 2,
        out_specs=[vmem] * 2,
        compiler_params=params,
        name="prepare",
    )(place, lengths, loss_scale, token_ids[None, :], row_map[None, :])

    logits = pl.pallas_call(
        functools.partial(logits_kernel, chips=chips),
        out_shape=vmem_array((tokens, shard_rows), jnp.float32),
        in_specs=[smem] + [vmem] * (2 * chips) + [hbm],
        out_specs=vmem,
        scratch_shapes=head_scratch,
        compiler_params=params,
        cost_estimate=pl.CostEstimate(
            flops=2 * tokens * head.size, bytes_accessed=2 * head.size, transcendentals=0
        ),
        name="logits",
    )(place, *near, *far, head)

    rows, stats = pl.pallas_call(
        softmax_kernel,
        out_shape=(
            vmem_array((3 * tokens, shard_rows), jnp.bfloat16),
            vmem_array((count, STATS, pl.cdiv(tokens, LANES) * LANES), jnp.float32),
        ),
        in_specs=[vmem] * 4,
        out_specs=[vmem] * 2,
        compiler_params=params,
        name="softmax",
    )(in_vmem(logits), in_vmem(arrived), in_vmem(owner), in_vmem(table))

    all_stats = lax.all_to_all(stats, "vocab", split_axis=0, concat_axis=0, tiled=True)

    terms, picks = pl.pallas_call(
        products_kernel,
        out_shape=(
            vmem_array((chips, 2 * tokens, width), jnp.float32),
            vmem_array((chips, tokens, width), jnp.bfloat16),
        ),
        in_specs=[smem, vmem, hbm],
        out_specs=[vmem] * 2,
        scratch_shapes=head_scratch,
        compiler_params=params,
        cost_estimate=pl.CostEstimate(
            flops=6 * tokens * head.size, bytes_accessed=2 * head.size, transcendentals=0
        ),
        name="products",
    )(place, in_vmem(rows), head)

    keep, give, loss = pl.pallas_call(
        combine_kernel,
        out_shape=(
            vmem_array((chips, tokens, half), jnp.float32),
            vmem_array((chips, tokens, half), jnp.bfloat16),
            jax.ShapeDtypeStruct((1, 1), jnp.float32),
        ),
        in_specs=[smem] + [vmem] * 5,
        out_specs=[vmem] * 3,
        compiler_params=params,
        name="combine",
    )(
        place,
        in_vmem(all_stats),
        in_vmem(stats),
        in_vmem(table),
        in_vmem(terms),
        in_vmem(picks),
    )

    sums = keep + swap_cores(give).astype(jnp.float32)
    shares = [across_chips(sums[step].astype(jnp.bfloat16), step) for step in steps]
    total = pl.pallas_call(
        sum_kernel,
        out_shape=jax.ShapeDtypeStruct((tokens, half), jnp.bfloat16),
        in_specs=[vmem] * chips,
        out_specs=vmem,
        compiler_params=params,
        name="total",
    )(sums[0], *shares)
    return total, jnp.reshape(loss, (1,))


VMEM_LIMIT = 24 * 1024 * 1024


def shards(
    hidden_states, head, teacher_values, teacher_scales, token_ids, lengths, row_map, loss_scale
):
    count = lax.axis_size("vocab")
    own_index = lax.axis_index("vocab")
    tokens = hidden_states.shape[0]
    own_features = hidden_states.shape[1]
    shard_rows = head.shape[0]
    seq_length = tokens // lengths.shape[0]
    contract_last = (((1,), (1,)), ((), ()))

    scaled = scaled_teacher(teacher_values, teacher_scales, count, shard_rows)
    arrived = lax.all_to_all(scaled, "vocab", split_axis=0, concat_axis=0, tiled=True)
    arrived = arrived.reshape(tokens, shard_rows)
    gathered = to_all(hidden_states, count).transpose(1, 0, 2).reshape(tokens, -1)
    logits = lax.dot_general(gathered, head, contract_last, preferred_element_type=jnp.float32)

    positions = jnp.arange(tokens, dtype=jnp.int32)
    owner = row_map[None, :] == positions[:, None]
    slot_of = jnp.sum(jnp.where(owner, positions[None, :], 0), axis=1)
    teacher = jnp.take(arrived, slot_of, axis=0).astype(jnp.float32)

    seq_ids = jnp.arange(lengths.shape[0], dtype=jnp.int32)
    own_length = jnp.sum(
        jnp.where((positions // seq_length)[:, None] == seq_ids[None, :], lengths[None, :], 0),
        axis=1,
    )
    live_mask = (positions % seq_length < own_length).astype(jnp.float32)
    live_count = jnp.sum(live_mask)

    local_ids = token_ids - own_index * shard_rows
    target_hit = local_ids[:, None] == jnp.arange(shard_rows, dtype=jnp.int32)[None, :]
    target_part = jnp.sum(jnp.where(target_hit, logits, 0.0), axis=1)
    student_top = jnp.max(logits, axis=1)
    teacher_top = jnp.max(teacher, axis=1)
    student_off = logits - student_top[:, None]
    teacher_off = teacher - teacher_top[:, None]
    student_exp = jnp.exp(student_off)
    student_sum = jnp.sum(student_exp, axis=1)
    teacher_sum = jnp.sum(jnp.exp(teacher_off), axis=1)
    cross_sum = jnp.sum(student_exp * (student_off - teacher_off), axis=1)

    stats = to_all(
        jnp.stack(
            [student_top, student_sum, teacher_top, teacher_sum, cross_sum, target_part]
        ),
        count,
    )
    tops, sums, teacher_tops, teacher_sums, crosses, targets = [stats[:, i] for i in range(6)]
    student_max, student_total, teacher_max, teacher_total, cross_total = merge_stats(
        tops, sums, teacher_tops, teacher_sums, crosses
    )
    student_log = jnp.log(student_total)
    teacher_log = jnp.log(teacher_total)
    student_lse = student_max + student_log
    teacher_lse = teacher_max + teacher_log
    divergence = cross_total / student_total - (student_log - teacher_log)
    target = jnp.sum(targets, axis=0)

    per_token = divergence + sample_weight * (student_lse - target)
    loss = jnp.reshape(jnp.sum(live_mask * per_token) / live_count, (1,))
    token_weight = live_mask * loss_scale[0] / live_count
    log_student = logits - student_lse[:, None]
    log_teacher = teacher - teacher_lse[:, None]
    student_prob = jnp.exp(log_student)
    grad_logits = (
        token_weight[:, None]
        * (
            student_prob * (log_student - log_teacher - divergence[:, None])
            + sample_weight * (student_prob - target_hit.astype(jnp.float32))
        )
    ).astype(jnp.bfloat16)
    terms = jnp.dot(grad_logits, head, preferred_element_type=jnp.float32).astype(jnp.bfloat16)
    terms = terms.reshape(tokens, count, own_features).transpose(1, 0, 2)
    shares = lax.all_to_all(terms, "vocab", split_axis=0, concat_axis=0, tiled=True)
    grad_hidden = jnp.sum(shares.astype(jnp.float32), axis=0)
    return (grad_hidden.astype(jnp.bfloat16), loss)


def any_shards(*arrays):
    count = lax.axis_size("vocab")
    pair_width = 2 * arrays[0].shape[1]
    if count > 2 and count & (count - 1) == 0 and pair_width % LANES == 0:
        return paired_shards(*arrays)
    return shards(*arrays)


def solution(mesh):
    in_specs = (
        P("dom", "vocab"),
        P("vocab", None),
        P(("dom", "vocab"), None),
        P(("dom", "vocab"), None),
        P("dom"),
        P("dom"),
        P("dom"),
        P(),
    )
    out_specs = (P("dom", "vocab"), P("dom"))
    return jax.shard_map(
        any_shards, mesh=mesh, in_specs=in_specs, out_specs=out_specs, check_vma=False
    )
```

```python
import functools

import jax
import jax.numpy as jnp
from jax import lax
from jax.experimental import pallas as pl
from jax.experimental.pallas import tpu as pltpu
from jax.sharding import PartitionSpec as P

BLOCK = 32
LANES = 128
STATS = 8


sample_weight = 0.5


def to_all(piece, count):
    copies = jnp.broadcast_to(piece[None], (count,) + piece.shape)
    return lax.all_to_all(copies, "vocab", split_axis=0, concat_axis=0, tiled=True)


def scaled_teacher(teacher_values, teacher_scales, count, shard_rows):
    slot_rows = teacher_values.shape[0]
    scaled = (
        teacher_values.astype(jnp.float32).reshape(slot_rows, -1, BLOCK) * teacher_scales[:, :, None]
    ).astype(jnp.bfloat16)
    return scaled.reshape(slot_rows, count, shard_rows).transpose(1, 0, 2)


def merge_stats(tops, sums, teacher_tops, teacher_sums, crosses):
    top = jnp.max(tops, axis=0)
    teacher_top = jnp.max(teacher_tops, axis=0)
    shift = tops - top[None]
    teacher_shift = teacher_tops - teacher_top[None]
    weight = jnp.exp(shift)
    total = jnp.sum(sums * weight, axis=0)
    teacher_total = jnp.sum(teacher_sums * jnp.exp(teacher_shift), axis=0)
    cross = jnp.sum(weight * (crosses + sums * (shift - teacher_shift)), axis=0)
    return top, total, teacher_top, teacher_total, cross


def swap_cores(array):
    count = lax.axis_size("vocab")
    return lax.ppermute(array, "vocab", [(i, i ^ 1) for i in range(count)])


def across_chips(blocks):
    count = lax.axis_size("vocab")
    groups = [list(range(core, count, 2)) for core in range(2)]
    return lax.all_to_all(
        blocks, "vocab", split_axis=0, concat_axis=0, axis_index_groups=groups, tiled=True
    )


def along_chips(array, step):
    count = lax.axis_size("vocab")
    return lax.ppermute(array, "vocab", [(i, (i + 2 * step) % count) for i in range(count)])


def vmem_array(shape, dtype):
    return pltpu.VMEM(shape, dtype)


def in_vmem(array):
    return pltpu.with_memory_space_constraint(array, pltpu.VMEM)


def in_hbm(array):
    return pltpu.with_memory_space_constraint(array, pltpu.HBM)


def column_of(row):
    size = row.shape[1]
    down = lax.broadcasted_iota(jnp.int32, (size, size), 0)
    along = lax.broadcasted_iota(jnp.int32, (size, size), 1)
    return jnp.sum(jnp.where(down == along, row, jnp.zeros_like(row)), axis=1, keepdims=True)


def prepare_kernel(
    place_ref, lengths_ref, scale_ref, ids_ref, map_ref, owner_ref, tokens_ref, *, shard_rows
):
    tokens = map_ref.shape[1]
    token = lax.broadcasted_iota(jnp.int32, (tokens, tokens), 0)
    slot = lax.broadcasted_iota(jnp.int32, (tokens, tokens), 1)
    owner = (map_ref[...] == token).astype(jnp.float32)
    named = jnp.max(owner, axis=1, keepdims=True)
    owner = jnp.where((slot == 0) & (named == 0.0), 1.0, owner)
    owner_ref[...] = owner.astype(jnp.bfloat16)

    seqs = lengths_ref.shape[0]
    seq_length = tokens // seqs
    position = lax.broadcasted_iota(jnp.int32, (tokens, 1), 0)
    live_until = jnp.zeros((tokens, 1), jnp.int32)
    for seq in range(seqs):
        inside = (position >= seq * seq_length) & (position < (seq + 1) * seq_length)
        live_until = jnp.where(inside, lengths_ref[seq] + seq * seq_length, live_until)
    live = (position < live_until).astype(jnp.float32)
    share = live / jnp.sum(live, axis=0, keepdims=True)
    weight = live * scale_ref[0] / jnp.sum(live, axis=0, keepdims=True)
    entry = (column_of(ids_ref[...]) - place_ref[0] * shard_rows).astype(jnp.float32)
    lane = lax.broadcasted_iota(jnp.int32, (tokens, LANES), 1)
    tokens_ref[...] = jnp.where(lane == 0, entry, jnp.where(lane == 1, share, weight))


def head_copies(head_ref, held_ref, sems, first):
    chips, _, width = held_ref.shape
    copies = []
    for step in range(chips):
        columns = pl.ds(pl.multiple_of(lax.rem(first + step, chips) * width, LANES), width)
        copies.append(
            pltpu.make_async_copy(head_ref.at[:, columns], held_ref.at[step], sems.at[step])
        )
    return copies


def logits_kernel(place_ref, own_ref, other_ref, head_ref, logits_ref, held_ref, sems):
    copies = head_copies(head_ref, held_ref, sems, 0)
    for copy in copies:
        copy.start()
    core = place_ref[0] % 2
    logits = jnp.zeros(logits_ref.shape, jnp.float32)
    for chip, copy in enumerate(copies):
        own, other = own_ref[chip], other_ref[chip]
        block = jnp.where(
            core == 0,
            jnp.concatenate([own, other], axis=1),
            jnp.concatenate([other, own], axis=1),
        )
        copy.wait()
        logits += lax.dot_general(
            block, held_ref[chip], (((1,), (1,)), ((), ())), preferred_element_type=jnp.float32
        )
    logits_ref[...] = logits


def softmax_kernel(logits_ref, arrived_ref, owner_ref, tokens_ref, rows_ref, stats_ref):
    tokens, shard_rows = logits_ref.shape
    logits = logits_ref[...]
    teacher = jnp.dot(owner_ref[...], arrived_ref[...], preferred_element_type=jnp.float32)
    top = jnp.max(logits, axis=1, keepdims=True)
    teacher_top = jnp.max(teacher, axis=1, keepdims=True)
    off = logits - top
    teacher_off = teacher - teacher_top
    exps = jnp.exp(off)
    total = jnp.sum(exps, axis=1, keepdims=True)
    teacher_total = jnp.sum(jnp.exp(teacher_off), axis=1, keepdims=True)
    gap = off - teacher_off
    cross = jnp.sum(exps * gap, axis=1, keepdims=True)
    centre = cross / total
    entry = lax.broadcasted_iota(jnp.int32, (tokens, shard_rows), 1)
    hit = entry == tokens_ref[:, :1].astype(jnp.int32)
    target = jnp.sum(jnp.where(hit, logits, 0.0), axis=1, keepdims=True)
    rows_ref[:tokens] = (exps * (gap - centre)).astype(jnp.bfloat16)
    rows_ref[tokens : 2 * tokens] = exps.astype(jnp.bfloat16)
    rows_ref[2 * tokens :] = hit.astype(jnp.bfloat16)

    lane = lax.broadcasted_iota(jnp.int32, (tokens, LANES), 1)
    table = jnp.zeros((tokens, LANES), jnp.float32)
    for place, column in enumerate(
        (top, total, teacher_top, teacher_total, cross, target, centre)
    ):
        table = jnp.where(lane == place, column, table)
    stats = jnp.concatenate([table, jnp.zeros((stats_ref.shape[2] - tokens, LANES), jnp.float32)])
    stats_ref[...] = jnp.broadcast_to(stats.T[None, :STATS], stats_ref.shape)


def products_kernel(place_ref, rows_ref, head_ref, terms_ref, picks_ref, held_ref, sems):
    copies = head_copies(head_ref, held_ref, sems, place_ref[0] // 2)
    for copy in copies:
        copy.start()
    sums_rows = terms_ref.shape[1]
    for step, copy in enumerate(copies):
        copy.wait()
        products = jnp.dot(rows_ref[...], held_ref[step], preferred_element_type=jnp.float32)
        terms_ref[step] = products[:sums_rows]
        picks_ref[step] = products[sums_rows:].astype(jnp.bfloat16)


def combine_kernel(
    place_ref, stats_ref, own_ref, tokens_ref, terms_ref, picks_ref, keep_ref, give_ref, loss_ref
):
    core = place_ref[0] % 2
    chips, _, width = terms_ref.shape
    tokens = tokens_ref.shape[0]
    half = width // 2
    tops, sums, teacher_tops, teacher_sums, crosses, targets = [
        stats_ref[:, i, :tokens] for i in range(6)
    ]
    top, total, teacher_top, teacher_total, cross = [
        part[None] for part in merge_stats(tops, sums, teacher_tops, teacher_sums, crosses)
    ]
    target = jnp.sum(targets, axis=0, keepdims=True)
    student_log = jnp.log(total)
    teacher_log = jnp.log(teacher_total)
    divergence = cross / total - (student_log - teacher_log)
    student_lse = top + student_log
    per_token = divergence + sample_weight * (student_lse - target)
    student_shift = own_ref[0, 0:1, :tokens] - top - student_log
    teacher_shift = own_ref[0, 2:3, :tokens] - teacher_top - teacher_log
    factor = jnp.exp(student_shift)
    level = (
        own_ref[0, 6:7, :tokens] + student_shift - teacher_shift - divergence + sample_weight
    )
    zeros = jnp.zeros((LANES - 3, tokens), jnp.float32)
    columns = jnp.concatenate([factor, level, per_token, zeros], axis=0).T
    share, weight = tokens_ref[:, 1:2], tokens_ref[:, 2:3]
    loss_ref[...] = jnp.sum(share * columns[:, 2:3], axis=0, keepdims=True)
    factor = weight * columns[:, 0:1]
    level = columns[:, 1:2]
    weight = sample_weight * weight
    for step in range(chips):
        block = (
            factor * (terms_ref[step, :tokens] + level * terms_ref[step, tokens:])
            - weight * picks_ref[step].astype(jnp.float32)
        )
        first, second = block[:, :half], block[:, half:]
        keep_ref[step] = jnp.where(core == 0, first, second)
        give_ref[step] = jnp.where(core == 0, second, first).astype(jnp.bfloat16)


def sum_kernel(own_ref, *refs):
    total = own_ref[...]
    for share_ref in refs[:-1]:
        total += share_ref[...].astype(jnp.float32)
    refs[-1][...] = total.astype(refs[-1].dtype)


def paired_shards(
    hidden_states, head, teacher_values, teacher_scales, token_ids, lengths, row_map, loss_scale
):
    count = lax.axis_size("vocab")
    own_index = lax.axis_index("vocab")
    chips = count // 2
    tokens, half = hidden_states.shape
    width = 2 * half
    shard_rows = head.shape[0]
    place = jnp.reshape(own_index, (1,))
    vmem = pl.BlockSpec(memory_space=pltpu.VMEM)
    smem = pl.BlockSpec(memory_space=pltpu.SMEM)
    hbm = pl.BlockSpec(memory_space=pl.ANY)
    params = pltpu.CompilerParams(vmem_limit_bytes=VMEM_LIMIT)
    head = in_hbm(head)
    head_scratch = [
        pltpu.VMEM((chips, shard_rows, width), head.dtype),
        pltpu.SemaphoreType.DMA((chips,)),
    ]

    gathered = across_chips(jnp.broadcast_to(hidden_states[None], (chips, tokens, half)))
    scaled = scaled_teacher(teacher_values, teacher_scales, count, shard_rows)
    gathered, scaled = lax.optimization_barrier((gathered, scaled))
    other = swap_cores(gathered)
    arrived = lax.all_to_all(scaled, "vocab", split_axis=0, concat_axis=0, tiled=True)
    arrived = arrived.reshape(tokens, shard_rows)

    owner, table = pl.pallas_call(
        functools.partial(prepare_kernel, shard_rows=shard_rows),
        out_shape=(
            vmem_array((tokens, tokens), jnp.bfloat16),
            vmem_array((tokens, LANES), jnp.float32),
        ),
        in_specs=[smem] * 3 + [vmem] * 2,
        out_specs=[vmem] * 2,
        compiler_params=params,
        name="prepare",
    )(place, lengths, loss_scale, token_ids[None, :], row_map[None, :])

    logits = pl.pallas_call(
        logits_kernel,
        out_shape=vmem_array((tokens, shard_rows), jnp.float32),
        in_specs=[smem] + [vmem] * 2 + [hbm],
        out_specs=vmem,
        scratch_shapes=head_scratch,
        compiler_params=params,
        cost_estimate=pl.CostEstimate(
            flops=2 * tokens * head.size, bytes_accessed=2 * head.size, transcendentals=0
        ),
        name="logits",
    )(place, gathered, other, head)

    rows, stats = pl.pallas_call(
        softmax_kernel,
        out_shape=(
            jax.ShapeDtypeStruct((3 * tokens, shard_rows), jnp.bfloat16),
            jax.ShapeDtypeStruct((count, STATS, pl.cdiv(tokens, LANES) * LANES), jnp.float32),
        ),
        in_specs=[vmem] * 4,
        out_specs=[vmem] * 2,
        compiler_params=params,
        name="softmax",
    )(in_vmem(logits), arrived, in_vmem(owner), in_vmem(table))

    all_stats = lax.all_to_all(stats, "vocab", split_axis=0, concat_axis=0, tiled=True)

    terms, picks = pl.pallas_call(
        products_kernel,
        out_shape=(
            vmem_array((chips, 2 * tokens, width), jnp.float32),
            vmem_array((chips, tokens, width), jnp.bfloat16),
        ),
        in_specs=[smem, vmem, hbm],
        out_specs=[vmem] * 2,
        scratch_shapes=head_scratch,
        compiler_params=params,
        cost_estimate=pl.CostEstimate(
            flops=6 * tokens * head.size, bytes_accessed=2 * head.size, transcendentals=0
        ),
        name="products",
    )(place, rows, head)

    keep, give, loss = pl.pallas_call(
        combine_kernel,
        out_shape=(
            vmem_array((chips, tokens, half), jnp.float32),
            vmem_array((chips, tokens, half), jnp.bfloat16),
            jax.ShapeDtypeStruct((1, 1), jnp.float32),
        ),
        in_specs=[smem] + [vmem] * 5,
        out_specs=[vmem] * 3,
        compiler_params=params,
        name="combine",
    )(
        place,
        all_stats,
        stats,
        in_vmem(table),
        in_vmem(terms),
        in_vmem(picks),
    )

    sums = keep + swap_cores(give).astype(jnp.float32)
    shares = [along_chips(sums[step].astype(jnp.bfloat16), step) for step in range(1, chips)]
    total = pl.pallas_call(
        sum_kernel,
        out_shape=jax.ShapeDtypeStruct((tokens, half), jnp.bfloat16),
        in_specs=[vmem] * chips,
        out_specs=vmem,
        compiler_params=params,
        name="total",
    )(sums[0], *shares)
    return total, jnp.reshape(loss, (1,))


VMEM_LIMIT = 24 * 1024 * 1024


def shards(
    hidden_states, head, teacher_values, teacher_scales, token_ids, lengths, row_map, loss_scale
):
    count = lax.axis_size("vocab")
    own_index = lax.axis_index("vocab")
    tokens = hidden_states.shape[0]
    own_features = hidden_states.shape[1]
    shard_rows = head.shape[0]
    seq_length = tokens // lengths.shape[0]
    contract_last = (((1,), (1,)), ((), ()))

    scaled = scaled_teacher(teacher_values, teacher_scales, count, shard_rows)
    arrived = lax.all_to_all(scaled, "vocab", split_axis=0, concat_axis=0, tiled=True)
    arrived = arrived.reshape(tokens, shard_rows)
    gathered = to_all(hidden_states, count).transpose(1, 0, 2).reshape(tokens, -1)
    logits = lax.dot_general(gathered, head, contract_last, preferred_element_type=jnp.float32)

    positions = jnp.arange(tokens, dtype=jnp.int32)
    owner = row_map[None, :] == positions[:, None]
    slot_of = jnp.sum(jnp.where(owner, positions[None, :], 0), axis=1)
    teacher = jnp.take(arrived, slot_of, axis=0).astype(jnp.float32)

    seq_ids = jnp.arange(lengths.shape[0], dtype=jnp.int32)
    own_length = jnp.sum(
        jnp.where((positions // seq_length)[:, None] == seq_ids[None, :], lengths[None, :], 0),
        axis=1,
    )
    live_mask = (positions % seq_length < own_length).astype(jnp.float32)
    live_count = jnp.sum(live_mask)

    local_ids = token_ids - own_index * shard_rows
    target_hit = local_ids[:, None] == jnp.arange(shard_rows, dtype=jnp.int32)[None, :]
    target_part = jnp.sum(jnp.where(target_hit, logits, 0.0), axis=1)
    student_top = jnp.max(logits, axis=1)
    teacher_top = jnp.max(teacher, axis=1)
    student_off = logits - student_top[:, None]
    teacher_off = teacher - teacher_top[:, None]
    student_exp = jnp.exp(student_off)
    student_sum = jnp.sum(student_exp, axis=1)
    teacher_sum = jnp.sum(jnp.exp(teacher_off), axis=1)
    cross_sum = jnp.sum(student_exp * (student_off - teacher_off), axis=1)

    stats = to_all(
        jnp.stack(
            [student_top, student_sum, teacher_top, teacher_sum, cross_sum, target_part]
        ),
        count,
    )
    tops, sums, teacher_tops, teacher_sums, crosses, targets = [stats[:, i] for i in range(6)]
    student_max, student_total, teacher_max, teacher_total, cross_total = merge_stats(
        tops, sums, teacher_tops, teacher_sums, crosses
    )
    student_log = jnp.log(student_total)
    teacher_log = jnp.log(teacher_total)
    student_lse = student_max + student_log
    teacher_lse = teacher_max + teacher_log
    divergence = cross_total / student_total - (student_log - teacher_log)
    target = jnp.sum(targets, axis=0)

    per_token = divergence + sample_weight * (student_lse - target)
    loss = jnp.reshape(jnp.sum(live_mask * per_token) / live_count, (1,))
    token_weight = live_mask * loss_scale[0] / live_count
    log_student = logits - student_lse[:, None]
    log_teacher = teacher - teacher_lse[:, None]
    student_prob = jnp.exp(log_student)
    grad_logits = (
        token_weight[:, None]
        * (
            student_prob * (log_student - log_teacher - divergence[:, None])
            + sample_weight * (student_prob - target_hit.astype(jnp.float32))
        )
    ).astype(jnp.bfloat16)
    terms = jnp.dot(grad_logits, head, preferred_element_type=jnp.float32).astype(jnp.bfloat16)
    terms = terms.reshape(tokens, count, own_features).transpose(1, 0, 2)
    shares = lax.all_to_all(terms, "vocab", split_axis=0, concat_axis=0, tiled=True)
    grad_hidden = jnp.sum(shares.astype(jnp.float32), axis=0)
    return (grad_hidden.astype(jnp.bfloat16), loss)


def any_shards(*arrays):
    count = lax.axis_size("vocab")
    pair_width = 2 * arrays[0].shape[1]
    if count > 2 and count & (count - 1) == 0 and pair_width % LANES == 0:
        return paired_shards(*arrays)
    return shards(*arrays)


def solution(mesh):
    in_specs = (
        P("dom", "vocab"),
        P("vocab", None),
        P(("dom", "vocab"), None),
        P(("dom", "vocab"), None),
        P("dom"),
        P("dom"),
        P("dom"),
        P(),
    )
    out_specs = (P("dom", "vocab"), P("dom"))
    return jax.shard_map(
        any_shards, mesh=mesh, in_specs=in_specs, out_specs=out_specs, check_vma=False
    )
```

```python
import functools

import jax
import jax.numpy as jnp
from jax import lax
from jax.experimental import pallas as pl
from jax.experimental.pallas import tpu as pltpu
from jax.sharding import PartitionSpec as P

BLOCK = 32
LANES = 128
STATS = 8


sample_weight = 0.5


def to_all(piece, count):
    copies = jnp.broadcast_to(piece[None], (count,) + piece.shape)
    return lax.all_to_all(copies, "vocab", split_axis=0, concat_axis=0, tiled=True)


def scaled_teacher(teacher_values, teacher_scales, count, shard_rows):
    slot_rows = teacher_values.shape[0]
    scaled = (
        teacher_values.astype(jnp.float32).reshape(slot_rows, -1, BLOCK) * teacher_scales[:, :, None]
    ).astype(jnp.bfloat16)
    return scaled.reshape(slot_rows, count, shard_rows).transpose(1, 0, 2)


def merge_stats(tops, sums, teacher_tops, teacher_sums, crosses):
    top = jnp.max(tops, axis=0)
    teacher_top = jnp.max(teacher_tops, axis=0)
    shift = tops - top[None]
    teacher_shift = teacher_tops - teacher_top[None]
    weight = jnp.exp(shift)
    total = jnp.sum(sums * weight, axis=0)
    teacher_total = jnp.sum(teacher_sums * jnp.exp(teacher_shift), axis=0)
    cross = jnp.sum(weight * (crosses + sums * (shift - teacher_shift)), axis=0)
    return top, total, teacher_top, teacher_total, cross


def swap_cores(array):
    count = lax.axis_size("vocab")
    return lax.ppermute(array, "vocab", [(i, i ^ 1) for i in range(count)])


def across_chips(blocks):
    count = lax.axis_size("vocab")
    groups = [list(range(core, count, 2)) for core in range(2)]
    return lax.all_to_all(
        blocks, "vocab", split_axis=0, concat_axis=0, axis_index_groups=groups, tiled=True
    )


def along_chips(array, step):
    count = lax.axis_size("vocab")
    return lax.ppermute(array, "vocab", [(i, (i + 2 * step) % count) for i in range(count)])


def vmem_array(shape, dtype):
    return pltpu.VMEM(shape, dtype)


def in_vmem(array):
    return pltpu.with_memory_space_constraint(array, pltpu.VMEM)


def in_hbm(array):
    return pltpu.with_memory_space_constraint(array, pltpu.HBM)


def hbm_array(shape, dtype):
    return pltpu.HBM(shape, dtype)


def low_lanes(shape):
    return lax.broadcasted_iota(jnp.int32, shape, len(shape) - 1) < LANES // 2


def low_rows(shape, count):
    return lax.broadcasted_iota(jnp.int32, shape, 0) < count


def turned(array):
    return pltpu.roll(array, LANES // 2, 1)


def packed_half(tiles):
    rows = tiles[2].shape[0] // 2
    upper, lower = tiles[2][:rows], tiles[2][rows:]
    rest = jnp.where(low_lanes(upper.shape), upper, turned(lower))
    return jnp.concatenate([tiles[0], tiles[1], rest], axis=0)


def unpacked_half(packed, tokens):
    rest = packed[2 * tokens :]
    return [packed[:tokens], packed[tokens : 2 * tokens], jnp.concatenate([rest, turned(rest)])]


def joined(first, second):
    low = low_lanes(first[0].shape)
    turns = [turned(tile) for tile in second]
    return [
        first[0],
        first[1],
        jnp.where(low, first[2], turns[0]),
        jnp.where(low, turns[0], turns[1]),
        jnp.where(low, turns[1], turns[2]),
    ]


def parted(tiles):
    low = low_lanes(tiles[0].shape)
    turns = [turned(tile) for tile in tiles[2:]]
    return tiles[:3], [
        jnp.where(low, turns[0], turns[1]),
        jnp.where(low, turns[1], turns[2]),
        turns[2],
    ]


def column_of(row):
    size = row.shape[1]
    down = lax.broadcasted_iota(jnp.int32, (size, size), 0)
    along = lax.broadcasted_iota(jnp.int32, (size, size), 1)
    return jnp.sum(jnp.where(down == along, row, jnp.zeros_like(row)), axis=1, keepdims=True)


def pack_kernel(hidden_ref, values_ref, scales_ref, packed_ref, wide_ref):
    chips = packed_ref.shape[0]
    tokens, half = hidden_ref.shape
    slots, entries = values_ref.shape
    pair = entries // chips
    shard = pair // 2
    blocks = pair // BLOCK
    scales = jnp.concatenate([scales_ref[...]] * 2, axis=0)
    stacked = jnp.concatenate(
        [scales[:, blocks * chip : blocks * (chip + 1)] for chip in range(chips)], axis=0
    )
    block = lax.broadcasted_iota(jnp.int32, (blocks, pair), 0)
    entry = lax.broadcasted_iota(jnp.int32, (blocks, pair), 1)
    inside = (entry >= block * BLOCK) & (entry < block * BLOCK + BLOCK)
    spread = jnp.dot(
        stacked.astype(jnp.bfloat16),
        inside.astype(jnp.bfloat16),
        preferred_element_type=jnp.float32,
    )
    values = values_ref[...].astype(jnp.float32)
    values = jnp.concatenate([values, values], axis=0)
    for chip in range(chips):
        wide_ref[:, pair * chip : pair * (chip + 1)] = (
            values[:, pair * chip : pair * (chip + 1)]
            * spread[2 * slots * chip : 2 * slots * (chip + 1)]
        )
    wide_ref[:, entries:] = jnp.zeros((2 * slots, LANES), jnp.float32)

    hidden = hidden_ref[...].astype(jnp.float32)
    hidden = jnp.concatenate([hidden, jnp.zeros((tokens, LANES // 2), jnp.float32)], axis=1)
    hidden = packed_half([hidden[:, LANES * i : LANES * (i + 1)] for i in range(3)])
    hidden = hidden.astype(jnp.bfloat16)
    hidden_rows = hidden.shape[0]
    upper = low_rows((2 * slots, LANES), slots)
    low = low_lanes((2 * slots, LANES))
    tile_pairs = (shard + LANES // 2) // LANES // 2
    for chip in range(chips):
        rows = []
        for core in range(2):
            start = pair * chip + (shard - LANES // 2) * core
            tiles = [
                wide_ref[:, start + LANES * i : start + LANES * (i + 1)]
                for i in range(2 * tile_pairs + core)
            ]
            if core == 1:
                tiles = [turned(tile) for tile in tiles]
                tiles = [
                    jnp.where(low, tiles[i], tiles[i + 1]) for i in range(2 * tile_pairs)
                ]
            rows += [
                jnp.where(upper, tiles[2 * i], tiles[2 * i + 1]) for i in range(tile_pairs)
            ]
        packed_ref[chip, :hidden_rows] = hidden
        packed_ref[chip, hidden_rows:] = jnp.concatenate(rows, axis=0).astype(jnp.bfloat16)


def prepare_kernel(
    place_ref, lengths_ref, scale_ref, ids_ref, map_ref, owner_ref, tokens_ref, *, shard_rows
):
    tokens = map_ref.shape[1]
    token = lax.broadcasted_iota(jnp.int32, (tokens, tokens), 0)
    slot = lax.broadcasted_iota(jnp.int32, (tokens, tokens), 1)
    owner = (map_ref[...] == token).astype(jnp.float32)
    named = jnp.max(owner, axis=1, keepdims=True)
    owner = jnp.where((slot == 0) & (named == 0.0), 1.0, owner)
    owner_ref[...] = owner.astype(jnp.bfloat16)

    seqs = lengths_ref.shape[0]
    seq_length = tokens // seqs
    position = lax.broadcasted_iota(jnp.int32, (tokens, 1), 0)
    live_until = jnp.zeros((tokens, 1), jnp.int32)
    for seq in range(seqs):
        inside = (position >= seq * seq_length) & (position < (seq + 1) * seq_length)
        live_until = jnp.where(inside, lengths_ref[seq] + seq * seq_length, live_until)
    live = (position < live_until).astype(jnp.float32)
    share = live / jnp.sum(live, axis=0, keepdims=True)
    weight = live * scale_ref[0] / jnp.sum(live, axis=0, keepdims=True)
    entry = (column_of(ids_ref[...]) - place_ref[0] * shard_rows).astype(jnp.float32)
    lane = lax.broadcasted_iota(jnp.int32, (tokens, LANES), 1)
    tokens_ref[...] = jnp.where(lane == 0, entry, jnp.where(lane == 1, share, weight))


def head_copies(head_ref, held_ref, sems, first):
    chips, _, width = held_ref.shape
    copies = []
    for step in range(chips):
        columns = pl.ds(pl.multiple_of(lax.rem(first + step, chips) * width, LANES), width)
        copies.append(
            pltpu.make_async_copy(head_ref.at[:, columns], held_ref.at[step], sems.at[step])
        )
    return copies


def logits_kernel(
    place_ref,
    own_ref,
    other_ref,
    owner_ref,
    tokens_ref,
    head_ref,
    rows_ref,
    stats_ref,
    held_ref,
    made_ref,
    hidden_ref,
    arrived_ref,
    sems,
    made_sem,
):
    copies = head_copies(head_ref, held_ref, sems, 0)
    for copy in copies:
        copy.start()
    core = place_ref[0] % 2
    chips, tokens, width = hidden_ref.shape
    shard_rows = head_ref.shape[0]
    hidden_rows = tokens * width // 2 // LANES
    slots = tokens // (2 * chips)
    upper = low_rows((2 * slots, LANES), slots)
    for chip in range(chips):
        own, other = own_ref[chip].astype(jnp.float32), other_ref[chip].astype(jnp.float32)
        first = jnp.where(core == 0, own, other)
        second = jnp.where(core == 0, other, own)
        tiles = joined(
            unpacked_half(first[:hidden_rows], tokens),
            unpacked_half(second[:hidden_rows], tokens),
        )
        hidden_ref[chip] = jnp.concatenate(tiles, axis=1).astype(jnp.bfloat16)
        first, second = first[hidden_rows:], second[hidden_rows:]
        share = first.shape[0] // 2
        first = jnp.where(core == 0, first[:share], first[share:])
        second = jnp.where(core == 0, second[:share], second[share:])
        tiles = []
        for row in range(0, share, 2 * slots):
            one, two = first[row : row + 2 * slots], second[row : row + 2 * slots]
            tiles.append(jnp.where(upper, one, pltpu.roll(two, slots, 0)))
            tiles.append(jnp.where(upper, pltpu.roll(one, slots, 0), two))
        arrived_ref[2 * slots * chip : 2 * slots * (chip + 1)] = jnp.concatenate(tiles, axis=1)
    teacher = jnp.dot(
        owner_ref[...],
        arrived_ref[:, :shard_rows].astype(jnp.bfloat16),
        preferred_element_type=jnp.float32,
    )
    logits = jnp.zeros((tokens, shard_rows), jnp.float32)
    for chip, copy in enumerate(copies):
        copy.wait()
        logits += lax.dot_general(
            hidden_ref[chip],
            held_ref[chip],
            (((1,), (1,)), ((), ())),
            preferred_element_type=jnp.float32,
        )

    top = jnp.max(logits, axis=1, keepdims=True)
    teacher_top = jnp.max(teacher, axis=1, keepdims=True)
    off = logits - top
    teacher_off = teacher - teacher_top
    exps = jnp.exp(off)
    total = jnp.sum(exps, axis=1, keepdims=True)
    teacher_total = jnp.sum(jnp.exp(teacher_off), axis=1, keepdims=True)
    gap = off - teacher_off
    cross = jnp.sum(exps * gap, axis=1, keepdims=True)
    centre = cross / total
    entry = lax.broadcasted_iota(jnp.int32, (tokens, shard_rows), 1)
    hit = entry == tokens_ref[:, :1].astype(jnp.int32)
    target = jnp.sum(jnp.where(hit, logits, 0.0), axis=1, keepdims=True)
    made_ref[:tokens] = (exps * (gap - centre)).astype(jnp.bfloat16)
    made_ref[tokens : 2 * tokens] = exps.astype(jnp.bfloat16)
    made_ref[2 * tokens :] = hit.astype(jnp.bfloat16)
    out = pltpu.make_async_copy(made_ref, rows_ref, made_sem)
    out.start()

    lane = lax.broadcasted_iota(jnp.int32, (tokens, LANES), 1)
    table = jnp.zeros((tokens, LANES), jnp.float32)
    for place, column in enumerate(
        (top, total, teacher_top, teacher_total, cross, target, centre)
    ):
        table = jnp.where(lane == place, column, table)
    stats = jnp.concatenate([table, jnp.zeros((stats_ref.shape[2] - tokens, LANES), jnp.float32)])
    stats_ref[...] = jnp.broadcast_to(stats.T[None, :STATS], stats_ref.shape)
    out.wait()


def products_kernel(
    place_ref, rows_ref, head_ref, terms_ref, picks_ref, held_ref, made_ref, sems, made_sem
):
    into = pltpu.make_async_copy(rows_ref, made_ref, made_sem)
    into.start()
    copies = head_copies(head_ref, held_ref, sems, place_ref[0] // 2)
    for copy in copies:
        copy.start()
    into.wait()
    sums_rows = terms_ref.shape[1]
    for step, copy in enumerate(copies):
        copy.wait()
        products = jnp.dot(made_ref[...], held_ref[step], preferred_element_type=jnp.float32)
        terms_ref[step] = products[:sums_rows]
        picks_ref[step] = products[sums_rows:].astype(jnp.bfloat16)


def combine_kernel(
    place_ref, stats_ref, own_ref, tokens_ref, terms_ref, picks_ref, keep_ref, give_ref, loss_ref
):
    core = place_ref[0] % 2
    chips, _, width = terms_ref.shape
    tokens = tokens_ref.shape[0]
    tops, sums, teacher_tops, teacher_sums, crosses, targets = [
        stats_ref[:, i, :tokens] for i in range(6)
    ]
    top, total, teacher_top, teacher_total, cross = [
        part[None] for part in merge_stats(tops, sums, teacher_tops, teacher_sums, crosses)
    ]
    target = jnp.sum(targets, axis=0, keepdims=True)
    student_log = jnp.log(total)
    teacher_log = jnp.log(teacher_total)
    divergence = cross / total - (student_log - teacher_log)
    student_lse = top + student_log
    per_token = divergence + sample_weight * (student_lse - target)
    student_shift = own_ref[0, 0:1, :tokens] - top - student_log
    teacher_shift = own_ref[0, 2:3, :tokens] - teacher_top - teacher_log
    factor = jnp.exp(student_shift)
    level = (
        own_ref[0, 6:7, :tokens] + student_shift - teacher_shift - divergence + sample_weight
    )
    zeros = jnp.zeros((LANES - 3, tokens), jnp.float32)
    columns = jnp.concatenate([factor, level, per_token, zeros], axis=0).T
    share, weight = tokens_ref[:, 1:2], tokens_ref[:, 2:3]
    loss_ref[...] = jnp.sum(share * columns[:, 2:3], axis=0, keepdims=True)
    factor = weight * columns[:, 0:1]
    level = columns[:, 1:2]
    weight = sample_weight * weight
    for step in range(chips):
        block = (
            factor * (terms_ref[step, :tokens] + level * terms_ref[step, tokens:])
            - weight * picks_ref[step].astype(jnp.float32)
        )
        first, second = parted([block[:, i : i + LANES] for i in range(0, width, LANES)])
        first, second = packed_half(first), packed_half(second)
        keep_ref[step] = jnp.where(core == 0, first, second)
        give_ref[step] = jnp.where(core == 0, second, first).astype(jnp.bfloat16)


def sum_kernel(own_ref, *refs):
    tokens, half = refs[-1].shape
    total = own_ref[...]
    for share_ref in refs[:-1]:
        total += share_ref[...].astype(jnp.float32)
    tiles = jnp.concatenate(unpacked_half(total, tokens), axis=1)
    refs[-1][...] = tiles[:, :half].astype(refs[-1].dtype)


def paired_shards(
    hidden_states, head, teacher_values, teacher_scales, token_ids, lengths, row_map, loss_scale
):
    count = lax.axis_size("vocab")
    own_index = lax.axis_index("vocab")
    chips = count // 2
    tokens, half = hidden_states.shape
    width = 2 * half
    shard_rows = head.shape[0]
    place = jnp.reshape(own_index, (1,))
    vmem = pl.BlockSpec(memory_space=pltpu.VMEM)
    smem = pl.BlockSpec(memory_space=pltpu.SMEM)
    hbm = pl.BlockSpec(memory_space=pl.ANY)
    params = pltpu.CompilerParams(vmem_limit_bytes=VMEM_LIMIT)
    head = in_hbm(head)
    head_scratch = pltpu.VMEM((chips, shard_rows, width), head.dtype)
    head_sems = pltpu.SemaphoreType.DMA((chips,))
    rows_scratch = pltpu.VMEM((3 * tokens, shard_rows), jnp.bfloat16)
    rows_sem = pltpu.SemaphoreType.DMA
    slots, entries = teacher_values.shape
    hidden_rows = tokens * half // LANES
    teacher_rows = 2 * slots * (shard_rows + LANES // 2) // LANES

    packed = pl.pallas_call(
        pack_kernel,
        out_shape=jax.ShapeDtypeStruct((chips, hidden_rows + teacher_rows, LANES), jnp.bfloat16),
        in_specs=[vmem] * 3,
        out_specs=vmem,
        scratch_shapes=[pltpu.VMEM((2 * slots, entries + LANES), jnp.float32)],
        compiler_params=params,
        name="pack",
    )(hidden_states, teacher_values, teacher_scales)
    gathered = across_chips(packed)
    other = swap_cores(gathered)

    owner, table = pl.pallas_call(
        functools.partial(prepare_kernel, shard_rows=shard_rows),
        out_shape=(
            vmem_array((tokens, tokens), jnp.bfloat16),
            vmem_array((tokens, LANES), jnp.float32),
        ),
        in_specs=[smem] * 3 + [vmem] * 2,
        out_specs=[vmem] * 2,
        compiler_params=params,
        name="prepare",
    )(place, lengths, loss_scale, token_ids[None, :], row_map[None, :])

    rows, stats = pl.pallas_call(
        logits_kernel,
        out_shape=(
            hbm_array((3 * tokens, shard_rows), jnp.bfloat16),
            jax.ShapeDtypeStruct((count, STATS, pl.cdiv(tokens, LANES) * LANES), jnp.float32),
        ),
        in_specs=[smem] + [vmem] * 4 + [hbm],
        out_specs=[hbm, vmem],
        scratch_shapes=[
            head_scratch,
            rows_scratch,
            pltpu.VMEM((chips, tokens, width), jnp.bfloat16),
            pltpu.VMEM((tokens, shard_rows + LANES // 2), jnp.float32),
            head_sems,
            rows_sem,
        ],
        compiler_params=params,
        cost_estimate=pl.CostEstimate(
            flops=2 * tokens * head.size, bytes_accessed=2 * head.size, transcendentals=0
        ),
        name="logits",
    )(place, gathered, other, in_vmem(owner), in_vmem(table), head)

    all_stats = lax.all_to_all(stats, "vocab", split_axis=0, concat_axis=0, tiled=True)

    terms, picks = pl.pallas_call(
        products_kernel,
        out_shape=(
            vmem_array((chips, 2 * tokens, width), jnp.float32),
            vmem_array((chips, tokens, width), jnp.bfloat16),
        ),
        in_specs=[smem, hbm, hbm],
        out_specs=[vmem] * 2,
        scratch_shapes=[head_scratch, rows_scratch, head_sems, rows_sem],
        compiler_params=params,
        cost_estimate=pl.CostEstimate(
            flops=6 * tokens * head.size, bytes_accessed=2 * head.size, transcendentals=0
        ),
        name="products",
    )(place, in_hbm(rows), head)

    keep, give, loss = pl.pallas_call(
        combine_kernel,
        out_shape=(
            vmem_array((chips, hidden_rows, LANES), jnp.float32),
            vmem_array((chips, hidden_rows, LANES), jnp.bfloat16),
            jax.ShapeDtypeStruct((1, 1), jnp.float32),
        ),
        in_specs=[smem] + [vmem] * 5,
        out_specs=[vmem] * 3,
        compiler_params=params,
        name="combine",
    )(
        place,
        all_stats,
        stats,
        in_vmem(table),
        in_vmem(terms),
        in_vmem(picks),
    )

    sums = keep + swap_cores(give).astype(jnp.float32)
    steps = range(chips - 1, 0, -1)
    shares = [along_chips(sums[step].astype(jnp.bfloat16), step) for step in steps]
    total = pl.pallas_call(
        sum_kernel,
        out_shape=jax.ShapeDtypeStruct((tokens, half), jnp.bfloat16),
        in_specs=[vmem] * chips,
        out_specs=vmem,
        compiler_params=params,
        name="total",
    )(sums[0], *shares)
    return total, jnp.reshape(loss, (1,))


VMEM_LIMIT = 24 * 1024 * 1024


def shards(
    hidden_states, head, teacher_values, teacher_scales, token_ids, lengths, row_map, loss_scale
):
    count = lax.axis_size("vocab")
    own_index = lax.axis_index("vocab")
    tokens = hidden_states.shape[0]
    own_features = hidden_states.shape[1]
    shard_rows = head.shape[0]
    seq_length = tokens // lengths.shape[0]
    contract_last = (((1,), (1,)), ((), ()))

    scaled = scaled_teacher(teacher_values, teacher_scales, count, shard_rows)
    arrived = lax.all_to_all(scaled, "vocab", split_axis=0, concat_axis=0, tiled=True)
    arrived = arrived.reshape(tokens, shard_rows)
    gathered = to_all(hidden_states, count).transpose(1, 0, 2).reshape(tokens, -1)
    logits = lax.dot_general(gathered, head, contract_last, preferred_element_type=jnp.float32)

    positions = jnp.arange(tokens, dtype=jnp.int32)
    owner = row_map[None, :] == positions[:, None]
    slot_of = jnp.sum(jnp.where(owner, positions[None, :], 0), axis=1)
    teacher = jnp.take(arrived, slot_of, axis=0).astype(jnp.float32)

    seq_ids = jnp.arange(lengths.shape[0], dtype=jnp.int32)
    own_length = jnp.sum(
        jnp.where((positions // seq_length)[:, None] == seq_ids[None, :], lengths[None, :], 0),
        axis=1,
    )
    live_mask = (positions % seq_length < own_length).astype(jnp.float32)
    live_count = jnp.sum(live_mask)

    local_ids = token_ids - own_index * shard_rows
    target_hit = local_ids[:, None] == jnp.arange(shard_rows, dtype=jnp.int32)[None, :]
    target_part = jnp.sum(jnp.where(target_hit, logits, 0.0), axis=1)
    student_top = jnp.max(logits, axis=1)
    teacher_top = jnp.max(teacher, axis=1)
    student_off = logits - student_top[:, None]
    teacher_off = teacher - teacher_top[:, None]
    student_exp = jnp.exp(student_off)
    student_sum = jnp.sum(student_exp, axis=1)
    teacher_sum = jnp.sum(jnp.exp(teacher_off), axis=1)
    cross_sum = jnp.sum(student_exp * (student_off - teacher_off), axis=1)

    stats = to_all(
        jnp.stack(
            [student_top, student_sum, teacher_top, teacher_sum, cross_sum, target_part]
        ),
        count,
    )
    tops, sums, teacher_tops, teacher_sums, crosses, targets = [stats[:, i] for i in range(6)]
    student_max, student_total, teacher_max, teacher_total, cross_total = merge_stats(
        tops, sums, teacher_tops, teacher_sums, crosses
    )
    student_log = jnp.log(student_total)
    teacher_log = jnp.log(teacher_total)
    student_lse = student_max + student_log
    teacher_lse = teacher_max + teacher_log
    divergence = cross_total / student_total - (student_log - teacher_log)
    target = jnp.sum(targets, axis=0)

    per_token = divergence + sample_weight * (student_lse - target)
    loss = jnp.reshape(jnp.sum(live_mask * per_token) / live_count, (1,))
    token_weight = live_mask * loss_scale[0] / live_count
    log_student = logits - student_lse[:, None]
    log_teacher = teacher - teacher_lse[:, None]
    student_prob = jnp.exp(log_student)
    grad_logits = (
        token_weight[:, None]
        * (
            student_prob * (log_student - log_teacher - divergence[:, None])
            + sample_weight * (student_prob - target_hit.astype(jnp.float32))
        )
    ).astype(jnp.bfloat16)
    terms = jnp.dot(grad_logits, head, preferred_element_type=jnp.float32).astype(jnp.bfloat16)
    terms = terms.reshape(tokens, count, own_features).transpose(1, 0, 2)
    shares = lax.all_to_all(terms, "vocab", split_axis=0, concat_axis=0, tiled=True)
    grad_hidden = jnp.sum(shares.astype(jnp.float32), axis=0)
    return (grad_hidden.astype(jnp.bfloat16), loss)


def any_shards(*arrays):
    hidden_states, head, teacher_values = arrays[:3]
    count = lax.axis_size("vocab")
    fits = (
        count % 2 == 0
        and hidden_states.shape[1] == 5 * LANES // 2
        and hidden_states.shape[0] % 32 == 0
        and head.shape[0] % LANES == LANES // 2
        and (head.shape[0] + LANES // 2) // LANES % 2 == 0
        and teacher_values.shape[0] == 4
    )
    return paired_shards(*arrays) if fits else shards(*arrays)


def solution(mesh):
    in_specs = (
        P("dom", "vocab"),
        P("vocab", None),
        P(("dom", "vocab"), None),
        P(("dom", "vocab"), None),
        P("dom"),
        P("dom"),
        P("dom"),
        P(),
    )
    out_specs = (P("dom", "vocab"), P("dom"))
    return jax.shard_map(
        any_shards, mesh=mesh, in_specs=in_specs, out_specs=out_specs, check_vma=False
    )
```

```python
import functools

import jax
import jax.numpy as jnp
from jax import lax
from jax.experimental import pallas as pl
from jax.experimental.pallas import tpu as pltpu
from jax.sharding import PartitionSpec as P

BLOCK = 32
LANES = 128
STATS = 8
AHEAD = 3


sample_weight = 0.5


def to_all(piece, count):
    copies = jnp.broadcast_to(piece[None], (count,) + piece.shape)
    return lax.all_to_all(copies, "vocab", split_axis=0, concat_axis=0, tiled=True)


def scaled_teacher(teacher_values, teacher_scales, count, shard_rows):
    slot_rows = teacher_values.shape[0]
    scaled = (
        teacher_values.astype(jnp.float32).reshape(slot_rows, -1, BLOCK) * teacher_scales[:, :, None]
    ).astype(jnp.bfloat16)
    return scaled.reshape(slot_rows, count, shard_rows).transpose(1, 0, 2)


def merge_stats(tops, sums, teacher_tops, teacher_sums, crosses):
    top = jnp.max(tops, axis=0)
    teacher_top = jnp.max(teacher_tops, axis=0)
    shift = tops - top[None]
    teacher_shift = teacher_tops - teacher_top[None]
    weight = jnp.exp(shift)
    total = jnp.sum(sums * weight, axis=0)
    teacher_total = jnp.sum(teacher_sums * jnp.exp(teacher_shift), axis=0)
    cross = jnp.sum(weight * (crosses + sums * (shift - teacher_shift)), axis=0)
    return top, total, teacher_top, teacher_total, cross


def swap_cores(array):
    count = lax.axis_size("vocab")
    return lax.ppermute(array, "vocab", [(i, i ^ 1) for i in range(count)])


def across_chips(blocks):
    count = lax.axis_size("vocab")
    groups = [list(range(core, count, 2)) for core in range(2)]
    return lax.all_to_all(
        blocks, "vocab", split_axis=0, concat_axis=0, axis_index_groups=groups, tiled=True
    )


def along_chips(array, step):
    count = lax.axis_size("vocab")
    return lax.ppermute(array, "vocab", [(i, (i + 2 * step) % count) for i in range(count)])


def vmem_array(shape, dtype):
    return pltpu.VMEM(shape, dtype)


def in_vmem(array):
    return pltpu.with_memory_space_constraint(array, pltpu.VMEM)


def in_hbm(array):
    return pltpu.with_memory_space_constraint(array, pltpu.HBM)


def hbm_array(shape, dtype):
    return pltpu.HBM(shape, dtype)


def low_lanes(shape):
    return lax.broadcasted_iota(jnp.int32, shape, len(shape) - 1) < LANES // 2


def low_rows(shape, count):
    return lax.broadcasted_iota(jnp.int32, shape, 0) < count


def turned(array):
    return pltpu.roll(array, LANES // 2, 1)


def packed_half(tiles):
    rows = tiles[2].shape[0] // 2
    upper, lower = tiles[2][:rows], tiles[2][rows:]
    rest = jnp.where(low_lanes(upper.shape), upper, turned(lower))
    return jnp.concatenate([tiles[0], tiles[1], rest], axis=0)


def unpacked_half(packed, tokens):
    rest = packed[2 * tokens :]
    return [packed[:tokens], packed[tokens : 2 * tokens], jnp.concatenate([rest, turned(rest)])]


def joined(first, second):
    low = low_lanes(first[0].shape)
    turns = [turned(tile) for tile in second]
    return [
        first[0],
        first[1],
        jnp.where(low, first[2], turns[0]),
        jnp.where(low, turns[0], turns[1]),
        jnp.where(low, turns[1], turns[2]),
    ]


def parted(tiles):
    low = low_lanes(tiles[0].shape)
    turns = [turned(tile) for tile in tiles[2:]]
    return tiles[:3], [
        jnp.where(low, turns[0], turns[1]),
        jnp.where(low, turns[1], turns[2]),
        turns[2],
    ]


def column_of(row):
    size = row.shape[1]
    down = lax.broadcasted_iota(jnp.int32, (size, size), 0)
    along = lax.broadcasted_iota(jnp.int32, (size, size), 1)
    return jnp.sum(jnp.where(down == along, row, jnp.zeros_like(row)), axis=1, keepdims=True)


def token_facts(ids, row_map, lengths, loss_scale, first_entry):
    tokens = row_map.shape[1]
    token = lax.broadcasted_iota(jnp.int32, (tokens, tokens), 0)
    slot = lax.broadcasted_iota(jnp.int32, (tokens, tokens), 1)
    owner = (row_map == token).astype(jnp.float32)
    named = jnp.max(owner, axis=1, keepdims=True)
    owner = jnp.where((slot == 0) & (named == 0.0), 1.0, owner)

    seqs = lengths.shape[1]
    seq_length = tokens // seqs
    position = lax.broadcasted_iota(jnp.int32, (tokens, 1), 0)
    live_until = jnp.zeros((tokens, 1), jnp.int32)
    for seq in range(seqs):
        inside = (position >= seq * seq_length) & (position < (seq + 1) * seq_length)
        until = lengths[:, seq : seq + 1] + seq * seq_length
        live_until = jnp.where(inside, until, live_until)
    live = (position < live_until).astype(jnp.float32)
    count = jnp.sum(live, axis=0, keepdims=True)
    entry = (column_of(ids) - first_entry).astype(jnp.float32)
    lane = lax.broadcasted_iota(jnp.int32, (tokens, LANES), 1)
    table = jnp.where(
        lane == 0, entry, jnp.where(lane == 1, live / count, live * loss_scale / count)
    )
    return owner.astype(jnp.bfloat16), table


def pack_kernel(place_ref, scale_ref, *refs, shard_rows):
    outside, refs = refs[:6], refs[6:]
    packed_ref, owner_ref, table_ref = refs[:3]
    inside, wide_ref, sems = refs[3:9], refs[9], refs[10]
    copies = [
        pltpu.make_async_copy(source, target, sems.at[i])
        for i, (source, target) in enumerate(zip(outside, inside))
    ]
    for copy in copies:
        copy.start()
    for copy in copies:
        copy.wait()
    hidden_ref, values_ref, scales_ref, ids_ref, map_ref, lengths_ref = inside
    owner_ref[...], table_ref[...] = token_facts(
        ids_ref[...], map_ref[...], lengths_ref[...], scale_ref[0], place_ref[0] * shard_rows
    )
    chips = packed_ref.shape[0]
    tokens, half = hidden_ref.shape
    slots, entries = values_ref.shape
    pair = entries // chips
    shard = pair // 2
    blocks = pair // BLOCK
    scales = jnp.concatenate([scales_ref[...]] * 2, axis=0)
    stacked = jnp.concatenate(
        [scales[:, blocks * chip : blocks * (chip + 1)] for chip in range(chips)], axis=0
    )
    block = lax.broadcasted_iota(jnp.int32, (blocks, pair), 0)
    entry = lax.broadcasted_iota(jnp.int32, (blocks, pair), 1)
    inside = (entry >= block * BLOCK) & (entry < block * BLOCK + BLOCK)
    spread = jnp.dot(
        stacked.astype(jnp.bfloat16),
        inside.astype(jnp.bfloat16),
        preferred_element_type=jnp.float32,
    )
    values = values_ref[...].astype(jnp.float32)
    values = jnp.concatenate([values, values], axis=0)
    for chip in range(chips):
        wide_ref[:, pair * chip : pair * (chip + 1)] = (
            values[:, pair * chip : pair * (chip + 1)]
            * spread[2 * slots * chip : 2 * slots * (chip + 1)]
        )
    wide_ref[:, entries:] = jnp.zeros((2 * slots, LANES), jnp.float32)

    hidden = hidden_ref[...].astype(jnp.float32)
    hidden = jnp.concatenate([hidden, jnp.zeros((tokens, LANES // 2), jnp.float32)], axis=1)
    hidden = packed_half([hidden[:, LANES * i : LANES * (i + 1)] for i in range(3)])
    hidden = hidden.astype(jnp.bfloat16)
    hidden_rows = hidden.shape[0]
    upper = low_rows((2 * slots, LANES), slots)
    low = low_lanes((2 * slots, LANES))
    tile_pairs = (shard + LANES // 2) // LANES // 2
    for chip in range(chips):
        rows = []
        for core in range(2):
            start = pair * chip + (shard - LANES // 2) * core
            tiles = [
                wide_ref[:, start + LANES * i : start + LANES * (i + 1)]
                for i in range(2 * tile_pairs + core)
            ]
            if core == 1:
                tiles = [turned(tile) for tile in tiles]
                tiles = [
                    jnp.where(low, tiles[i], tiles[i + 1]) for i in range(2 * tile_pairs)
                ]
            rows += [
                jnp.where(upper, tiles[2 * i], tiles[2 * i + 1]) for i in range(tile_pairs)
            ]
        packed_ref[chip, :hidden_rows] = hidden
        packed_ref[chip, hidden_rows:] = jnp.concatenate(rows, axis=0).astype(jnp.bfloat16)


def head_copies(head_ref, held_ref, sems, first):
    chips, _, width = held_ref.shape
    copies = []
    for step in range(chips):
        columns = pl.ds(pl.multiple_of(lax.rem(first + step, chips) * width, LANES), width)
        copies.append(
            pltpu.make_async_copy(head_ref.at[:, columns], held_ref.at[step], sems.at[step])
        )
    return copies


def logits_kernel(
    place_ref,
    own_ref,
    other_ref,
    owner_ref,
    tokens_ref,
    head_ref,
    rows_ref,
    stats_ref,
    held_ref,
    made_ref,
    hidden_ref,
    arrived_ref,
    sems,
    made_sem,
):
    copies = head_copies(head_ref, held_ref, sems, 0)
    for copy in copies[:AHEAD]:
        copy.start()
    core = place_ref[0] % 2
    chips, tokens, width = hidden_ref.shape
    shard_rows = head_ref.shape[0]
    hidden_rows = tokens * width // 2 // LANES
    slots = tokens // (2 * chips)
    upper = low_rows((2 * slots, LANES), slots)
    for chip in range(chips):
        own, other = own_ref[chip].astype(jnp.float32), other_ref[chip].astype(jnp.float32)
        first = jnp.where(core == 0, own, other)
        second = jnp.where(core == 0, other, own)
        tiles = joined(
            unpacked_half(first[:hidden_rows], tokens),
            unpacked_half(second[:hidden_rows], tokens),
        )
        hidden_ref[chip] = jnp.concatenate(tiles, axis=1).astype(jnp.bfloat16)
        first, second = first[hidden_rows:], second[hidden_rows:]
        share = first.shape[0] // 2
        first = jnp.where(core == 0, first[:share], first[share:])
        second = jnp.where(core == 0, second[:share], second[share:])
        tiles = []
        for row in range(0, share, 2 * slots):
            one, two = first[row : row + 2 * slots], second[row : row + 2 * slots]
            tiles.append(jnp.where(upper, one, pltpu.roll(two, slots, 0)))
            tiles.append(jnp.where(upper, pltpu.roll(one, slots, 0), two))
        arrived_ref[2 * slots * chip : 2 * slots * (chip + 1)] = jnp.concatenate(tiles, axis=1)
    teacher = jnp.dot(
        owner_ref[...],
        arrived_ref[:, :shard_rows].astype(jnp.bfloat16),
        preferred_element_type=jnp.float32,
    )
    logits = jnp.zeros((tokens, shard_rows), jnp.float32)
    for chip, copy in enumerate(copies):
        copy.wait()
        if chip + AHEAD < chips:
            copies[chip + AHEAD].start()
        logits += lax.dot_general(
            hidden_ref[chip],
            held_ref[chip],
            (((1,), (1,)), ((), ())),
            preferred_element_type=jnp.float32,
        )

    top = jnp.max(logits, axis=1, keepdims=True)
    teacher_top = jnp.max(teacher, axis=1, keepdims=True)
    off = logits - top
    teacher_off = teacher - teacher_top
    exps = jnp.exp(off)
    total = jnp.sum(exps, axis=1, keepdims=True)
    teacher_total = jnp.sum(jnp.exp(teacher_off), axis=1, keepdims=True)
    gap = off - teacher_off
    cross = jnp.sum(exps * gap, axis=1, keepdims=True)
    centre = cross / total
    entry = lax.broadcasted_iota(jnp.int32, (tokens, shard_rows), 1)
    hit = entry == tokens_ref[:, :1].astype(jnp.int32)
    target = jnp.sum(jnp.where(hit, logits, 0.0), axis=1, keepdims=True)
    made_ref[:tokens] = (exps * (gap - centre)).astype(jnp.bfloat16)
    made_ref[tokens : 2 * tokens] = exps.astype(jnp.bfloat16)
    made_ref[2 * tokens :] = hit.astype(jnp.bfloat16)
    out = pltpu.make_async_copy(made_ref, rows_ref, made_sem)
    out.start()

    lane = lax.broadcasted_iota(jnp.int32, (tokens, LANES), 1)
    table = jnp.zeros((tokens, LANES), jnp.float32)
    for place, column in enumerate(
        (top, total, teacher_top, teacher_total, cross, target, centre)
    ):
        table = jnp.where(lane == place, column, table)
    stats = jnp.concatenate([table, jnp.zeros((stats_ref.shape[2] - tokens, LANES), jnp.float32)])
    stats_ref[...] = jnp.broadcast_to(stats.T[None, :STATS], stats_ref.shape)
    out.wait()


def products_kernel(
    place_ref, rows_ref, head_ref, terms_ref, picks_ref, held_ref, made_ref, sems, made_sem
):
    into = pltpu.make_async_copy(rows_ref, made_ref, made_sem)
    into.start()
    copies = head_copies(head_ref, held_ref, sems, place_ref[0] // 2)
    for copy in copies[:AHEAD]:
        copy.start()
    into.wait()
    sums_rows = terms_ref.shape[1]
    for step, copy in enumerate(copies):
        copy.wait()
        if step + AHEAD < len(copies):
            copies[step + AHEAD].start()
        products = jnp.dot(made_ref[...], held_ref[step], preferred_element_type=jnp.float32)
        terms_ref[step] = products[:sums_rows]
        picks_ref[step] = products[sums_rows:].astype(jnp.bfloat16)


def combine_kernel(
    place_ref, stats_ref, own_ref, tokens_ref, terms_ref, picks_ref, keep_ref, give_ref, loss_ref
):
    core = place_ref[0] % 2
    chips, _, width = terms_ref.shape
    tokens = tokens_ref.shape[0]
    tops, sums, teacher_tops, teacher_sums, crosses, targets = [
        stats_ref[:, i, :tokens] for i in range(6)
    ]
    top, total, teacher_top, teacher_total, cross = [
        part[None] for part in merge_stats(tops, sums, teacher_tops, teacher_sums, crosses)
    ]
    target = jnp.sum(targets, axis=0, keepdims=True)
    student_log = jnp.log(total)
    teacher_log = jnp.log(teacher_total)
    divergence = cross / total - (student_log - teacher_log)
    student_lse = top + student_log
    per_token = divergence + sample_weight * (student_lse - target)
    student_shift = own_ref[0, 0:1, :tokens] - top - student_log
    teacher_shift = own_ref[0, 2:3, :tokens] - teacher_top - teacher_log
    factor = jnp.exp(student_shift)
    level = (
        own_ref[0, 6:7, :tokens] + student_shift - teacher_shift - divergence + sample_weight
    )
    zeros = jnp.zeros((LANES - 3, tokens), jnp.float32)
    columns = jnp.concatenate([factor, level, per_token, zeros], axis=0).T
    share, weight = tokens_ref[:, 1:2], tokens_ref[:, 2:3]
    loss_ref[...] = jnp.sum(share * columns[:, 2:3], axis=0, keepdims=True)
    factor = weight * columns[:, 0:1]
    level = columns[:, 1:2]
    weight = sample_weight * weight
    for step in range(chips):
        block = (
            factor * (terms_ref[step, :tokens] + level * terms_ref[step, tokens:])
            - weight * picks_ref[step].astype(jnp.float32)
        )
        first, second = parted([block[:, i : i + LANES] for i in range(0, width, LANES)])
        first, second = packed_half(first), packed_half(second)
        keep_ref[step] = jnp.where(core == 0, first, second)
        give_ref[step] = jnp.where(core == 0, second, first).astype(jnp.bfloat16)


def sum_kernel(own_ref, *refs):
    tokens, half = refs[-1].shape
    total = own_ref[...]
    for share_ref in refs[:-1]:
        total += share_ref[...].astype(jnp.float32)
    tiles = jnp.concatenate(unpacked_half(total, tokens), axis=1)
    refs[-1][...] = tiles[:, :half].astype(refs[-1].dtype)


def paired_shards(
    hidden_states, head, teacher_values, teacher_scales, token_ids, lengths, row_map, loss_scale
):
    count = lax.axis_size("vocab")
    own_index = lax.axis_index("vocab")
    chips = count // 2
    tokens, half = hidden_states.shape
    width = 2 * half
    shard_rows = head.shape[0]
    place = jnp.reshape(own_index, (1,))
    vmem = pl.BlockSpec(memory_space=pltpu.VMEM)
    smem = pl.BlockSpec(memory_space=pltpu.SMEM)
    hbm = pl.BlockSpec(memory_space=pl.ANY)
    params = pltpu.CompilerParams(vmem_limit_bytes=VMEM_LIMIT)
    head = in_hbm(head)
    head_scratch = pltpu.VMEM((chips, shard_rows, width), head.dtype)
    head_sems = pltpu.SemaphoreType.DMA((chips,))
    rows_scratch = pltpu.VMEM((3 * tokens, shard_rows), jnp.bfloat16)
    rows_sem = pltpu.SemaphoreType.DMA
    slots, entries = teacher_values.shape
    hidden_rows = tokens * half // LANES
    teacher_rows = 2 * slots * (shard_rows + LANES // 2) // LANES

    operands = (
        hidden_states,
        teacher_values,
        teacher_scales,
        token_ids[None, :],
        row_map[None, :],
        lengths[None, :],
    )
    packed, owner, table = pl.pallas_call(
        functools.partial(pack_kernel, shard_rows=shard_rows),
        out_shape=(
            jax.ShapeDtypeStruct((chips, hidden_rows + teacher_rows, LANES), jnp.bfloat16),
            vmem_array((tokens, tokens), jnp.bfloat16),
            vmem_array((tokens, LANES), jnp.float32),
        ),
        in_specs=[smem] * 2 + [hbm] * len(operands),
        out_specs=[vmem] * 3,
        scratch_shapes=[pltpu.VMEM(operand.shape, operand.dtype) for operand in operands]
        + [
            pltpu.VMEM((2 * slots, entries + LANES), jnp.float32),
            pltpu.SemaphoreType.DMA((len(operands),)),
        ],
        compiler_params=params,
        name="pack",
    )(place, loss_scale, *[in_hbm(operand) for operand in operands])
    gathered = across_chips(packed)
    other = swap_cores(gathered)

    rows, stats = pl.pallas_call(
        logits_kernel,
        out_shape=(
            hbm_array((3 * tokens, shard_rows), jnp.bfloat16),
            jax.ShapeDtypeStruct((count, STATS, pl.cdiv(tokens, LANES) * LANES), jnp.float32),
        ),
        in_specs=[smem] + [vmem] * 4 + [hbm],
        out_specs=[hbm, vmem],
        scratch_shapes=[
            head_scratch,
            rows_scratch,
            pltpu.VMEM((chips, tokens, width), jnp.bfloat16),
            pltpu.VMEM((tokens, shard_rows + LANES // 2), jnp.float32),
            head_sems,
            rows_sem,
        ],
        compiler_params=params,
        cost_estimate=pl.CostEstimate(
            flops=2 * tokens * head.size, bytes_accessed=2 * head.size, transcendentals=0
        ),
        name="logits",
    )(place, gathered, other, in_vmem(owner), in_vmem(table), head)

    all_stats = lax.all_to_all(stats, "vocab", split_axis=0, concat_axis=0, tiled=True)

    terms, picks = pl.pallas_call(
        products_kernel,
        out_shape=(
            vmem_array((chips, 2 * tokens, width), jnp.float32),
            vmem_array((chips, tokens, width), jnp.bfloat16),
        ),
        in_specs=[smem, hbm, hbm],
        out_specs=[vmem] * 2,
        scratch_shapes=[head_scratch, rows_scratch, head_sems, rows_sem],
        compiler_params=params,
        cost_estimate=pl.CostEstimate(
            flops=6 * tokens * head.size, bytes_accessed=2 * head.size, transcendentals=0
        ),
        name="products",
    )(place, in_hbm(rows), head)

    keep, give, loss = pl.pallas_call(
        combine_kernel,
        out_shape=(
            vmem_array((chips, hidden_rows, LANES), jnp.float32),
            vmem_array((chips, hidden_rows, LANES), jnp.bfloat16),
            jax.ShapeDtypeStruct((1, 1), jnp.float32),
        ),
        in_specs=[smem] + [vmem] * 5,
        out_specs=[vmem] * 3,
        compiler_params=params,
        name="combine",
    )(
        place,
        all_stats,
        stats,
        in_vmem(table),
        in_vmem(terms),
        in_vmem(picks),
    )

    sums = keep + swap_cores(give).astype(jnp.float32)
    steps = range(chips - 1, 0, -1)
    shares = [along_chips(sums[step].astype(jnp.bfloat16), step) for step in steps]
    total = pl.pallas_call(
        sum_kernel,
        out_shape=jax.ShapeDtypeStruct((tokens, half), jnp.bfloat16),
        in_specs=[vmem] * chips,
        out_specs=vmem,
        compiler_params=params,
        name="total",
    )(sums[0], *shares)
    return total, jnp.reshape(loss, (1,))


VMEM_LIMIT = 24 * 1024 * 1024


def shards(
    hidden_states, head, teacher_values, teacher_scales, token_ids, lengths, row_map, loss_scale
):
    count = lax.axis_size("vocab")
    own_index = lax.axis_index("vocab")
    tokens = hidden_states.shape[0]
    own_features = hidden_states.shape[1]
    shard_rows = head.shape[0]
    seq_length = tokens // lengths.shape[0]
    contract_last = (((1,), (1,)), ((), ()))

    scaled = scaled_teacher(teacher_values, teacher_scales, count, shard_rows)
    arrived = lax.all_to_all(scaled, "vocab", split_axis=0, concat_axis=0, tiled=True)
    arrived = arrived.reshape(tokens, shard_rows)
    gathered = to_all(hidden_states, count).transpose(1, 0, 2).reshape(tokens, -1)
    logits = lax.dot_general(gathered, head, contract_last, preferred_element_type=jnp.float32)

    positions = jnp.arange(tokens, dtype=jnp.int32)
    owner = row_map[None, :] == positions[:, None]
    slot_of = jnp.sum(jnp.where(owner, positions[None, :], 0), axis=1)
    teacher = jnp.take(arrived, slot_of, axis=0).astype(jnp.float32)

    seq_ids = jnp.arange(lengths.shape[0], dtype=jnp.int32)
    own_length = jnp.sum(
        jnp.where((positions // seq_length)[:, None] == seq_ids[None, :], lengths[None, :], 0),
        axis=1,
    )
    live_mask = (positions % seq_length < own_length).astype(jnp.float32)
    live_count = jnp.sum(live_mask)

    local_ids = token_ids - own_index * shard_rows
    target_hit = local_ids[:, None] == jnp.arange(shard_rows, dtype=jnp.int32)[None, :]
    target_part = jnp.sum(jnp.where(target_hit, logits, 0.0), axis=1)
    student_top = jnp.max(logits, axis=1)
    teacher_top = jnp.max(teacher, axis=1)
    student_off = logits - student_top[:, None]
    teacher_off = teacher - teacher_top[:, None]
    student_exp = jnp.exp(student_off)
    student_sum = jnp.sum(student_exp, axis=1)
    teacher_sum = jnp.sum(jnp.exp(teacher_off), axis=1)
    cross_sum = jnp.sum(student_exp * (student_off - teacher_off), axis=1)

    stats = to_all(
        jnp.stack(
            [student_top, student_sum, teacher_top, teacher_sum, cross_sum, target_part]
        ),
        count,
    )
    tops, sums, teacher_tops, teacher_sums, crosses, targets = [stats[:, i] for i in range(6)]
    student_max, student_total, teacher_max, teacher_total, cross_total = merge_stats(
        tops, sums, teacher_tops, teacher_sums, crosses
    )
    student_log = jnp.log(student_total)
    teacher_log = jnp.log(teacher_total)
    student_lse = student_max + student_log
    teacher_lse = teacher_max + teacher_log
    divergence = cross_total / student_total - (student_log - teacher_log)
    target = jnp.sum(targets, axis=0)

    per_token = divergence + sample_weight * (student_lse - target)
    loss = jnp.reshape(jnp.sum(live_mask * per_token) / live_count, (1,))
    token_weight = live_mask * loss_scale[0] / live_count
    log_student = logits - student_lse[:, None]
    log_teacher = teacher - teacher_lse[:, None]
    student_prob = jnp.exp(log_student)
    grad_logits = (
        token_weight[:, None]
        * (
            student_prob * (log_student - log_teacher - divergence[:, None])
            + sample_weight * (student_prob - target_hit.astype(jnp.float32))
        )
    ).astype(jnp.bfloat16)
    terms = jnp.dot(grad_logits, head, preferred_element_type=jnp.float32).astype(jnp.bfloat16)
    terms = terms.reshape(tokens, count, own_features).transpose(1, 0, 2)
    shares = lax.all_to_all(terms, "vocab", split_axis=0, concat_axis=0, tiled=True)
    grad_hidden = jnp.sum(shares.astype(jnp.float32), axis=0)
    return (grad_hidden.astype(jnp.bfloat16), loss)


def any_shards(*arrays):
    hidden_states, head, teacher_values = arrays[:3]
    count = lax.axis_size("vocab")
    fits = (
        count % 2 == 0
        and hidden_states.shape[1] == 5 * LANES // 2
        and hidden_states.shape[0] % 32 == 0
        and head.shape[0] % LANES == LANES // 2
        and (head.shape[0] + LANES // 2) // LANES % 2 == 0
        and teacher_values.shape[0] == 4
    )
    return paired_shards(*arrays) if fits else shards(*arrays)


def solution(mesh):
    in_specs = (
        P("dom", "vocab"),
        P("vocab", None),
        P(("dom", "vocab"), None),
        P(("dom", "vocab"), None),
        P("dom"),
        P("dom"),
        P("dom"),
        P(),
    )
    out_specs = (P("dom", "vocab"), P("dom"))
    return jax.shard_map(
        any_shards, mesh=mesh, in_specs=in_specs, out_specs=out_specs, check_vma=False
    )
```

```python
import functools

import jax
import jax.numpy as jnp
from jax import lax
from jax.experimental import pallas as pl
from jax.experimental.pallas import tpu as pltpu
from jax.sharding import PartitionSpec as P

BLOCK = 32
LANES = 128
STATS = 8
AHEAD = 3


sample_weight = 0.5


def to_all(piece, count):
    copies = jnp.broadcast_to(piece[None], (count,) + piece.shape)
    return lax.all_to_all(copies, "vocab", split_axis=0, concat_axis=0, tiled=True)


def scaled_teacher(teacher_values, teacher_scales, count, shard_rows):
    slot_rows = teacher_values.shape[0]
    scaled = (
        teacher_values.astype(jnp.float32).reshape(slot_rows, -1, BLOCK) * teacher_scales[:, :, None]
    ).astype(jnp.bfloat16)
    return scaled.reshape(slot_rows, count, shard_rows).transpose(1, 0, 2)


def merge_stats(tops, sums, teacher_tops, teacher_sums, crosses):
    top = jnp.max(tops, axis=0)
    teacher_top = jnp.max(teacher_tops, axis=0)
    shift = tops - top[None]
    teacher_shift = teacher_tops - teacher_top[None]
    weight = jnp.exp(shift)
    total = jnp.sum(sums * weight, axis=0)
    teacher_total = jnp.sum(teacher_sums * jnp.exp(teacher_shift), axis=0)
    cross = jnp.sum(weight * (crosses + sums * (shift - teacher_shift)), axis=0)
    return top, total, teacher_top, teacher_total, cross


def swap_cores(array):
    count = lax.axis_size("vocab")
    return lax.ppermute(array, "vocab", [(i, i ^ 1) for i in range(count)])


def across_chips(blocks):
    count = lax.axis_size("vocab")
    groups = [list(range(core, count, 2)) for core in range(2)]
    return lax.all_to_all(
        blocks, "vocab", split_axis=0, concat_axis=0, axis_index_groups=groups, tiled=True
    )


def along_chips(array, step):
    count = lax.axis_size("vocab")
    return lax.ppermute(array, "vocab", [(i, (i + 2 * step) % count) for i in range(count)])


def vmem_array(shape, dtype):
    return pltpu.VMEM(shape, dtype)


def in_vmem(array):
    return pltpu.with_memory_space_constraint(array, pltpu.VMEM)


def in_hbm(array):
    return pltpu.with_memory_space_constraint(array, pltpu.HBM)


def hbm_array(shape, dtype):
    return pltpu.HBM(shape, dtype)


def low_lanes(shape):
    return lax.broadcasted_iota(jnp.int32, shape, len(shape) - 1) < LANES // 2


def low_rows(shape, count):
    return lax.broadcasted_iota(jnp.int32, shape, 0) < count


def turned(array):
    return pltpu.roll(array, LANES // 2, 1)


def packed_half(tiles):
    rows = tiles[2].shape[0] // 2
    upper, lower = tiles[2][:rows], tiles[2][rows:]
    rest = jnp.where(low_lanes(upper.shape), upper, turned(lower))
    return jnp.concatenate([tiles[0], tiles[1], rest], axis=0)


def unpacked_half(packed, tokens):
    rest = packed[2 * tokens :]
    return [packed[:tokens], packed[tokens : 2 * tokens], jnp.concatenate([rest, turned(rest)])]


def joined(first, second):
    low = low_lanes(first[0].shape)
    turns = [turned(tile) for tile in second]
    return [
        first[0],
        first[1],
        jnp.where(low, first[2], turns[0]),
        jnp.where(low, turns[0], turns[1]),
        jnp.where(low, turns[1], turns[2]),
    ]


def column_of(row):
    size = row.shape[1]
    down = lax.broadcasted_iota(jnp.int32, (size, size), 0)
    along = lax.broadcasted_iota(jnp.int32, (size, size), 1)
    return jnp.sum(jnp.where(down == along, row, jnp.zeros_like(row)), axis=1, keepdims=True)


def token_facts(ids, row_map, lengths, first_entry):
    tokens = row_map.shape[1]
    token = lax.broadcasted_iota(jnp.int32, (tokens, tokens), 0)
    slot = lax.broadcasted_iota(jnp.int32, (tokens, tokens), 1)
    owner = (row_map == token).astype(jnp.float32)
    named = jnp.max(owner, axis=1, keepdims=True)
    owner = jnp.where((slot == 0) & (named == 0.0), 1.0, owner)

    seqs = lengths.shape[1]
    seq_length = tokens // seqs
    position = lax.broadcasted_iota(jnp.int32, (tokens, 1), 0)
    live_until = jnp.zeros((tokens, 1), jnp.int32)
    for seq in range(seqs):
        inside = (position >= seq * seq_length) & (position < (seq + 1) * seq_length)
        until = lengths[:, seq : seq + 1] + seq * seq_length
        live_until = jnp.where(inside, until, live_until)
    live = (position < live_until).astype(jnp.float32)
    count = jnp.sum(live, axis=0, keepdims=True)
    entry = (column_of(ids) - first_entry).astype(jnp.float32)
    lane = lax.broadcasted_iota(jnp.int32, (tokens, LANES), 1)
    return owner.astype(jnp.bfloat16), jnp.where(lane == 0, entry, live / count)


def pack_kernel(place_ref, *refs, shard_rows):
    outside, refs = refs[:6], refs[6:]
    packed_ref, owner_ref, table_ref = refs[:3]
    inside, wide_ref, sems = refs[3:9], refs[9], refs[10]
    copies = [
        pltpu.make_async_copy(source, target, sems.at[i])
        for i, (source, target) in enumerate(zip(outside, inside))
    ]
    for copy in copies:
        copy.start()
    for copy in copies:
        copy.wait()
    hidden_ref, values_ref, scales_ref, ids_ref, map_ref, lengths_ref = inside
    owner_ref[...], table_ref[...] = token_facts(
        ids_ref[...], map_ref[...], lengths_ref[...], place_ref[0] * shard_rows
    )
    chips = packed_ref.shape[0]
    tokens, half = hidden_ref.shape
    slots, entries = values_ref.shape
    pair = entries // chips
    shard = pair // 2
    blocks = pair // BLOCK
    scales = jnp.concatenate([scales_ref[...]] * 2, axis=0)
    stacked = jnp.concatenate(
        [scales[:, blocks * chip : blocks * (chip + 1)] for chip in range(chips)], axis=0
    )
    block = lax.broadcasted_iota(jnp.int32, (blocks, pair), 0)
    entry = lax.broadcasted_iota(jnp.int32, (blocks, pair), 1)
    inside = (entry >= block * BLOCK) & (entry < block * BLOCK + BLOCK)
    spread = jnp.dot(
        stacked.astype(jnp.bfloat16),
        inside.astype(jnp.bfloat16),
        preferred_element_type=jnp.float32,
    )
    values = values_ref[...].astype(jnp.float32)
    values = jnp.concatenate([values, values], axis=0)
    for chip in range(chips):
        wide_ref[:, pair * chip : pair * (chip + 1)] = (
            values[:, pair * chip : pair * (chip + 1)]
            * spread[2 * slots * chip : 2 * slots * (chip + 1)]
        )
    wide_ref[:, entries:] = jnp.zeros((2 * slots, LANES), jnp.float32)

    hidden = hidden_ref[...].astype(jnp.float32)
    hidden = jnp.concatenate([hidden, jnp.zeros((tokens, LANES // 2), jnp.float32)], axis=1)
    hidden = packed_half([hidden[:, LANES * i : LANES * (i + 1)] for i in range(3)])
    hidden = hidden.astype(jnp.bfloat16)
    hidden_rows = hidden.shape[0]
    upper = low_rows((2 * slots, LANES), slots)
    low = low_lanes((2 * slots, LANES))
    tile_pairs = (shard + LANES // 2) // LANES // 2
    for chip in range(chips):
        rows = []
        for core in range(2):
            start = pair * chip + (shard - LANES // 2) * core
            tiles = [
                wide_ref[:, start + LANES * i : start + LANES * (i + 1)]
                for i in range(2 * tile_pairs + core)
            ]
            if core == 1:
                tiles = [turned(tile) for tile in tiles]
                tiles = [
                    jnp.where(low, tiles[i], tiles[i + 1]) for i in range(2 * tile_pairs)
                ]
            rows += [
                jnp.where(upper, tiles[2 * i], tiles[2 * i + 1]) for i in range(tile_pairs)
            ]
        packed_ref[chip, :hidden_rows] = hidden
        packed_ref[chip, hidden_rows:] = jnp.concatenate(rows, axis=0).astype(jnp.bfloat16)


def head_copies(head_ref, held_ref, sems, first):
    chips, _, width = held_ref.shape
    copies = []
    for step in range(chips):
        columns = pl.ds(pl.multiple_of(lax.rem(first + step, chips) * width, LANES), width)
        copies.append(
            pltpu.make_async_copy(head_ref.at[:, columns], held_ref.at[step], sems.at[step])
        )
    return copies


def logits_kernel(
    place_ref,
    own_ref,
    other_ref,
    owner_ref,
    tokens_ref,
    head_ref,
    rows_ref,
    stats_ref,
    held_ref,
    made_ref,
    hidden_ref,
    arrived_ref,
    teacher_ref,
    sems,
    made_sem,
):
    copies = head_copies(head_ref, held_ref, sems, 0)
    for copy in copies[:AHEAD]:
        copy.start()
    core = place_ref[0] % 2
    chips, tokens, width = hidden_ref.shape
    shard_rows = head_ref.shape[0]
    hidden_rows = tokens * width // 2 // LANES
    slots = tokens // (2 * chips)
    upper = low_rows((2 * slots, LANES), slots)

    def both(chip, rows):
        own = own_ref[chip, rows].astype(jnp.float32)
        other = other_ref[chip, rows].astype(jnp.float32)
        return jnp.where(core == 0, own, other), jnp.where(core == 0, other, own)

    def unpack_hidden(chip):
        first, second = both(chip, slice(0, hidden_rows))
        tiles = joined(unpacked_half(first, tokens), unpacked_half(second, tokens))
        hidden_ref[chip] = jnp.concatenate(tiles, axis=1).astype(jnp.bfloat16)

    def unpack_teacher(chip):
        first, second = both(chip, slice(hidden_rows, own_ref.shape[1]))
        share = first.shape[0] // 2
        first = jnp.where(core == 0, first[:share], first[share:])
        second = jnp.where(core == 0, second[:share], second[share:])
        tiles = []
        for row in range(0, share, 2 * slots):
            one, two = first[row : row + 2 * slots], second[row : row + 2 * slots]
            tiles.append(jnp.where(upper, one, pltpu.roll(two, slots, 0)))
            tiles.append(jnp.where(upper, pltpu.roll(one, slots, 0), two))
        arrived_ref[2 * slots * chip : 2 * slots * (chip + 1)] = jnp.concatenate(tiles, axis=1)

    unpack_hidden(0)
    logits = jnp.zeros((tokens, shard_rows), jnp.float32)
    for chip, copy in enumerate(copies):
        copy.wait()
        if chip + AHEAD < chips:
            copies[chip + AHEAD].start()
        if chip + 1 < chips:
            unpack_hidden(chip + 1)
        if chip < chips // 2:
            unpack_teacher(2 * chip)
            unpack_teacher(2 * chip + 1)
        if chip == chips // 2:
            teacher = jnp.dot(
                owner_ref[...],
                arrived_ref[:, :shard_rows].astype(jnp.bfloat16),
                preferred_element_type=jnp.float32,
            )
            teacher_top = jnp.max(teacher, axis=1, keepdims=True)
            teacher_off = teacher - teacher_top
            teacher_total = jnp.sum(jnp.exp(teacher_off), axis=1, keepdims=True)
            teacher_ref[...] = teacher_off
        logits += lax.dot_general(
            hidden_ref[chip],
            held_ref[chip],
            (((1,), (1,)), ((), ())),
            preferred_element_type=jnp.float32,
        )

    top = jnp.max(logits, axis=1, keepdims=True)
    off = logits - top
    exps = jnp.exp(off)
    total = jnp.sum(exps, axis=1, keepdims=True)
    gap = off - teacher_ref[...]
    cross = jnp.sum(exps * gap, axis=1, keepdims=True)
    centre = cross / total
    entry = lax.broadcasted_iota(jnp.int32, (tokens, shard_rows), 1)
    hit = entry == tokens_ref[:, :1].astype(jnp.int32)
    target = jnp.sum(jnp.where(hit, logits, 0.0), axis=1, keepdims=True)
    made_ref[:tokens] = (exps * (gap - centre)).astype(jnp.bfloat16)
    made_ref[tokens : 2 * tokens] = exps.astype(jnp.bfloat16)
    made_ref[2 * tokens :] = hit.astype(jnp.bfloat16)
    out = pltpu.make_async_copy(made_ref, rows_ref, made_sem)
    out.start()

    lane = lax.broadcasted_iota(jnp.int32, (tokens, LANES), 1)
    table = jnp.zeros((tokens, LANES), jnp.float32)
    for place, column in enumerate(
        (top, total, teacher_top, teacher_total, cross, target, centre)
    ):
        table = jnp.where(lane == place, column, table)
    stats = jnp.concatenate([table, jnp.zeros((stats_ref.shape[2] - tokens, LANES), jnp.float32)])
    stats_ref[...] = jnp.broadcast_to(stats.T[None, :STATS], stats_ref.shape)
    out.wait()


def products_kernel(
    place_ref, rows_ref, head_ref, terms_ref, picks_ref, held_ref, made_ref, sems, made_sem
):
    into = pltpu.make_async_copy(rows_ref, made_ref, made_sem)
    into.start()
    copies = head_copies(head_ref, held_ref, sems, place_ref[0] // 2)
    for copy in copies[:AHEAD]:
        copy.start()
    into.wait()
    sums_rows = terms_ref.shape[1]
    for step, copy in enumerate(copies):
        copy.wait()
        if step + AHEAD < len(copies):
            copies[step + AHEAD].start()
        products = jnp.dot(made_ref[...], held_ref[step], preferred_element_type=jnp.float32)
        terms_ref[step] = products[:sums_rows]
        picks_ref[step] = products[sums_rows:].astype(jnp.bfloat16)


def parity_half(parity, step, factors_ref, terms_ref, picks_ref):
    tokens = picks_ref.shape[1]
    lanes = pl.ds(pl.multiple_of(parity * 2 * LANES, LANES), 3 * LANES)
    factor, level, weight = [factors_ref[:, i : i + 1] for i in range(3)]
    block = (
        factor * (terms_ref[step, :tokens, lanes] + level * terms_ref[step, tokens:, lanes])
        - weight * picks_ref[step, :, lanes].astype(jnp.float32)
    )
    tiles = [block[:, i : i + LANES] for i in range(0, 3 * LANES, LANES)]
    turns = [turned(tile) for tile in tiles]
    low = low_lanes(tiles[0].shape)
    first = parity == 0
    return packed_half(
        [
            jnp.where(first, tiles[0], jnp.where(low, turns[0], turns[1])),
            jnp.where(first, tiles[1], jnp.where(low, turns[1], turns[2])),
            jnp.where(first, tiles[2], turns[2]),
        ]
    )


def give_kernel(
    place_ref,
    stats_ref,
    own_ref,
    tokens_ref,
    terms_ref,
    picks_ref,
    give_ref,
    factors_ref,
    loss_ref,
):
    tokens = tokens_ref.shape[0]
    tops, sums, teacher_tops, teacher_sums, crosses, targets = [
        stats_ref[:, i, :tokens] for i in range(6)
    ]
    top, total, teacher_top, teacher_total, cross = [
        part[None] for part in merge_stats(tops, sums, teacher_tops, teacher_sums, crosses)
    ]
    target = jnp.sum(targets, axis=0, keepdims=True)
    student_log = jnp.log(total)
    teacher_log = jnp.log(teacher_total)
    divergence = cross / total - (student_log - teacher_log)
    student_lse = top + student_log
    per_token = divergence + sample_weight * (student_lse - target)
    student_shift = own_ref[0, 0:1, :tokens] - top - student_log
    teacher_shift = own_ref[0, 2:3, :tokens] - teacher_top - teacher_log
    factor = jnp.exp(student_shift)
    level = (
        own_ref[0, 6:7, :tokens] + student_shift - teacher_shift - divergence + sample_weight
    )
    zeros = jnp.zeros((LANES - 3, tokens), jnp.float32)
    columns = jnp.concatenate([factor, level, per_token, zeros], axis=0).T
    share = tokens_ref[:, 1:2]
    loss_ref[...] = jnp.sum(share * columns[:, 2:3], axis=0, keepdims=True)
    lane = lax.broadcasted_iota(jnp.int32, (tokens, LANES), 1)
    factors_ref[...] = jnp.where(
        lane == 0,
        share * columns[:, 0:1],
        jnp.where(lane == 1, columns[:, 1:2], sample_weight * share),
    )
    parity = 1 - place_ref[0] % 2
    for step in range(terms_ref.shape[0]):
        give_ref[step] = parity_half(parity, step, factors_ref, terms_ref, picks_ref).astype(
            jnp.bfloat16
        )


def keep_kernel(place_ref, factors_ref, terms_ref, picks_ref, keep_ref):
    parity = place_ref[0] % 2
    for step in range(terms_ref.shape[0]):
        keep_ref[step] = parity_half(parity, step, factors_ref, terms_ref, picks_ref)


def sum_kernel(scale_ref, own_ref, *refs):
    tokens, half = refs[-1].shape
    total = own_ref[...]
    for share_ref in refs[:-1]:
        total += share_ref[...].astype(jnp.float32)
    tiles = jnp.concatenate(unpacked_half(total * scale_ref[0], tokens), axis=1)
    refs[-1][...] = tiles[:, :half].astype(refs[-1].dtype)


def paired_shards(
    hidden_states, head, teacher_values, teacher_scales, token_ids, lengths, row_map, loss_scale
):
    count = lax.axis_size("vocab")
    own_index = lax.axis_index("vocab")
    chips = count // 2
    tokens, half = hidden_states.shape
    width = 2 * half
    shard_rows = head.shape[0]
    place = jnp.reshape(own_index, (1,))
    vmem = pl.BlockSpec(memory_space=pltpu.VMEM)
    smem = pl.BlockSpec(memory_space=pltpu.SMEM)
    hbm = pl.BlockSpec(memory_space=pl.ANY)
    params = pltpu.CompilerParams(vmem_limit_bytes=VMEM_LIMIT)
    head = in_hbm(head)
    head_scratch = pltpu.VMEM((chips, shard_rows, width), head.dtype)
    head_sems = pltpu.SemaphoreType.DMA((chips,))
    rows_scratch = pltpu.VMEM((3 * tokens, shard_rows), jnp.bfloat16)
    rows_sem = pltpu.SemaphoreType.DMA
    slots, entries = teacher_values.shape
    hidden_rows = tokens * half // LANES
    teacher_rows = 2 * slots * (shard_rows + LANES // 2) // LANES

    operands = (
        hidden_states,
        teacher_values,
        teacher_scales,
        token_ids[None, :],
        row_map[None, :],
        lengths[None, :],
    )
    packed, owner, table = pl.pallas_call(
        functools.partial(pack_kernel, shard_rows=shard_rows),
        out_shape=(
            jax.ShapeDtypeStruct((chips, hidden_rows + teacher_rows, LANES), jnp.bfloat16),
            vmem_array((tokens, tokens), jnp.bfloat16),
            vmem_array((tokens, LANES), jnp.float32),
        ),
        in_specs=[smem] + [hbm] * len(operands),
        out_specs=[vmem] * 3,
        scratch_shapes=[pltpu.VMEM(operand.shape, operand.dtype) for operand in operands]
        + [
            pltpu.VMEM((2 * slots, entries + LANES), jnp.float32),
            pltpu.SemaphoreType.DMA((len(operands),)),
        ],
        compiler_params=params,
        name="pack",
    )(place, *[in_hbm(operand) for operand in operands])
    gathered = across_chips(packed)
    other = swap_cores(gathered)

    rows, stats = pl.pallas_call(
        logits_kernel,
        out_shape=(
            hbm_array((3 * tokens, shard_rows), jnp.bfloat16),
            jax.ShapeDtypeStruct((count, STATS, pl.cdiv(tokens, LANES) * LANES), jnp.float32),
        ),
        in_specs=[smem] + [vmem] * 4 + [hbm],
        out_specs=[hbm, vmem],
        scratch_shapes=[
            head_scratch,
            rows_scratch,
            pltpu.VMEM((chips, tokens, width), jnp.bfloat16),
            pltpu.VMEM((tokens, shard_rows + LANES // 2), jnp.float32),
            pltpu.VMEM((tokens, shard_rows), jnp.float32),
            head_sems,
            rows_sem,
        ],
        compiler_params=params,
        cost_estimate=pl.CostEstimate(
            flops=2 * tokens * head.size, bytes_accessed=2 * head.size, transcendentals=0
        ),
        name="logits",
    )(place, gathered, other, in_vmem(owner), in_vmem(table), head)

    all_stats = lax.all_to_all(stats, "vocab", split_axis=0, concat_axis=0, tiled=True)

    terms, picks = pl.pallas_call(
        products_kernel,
        out_shape=(
            vmem_array((chips, 2 * tokens, width), jnp.float32),
            vmem_array((chips, tokens, width), jnp.bfloat16),
        ),
        in_specs=[smem, hbm, hbm],
        out_specs=[vmem] * 2,
        scratch_shapes=[head_scratch, rows_scratch, head_sems, rows_sem],
        compiler_params=params,
        cost_estimate=pl.CostEstimate(
            flops=6 * tokens * head.size, bytes_accessed=2 * head.size, transcendentals=0
        ),
        name="products",
    )(place, in_hbm(rows), head)

    terms, picks = in_vmem(terms), in_vmem(picks)
    give, factors, loss = pl.pallas_call(
        give_kernel,
        out_shape=(
            vmem_array((chips, hidden_rows, LANES), jnp.bfloat16),
            vmem_array((tokens, LANES), jnp.float32),
            jax.ShapeDtypeStruct((1, 1), jnp.float32),
        ),
        in_specs=[smem] + [vmem] * 5,
        out_specs=[vmem] * 3,
        compiler_params=params,
        name="give",
    )(place, all_stats, stats, in_vmem(table), terms, picks)
    taken = swap_cores(give)
    keep = pl.pallas_call(
        keep_kernel,
        out_shape=vmem_array((chips, hidden_rows, LANES), jnp.float32),
        in_specs=[smem] + [vmem] * 3,
        out_specs=vmem,
        compiler_params=params,
        cost_estimate=pl.CostEstimate(
            flops=8 * terms.size, bytes_accessed=8 * terms.size, transcendentals=0
        ),
        name="keep",
    )(place, in_vmem(factors), terms, picks)
    sums = keep + taken.astype(jnp.float32)
    steps = range(chips - 1, 0, -1)
    shares = [along_chips(sums[step].astype(jnp.bfloat16), step) for step in steps]
    total = pl.pallas_call(
        sum_kernel,
        out_shape=jax.ShapeDtypeStruct((tokens, half), jnp.bfloat16),
        in_specs=[smem] + [vmem] * chips,
        out_specs=vmem,
        compiler_params=params,
        name="total",
    )(loss_scale, sums[0], *shares)
    return total, jnp.reshape(loss, (1,))


VMEM_LIMIT = 24 * 1024 * 1024


def shards(
    hidden_states, head, teacher_values, teacher_scales, token_ids, lengths, row_map, loss_scale
):
    count = lax.axis_size("vocab")
    own_index = lax.axis_index("vocab")
    tokens = hidden_states.shape[0]
    own_features = hidden_states.shape[1]
    shard_rows = head.shape[0]
    seq_length = tokens // lengths.shape[0]
    contract_last = (((1,), (1,)), ((), ()))

    scaled = scaled_teacher(teacher_values, teacher_scales, count, shard_rows)
    arrived = lax.all_to_all(scaled, "vocab", split_axis=0, concat_axis=0, tiled=True)
    arrived = arrived.reshape(tokens, shard_rows)
    gathered = to_all(hidden_states, count).transpose(1, 0, 2).reshape(tokens, -1)
    logits = lax.dot_general(gathered, head, contract_last, preferred_element_type=jnp.float32)

    positions = jnp.arange(tokens, dtype=jnp.int32)
    owner = row_map[None, :] == positions[:, None]
    slot_of = jnp.sum(jnp.where(owner, positions[None, :], 0), axis=1)
    teacher = jnp.take(arrived, slot_of, axis=0).astype(jnp.float32)

    seq_ids = jnp.arange(lengths.shape[0], dtype=jnp.int32)
    own_length = jnp.sum(
        jnp.where((positions // seq_length)[:, None] == seq_ids[None, :], lengths[None, :], 0),
        axis=1,
    )
    live_mask = (positions % seq_length < own_length).astype(jnp.float32)
    live_count = jnp.sum(live_mask)

    local_ids = token_ids - own_index * shard_rows
    target_hit = local_ids[:, None] == jnp.arange(shard_rows, dtype=jnp.int32)[None, :]
    target_part = jnp.sum(jnp.where(target_hit, logits, 0.0), axis=1)
    student_top = jnp.max(logits, axis=1)
    teacher_top = jnp.max(teacher, axis=1)
    student_off = logits - student_top[:, None]
    teacher_off = teacher - teacher_top[:, None]
    student_exp = jnp.exp(student_off)
    student_sum = jnp.sum(student_exp, axis=1)
    teacher_sum = jnp.sum(jnp.exp(teacher_off), axis=1)
    cross_sum = jnp.sum(student_exp * (student_off - teacher_off), axis=1)

    stats = to_all(
        jnp.stack(
            [student_top, student_sum, teacher_top, teacher_sum, cross_sum, target_part]
        ),
        count,
    )
    tops, sums, teacher_tops, teacher_sums, crosses, targets = [stats[:, i] for i in range(6)]
    student_max, student_total, teacher_max, teacher_total, cross_total = merge_stats(
        tops, sums, teacher_tops, teacher_sums, crosses
    )
    student_log = jnp.log(student_total)
    teacher_log = jnp.log(teacher_total)
    student_lse = student_max + student_log
    teacher_lse = teacher_max + teacher_log
    divergence = cross_total / student_total - (student_log - teacher_log)
    target = jnp.sum(targets, axis=0)

    per_token = divergence + sample_weight * (student_lse - target)
    loss = jnp.reshape(jnp.sum(live_mask * per_token) / live_count, (1,))
    token_weight = live_mask * loss_scale[0] / live_count
    log_student = logits - student_lse[:, None]
    log_teacher = teacher - teacher_lse[:, None]
    student_prob = jnp.exp(log_student)
    grad_logits = (
        token_weight[:, None]
        * (
            student_prob * (log_student - log_teacher - divergence[:, None])
            + sample_weight * (student_prob - target_hit.astype(jnp.float32))
        )
    ).astype(jnp.bfloat16)
    terms = jnp.dot(grad_logits, head, preferred_element_type=jnp.float32).astype(jnp.bfloat16)
    terms = terms.reshape(tokens, count, own_features).transpose(1, 0, 2)
    shares = lax.all_to_all(terms, "vocab", split_axis=0, concat_axis=0, tiled=True)
    grad_hidden = jnp.sum(shares.astype(jnp.float32), axis=0)
    return (grad_hidden.astype(jnp.bfloat16), loss)


def any_shards(*arrays):
    hidden_states, head, teacher_values = arrays[:3]
    count = lax.axis_size("vocab")
    fits = (
        count % 2 == 0
        and hidden_states.shape[1] == 5 * LANES // 2
        and hidden_states.shape[0] % 32 == 0
        and head.shape[0] % LANES == LANES // 2
        and (head.shape[0] + LANES // 2) // LANES % 2 == 0
        and teacher_values.shape[0] == 4
    )
    return paired_shards(*arrays) if fits else shards(*arrays)


def solution(mesh):
    in_specs = (
        P("dom", "vocab"),
        P("vocab", None),
        P(("dom", "vocab"), None),
        P(("dom", "vocab"), None),
        P("dom"),
        P("dom"),
        P("dom"),
        P(),
    )
    out_specs = (P("dom", "vocab"), P("dom"))
    return jax.shard_map(
        any_shards, mesh=mesh, in_specs=in_specs, out_specs=out_specs, check_vma=False
    )
```

```python
import functools

import jax
import jax.numpy as jnp
from jax import lax
from jax.experimental import pallas as pl
from jax.experimental.pallas import tpu as pltpu
from jax.sharding import PartitionSpec as P

BLOCK = 32
LANES = 128
STATS = 8
AHEAD = 3


sample_weight = 0.5


def to_all(piece, count):
    copies = jnp.broadcast_to(piece[None], (count,) + piece.shape)
    return lax.all_to_all(copies, "vocab", split_axis=0, concat_axis=0, tiled=True)


def scaled_teacher(teacher_values, teacher_scales, count, shard_rows):
    slot_rows = teacher_values.shape[0]
    scaled = (
        teacher_values.astype(jnp.float32).reshape(slot_rows, -1, BLOCK) * teacher_scales[:, :, None]
    ).astype(jnp.bfloat16)
    return scaled.reshape(slot_rows, count, shard_rows).transpose(1, 0, 2)


def merge_stats(tops, sums, teacher_tops, teacher_sums, crosses):
    top = jnp.max(tops, axis=0)
    teacher_top = jnp.max(teacher_tops, axis=0)
    shift = tops - top[None]
    teacher_shift = teacher_tops - teacher_top[None]
    weight = jnp.exp(shift)
    total = jnp.sum(sums * weight, axis=0)
    teacher_total = jnp.sum(teacher_sums * jnp.exp(teacher_shift), axis=0)
    cross = jnp.sum(weight * (crosses + sums * (shift - teacher_shift)), axis=0)
    return top, total, teacher_top, teacher_total, cross


def swap_cores(array):
    count = lax.axis_size("vocab")
    return lax.ppermute(array, "vocab", [(i, i ^ 1) for i in range(count)])


def across_chips(blocks):
    count = lax.axis_size("vocab")
    groups = [list(range(core, count, 2)) for core in range(2)]
    return lax.all_to_all(
        blocks, "vocab", split_axis=0, concat_axis=0, axis_index_groups=groups, tiled=True
    )


def along_chips(array, step):
    count = lax.axis_size("vocab")
    return lax.ppermute(array, "vocab", [(i, (i + 2 * step) % count) for i in range(count)])


def vmem_array(shape, dtype):
    return pltpu.VMEM(shape, dtype)


def in_vmem(array):
    return pltpu.with_memory_space_constraint(array, pltpu.VMEM)


def in_hbm(array):
    return pltpu.with_memory_space_constraint(array, pltpu.HBM)


def hbm_array(shape, dtype):
    return pltpu.HBM(shape, dtype)


def low_lanes(shape):
    return lax.broadcasted_iota(jnp.int32, shape, len(shape) - 1) < LANES // 2


def low_rows(shape, count):
    return lax.broadcasted_iota(jnp.int32, shape, 0) < count


def turned(array):
    return pltpu.roll(array, LANES // 2, 1)


def packed_half(tiles):
    rows = tiles[2].shape[0] // 2
    upper, lower = tiles[2][:rows], tiles[2][rows:]
    rest = jnp.where(low_lanes(upper.shape), upper, turned(lower))
    return jnp.concatenate([tiles[0], tiles[1], rest], axis=0)


def unpacked_half(packed, tokens):
    rest = packed[2 * tokens :]
    return [packed[:tokens], packed[tokens : 2 * tokens], jnp.concatenate([rest, turned(rest)])]


def joined(first, second):
    low = low_lanes(first[0].shape)
    turns = [turned(tile) for tile in second]
    return [
        first[0],
        first[1],
        jnp.where(low, first[2], turns[0]),
        jnp.where(low, turns[0], turns[1]),
        jnp.where(low, turns[1], turns[2]),
    ]


def parted(tiles):
    low = low_lanes(tiles[0].shape)
    turns = [turned(tile) for tile in tiles[2:]]
    return tiles[:3], [
        jnp.where(low, turns[0], turns[1]),
        jnp.where(low, turns[1], turns[2]),
        turns[2],
    ]


def column_of(row):
    size = row.shape[1]
    down = lax.broadcasted_iota(jnp.int32, (size, size), 0)
    along = lax.broadcasted_iota(jnp.int32, (size, size), 1)
    return jnp.sum(jnp.where(down == along, row, jnp.zeros_like(row)), axis=1, keepdims=True)


def token_facts(ids, row_map, lengths, first_entry):
    tokens = row_map.shape[1]
    token = lax.broadcasted_iota(jnp.int32, (tokens, tokens), 0)
    slot = lax.broadcasted_iota(jnp.int32, (tokens, tokens), 1)
    owner = (row_map == token).astype(jnp.float32)
    named = jnp.max(owner, axis=1, keepdims=True)
    owner = jnp.where((slot == 0) & (named == 0.0), 1.0, owner)

    seqs = lengths.shape[1]
    seq_length = tokens // seqs
    position = lax.broadcasted_iota(jnp.int32, (tokens, 1), 0)
    live_until = jnp.zeros((tokens, 1), jnp.int32)
    for seq in range(seqs):
        inside = (position >= seq * seq_length) & (position < (seq + 1) * seq_length)
        until = lengths[:, seq : seq + 1] + seq * seq_length
        live_until = jnp.where(inside, until, live_until)
    live = (position < live_until).astype(jnp.float32)
    count = jnp.sum(live, axis=0, keepdims=True)
    entry = (column_of(ids) - first_entry).astype(jnp.float32)
    lane = lax.broadcasted_iota(jnp.int32, (tokens, LANES), 1)
    return owner.astype(jnp.bfloat16), jnp.where(lane == 0, entry, live / count)


def pack_kernel(place_ref, *refs, shard_rows):
    outside, refs = refs[:6], refs[6:]
    packed_ref, owner_ref, table_ref = refs[:3]
    inside, wide_ref, sems = refs[3:9], refs[9], refs[10]
    copies = [
        pltpu.make_async_copy(source, target, sems.at[i])
        for i, (source, target) in enumerate(zip(outside, inside))
    ]
    for copy in copies:
        copy.start()
    for copy in copies:
        copy.wait()
    hidden_ref, values_ref, scales_ref, ids_ref, map_ref, lengths_ref = inside
    owner_ref[...], table_ref[...] = token_facts(
        ids_ref[...], map_ref[...], lengths_ref[...], place_ref[0] * shard_rows
    )
    chips = packed_ref.shape[0]
    tokens, half = hidden_ref.shape
    slots, entries = values_ref.shape
    pair = entries // chips
    shard = pair // 2
    blocks = pair // BLOCK
    scales = jnp.concatenate([scales_ref[...]] * 2, axis=0)
    stacked = jnp.concatenate(
        [scales[:, blocks * chip : blocks * (chip + 1)] for chip in range(chips)], axis=0
    )
    block = lax.broadcasted_iota(jnp.int32, (blocks, pair), 0)
    entry = lax.broadcasted_iota(jnp.int32, (blocks, pair), 1)
    inside = (entry >= block * BLOCK) & (entry < block * BLOCK + BLOCK)
    spread = jnp.dot(
        stacked.astype(jnp.bfloat16),
        inside.astype(jnp.bfloat16),
        preferred_element_type=jnp.float32,
    )
    values = values_ref[...].astype(jnp.float32)
    values = jnp.concatenate([values, values], axis=0)
    for chip in range(chips):
        wide_ref[:, pair * chip : pair * (chip + 1)] = (
            values[:, pair * chip : pair * (chip + 1)]
            * spread[2 * slots * chip : 2 * slots * (chip + 1)]
        )
    wide_ref[:, entries:] = jnp.zeros((2 * slots, LANES), jnp.float32)

    hidden = hidden_ref[...].astype(jnp.float32)
    hidden = jnp.concatenate([hidden, jnp.zeros((tokens, LANES // 2), jnp.float32)], axis=1)
    hidden = packed_half([hidden[:, LANES * i : LANES * (i + 1)] for i in range(3)])
    hidden = hidden.astype(jnp.bfloat16)
    hidden_rows = hidden.shape[0]
    upper = low_rows((2 * slots, LANES), slots)
    low = low_lanes((2 * slots, LANES))
    tile_pairs = (shard + LANES // 2) // LANES // 2
    for chip in range(chips):
        rows = []
        for core in range(2):
            start = pair * chip + (shard - LANES // 2) * core
            tiles = [
                wide_ref[:, start + LANES * i : start + LANES * (i + 1)]
                for i in range(2 * tile_pairs + core)
            ]
            if core == 1:
                tiles = [turned(tile) for tile in tiles]
                tiles = [
                    jnp.where(low, tiles[i], tiles[i + 1]) for i in range(2 * tile_pairs)
                ]
            rows += [
                jnp.where(upper, tiles[2 * i], tiles[2 * i + 1]) for i in range(tile_pairs)
            ]
        packed_ref[chip, :hidden_rows] = hidden
        packed_ref[chip, hidden_rows:] = jnp.concatenate(rows, axis=0).astype(jnp.bfloat16)


def head_copies(head_ref, held_ref, sems, first):
    chips, _, width = held_ref.shape
    copies = []
    for step in range(chips):
        columns = pl.ds(pl.multiple_of(lax.rem(first + step, chips) * width, LANES), width)
        copies.append(
            pltpu.make_async_copy(head_ref.at[:, columns], held_ref.at[step], sems.at[step])
        )
    return copies


def logits_kernel(
    place_ref,
    own_ref,
    other_ref,
    owner_ref,
    tokens_ref,
    head_ref,
    rows_ref,
    stats_ref,
    held_ref,
    hidden_ref,
    arrived_ref,
    teacher_ref,
    sems,
):
    copies = head_copies(head_ref, held_ref, sems, 0)
    for copy in copies[:AHEAD]:
        copy.start()
    core = place_ref[0] % 2
    chips, tokens, width = hidden_ref.shape
    shard_rows = head_ref.shape[0]
    hidden_rows = tokens * width // 2 // LANES
    slots = tokens // (2 * chips)
    upper = low_rows((2 * slots, LANES), slots)

    def both(chip, rows):
        own = own_ref[chip, rows].astype(jnp.float32)
        other = other_ref[chip, rows].astype(jnp.float32)
        return jnp.where(core == 0, own, other), jnp.where(core == 0, other, own)

    def unpack_hidden(chip):
        first, second = both(chip, slice(0, hidden_rows))
        tiles = joined(unpacked_half(first, tokens), unpacked_half(second, tokens))
        hidden_ref[chip] = jnp.concatenate(tiles, axis=1).astype(jnp.bfloat16)

    def unpack_teacher(chip):
        first, second = both(chip, slice(hidden_rows, own_ref.shape[1]))
        share = first.shape[0] // 2
        first = jnp.where(core == 0, first[:share], first[share:])
        second = jnp.where(core == 0, second[:share], second[share:])
        tiles = []
        for row in range(0, share, 2 * slots):
            one, two = first[row : row + 2 * slots], second[row : row + 2 * slots]
            tiles.append(jnp.where(upper, one, pltpu.roll(two, slots, 0)))
            tiles.append(jnp.where(upper, pltpu.roll(one, slots, 0), two))
        arrived_ref[2 * slots * chip : 2 * slots * (chip + 1)] = jnp.concatenate(tiles, axis=1)

    unpack_hidden(0)
    logits = jnp.zeros((tokens, shard_rows), jnp.float32)
    for chip, copy in enumerate(copies):
        copy.wait()
        if chip + AHEAD < chips:
            copies[chip + AHEAD].start()
        if chip + 1 < chips:
            unpack_hidden(chip + 1)
        if chip < chips // 2:
            unpack_teacher(2 * chip)
            unpack_teacher(2 * chip + 1)
        if chip == chips // 2:
            teacher = jnp.dot(
                owner_ref[...],
                arrived_ref[:, :shard_rows].astype(jnp.bfloat16),
                preferred_element_type=jnp.float32,
            )
            teacher_top = jnp.max(teacher, axis=1, keepdims=True)
            teacher_off = teacher - teacher_top
            teacher_total = jnp.sum(jnp.exp(teacher_off), axis=1, keepdims=True)
            teacher_ref[...] = teacher_off
        logits += lax.dot_general(
            hidden_ref[chip],
            held_ref[chip],
            (((1,), (1,)), ((), ())),
            preferred_element_type=jnp.float32,
        )

    top = jnp.max(logits, axis=1, keepdims=True)
    off = logits - top
    exps = jnp.exp(off)
    total = jnp.sum(exps, axis=1, keepdims=True)
    gap = off - teacher_ref[...]
    cross = jnp.sum(exps * gap, axis=1, keepdims=True)
    centre = cross / total
    entry = lax.broadcasted_iota(jnp.int32, (tokens, shard_rows), 1)
    hit = entry == tokens_ref[:, :1].astype(jnp.int32)
    target = jnp.sum(jnp.where(hit, logits, 0.0), axis=1, keepdims=True)
    rows_ref[:tokens] = (exps * (gap - centre)).astype(jnp.bfloat16)
    rows_ref[tokens : 2 * tokens] = exps.astype(jnp.bfloat16)
    rows_ref[2 * tokens :] = hit.astype(jnp.bfloat16)

    lane = lax.broadcasted_iota(jnp.int32, (tokens, LANES), 1)
    table = jnp.zeros((tokens, LANES), jnp.float32)
    for place, column in enumerate(
        (top, total, teacher_top, teacher_total, cross, target, centre)
    ):
        table = jnp.where(lane == place, column, table)
    stats = jnp.concatenate([table, jnp.zeros((stats_ref.shape[2] - tokens, LANES), jnp.float32)])
    stats_ref[...] = jnp.broadcast_to(stats.T[None, :STATS], stats_ref.shape)


def products_kernel(
    place_ref, rows_ref, head_ref, terms_ref, picks_ref, held_ref, made_ref, sems, made_sems
):
    copies = head_copies(head_ref, held_ref, sems, place_ref[0] // 2)
    for copy in copies[:AHEAD]:
        copy.start()
    sums_rows = terms_ref.shape[1]
    outs = []
    for step, copy in enumerate(copies):
        copy.wait()
        if step + AHEAD < len(copies):
            copies[step + AHEAD].start()
        made_ref[step] = jnp.dot(
            rows_ref[sums_rows:], held_ref[step], preferred_element_type=jnp.float32
        ).astype(jnp.bfloat16)
        outs.append(
            pltpu.make_async_copy(made_ref.at[step], picks_ref.at[step], made_sems.at[step])
        )
        outs[-1].start()
        terms_ref[step] = jnp.dot(
            rows_ref[:sums_rows], held_ref[step], preferred_element_type=jnp.float32
        )
    for out in outs:
        out.wait()


def combine_kernel(
    place_ref,
    stats_ref,
    own_ref,
    tokens_ref,
    terms_ref,
    picks_ref,
    keep_ref,
    give_ref,
    loss_ref,
    got_ref,
    sem,
):
    into = pltpu.make_async_copy(picks_ref, got_ref, sem)
    into.start()
    core = place_ref[0] % 2
    chips, _, width = terms_ref.shape
    tokens = tokens_ref.shape[0]
    tops, sums, teacher_tops, teacher_sums, crosses, targets = [
        stats_ref[:, i, :tokens] for i in range(6)
    ]
    top, total, teacher_top, teacher_total, cross = [
        part[None] for part in merge_stats(tops, sums, teacher_tops, teacher_sums, crosses)
    ]
    target = jnp.sum(targets, axis=0, keepdims=True)
    student_log = jnp.log(total)
    teacher_log = jnp.log(teacher_total)
    divergence = cross / total - (student_log - teacher_log)
    student_lse = top + student_log
    per_token = divergence + sample_weight * (student_lse - target)
    student_shift = own_ref[0, 0:1, :tokens] - top - student_log
    teacher_shift = own_ref[0, 2:3, :tokens] - teacher_top - teacher_log
    factor = jnp.exp(student_shift)
    level = (
        own_ref[0, 6:7, :tokens] + student_shift - teacher_shift - divergence + sample_weight
    )
    zeros = jnp.zeros((LANES - 3, tokens), jnp.float32)
    columns = jnp.concatenate([factor, level, per_token, zeros], axis=0).T
    share = tokens_ref[:, 1:2]
    loss_ref[...] = jnp.sum(share * columns[:, 2:3], axis=0, keepdims=True)
    factor = share * columns[:, 0:1]
    level = columns[:, 1:2]
    weight = sample_weight * share
    into.wait()
    for step in range(chips):
        block = (
            factor * (terms_ref[step, :tokens] + level * terms_ref[step, tokens:])
            - weight * got_ref[step].astype(jnp.float32)
        )
        first, second = parted([block[:, i : i + LANES] for i in range(0, width, LANES)])
        first, second = packed_half(first), packed_half(second)
        keep_ref[step] = jnp.where(core == 0, first, second)
        give_ref[step] = jnp.where(core == 0, second, first).astype(jnp.bfloat16)


def sum_kernel(scale_ref, own_ref, *refs):
    tokens, half = refs[-1].shape
    total = own_ref[...]
    for share_ref in refs[:-1]:
        total += share_ref[...].astype(jnp.float32)
    tiles = jnp.concatenate(unpacked_half(total * scale_ref[0], tokens), axis=1)
    refs[-1][...] = tiles[:, :half].astype(refs[-1].dtype)


def paired_shards(
    hidden_states, head, teacher_values, teacher_scales, token_ids, lengths, row_map, loss_scale
):
    count = lax.axis_size("vocab")
    own_index = lax.axis_index("vocab")
    chips = count // 2
    tokens, half = hidden_states.shape
    width = 2 * half
    shard_rows = head.shape[0]
    place = jnp.reshape(own_index, (1,))
    vmem = pl.BlockSpec(memory_space=pltpu.VMEM)
    smem = pl.BlockSpec(memory_space=pltpu.SMEM)
    hbm = pl.BlockSpec(memory_space=pl.ANY)
    params = pltpu.CompilerParams(vmem_limit_bytes=VMEM_LIMIT)
    head = in_hbm(head)
    head_scratch = pltpu.VMEM((chips, shard_rows, width), head.dtype)
    head_sems = pltpu.SemaphoreType.DMA((chips,))
    picks_scratch = pltpu.VMEM((chips, tokens, width), jnp.bfloat16)
    slots, entries = teacher_values.shape
    hidden_rows = tokens * half // LANES
    teacher_rows = 2 * slots * (shard_rows + LANES // 2) // LANES

    operands = (
        hidden_states,
        teacher_values,
        teacher_scales,
        token_ids[None, :],
        row_map[None, :],
        lengths[None, :],
    )
    packed, owner, table = pl.pallas_call(
        functools.partial(pack_kernel, shard_rows=shard_rows),
        out_shape=(
            jax.ShapeDtypeStruct((chips, hidden_rows + teacher_rows, LANES), jnp.bfloat16),
            vmem_array((tokens, tokens), jnp.bfloat16),
            vmem_array((tokens, LANES), jnp.float32),
        ),
        in_specs=[smem] + [hbm] * len(operands),
        out_specs=[vmem] * 3,
        scratch_shapes=[pltpu.VMEM(operand.shape, operand.dtype) for operand in operands]
        + [
            pltpu.VMEM((2 * slots, entries + LANES), jnp.float32),
            pltpu.SemaphoreType.DMA((len(operands),)),
        ],
        compiler_params=params,
        name="pack",
    )(place, *[in_hbm(operand) for operand in operands])
    gathered = across_chips(packed)
    other = swap_cores(gathered)

    rows, stats = pl.pallas_call(
        logits_kernel,
        out_shape=(
            vmem_array((3 * tokens, shard_rows), jnp.bfloat16),
            jax.ShapeDtypeStruct((count, STATS, pl.cdiv(tokens, LANES) * LANES), jnp.float32),
        ),
        in_specs=[smem] + [vmem] * 4 + [hbm],
        out_specs=[vmem] * 2,
        scratch_shapes=[
            head_scratch,
            pltpu.VMEM((chips, tokens, width), jnp.bfloat16),
            pltpu.VMEM((tokens, shard_rows + LANES // 2), jnp.float32),
            pltpu.VMEM((tokens, shard_rows), jnp.float32),
            head_sems,
        ],
        compiler_params=params,
        cost_estimate=pl.CostEstimate(
            flops=2 * tokens * head.size, bytes_accessed=2 * head.size, transcendentals=0
        ),
        name="logits",
    )(place, gathered, other, in_vmem(owner), in_vmem(table), head)

    all_stats = lax.all_to_all(stats, "vocab", split_axis=0, concat_axis=0, tiled=True)

    terms, picks = pl.pallas_call(
        products_kernel,
        out_shape=(
            vmem_array((chips, 2 * tokens, width), jnp.float32),
            hbm_array((chips, tokens, width), jnp.bfloat16),
        ),
        in_specs=[smem, vmem, hbm],
        out_specs=[vmem, hbm],
        scratch_shapes=[head_scratch, picks_scratch, head_sems, head_sems],
        compiler_params=params,
        cost_estimate=pl.CostEstimate(
            flops=6 * tokens * head.size, bytes_accessed=2 * head.size, transcendentals=0
        ),
        name="products",
    )(place, in_vmem(rows), head)

    keep, give, loss = pl.pallas_call(
        combine_kernel,
        out_shape=(
            vmem_array((chips, hidden_rows, LANES), jnp.float32),
            vmem_array((chips, hidden_rows, LANES), jnp.bfloat16),
            jax.ShapeDtypeStruct((1, 1), jnp.float32),
        ),
        in_specs=[smem] + [vmem] * 4 + [hbm],
        out_specs=[vmem] * 3,
        scratch_shapes=[picks_scratch, pltpu.SemaphoreType.DMA],
        compiler_params=params,
        name="combine",
    )(place, all_stats, stats, in_vmem(table), in_vmem(terms), in_hbm(picks))

    sums = keep + swap_cores(give).astype(jnp.float32)
    steps = range(1, chips)
    shares = [along_chips(sums[step].astype(jnp.bfloat16), step) for step in steps]
    total = pl.pallas_call(
        sum_kernel,
        out_shape=jax.ShapeDtypeStruct((tokens, half), jnp.bfloat16),
        in_specs=[smem] + [vmem] * chips,
        out_specs=vmem,
        compiler_params=params,
        name="total",
    )(loss_scale, sums[0], *shares)
    return total, jnp.reshape(loss, (1,))


VMEM_LIMIT = 24 * 1024 * 1024


def shards(
    hidden_states, head, teacher_values, teacher_scales, token_ids, lengths, row_map, loss_scale
):
    count = lax.axis_size("vocab")
    own_index = lax.axis_index("vocab")
    tokens = hidden_states.shape[0]
    own_features = hidden_states.shape[1]
    shard_rows = head.shape[0]
    seq_length = tokens // lengths.shape[0]
    contract_last = (((1,), (1,)), ((), ()))

    scaled = scaled_teacher(teacher_values, teacher_scales, count, shard_rows)
    arrived = lax.all_to_all(scaled, "vocab", split_axis=0, concat_axis=0, tiled=True)
    arrived = arrived.reshape(tokens, shard_rows)
    gathered = to_all(hidden_states, count).transpose(1, 0, 2).reshape(tokens, -1)
    logits = lax.dot_general(gathered, head, contract_last, preferred_element_type=jnp.float32)

    positions = jnp.arange(tokens, dtype=jnp.int32)
    owner = row_map[None, :] == positions[:, None]
    slot_of = jnp.sum(jnp.where(owner, positions[None, :], 0), axis=1)
    teacher = jnp.take(arrived, slot_of, axis=0).astype(jnp.float32)

    seq_ids = jnp.arange(lengths.shape[0], dtype=jnp.int32)
    own_length = jnp.sum(
        jnp.where((positions // seq_length)[:, None] == seq_ids[None, :], lengths[None, :], 0),
        axis=1,
    )
    live_mask = (positions % seq_length < own_length).astype(jnp.float32)
    live_count = jnp.sum(live_mask)

    local_ids = token_ids - own_index * shard_rows
    target_hit = local_ids[:, None] == jnp.arange(shard_rows, dtype=jnp.int32)[None, :]
    target_part = jnp.sum(jnp.where(target_hit, logits, 0.0), axis=1)
    student_top = jnp.max(logits, axis=1)
    teacher_top = jnp.max(teacher, axis=1)
    student_off = logits - student_top[:, None]
    teacher_off = teacher - teacher_top[:, None]
    student_exp = jnp.exp(student_off)
    student_sum = jnp.sum(student_exp, axis=1)
    teacher_sum = jnp.sum(jnp.exp(teacher_off), axis=1)
    cross_sum = jnp.sum(student_exp * (student_off - teacher_off), axis=1)

    stats = to_all(
        jnp.stack(
            [student_top, student_sum, teacher_top, teacher_sum, cross_sum, target_part]
        ),
        count,
    )
    tops, sums, teacher_tops, teacher_sums, crosses, targets = [stats[:, i] for i in range(6)]
    student_max, student_total, teacher_max, teacher_total, cross_total = merge_stats(
        tops, sums, teacher_tops, teacher_sums, crosses
    )
    student_log = jnp.log(student_total)
    teacher_log = jnp.log(teacher_total)
    student_lse = student_max + student_log
    teacher_lse = teacher_max + teacher_log
    divergence = cross_total / student_total - (student_log - teacher_log)
    target = jnp.sum(targets, axis=0)

    per_token = divergence + sample_weight * (student_lse - target)
    loss = jnp.reshape(jnp.sum(live_mask * per_token) / live_count, (1,))
    token_weight = live_mask * loss_scale[0] / live_count
    log_student = logits - student_lse[:, None]
    log_teacher = teacher - teacher_lse[:, None]
    student_prob = jnp.exp(log_student)
    grad_logits = (
        token_weight[:, None]
        * (
            student_prob * (log_student - log_teacher - divergence[:, None])
            + sample_weight * (student_prob - target_hit.astype(jnp.float32))
        )
    ).astype(jnp.bfloat16)
    terms = jnp.dot(grad_logits, head, preferred_element_type=jnp.float32).astype(jnp.bfloat16)
    terms = terms.reshape(tokens, count, own_features).transpose(1, 0, 2)
    shares = lax.all_to_all(terms, "vocab", split_axis=0, concat_axis=0, tiled=True)
    grad_hidden = jnp.sum(shares.astype(jnp.float32), axis=0)
    return (grad_hidden.astype(jnp.bfloat16), loss)


def any_shards(*arrays):
    hidden_states, head, teacher_values = arrays[:3]
    count = lax.axis_size("vocab")
    fits = (
        count % 2 == 0
        and hidden_states.shape[1] == 5 * LANES // 2
        and hidden_states.shape[0] % 32 == 0
        and head.shape[0] % LANES == LANES // 2
        and (head.shape[0] + LANES // 2) // LANES % 2 == 0
        and teacher_values.shape[0] == 4
    )
    return paired_shards(*arrays) if fits else shards(*arrays)


def solution(mesh):
    in_specs = (
        P("dom", "vocab"),
        P("vocab", None),
        P(("dom", "vocab"), None),
        P(("dom", "vocab"), None),
        P("dom"),
        P("dom"),
        P("dom"),
        P(),
    )
    out_specs = (P("dom", "vocab"), P("dom"))
    return jax.shard_map(
        any_shards, mesh=mesh, in_specs=in_specs, out_specs=out_specs, check_vma=False
    )
```

```python
import functools

import jax
import jax.numpy as jnp
from jax import lax
from jax.experimental import pallas as pl
from jax.experimental.pallas import tpu as pltpu
from jax.sharding import PartitionSpec as P

BLOCK = 32
LANES = 128
STATS = 8
AHEAD = 3


sample_weight = 0.5


def to_all(piece, count):
    copies = jnp.broadcast_to(piece[None], (count,) + piece.shape)
    return lax.all_to_all(copies, "vocab", split_axis=0, concat_axis=0, tiled=True)


def scaled_teacher(teacher_values, teacher_scales, count, shard_rows):
    slot_rows = teacher_values.shape[0]
    scaled = (
        teacher_values.astype(jnp.float32).reshape(slot_rows, -1, BLOCK) * teacher_scales[:, :, None]
    ).astype(jnp.bfloat16)
    return scaled.reshape(slot_rows, count, shard_rows).transpose(1, 0, 2)


def merge_stats(tops, sums, teacher_tops, teacher_sums, crosses):
    top = jnp.max(tops, axis=0)
    teacher_top = jnp.max(teacher_tops, axis=0)
    shift = tops - top[None]
    teacher_shift = teacher_tops - teacher_top[None]
    weight = jnp.exp(shift)
    total = jnp.sum(sums * weight, axis=0)
    teacher_total = jnp.sum(teacher_sums * jnp.exp(teacher_shift), axis=0)
    cross = jnp.sum(weight * (crosses + sums * (shift - teacher_shift)), axis=0)
    return top, total, teacher_top, teacher_total, cross


def swap_cores(array):
    count = lax.axis_size("vocab")
    return lax.ppermute(array, "vocab", [(i, i ^ 1) for i in range(count)])


def along_chips(array, step):
    count = lax.axis_size("vocab")
    return lax.ppermute(array, "vocab", [(i, (i + 2 * step) % count) for i in range(count)])


def vmem_array(shape, dtype):
    return pltpu.VMEM(shape, dtype)


def in_vmem(array):
    return pltpu.with_memory_space_constraint(array, pltpu.VMEM)


def in_hbm(array):
    return pltpu.with_memory_space_constraint(array, pltpu.HBM)


def hbm_array(shape, dtype):
    return pltpu.HBM(shape, dtype)


def low_lanes(shape):
    return lax.broadcasted_iota(jnp.int32, shape, len(shape) - 1) < LANES // 2


def low_rows(shape, count):
    return lax.broadcasted_iota(jnp.int32, shape, 0) < count


def turned(array):
    return pltpu.roll(array, LANES // 2, 1)


def packed_half(tiles):
    rows = tiles[2].shape[0] // 2
    upper, lower = tiles[2][:rows], tiles[2][rows:]
    rest = jnp.where(low_lanes(upper.shape), upper, turned(lower))
    return jnp.concatenate([tiles[0], tiles[1], rest], axis=0)


def unpacked_half(packed, tokens):
    rest = packed[2 * tokens :]
    return [packed[:tokens], packed[tokens : 2 * tokens], jnp.concatenate([rest, turned(rest)])]


def joined(first, second):
    low = low_lanes(first[0].shape)
    turns = [turned(tile) for tile in second]
    return [
        first[0],
        first[1],
        jnp.where(low, first[2], turns[0]),
        jnp.where(low, turns[0], turns[1]),
        jnp.where(low, turns[1], turns[2]),
    ]


def parted(tiles):
    low = low_lanes(tiles[0].shape)
    turns = [turned(tile) for tile in tiles[2:]]
    return tiles[:3], [
        jnp.where(low, turns[0], turns[1]),
        jnp.where(low, turns[1], turns[2]),
        turns[2],
    ]


def column_of(row):
    size = row.shape[1]
    down = lax.broadcasted_iota(jnp.int32, (size, size), 0)
    along = lax.broadcasted_iota(jnp.int32, (size, size), 1)
    return jnp.sum(jnp.where(down == along, row, jnp.zeros_like(row)), axis=1, keepdims=True)


def token_facts(ids, row_map, lengths, first_entry):
    tokens = row_map.shape[1]
    token = lax.broadcasted_iota(jnp.int32, (tokens, tokens), 0)
    slot = lax.broadcasted_iota(jnp.int32, (tokens, tokens), 1)
    owner = (row_map == token).astype(jnp.float32)
    named = jnp.max(owner, axis=1, keepdims=True)
    owner = jnp.where((slot == 0) & (named == 0.0), 1.0, owner)

    seqs = lengths.shape[1]
    seq_length = tokens // seqs
    position = lax.broadcasted_iota(jnp.int32, (tokens, 1), 0)
    live_until = jnp.zeros((tokens, 1), jnp.int32)
    for seq in range(seqs):
        inside = (position >= seq * seq_length) & (position < (seq + 1) * seq_length)
        until = lengths[:, seq : seq + 1] + seq * seq_length
        live_until = jnp.where(inside, until, live_until)
    live = (position < live_until).astype(jnp.float32)
    count = jnp.sum(live, axis=0, keepdims=True)
    entry = (column_of(ids) - first_entry).astype(jnp.float32)
    lane = lax.broadcasted_iota(jnp.int32, (tokens, LANES), 1)
    return owner.astype(jnp.bfloat16), jnp.where(lane == 0, entry, live / count)


def pack_kernel(place_ref, *refs, shard_rows):
    outside, refs = refs[:6], refs[6:]
    packed_ref, owner_ref, table_ref = refs[:3]
    inside, wide_ref, sems = refs[3:9], refs[9], refs[10]
    copies = [
        pltpu.make_async_copy(source, target, sems.at[i])
        for i, (source, target) in enumerate(zip(outside, inside))
    ]
    for copy in copies:
        copy.start()
    for copy in copies:
        copy.wait()
    hidden_ref, values_ref, scales_ref, ids_ref, map_ref, lengths_ref = inside
    owner_ref[...], table_ref[...] = token_facts(
        ids_ref[...], map_ref[...], lengths_ref[...], place_ref[0] * shard_rows
    )
    chips = packed_ref.shape[0]
    tokens, half = hidden_ref.shape
    slots, entries = values_ref.shape
    pair = entries // chips
    shard = pair // 2
    blocks = pair // BLOCK
    scales = jnp.concatenate([scales_ref[...]] * 2, axis=0)
    stacked = jnp.concatenate(
        [scales[:, blocks * chip : blocks * (chip + 1)] for chip in range(chips)], axis=0
    )
    block = lax.broadcasted_iota(jnp.int32, (blocks, pair), 0)
    entry = lax.broadcasted_iota(jnp.int32, (blocks, pair), 1)
    inside = (entry >= block * BLOCK) & (entry < block * BLOCK + BLOCK)
    spread = jnp.dot(
        stacked.astype(jnp.bfloat16),
        inside.astype(jnp.bfloat16),
        preferred_element_type=jnp.float32,
    )
    values = values_ref[...].astype(jnp.float32)
    values = jnp.concatenate([values, values], axis=0)
    for chip in range(chips):
        wide_ref[:, pair * chip : pair * (chip + 1)] = (
            values[:, pair * chip : pair * (chip + 1)]
            * spread[2 * slots * chip : 2 * slots * (chip + 1)]
        )
    wide_ref[:, entries:] = jnp.zeros((2 * slots, LANES), jnp.float32)

    hidden = hidden_ref[...].astype(jnp.float32)
    hidden = jnp.concatenate([hidden, jnp.zeros((tokens, LANES // 2), jnp.float32)], axis=1)
    hidden = packed_half([hidden[:, LANES * i : LANES * (i + 1)] for i in range(3)])
    hidden = hidden.astype(jnp.bfloat16)
    hidden_rows = hidden.shape[0]
    upper = low_rows((2 * slots, LANES), slots)
    low = low_lanes((2 * slots, LANES))
    tile_pairs = (shard + LANES // 2) // LANES // 2
    for chip in range(chips):
        rows = []
        for core in range(2):
            start = pair * chip + (shard - LANES // 2) * core
            tiles = [
                wide_ref[:, start + LANES * i : start + LANES * (i + 1)]
                for i in range(2 * tile_pairs + core)
            ]
            if core == 1:
                tiles = [turned(tile) for tile in tiles]
                tiles = [
                    jnp.where(low, tiles[i], tiles[i + 1]) for i in range(2 * tile_pairs)
                ]
            rows += [
                jnp.where(upper, tiles[2 * i], tiles[2 * i + 1]) for i in range(tile_pairs)
            ]
        step = lax.rem(chip - place_ref[0] // 2 + chips, chips)
        packed_ref[step, :hidden_rows] = hidden
        packed_ref[step, hidden_rows:] = jnp.concatenate(rows, axis=0).astype(jnp.bfloat16)


def head_copies(head_ref, held_ref, sems, chips):
    width = held_ref.shape[2]
    copies = []
    for step, chip in enumerate(chips):
        columns = pl.ds(pl.multiple_of(chip * width, LANES), width)
        copies.append(
            pltpu.make_async_copy(head_ref.at[:, columns], held_ref.at[step], sems.at[step])
        )
    return copies


def logits_kernel(place_ref, *refs, chips):
    near, far, refs = refs[:chips], refs[chips : chips + 2], refs[chips + 2 :]
    owner_ref, tokens_ref, head_ref, rows_ref, stats_ref = refs[:5]
    held_ref, made_ref, hidden_ref, arrived_ref, teacher_ref, sems, made_sem = refs[5:]
    place = place_ref[0] // 2
    core = place_ref[0] % 2
    sources = [lax.rem(place - step + chips, chips) for step in range(chips)]
    copies = head_copies(head_ref, held_ref, sems, sources)
    for copy in copies[:AHEAD]:
        copy.start()
    _, tokens, width = hidden_ref.shape
    shard_rows = head_ref.shape[0]
    hidden_rows = tokens * width // 2 // LANES
    slots = tokens // (2 * chips)
    upper = low_rows((2 * slots, LANES), slots)

    def both(step, rows):
        own = near[step][rows].astype(jnp.float32)
        group = far[step // (chips // 2)]
        other = group[step % (chips // 2), rows].astype(jnp.float32)
        return jnp.where(core == 0, own, other), jnp.where(core == 0, other, own)

    def unpack_hidden(step):
        first, second = both(step, slice(0, hidden_rows))
        tiles = joined(unpacked_half(first, tokens), unpacked_half(second, tokens))
        hidden_ref[step] = jnp.concatenate(tiles, axis=1).astype(jnp.bfloat16)

    def unpack_teacher(step):
        first, second = both(step, slice(hidden_rows, near[0].shape[0]))
        share = first.shape[0] // 2
        first = jnp.where(core == 0, first[:share], first[share:])
        second = jnp.where(core == 0, second[:share], second[share:])
        tiles = []
        for row in range(0, share, 2 * slots):
            one, two = first[row : row + 2 * slots], second[row : row + 2 * slots]
            tiles.append(jnp.where(upper, one, pltpu.roll(two, slots, 0)))
            tiles.append(jnp.where(upper, pltpu.roll(one, slots, 0), two))
        rows = pl.ds(pl.multiple_of(2 * slots * sources[step], 2 * slots), 2 * slots)
        arrived_ref[rows] = jnp.concatenate(tiles, axis=1)

    unpack_hidden(0)
    logits = jnp.zeros((tokens, shard_rows), jnp.float32)
    for chip, copy in enumerate(copies):
        copy.wait()
        if chip + AHEAD < chips:
            copies[chip + AHEAD].start()
        if chip + 1 < chips:
            unpack_hidden(chip + 1)
        if chip < chips // 2:
            unpack_teacher(2 * chip)
            unpack_teacher(2 * chip + 1)
        if chip == chips // 2:
            teacher = jnp.dot(
                owner_ref[...],
                arrived_ref[:, :shard_rows].astype(jnp.bfloat16),
                preferred_element_type=jnp.float32,
            )
            teacher_top = jnp.max(teacher, axis=1, keepdims=True)
            teacher_off = teacher - teacher_top
            teacher_total = jnp.sum(jnp.exp(teacher_off), axis=1, keepdims=True)
            teacher_ref[...] = teacher_off
        logits += lax.dot_general(
            hidden_ref[chip],
            held_ref[chip],
            (((1,), (1,)), ((), ())),
            preferred_element_type=jnp.float32,
        )

    top = jnp.max(logits, axis=1, keepdims=True)
    off = logits - top
    exps = jnp.exp(off)
    total = jnp.sum(exps, axis=1, keepdims=True)
    gap = off - teacher_ref[...]
    cross = jnp.sum(exps * gap, axis=1, keepdims=True)
    centre = cross / total
    entry = lax.broadcasted_iota(jnp.int32, (tokens, shard_rows), 1)
    hit = entry == tokens_ref[:, :1].astype(jnp.int32)
    target = jnp.sum(jnp.where(hit, logits, 0.0), axis=1, keepdims=True)
    made_ref[:tokens] = (exps * (gap - centre)).astype(jnp.bfloat16)
    made_ref[tokens : 2 * tokens] = exps.astype(jnp.bfloat16)
    made_ref[2 * tokens :] = hit.astype(jnp.bfloat16)
    out = pltpu.make_async_copy(made_ref, rows_ref, made_sem)
    out.start()

    lane = lax.broadcasted_iota(jnp.int32, (tokens, LANES), 1)
    table = jnp.zeros((tokens, LANES), jnp.float32)
    for place, column in enumerate(
        (top, total, teacher_top, teacher_total, cross, target, centre)
    ):
        table = jnp.where(lane == place, column, table)
    stats = jnp.concatenate([table, jnp.zeros((stats_ref.shape[2] - tokens, LANES), jnp.float32)])
    stats_ref[...] = jnp.broadcast_to(stats.T[None, :STATS], stats_ref.shape)
    out.wait()


def products_kernel(
    place_ref, rows_ref, head_ref, terms_ref, picks_ref, held_ref, made_ref, sems, made_sem
):
    into = pltpu.make_async_copy(rows_ref, made_ref, made_sem)
    into.start()
    chips = held_ref.shape[0]
    targets = [lax.rem(place_ref[0] // 2 + step, chips) for step in range(chips)]
    copies = head_copies(head_ref, held_ref, sems, targets)
    for copy in copies[:AHEAD]:
        copy.start()
    into.wait()
    sums_rows = terms_ref.shape[1]
    for step, copy in enumerate(copies):
        copy.wait()
        if step + AHEAD < len(copies):
            copies[step + AHEAD].start()
        products = jnp.dot(made_ref[...], held_ref[step], preferred_element_type=jnp.float32)
        terms_ref[step] = products[:sums_rows]
        picks_ref[step] = products[sums_rows:].astype(jnp.bfloat16)


def combine_kernel(
    place_ref,
    stats_ref,
    own_ref,
    tokens_ref,
    terms_ref,
    picks_ref,
    keep_ref,
    give_ref,
    loss_ref,
):
    core = place_ref[0] % 2
    chips, _, width = terms_ref.shape
    tokens = tokens_ref.shape[0]
    tops, sums, teacher_tops, teacher_sums, crosses, targets = [
        stats_ref[:, i, :tokens] for i in range(6)
    ]
    top, total, teacher_top, teacher_total, cross = [
        part[None] for part in merge_stats(tops, sums, teacher_tops, teacher_sums, crosses)
    ]
    target = jnp.sum(targets, axis=0, keepdims=True)
    student_log = jnp.log(total)
    teacher_log = jnp.log(teacher_total)
    divergence = cross / total - (student_log - teacher_log)
    student_lse = top + student_log
    per_token = divergence + sample_weight * (student_lse - target)
    student_shift = own_ref[0, 0:1, :tokens] - top - student_log
    teacher_shift = own_ref[0, 2:3, :tokens] - teacher_top - teacher_log
    factor = jnp.exp(student_shift)
    level = (
        own_ref[0, 6:7, :tokens] + student_shift - teacher_shift - divergence + sample_weight
    )
    zeros = jnp.zeros((LANES - 3, tokens), jnp.float32)
    columns = jnp.concatenate([factor, level, per_token, zeros], axis=0).T
    share = tokens_ref[:, 1:2]
    loss_ref[...] = jnp.sum(share * columns[:, 2:3], axis=0, keepdims=True)
    factor = share * columns[:, 0:1]
    level = columns[:, 1:2]
    weight = sample_weight * share
    for step in range(chips):
        block = (
            factor * (terms_ref[step, :tokens] + level * terms_ref[step, tokens:])
            - weight * picks_ref[step].astype(jnp.float32)
        )
        first, second = parted([block[:, i : i + LANES] for i in range(0, width, LANES)])
        first, second = packed_half(first), packed_half(second)
        keep_ref[step] = jnp.where(core == 0, first, second)
        give_ref[step] = jnp.where(core == 0, second, first).astype(jnp.bfloat16)


def sum_kernel(scale_ref, own_ref, *refs):
    tokens, half = refs[-1].shape
    total = own_ref[...]
    for share_ref in refs[:-1]:
        total += share_ref[...].astype(jnp.float32)
    tiles = jnp.concatenate(unpacked_half(total * scale_ref[...], tokens), axis=1)
    refs[-1][...] = tiles[:, :half].astype(refs[-1].dtype)


def paired_shards(
    hidden_states, head, teacher_values, teacher_scales, token_ids, lengths, row_map, loss_scale
):
    count = lax.axis_size("vocab")
    own_index = lax.axis_index("vocab")
    chips = count // 2
    tokens, half = hidden_states.shape
    width = 2 * half
    shard_rows = head.shape[0]
    place = jnp.reshape(own_index, (1,))
    vmem = pl.BlockSpec(memory_space=pltpu.VMEM)
    smem = pl.BlockSpec(memory_space=pltpu.SMEM)
    hbm = pl.BlockSpec(memory_space=pl.ANY)
    params = pltpu.CompilerParams(vmem_limit_bytes=VMEM_LIMIT)
    head = in_hbm(head)
    head_scratch = pltpu.VMEM((chips, shard_rows, width), head.dtype)
    head_sems = pltpu.SemaphoreType.DMA((chips,))
    rows_scratch = pltpu.VMEM((3 * tokens, shard_rows), jnp.bfloat16)
    rows_sem = pltpu.SemaphoreType.DMA
    slots, entries = teacher_values.shape
    hidden_rows = tokens * half // LANES
    teacher_rows = 2 * slots * (shard_rows + LANES // 2) // LANES

    operands = (
        hidden_states,
        teacher_values,
        teacher_scales,
        token_ids[None, :],
        row_map[None, :],
        lengths[None, :],
    )
    packed, owner, table = pl.pallas_call(
        functools.partial(pack_kernel, shard_rows=shard_rows),
        out_shape=(
            jax.ShapeDtypeStruct((chips, hidden_rows + teacher_rows, LANES), jnp.bfloat16),
            vmem_array((tokens, tokens), jnp.bfloat16),
            vmem_array((tokens, LANES), jnp.float32),
        ),
        in_specs=[smem] + [hbm] * len(operands),
        out_specs=[vmem] * 3,
        scratch_shapes=[pltpu.VMEM(operand.shape, operand.dtype) for operand in operands]
        + [
            pltpu.VMEM((2 * slots, entries + LANES), jnp.float32),
            pltpu.SemaphoreType.DMA((len(operands),)),
        ],
        compiler_params=params,
        name="pack",
    )(place, *[in_hbm(operand) for operand in operands])
    steps = range(1, chips)
    near = [packed[0]] + [along_chips(packed[step], step) for step in steps]
    far = [
        swap_cores(jnp.stack(near[: chips // 2])),
        swap_cores(jnp.stack(near[chips // 2 :])),
    ]

    rows, stats = pl.pallas_call(
        functools.partial(logits_kernel, chips=chips),
        out_shape=(
            hbm_array((3 * tokens, shard_rows), jnp.bfloat16),
            jax.ShapeDtypeStruct((count, STATS, pl.cdiv(tokens, LANES) * LANES), jnp.float32),
        ),
        in_specs=[smem] + [vmem] * (chips + 4) + [hbm],
        out_specs=[hbm, vmem],
        scratch_shapes=[
            head_scratch,
            rows_scratch,
            pltpu.VMEM((chips, tokens, width), jnp.bfloat16),
            pltpu.VMEM((tokens, shard_rows + LANES // 2), jnp.float32),
            pltpu.VMEM((tokens, shard_rows), jnp.float32),
            head_sems,
            rows_sem,
        ],
        compiler_params=params,
        cost_estimate=pl.CostEstimate(
            flops=2 * tokens * head.size, bytes_accessed=2 * head.size, transcendentals=0
        ),
        name="logits",
    )(place, *near, *far, in_vmem(owner), in_vmem(table), head)

    all_stats = lax.all_to_all(stats, "vocab", split_axis=0, concat_axis=0, tiled=True)

    terms, picks = pl.pallas_call(
        products_kernel,
        out_shape=(
            vmem_array((chips, 2 * tokens, width), jnp.float32),
            vmem_array((chips, tokens, width), jnp.bfloat16),
        ),
        in_specs=[smem, hbm, hbm],
        out_specs=[vmem] * 2,
        scratch_shapes=[head_scratch, rows_scratch, head_sems, rows_sem],
        compiler_params=params,
        cost_estimate=pl.CostEstimate(
            flops=6 * tokens * head.size, bytes_accessed=2 * head.size, transcendentals=0
        ),
        name="products",
    )(place, in_hbm(rows), head)

    keep, give, loss = pl.pallas_call(
        combine_kernel,
        out_shape=(
            vmem_array((chips, hidden_rows, LANES), jnp.float32),
            vmem_array((chips, hidden_rows, LANES), jnp.bfloat16),
            jax.ShapeDtypeStruct((1, 1), jnp.float32),
        ),
        in_specs=[smem] + [vmem] * 5,
        out_specs=[vmem] * 3,
        compiler_params=params,
        name="combine",
    )(place, all_stats, stats, in_vmem(table), in_vmem(terms), in_vmem(picks))

    sums = keep + swap_cores(give).astype(jnp.float32)
    shares = [along_chips(sums[step].astype(jnp.bfloat16), step) for step in steps]
    total = pl.pallas_call(
        sum_kernel,
        out_shape=jax.ShapeDtypeStruct((tokens, half), jnp.bfloat16),
        in_specs=[vmem] * (chips + 1),
        out_specs=vmem,
        compiler_params=params,
        name="total",
    )(loss_scale[None, :], sums[0], *shares)
    return total, jnp.reshape(loss, (1,))


VMEM_LIMIT = 24 * 1024 * 1024


def shards(
    hidden_states, head, teacher_values, teacher_scales, token_ids, lengths, row_map, loss_scale
):
    count = lax.axis_size("vocab")
    own_index = lax.axis_index("vocab")
    tokens = hidden_states.shape[0]
    own_features = hidden_states.shape[1]
    shard_rows = head.shape[0]
    seq_length = tokens // lengths.shape[0]
    contract_last = (((1,), (1,)), ((), ()))

    scaled = scaled_teacher(teacher_values, teacher_scales, count, shard_rows)
    arrived = lax.all_to_all(scaled, "vocab", split_axis=0, concat_axis=0, tiled=True)
    arrived = arrived.reshape(tokens, shard_rows)
    gathered = to_all(hidden_states, count).transpose(1, 0, 2).reshape(tokens, -1)
    logits = lax.dot_general(gathered, head, contract_last, preferred_element_type=jnp.float32)

    positions = jnp.arange(tokens, dtype=jnp.int32)
    owner = row_map[None, :] == positions[:, None]
    slot_of = jnp.sum(jnp.where(owner, positions[None, :], 0), axis=1)
    teacher = jnp.take(arrived, slot_of, axis=0).astype(jnp.float32)

    seq_ids = jnp.arange(lengths.shape[0], dtype=jnp.int32)
    own_length = jnp.sum(
        jnp.where((positions // seq_length)[:, None] == seq_ids[None, :], lengths[None, :], 0),
        axis=1,
    )
    live_mask = (positions % seq_length < own_length).astype(jnp.float32)
    live_count = jnp.sum(live_mask)

    local_ids = token_ids - own_index * shard_rows
    target_hit = local_ids[:, None] == jnp.arange(shard_rows, dtype=jnp.int32)[None, :]
    target_part = jnp.sum(jnp.where(target_hit, logits, 0.0), axis=1)
    student_top = jnp.max(logits, axis=1)
    teacher_top = jnp.max(teacher, axis=1)
    student_off = logits - student_top[:, None]
    teacher_off = teacher - teacher_top[:, None]
    student_exp = jnp.exp(student_off)
    student_sum = jnp.sum(student_exp, axis=1)
    teacher_sum = jnp.sum(jnp.exp(teacher_off), axis=1)
    cross_sum = jnp.sum(student_exp * (student_off - teacher_off), axis=1)

    stats = to_all(
        jnp.stack(
            [student_top, student_sum, teacher_top, teacher_sum, cross_sum, target_part]
        ),
        count,
    )
    tops, sums, teacher_tops, teacher_sums, crosses, targets = [stats[:, i] for i in range(6)]
    student_max, student_total, teacher_max, teacher_total, cross_total = merge_stats(
        tops, sums, teacher_tops, teacher_sums, crosses
    )
    student_log = jnp.log(student_total)
    teacher_log = jnp.log(teacher_total)
    student_lse = student_max + student_log
    teacher_lse = teacher_max + teacher_log
    divergence = cross_total / student_total - (student_log - teacher_log)
    target = jnp.sum(targets, axis=0)

    per_token = divergence + sample_weight * (student_lse - target)
    loss = jnp.reshape(jnp.sum(live_mask * per_token) / live_count, (1,))
    token_weight = live_mask * loss_scale[0] / live_count
    log_student = logits - student_lse[:, None]
    log_teacher = teacher - teacher_lse[:, None]
    student_prob = jnp.exp(log_student)
    grad_logits = (
        token_weight[:, None]
        * (
            student_prob * (log_student - log_teacher - divergence[:, None])
            + sample_weight * (student_prob - target_hit.astype(jnp.float32))
        )
    ).astype(jnp.bfloat16)
    terms = jnp.dot(grad_logits, head, preferred_element_type=jnp.float32).astype(jnp.bfloat16)
    terms = terms.reshape(tokens, count, own_features).transpose(1, 0, 2)
    shares = lax.all_to_all(terms, "vocab", split_axis=0, concat_axis=0, tiled=True)
    grad_hidden = jnp.sum(shares.astype(jnp.float32), axis=0)
    return (grad_hidden.astype(jnp.bfloat16), loss)


def any_shards(*arrays):
    hidden_states, head, teacher_values = arrays[:3]
    count = lax.axis_size("vocab")
    fits = (
        count % 2 == 0
        and hidden_states.shape[1] == 5 * LANES // 2
        and hidden_states.shape[0] % 32 == 0
        and head.shape[0] % LANES == LANES // 2
        and (head.shape[0] + LANES // 2) // LANES % 2 == 0
        and teacher_values.shape[0] == 4
    )
    return paired_shards(*arrays) if fits else shards(*arrays)


def solution(mesh):
    in_specs = (
        P("dom", "vocab"),
        P("vocab", None),
        P(("dom", "vocab"), None),
        P(("dom", "vocab"), None),
        P("dom"),
        P("dom"),
        P("dom"),
        P(),
    )
    out_specs = (P("dom", "vocab"), P("dom"))
    return jax.shard_map(
        any_shards, mesh=mesh, in_specs=in_specs, out_specs=out_specs, check_vma=False
    )
```

```python
import functools

import jax
import jax.numpy as jnp
from jax import lax
from jax.experimental import pallas as pl
from jax.experimental.pallas import tpu as pltpu
from jax.sharding import PartitionSpec as P

BLOCK = 32
LANES = 128
STATS = 8
AHEAD = 3


sample_weight = 0.5


def to_all(piece, count):
    copies = jnp.broadcast_to(piece[None], (count,) + piece.shape)
    return lax.all_to_all(copies, "vocab", split_axis=0, concat_axis=0, tiled=True)


def scaled_teacher(teacher_values, teacher_scales, count, shard_rows):
    slot_rows = teacher_values.shape[0]
    scaled = (
        teacher_values.astype(jnp.float32).reshape(slot_rows, -1, BLOCK) * teacher_scales[:, :, None]
    ).astype(jnp.bfloat16)
    return scaled.reshape(slot_rows, count, shard_rows).transpose(1, 0, 2)


def merge_stats(tops, sums, teacher_tops, teacher_sums, crosses):
    top = jnp.max(tops, axis=0)
    teacher_top = jnp.max(teacher_tops, axis=0)
    shift = tops - top[None]
    teacher_shift = teacher_tops - teacher_top[None]
    weight = jnp.exp(shift)
    total = jnp.sum(sums * weight, axis=0)
    teacher_total = jnp.sum(teacher_sums * jnp.exp(teacher_shift), axis=0)
    cross = jnp.sum(weight * (crosses + sums * (shift - teacher_shift)), axis=0)
    return top, total, teacher_top, teacher_total, cross


def swap_cores(array):
    count = lax.axis_size("vocab")
    return lax.ppermute(array, "vocab", [(i, i ^ 1) for i in range(count)])


def along_chips(array, step):
    count = lax.axis_size("vocab")
    return lax.ppermute(array, "vocab", [(i, (i + 2 * step) % count) for i in range(count)])


def vmem_array(shape, dtype):
    return pltpu.VMEM(shape, dtype)


def in_vmem(array):
    return pltpu.with_memory_space_constraint(array, pltpu.VMEM)


def in_hbm(array):
    return pltpu.with_memory_space_constraint(array, pltpu.HBM)


def hbm_array(shape, dtype):
    return pltpu.HBM(shape, dtype)


def low_lanes(shape):
    return lax.broadcasted_iota(jnp.int32, shape, len(shape) - 1) < LANES // 2


def low_rows(shape, count):
    return lax.broadcasted_iota(jnp.int32, shape, 0) < count


def turned(array):
    return pltpu.roll(array, LANES // 2, 1)


def packed_half(tiles):
    rows = tiles[2].shape[0] // 2
    upper, lower = tiles[2][:rows], tiles[2][rows:]
    rest = jnp.where(low_lanes(upper.shape), upper, turned(lower))
    return jnp.concatenate([tiles[0], tiles[1], rest], axis=0)


def unpacked_half(packed, tokens):
    rest = packed[2 * tokens :]
    return [packed[:tokens], packed[tokens : 2 * tokens], jnp.concatenate([rest, turned(rest)])]


def joined(first, second):
    low = low_lanes(first[0].shape)
    turns = [turned(tile) for tile in second]
    return [
        first[0],
        first[1],
        jnp.where(low, first[2], turns[0]),
        jnp.where(low, turns[0], turns[1]),
        jnp.where(low, turns[1], turns[2]),
    ]


def parted(tiles):
    low = low_lanes(tiles[0].shape)
    turns = [turned(tile) for tile in tiles[2:]]
    return tiles[:3], [
        jnp.where(low, turns[0], turns[1]),
        jnp.where(low, turns[1], turns[2]),
        turns[2],
    ]


def column_of(row):
    size = row.shape[1]
    down = lax.broadcasted_iota(jnp.int32, (size, size), 0)
    along = lax.broadcasted_iota(jnp.int32, (size, size), 1)
    return jnp.sum(jnp.where(down == along, row, jnp.zeros_like(row)), axis=1, keepdims=True)


def token_facts(ids, row_map, lengths, first_entry):
    tokens = row_map.shape[1]
    token = lax.broadcasted_iota(jnp.int32, (tokens, tokens), 0)
    slot = lax.broadcasted_iota(jnp.int32, (tokens, tokens), 1)
    owner = (row_map == token).astype(jnp.float32)
    named = jnp.max(owner, axis=1, keepdims=True)
    owner = jnp.where((slot == 0) & (named == 0.0), 1.0, owner)

    seqs = lengths.shape[1]
    seq_length = tokens // seqs
    position = lax.broadcasted_iota(jnp.int32, (tokens, 1), 0)
    live_until = jnp.zeros((tokens, 1), jnp.int32)
    for seq in range(seqs):
        inside = (position >= seq * seq_length) & (position < (seq + 1) * seq_length)
        until = lengths[:, seq : seq + 1] + seq * seq_length
        live_until = jnp.where(inside, until, live_until)
    live = (position < live_until).astype(jnp.float32)
    count = jnp.sum(live, axis=0, keepdims=True)
    entry = (column_of(ids) - first_entry).astype(jnp.float32)
    lane = lax.broadcasted_iota(jnp.int32, (tokens, LANES), 1)
    return owner.astype(jnp.bfloat16), jnp.where(lane == 0, entry, live / count)


def pack_kernel(place_ref, *refs, shard_rows):
    outside, refs = refs[:6], refs[6:]
    packed_ref, owner_ref, table_ref = refs[:3]
    inside, wide_ref, sems = refs[3:9], refs[9], refs[10]
    copies = [
        pltpu.make_async_copy(source, target, sems.at[i])
        for i, (source, target) in enumerate(zip(outside, inside))
    ]
    for copy in copies:
        copy.start()
    for copy in copies:
        copy.wait()
    hidden_ref, values_ref, scales_ref, ids_ref, map_ref, lengths_ref = inside
    owner_ref[...], table_ref[...] = token_facts(
        ids_ref[...], map_ref[...], lengths_ref[...], place_ref[0] * shard_rows
    )
    chips = packed_ref.shape[0]
    tokens, half = hidden_ref.shape
    slots, entries = values_ref.shape
    pair = entries // chips
    shard = pair // 2
    blocks = pair // BLOCK
    scales = jnp.concatenate([scales_ref[...]] * 2, axis=0)
    stacked = jnp.concatenate(
        [scales[:, blocks * chip : blocks * (chip + 1)] for chip in range(chips)], axis=0
    )
    block = lax.broadcasted_iota(jnp.int32, (blocks, pair), 0)
    entry = lax.broadcasted_iota(jnp.int32, (blocks, pair), 1)
    inside = (entry >= block * BLOCK) & (entry < block * BLOCK + BLOCK)
    spread = jnp.dot(
        stacked.astype(jnp.bfloat16),
        inside.astype(jnp.bfloat16),
        preferred_element_type=jnp.float32,
    )
    values = values_ref[...].astype(jnp.float32)
    values = jnp.concatenate([values, values], axis=0)
    for chip in range(chips):
        wide_ref[:, pair * chip : pair * (chip + 1)] = (
            values[:, pair * chip : pair * (chip + 1)]
            * spread[2 * slots * chip : 2 * slots * (chip + 1)]
        )
    wide_ref[:, entries:] = jnp.zeros((2 * slots, LANES), jnp.float32)

    hidden = hidden_ref[...].astype(jnp.float32)
    hidden = jnp.concatenate([hidden, jnp.zeros((tokens, LANES // 2), jnp.float32)], axis=1)
    hidden = packed_half([hidden[:, LANES * i : LANES * (i + 1)] for i in range(3)])
    hidden = hidden.astype(jnp.bfloat16)
    hidden_rows = hidden.shape[0]
    upper = low_rows((2 * slots, LANES), slots)
    low = low_lanes((2 * slots, LANES))
    tile_pairs = (shard + LANES // 2) // LANES // 2
    for chip in range(chips):
        rows = []
        for core in range(2):
            start = pair * chip + (shard - LANES // 2) * core
            tiles = [
                wide_ref[:, start + LANES * i : start + LANES * (i + 1)]
                for i in range(2 * tile_pairs + core)
            ]
            if core == 1:
                tiles = [turned(tile) for tile in tiles]
                tiles = [
                    jnp.where(low, tiles[i], tiles[i + 1]) for i in range(2 * tile_pairs)
                ]
            rows += [
                jnp.where(upper, tiles[2 * i], tiles[2 * i + 1]) for i in range(tile_pairs)
            ]
        step = lax.rem(chip - place_ref[0] // 2 + chips, chips)
        packed_ref[step, :hidden_rows] = hidden
        packed_ref[step, hidden_rows:] = jnp.concatenate(rows, axis=0).astype(jnp.bfloat16)


def head_copies(head_ref, held_ref, sems, chips):
    width = held_ref.shape[2]
    copies = []
    for step, chip in enumerate(chips):
        columns = pl.ds(pl.multiple_of(chip * width, LANES), width)
        copies.append(
            pltpu.make_async_copy(head_ref.at[:, columns], held_ref.at[step], sems.at[step])
        )
    return copies


def logits_kernel(place_ref, *refs, chips):
    near, far, refs = refs[:chips][::-1], refs[chips : chips + 2], refs[chips + 2 :]
    owner_ref, tokens_ref, head_ref, rows_ref, stats_ref = refs[:5]
    held_ref, made_ref, hidden_ref, arrived_ref, teacher_ref, sems, made_sem = refs[5:]
    place = place_ref[0] // 2
    core = place_ref[0] % 2
    sources = [lax.rem(place - step + chips, chips) for step in range(chips)]
    copies = head_copies(head_ref, held_ref, sems, sources)
    for copy in copies[:AHEAD]:
        copy.start()
    _, tokens, width = hidden_ref.shape
    shard_rows = head_ref.shape[0]
    hidden_rows = tokens * width // 2 // LANES
    slots = tokens // (2 * chips)
    upper = low_rows((2 * slots, LANES), slots)

    def both(step, rows):
        own = near[step][rows].astype(jnp.float32)
        late = step > chips // 2
        group = far[0] if late else far[1]
        other = group[step - chips // 2 - 1 if late else step, rows].astype(jnp.float32)
        return jnp.where(core == 0, own, other), jnp.where(core == 0, other, own)

    def unpack_hidden(step):
        first, second = both(step, slice(0, hidden_rows))
        tiles = joined(unpacked_half(first, tokens), unpacked_half(second, tokens))
        hidden_ref[step] = jnp.concatenate(tiles, axis=1).astype(jnp.bfloat16)

    def unpack_teacher(step):
        first, second = both(step, slice(hidden_rows, near[0].shape[0]))
        share = first.shape[0] // 2
        first = jnp.where(core == 0, first[:share], first[share:])
        second = jnp.where(core == 0, second[:share], second[share:])
        tiles = []
        for row in range(0, share, 2 * slots):
            one, two = first[row : row + 2 * slots], second[row : row + 2 * slots]
            tiles.append(jnp.where(upper, one, pltpu.roll(two, slots, 0)))
            tiles.append(jnp.where(upper, pltpu.roll(one, slots, 0), two))
        rows = pl.ds(pl.multiple_of(2 * slots * sources[step], 2 * slots), 2 * slots)
        arrived_ref[rows] = jnp.concatenate(tiles, axis=1)

    unpack_hidden(0)
    logits = jnp.zeros((tokens, shard_rows), jnp.float32)
    for chip, copy in enumerate(copies):
        copy.wait()
        if chip + AHEAD < chips:
            copies[chip + AHEAD].start()
        if chip + 1 < chips:
            unpack_hidden(chip + 1)
        if chip < chips // 2:
            unpack_teacher(2 * chip)
            unpack_teacher(2 * chip + 1)
        if chip == chips // 2:
            teacher = jnp.dot(
                owner_ref[...],
                arrived_ref[:, :shard_rows].astype(jnp.bfloat16),
                preferred_element_type=jnp.float32,
            )
            teacher_top = jnp.max(teacher, axis=1, keepdims=True)
            teacher_off = teacher - teacher_top
            teacher_total = jnp.sum(jnp.exp(teacher_off), axis=1, keepdims=True)
            teacher_ref[...] = teacher_off
        logits += lax.dot_general(
            hidden_ref[chip],
            held_ref[chip],
            (((1,), (1,)), ((), ())),
            preferred_element_type=jnp.float32,
        )

    top = jnp.max(logits, axis=1, keepdims=True)
    off = logits - top
    exps = jnp.exp(off)
    total = jnp.sum(exps, axis=1, keepdims=True)
    gap = off - teacher_ref[...]
    cross = jnp.sum(exps * gap, axis=1, keepdims=True)
    centre = cross / total
    entry = lax.broadcasted_iota(jnp.int32, (tokens, shard_rows), 1)
    hit = entry == tokens_ref[:, :1].astype(jnp.int32)
    target = jnp.sum(jnp.where(hit, logits, 0.0), axis=1, keepdims=True)
    made_ref[:tokens] = (exps * (gap - centre)).astype(jnp.bfloat16)
    made_ref[tokens : 2 * tokens] = exps.astype(jnp.bfloat16)
    made_ref[2 * tokens :] = hit.astype(jnp.bfloat16)
    out = pltpu.make_async_copy(made_ref, rows_ref, made_sem)
    out.start()

    lane = lax.broadcasted_iota(jnp.int32, (tokens, LANES), 1)
    table = jnp.zeros((tokens, LANES), jnp.float32)
    for place, column in enumerate(
        (top, total, teacher_top, teacher_total, cross, target, centre)
    ):
        table = jnp.where(lane == place, column, table)
    stats = jnp.concatenate([table, jnp.zeros((stats_ref.shape[2] - tokens, LANES), jnp.float32)])
    stats_ref[...] = jnp.broadcast_to(stats.T[None, :STATS], stats_ref.shape)
    out.wait()


def products_kernel(
    place_ref, rows_ref, head_ref, terms_ref, picks_ref, held_ref, made_ref, sems, made_sem
):
    into = pltpu.make_async_copy(rows_ref, made_ref, made_sem)
    into.start()
    chips = held_ref.shape[0]
    targets = [lax.rem(place_ref[0] // 2 + step, chips) for step in range(chips)]
    copies = head_copies(head_ref, held_ref, sems, targets)
    for copy in copies[:AHEAD]:
        copy.start()
    into.wait()
    sums_rows = terms_ref.shape[1]
    for step, copy in enumerate(copies):
        copy.wait()
        if step + AHEAD < len(copies):
            copies[step + AHEAD].start()
        products = jnp.dot(made_ref[...], held_ref[step], preferred_element_type=jnp.float32)
        terms_ref[step] = products[:sums_rows]
        picks_ref[step] = products[sums_rows:].astype(jnp.bfloat16)


def combine_kernel(
    place_ref,
    scale_ref,
    stats_ref,
    own_ref,
    tokens_ref,
    terms_ref,
    picks_ref,
    keep_ref,
    give_ref,
    loss_ref,
):
    core = place_ref[0] % 2
    chips, _, width = terms_ref.shape
    tokens = tokens_ref.shape[0]
    tops, sums, teacher_tops, teacher_sums, crosses, targets = [
        stats_ref[:, i, :tokens] for i in range(6)
    ]
    top, total, teacher_top, teacher_total, cross = [
        part[None] for part in merge_stats(tops, sums, teacher_tops, teacher_sums, crosses)
    ]
    target = jnp.sum(targets, axis=0, keepdims=True)
    student_log = jnp.log(total)
    teacher_log = jnp.log(teacher_total)
    divergence = cross / total - (student_log - teacher_log)
    student_lse = top + student_log
    per_token = divergence + sample_weight * (student_lse - target)
    student_shift = own_ref[0, 0:1, :tokens] - top - student_log
    teacher_shift = own_ref[0, 2:3, :tokens] - teacher_top - teacher_log
    factor = jnp.exp(student_shift)
    level = (
        own_ref[0, 6:7, :tokens] + student_shift - teacher_shift - divergence + sample_weight
    )
    zeros = jnp.zeros((LANES - 3, tokens), jnp.float32)
    columns = jnp.concatenate([factor, level, per_token, zeros], axis=0).T
    share = tokens_ref[:, 1:2]
    weight = share * scale_ref[0]
    loss_ref[...] = jnp.sum(share * columns[:, 2:3], axis=0, keepdims=True)
    factor = weight * columns[:, 0:1]
    level = columns[:, 1:2]
    weight = sample_weight * weight
    for step in range(chips):
        block = (
            factor * (terms_ref[step, :tokens] + level * terms_ref[step, tokens:])
            - weight * picks_ref[step].astype(jnp.float32)
        )
        first, second = parted([block[:, i : i + LANES] for i in range(0, width, LANES)])
        first, second = packed_half(first), packed_half(second)
        keep_ref[step] = jnp.where(core == 0, first, second)
        give_ref[step] = jnp.where(core == 0, second, first).astype(jnp.bfloat16)


def sum_kernel(own_ref, *refs):
    tokens, half = refs[-1].shape
    total = own_ref[...]
    for share_ref in refs[:-1]:
        total += share_ref[...].astype(jnp.float32)
    tiles = jnp.concatenate(unpacked_half(total, tokens), axis=1)
    refs[-1][...] = tiles[:, :half].astype(refs[-1].dtype)


def paired_shards(
    hidden_states, head, teacher_values, teacher_scales, token_ids, lengths, row_map, loss_scale
):
    count = lax.axis_size("vocab")
    own_index = lax.axis_index("vocab")
    chips = count // 2
    tokens, half = hidden_states.shape
    width = 2 * half
    shard_rows = head.shape[0]
    place = jnp.reshape(own_index, (1,))
    vmem = pl.BlockSpec(memory_space=pltpu.VMEM)
    smem = pl.BlockSpec(memory_space=pltpu.SMEM)
    hbm = pl.BlockSpec(memory_space=pl.ANY)
    params = pltpu.CompilerParams(vmem_limit_bytes=VMEM_LIMIT)
    head = in_hbm(head)
    head_scratch = pltpu.VMEM((chips, shard_rows, width), head.dtype)
    head_sems = pltpu.SemaphoreType.DMA((chips,))
    rows_scratch = pltpu.VMEM((3 * tokens, shard_rows), jnp.bfloat16)
    rows_sem = pltpu.SemaphoreType.DMA
    slots, entries = teacher_values.shape
    hidden_rows = tokens * half // LANES
    teacher_rows = 2 * slots * (shard_rows + LANES // 2) // LANES

    operands = (
        hidden_states,
        teacher_values,
        teacher_scales,
        token_ids[None, :],
        row_map[None, :],
        lengths[None, :],
    )
    packed, owner, table = pl.pallas_call(
        functools.partial(pack_kernel, shard_rows=shard_rows),
        out_shape=(
            jax.ShapeDtypeStruct((chips, hidden_rows + teacher_rows, LANES), jnp.bfloat16),
            vmem_array((tokens, tokens), jnp.bfloat16),
            vmem_array((tokens, LANES), jnp.float32),
        ),
        in_specs=[smem] + [hbm] * len(operands),
        out_specs=[vmem] * 3,
        scratch_shapes=[pltpu.VMEM(operand.shape, operand.dtype) for operand in operands]
        + [
            pltpu.VMEM((2 * slots, entries + LANES), jnp.float32),
            pltpu.SemaphoreType.DMA((len(operands),)),
        ],
        compiler_params=params,
        name="pack",
    )(place, *[in_hbm(operand) for operand in operands])
    steps = range(1, chips)
    near = [packed[0]] + [along_chips(packed[step], step) for step in steps]
    far = [
        swap_cores(jnp.stack(near[chips // 2 + 1 :])),
        swap_cores(jnp.stack(near[: chips // 2 + 1])),
    ]

    rows, stats = pl.pallas_call(
        functools.partial(logits_kernel, chips=chips),
        out_shape=(
            hbm_array((3 * tokens, shard_rows), jnp.bfloat16),
            jax.ShapeDtypeStruct((count, STATS, pl.cdiv(tokens, LANES) * LANES), jnp.float32),
        ),
        in_specs=[smem] + [vmem] * (chips + 4) + [hbm],
        out_specs=[hbm, vmem],
        scratch_shapes=[
            head_scratch,
            rows_scratch,
            pltpu.VMEM((chips, tokens, width), jnp.bfloat16),
            pltpu.VMEM((tokens, shard_rows + LANES // 2), jnp.float32),
            pltpu.VMEM((tokens, shard_rows), jnp.float32),
            head_sems,
            rows_sem,
        ],
        compiler_params=params,
        cost_estimate=pl.CostEstimate(
            flops=2 * tokens * head.size, bytes_accessed=2 * head.size, transcendentals=0
        ),
        name="logits",
    )(place, *near[::-1], *far, in_vmem(owner), in_vmem(table), head)

    all_stats = lax.all_to_all(stats, "vocab", split_axis=0, concat_axis=0, tiled=True)

    terms, picks = pl.pallas_call(
        products_kernel,
        out_shape=(
            vmem_array((chips, 2 * tokens, width), jnp.float32),
            vmem_array((chips, tokens, width), jnp.bfloat16),
        ),
        in_specs=[smem, hbm, hbm],
        out_specs=[vmem] * 2,
        scratch_shapes=[head_scratch, rows_scratch, head_sems, rows_sem],
        compiler_params=params,
        cost_estimate=pl.CostEstimate(
            flops=6 * tokens * head.size, bytes_accessed=2 * head.size, transcendentals=0
        ),
        name="products",
    )(place, in_hbm(rows), head)

    keep, give, loss = pl.pallas_call(
        combine_kernel,
        out_shape=(
            vmem_array((chips, hidden_rows, LANES), jnp.float32),
            vmem_array((chips, hidden_rows, LANES), jnp.bfloat16),
            jax.ShapeDtypeStruct((1, 1), jnp.float32),
        ),
        in_specs=[smem] * 2 + [vmem] * 5,
        out_specs=[vmem] * 3,
        compiler_params=params,
        name="combine",
    )(place, loss_scale, all_stats, stats, in_vmem(table), in_vmem(terms), in_vmem(picks))

    sums = keep + swap_cores(give).astype(jnp.float32)
    shares = [along_chips(sums[step].astype(jnp.bfloat16), step) for step in steps[::-1]]
    total = pl.pallas_call(
        sum_kernel,
        out_shape=jax.ShapeDtypeStruct((tokens, half), jnp.bfloat16),
        in_specs=[vmem] * chips,
        out_specs=vmem,
        compiler_params=params,
        name="total",
    )(sums[0], *shares)
    return total, jnp.reshape(loss, (1,))


VMEM_LIMIT = 24 * 1024 * 1024


def shards(
    hidden_states, head, teacher_values, teacher_scales, token_ids, lengths, row_map, loss_scale
):
    count = lax.axis_size("vocab")
    own_index = lax.axis_index("vocab")
    tokens = hidden_states.shape[0]
    own_features = hidden_states.shape[1]
    shard_rows = head.shape[0]
    seq_length = tokens // lengths.shape[0]
    contract_last = (((1,), (1,)), ((), ()))

    scaled = scaled_teacher(teacher_values, teacher_scales, count, shard_rows)
    arrived = lax.all_to_all(scaled, "vocab", split_axis=0, concat_axis=0, tiled=True)
    arrived = arrived.reshape(tokens, shard_rows)
    gathered = to_all(hidden_states, count).transpose(1, 0, 2).reshape(tokens, -1)
    logits = lax.dot_general(gathered, head, contract_last, preferred_element_type=jnp.float32)

    positions = jnp.arange(tokens, dtype=jnp.int32)
    owner = row_map[None, :] == positions[:, None]
    slot_of = jnp.sum(jnp.where(owner, positions[None, :], 0), axis=1)
    teacher = jnp.take(arrived, slot_of, axis=0).astype(jnp.float32)

    seq_ids = jnp.arange(lengths.shape[0], dtype=jnp.int32)
    own_length = jnp.sum(
        jnp.where((positions // seq_length)[:, None] == seq_ids[None, :], lengths[None, :], 0),
        axis=1,
    )
    live_mask = (positions % seq_length < own_length).astype(jnp.float32)
    live_count = jnp.sum(live_mask)

    local_ids = token_ids - own_index * shard_rows
    target_hit = local_ids[:, None] == jnp.arange(shard_rows, dtype=jnp.int32)[None, :]
    target_part = jnp.sum(jnp.where(target_hit, logits, 0.0), axis=1)
    student_top = jnp.max(logits, axis=1)
    teacher_top = jnp.max(teacher, axis=1)
    student_off = logits - student_top[:, None]
    teacher_off = teacher - teacher_top[:, None]
    student_exp = jnp.exp(student_off)
    student_sum = jnp.sum(student_exp, axis=1)
    teacher_sum = jnp.sum(jnp.exp(teacher_off), axis=1)
    cross_sum = jnp.sum(student_exp * (student_off - teacher_off), axis=1)

    stats = to_all(
        jnp.stack(
            [student_top, student_sum, teacher_top, teacher_sum, cross_sum, target_part]
        ),
        count,
    )
    tops, sums, teacher_tops, teacher_sums, crosses, targets = [stats[:, i] for i in range(6)]
    student_max, student_total, teacher_max, teacher_total, cross_total = merge_stats(
        tops, sums, teacher_tops, teacher_sums, crosses
    )
    student_log = jnp.log(student_total)
    teacher_log = jnp.log(teacher_total)
    student_lse = student_max + student_log
    teacher_lse = teacher_max + teacher_log
    divergence = cross_total / student_total - (student_log - teacher_log)
    target = jnp.sum(targets, axis=0)

    per_token = divergence + sample_weight * (student_lse - target)
    loss = jnp.reshape(jnp.sum(live_mask * per_token) / live_count, (1,))
    token_weight = live_mask * loss_scale[0] / live_count
    log_student = logits - student_lse[:, None]
    log_teacher = teacher - teacher_lse[:, None]
    student_prob = jnp.exp(log_student)
    grad_logits = (
        token_weight[:, None]
        * (
            student_prob * (log_student - log_teacher - divergence[:, None])
            + sample_weight * (student_prob - target_hit.astype(jnp.float32))
        )
    ).astype(jnp.bfloat16)
    terms = jnp.dot(grad_logits, head, preferred_element_type=jnp.float32).astype(jnp.bfloat16)
    terms = terms.reshape(tokens, count, own_features).transpose(1, 0, 2)
    shares = lax.all_to_all(terms, "vocab", split_axis=0, concat_axis=0, tiled=True)
    grad_hidden = jnp.sum(shares.astype(jnp.float32), axis=0)
    return (grad_hidden.astype(jnp.bfloat16), loss)


def any_shards(*arrays):
    hidden_states, head, teacher_values = arrays[:3]
    count = lax.axis_size("vocab")
    fits = (
        count % 2 == 0
        and hidden_states.shape[1] == 5 * LANES // 2
        and hidden_states.shape[0] % 32 == 0
        and head.shape[0] % LANES == LANES // 2
        and (head.shape[0] + LANES // 2) // LANES % 2 == 0
        and teacher_values.shape[0] == 4
    )
    return paired_shards(*arrays) if fits else shards(*arrays)


def solution(mesh):
    in_specs = (
        P("dom", "vocab"),
        P("vocab", None),
        P(("dom", "vocab"), None),
        P(("dom", "vocab"), None),
        P("dom"),
        P("dom"),
        P("dom"),
        P(),
    )
    out_specs = (P("dom", "vocab"), P("dom"))
    return jax.shard_map(
        any_shards, mesh=mesh, in_specs=in_specs, out_specs=out_specs, check_vma=False
    )
```

```python
import functools

import jax
import jax.numpy as jnp
from jax import lax
from jax.experimental import pallas as pl
from jax.experimental.pallas import tpu as pltpu
from jax.sharding import PartitionSpec as P

BLOCK = 32
LANES = 128
STATS = 8
AHEAD = 3


sample_weight = 0.5


def to_all(piece, count):
    copies = jnp.broadcast_to(piece[None], (count,) + piece.shape)
    return lax.all_to_all(copies, "vocab", split_axis=0, concat_axis=0, tiled=True)


def scaled_teacher(teacher_values, teacher_scales, count, shard_rows):
    slot_rows = teacher_values.shape[0]
    scaled = (
        teacher_values.astype(jnp.float32).reshape(slot_rows, -1, BLOCK) * teacher_scales[:, :, None]
    ).astype(jnp.bfloat16)
    return scaled.reshape(slot_rows, count, shard_rows).transpose(1, 0, 2)


def merge_stats(tops, sums, teacher_tops, teacher_sums, crosses):
    top = jnp.max(tops, axis=0)
    teacher_top = jnp.max(teacher_tops, axis=0)
    shift = tops - top[None]
    teacher_shift = teacher_tops - teacher_top[None]
    weight = jnp.exp(shift)
    total = jnp.sum(sums * weight, axis=0)
    teacher_total = jnp.sum(teacher_sums * jnp.exp(teacher_shift), axis=0)
    cross = jnp.sum(weight * (crosses + sums * (shift - teacher_shift)), axis=0)
    return top, total, teacher_top, teacher_total, cross


def swap_cores(array):
    count = lax.axis_size("vocab")
    return lax.ppermute(array, "vocab", [(i, i ^ 1) for i in range(count)])


def across_chips(array, step):
    count = lax.axis_size("vocab")
    return lax.ppermute(array, "vocab", [(i, i ^ (2 * step)) for i in range(count)])


def vmem_array(shape, dtype):
    return pltpu.VMEM(shape, dtype)


def in_vmem(array):
    return pltpu.with_memory_space_constraint(array, pltpu.VMEM)


def in_hbm(array):
    return pltpu.with_memory_space_constraint(array, pltpu.HBM)


def hbm_array(shape, dtype):
    return pltpu.HBM(shape, dtype)


def low_lanes(shape):
    return lax.broadcasted_iota(jnp.int32, shape, len(shape) - 1) < LANES // 2


def low_rows(shape, count):
    return lax.broadcasted_iota(jnp.int32, shape, 0) < count


def turned(array):
    return pltpu.roll(array, LANES // 2, 1)


def packed_half(tiles):
    rows = tiles[2].shape[0] // 2
    upper, lower = tiles[2][:rows], tiles[2][rows:]
    rest = jnp.where(low_lanes(upper.shape), upper, turned(lower))
    return jnp.concatenate([tiles[0], tiles[1], rest], axis=0)


def unpacked_half(packed, tokens):
    rest = packed[2 * tokens :]
    return [packed[:tokens], packed[tokens : 2 * tokens], jnp.concatenate([rest, turned(rest)])]


def joined(first, second):
    low = low_lanes(first[0].shape)
    turns = [turned(tile) for tile in second]
    return [
        first[0],
        first[1],
        jnp.where(low, first[2], turns[0]),
        jnp.where(low, turns[0], turns[1]),
        jnp.where(low, turns[1], turns[2]),
    ]


def parted(tiles):
    low = low_lanes(tiles[0].shape)
    turns = [turned(tile) for tile in tiles[2:]]
    return tiles[:3], [
        jnp.where(low, turns[0], turns[1]),
        jnp.where(low, turns[1], turns[2]),
        turns[2],
    ]


def column_of(row):
    size = row.shape[1]
    down = lax.broadcasted_iota(jnp.int32, (size, size), 0)
    along = lax.broadcasted_iota(jnp.int32, (size, size), 1)
    return jnp.sum(jnp.where(down == along, row, jnp.zeros_like(row)), axis=1, keepdims=True)


def token_facts(ids, row_map, lengths, first_entry):
    tokens = row_map.shape[1]
    token = lax.broadcasted_iota(jnp.int32, (tokens, tokens), 0)
    slot = lax.broadcasted_iota(jnp.int32, (tokens, tokens), 1)
    owner = (row_map == token).astype(jnp.float32)
    named = jnp.max(owner, axis=1, keepdims=True)
    owner = jnp.where((slot == 0) & (named == 0.0), 1.0, owner)

    seqs = lengths.shape[1]
    seq_length = tokens // seqs
    position = lax.broadcasted_iota(jnp.int32, (tokens, 1), 0)
    live_until = jnp.zeros((tokens, 1), jnp.int32)
    for seq in range(seqs):
        inside = (position >= seq * seq_length) & (position < (seq + 1) * seq_length)
        until = lengths[:, seq : seq + 1] + seq * seq_length
        live_until = jnp.where(inside, until, live_until)
    live = (position < live_until).astype(jnp.float32)
    count = jnp.sum(live, axis=0, keepdims=True)
    entry = (column_of(ids) - first_entry).astype(jnp.float32)
    lane = lax.broadcasted_iota(jnp.int32, (tokens, LANES), 1)
    return owner.astype(jnp.bfloat16), jnp.where(lane == 0, entry, live / count)


def pack_kernel(place_ref, *refs, shard_rows):
    outside, refs = refs[:6], refs[6:]
    packed_ref, owner_ref, table_ref = refs[:3]
    inside, wide_ref, sems = refs[3:9], refs[9], refs[10]
    copies = [
        pltpu.make_async_copy(source, target, sems.at[i])
        for i, (source, target) in enumerate(zip(outside, inside))
    ]
    for copy in copies:
        copy.start()
    for copy in copies:
        copy.wait()
    hidden_ref, values_ref, scales_ref, ids_ref, map_ref, lengths_ref = inside
    owner_ref[...], table_ref[...] = token_facts(
        ids_ref[...], map_ref[...], lengths_ref[...], place_ref[0] * shard_rows
    )
    chips = packed_ref.shape[0]
    tokens, half = hidden_ref.shape
    slots, entries = values_ref.shape
    pair = entries // chips
    shard = pair // 2
    blocks = pair // BLOCK
    scales = jnp.concatenate([scales_ref[...]] * 2, axis=0)
    stacked = jnp.concatenate(
        [scales[:, blocks * chip : blocks * (chip + 1)] for chip in range(chips)], axis=0
    )
    block = lax.broadcasted_iota(jnp.int32, (blocks, pair), 0)
    entry = lax.broadcasted_iota(jnp.int32, (blocks, pair), 1)
    inside = (entry >= block * BLOCK) & (entry < block * BLOCK + BLOCK)
    spread = jnp.dot(
        stacked.astype(jnp.bfloat16),
        inside.astype(jnp.bfloat16),
        preferred_element_type=jnp.float32,
    )
    values = values_ref[...].astype(jnp.float32)
    values = jnp.concatenate([values, values], axis=0)
    for chip in range(chips):
        wide_ref[:, pair * chip : pair * (chip + 1)] = (
            values[:, pair * chip : pair * (chip + 1)]
            * spread[2 * slots * chip : 2 * slots * (chip + 1)]
        )
    wide_ref[:, entries:] = jnp.zeros((2 * slots, LANES), jnp.float32)

    hidden = hidden_ref[...].astype(jnp.float32)
    hidden = jnp.concatenate([hidden, jnp.zeros((tokens, LANES // 2), jnp.float32)], axis=1)
    hidden = packed_half([hidden[:, LANES * i : LANES * (i + 1)] for i in range(3)])
    hidden = hidden.astype(jnp.bfloat16)
    hidden_rows = hidden.shape[0]
    upper = low_rows((2 * slots, LANES), slots)
    low = low_lanes((2 * slots, LANES))
    tile_pairs = (shard + LANES // 2) // LANES // 2
    for chip in range(chips):
        rows = []
        for core in range(2):
            start = pair * chip + (shard - LANES // 2) * core
            tiles = [
                wide_ref[:, start + LANES * i : start + LANES * (i + 1)]
                for i in range(2 * tile_pairs + core)
            ]
            if core == 1:
                tiles = [turned(tile) for tile in tiles]
                tiles = [
                    jnp.where(low, tiles[i], tiles[i + 1]) for i in range(2 * tile_pairs)
                ]
            rows += [
                jnp.where(upper, tiles[2 * i], tiles[2 * i + 1]) for i in range(tile_pairs)
            ]
        step = jnp.bitwise_xor(place_ref[0] // 2, chip)
        packed_ref[step, :hidden_rows] = hidden
        packed_ref[step, hidden_rows:] = jnp.concatenate(rows, axis=0).astype(jnp.bfloat16)


def head_copies(head_ref, held_ref, sems, chips):
    width = held_ref.shape[2]
    copies = []
    for step, chip in enumerate(chips):
        columns = pl.ds(pl.multiple_of(chip * width, LANES), width)
        copies.append(
            pltpu.make_async_copy(head_ref.at[:, columns], held_ref.at[step], sems.at[step])
        )
    return copies


def logits_kernel(place_ref, *refs, chips):
    near, far, refs = refs[:chips][::-1], refs[chips : chips + 2], refs[chips + 2 :]
    owner_ref, tokens_ref, head_ref, rows_ref, stats_ref = refs[:5]
    held_ref, made_ref, hidden_ref, arrived_ref, teacher_ref, sems, made_sem = refs[5:]
    place = place_ref[0] // 2
    core = place_ref[0] % 2
    sources = [jnp.bitwise_xor(place, step) for step in range(chips)]
    copies = head_copies(head_ref, held_ref, sems, sources)
    for copy in copies[:AHEAD]:
        copy.start()
    _, tokens, width = hidden_ref.shape
    shard_rows = head_ref.shape[0]
    hidden_rows = tokens * width // 2 // LANES
    slots = tokens // (2 * chips)
    upper = low_rows((2 * slots, LANES), slots)

    def both(step, rows):
        own = near[step][rows].astype(jnp.float32)
        late = step > chips // 2
        group = far[0] if late else far[1]
        other = group[step - chips // 2 - 1 if late else step, rows].astype(jnp.float32)
        return jnp.where(core == 0, own, other), jnp.where(core == 0, other, own)

    def unpack_hidden(step):
        first, second = both(step, slice(0, hidden_rows))
        tiles = joined(unpacked_half(first, tokens), unpacked_half(second, tokens))
        hidden_ref[step] = jnp.concatenate(tiles, axis=1).astype(jnp.bfloat16)

    def unpack_teacher(step):
        first, second = both(step, slice(hidden_rows, near[0].shape[0]))
        share = first.shape[0] // 2
        first = jnp.where(core == 0, first[:share], first[share:])
        second = jnp.where(core == 0, second[:share], second[share:])
        tiles = []
        for row in range(0, share, 2 * slots):
            one, two = first[row : row + 2 * slots], second[row : row + 2 * slots]
            tiles.append(jnp.where(upper, one, pltpu.roll(two, slots, 0)))
            tiles.append(jnp.where(upper, pltpu.roll(one, slots, 0), two))
        rows = pl.ds(pl.multiple_of(2 * slots * sources[step], 2 * slots), 2 * slots)
        arrived_ref[rows] = jnp.concatenate(tiles, axis=1)

    unpack_hidden(0)
    logits = jnp.zeros((tokens, shard_rows), jnp.float32)
    for chip, copy in enumerate(copies):
        copy.wait()
        if chip + AHEAD < chips:
            copies[chip + AHEAD].start()
        if chip + 1 < chips:
            unpack_hidden(chip + 1)
        if chip < chips // 2:
            unpack_teacher(2 * chip)
            unpack_teacher(2 * chip + 1)
        if chip == chips // 2:
            teacher = jnp.dot(
                owner_ref[...],
                arrived_ref[:, :shard_rows].astype(jnp.bfloat16),
                preferred_element_type=jnp.float32,
            )
            teacher_top = jnp.max(teacher, axis=1, keepdims=True)
            teacher_off = teacher - teacher_top
            teacher_total = jnp.sum(jnp.exp(teacher_off), axis=1, keepdims=True)
            teacher_ref[...] = teacher_off
        logits += lax.dot_general(
            hidden_ref[chip],
            held_ref[chip],
            (((1,), (1,)), ((), ())),
            preferred_element_type=jnp.float32,
        )

    top = jnp.max(logits, axis=1, keepdims=True)
    off = logits - top
    exps = jnp.exp(off)
    total = jnp.sum(exps, axis=1, keepdims=True)
    gap = off - teacher_ref[...]
    cross = jnp.sum(exps * gap, axis=1, keepdims=True)
    centre = cross / total
    entry = lax.broadcasted_iota(jnp.int32, (tokens, shard_rows), 1)
    hit = entry == tokens_ref[:, :1].astype(jnp.int32)
    target = jnp.sum(jnp.where(hit, logits, 0.0), axis=1, keepdims=True)
    made_ref[:tokens] = (exps * (gap - centre)).astype(jnp.bfloat16)
    made_ref[tokens : 2 * tokens] = exps.astype(jnp.bfloat16)
    made_ref[2 * tokens :] = hit.astype(jnp.bfloat16)
    out = pltpu.make_async_copy(made_ref, rows_ref, made_sem)
    out.start()

    lane = lax.broadcasted_iota(jnp.int32, (tokens, LANES), 1)
    table = jnp.zeros((tokens, LANES), jnp.float32)
    for place, column in enumerate(
        (top, total, teacher_top, teacher_total, cross, target, centre)
    ):
        table = jnp.where(lane == place, column, table)
    stats = jnp.concatenate([table, jnp.zeros((stats_ref.shape[2] - tokens, LANES), jnp.float32)])
    stats_ref[...] = jnp.broadcast_to(stats.T[None, :STATS], stats_ref.shape)
    out.wait()


def products_kernel(
    place_ref, rows_ref, head_ref, terms_ref, picks_ref, held_ref, made_ref, sems, made_sem
):
    into = pltpu.make_async_copy(rows_ref, made_ref, made_sem)
    into.start()
    chips = held_ref.shape[0]
    targets = [jnp.bitwise_xor(place_ref[0] // 2, step) for step in range(chips)]
    copies = head_copies(head_ref, held_ref, sems, targets)
    for copy in copies[:AHEAD]:
        copy.start()
    into.wait()
    sums_rows = terms_ref.shape[1]
    for step, copy in enumerate(copies):
        copy.wait()
        if step + AHEAD < len(copies):
            copies[step + AHEAD].start()
        products = jnp.dot(made_ref[...], held_ref[step], preferred_element_type=jnp.float32)
        terms_ref[step] = products[:sums_rows]
        picks_ref[step] = products[sums_rows:].astype(jnp.bfloat16)


def combine_kernel(
    place_ref,
    scale_ref,
    stats_ref,
    own_ref,
    tokens_ref,
    terms_ref,
    picks_ref,
    keep_ref,
    give_ref,
    loss_ref,
):
    core = place_ref[0] % 2
    chips, _, width = terms_ref.shape
    tokens = tokens_ref.shape[0]
    tops, sums, teacher_tops, teacher_sums, crosses, targets = [
        stats_ref[:, i, :tokens] for i in range(6)
    ]
    top, total, teacher_top, teacher_total, cross = [
        part[None] for part in merge_stats(tops, sums, teacher_tops, teacher_sums, crosses)
    ]
    target = jnp.sum(targets, axis=0, keepdims=True)
    student_log = jnp.log(total)
    teacher_log = jnp.log(teacher_total)
    divergence = cross / total - (student_log - teacher_log)
    student_lse = top + student_log
    per_token = divergence + sample_weight * (student_lse - target)
    student_shift = own_ref[0, 0:1, :tokens] - top - student_log
    teacher_shift = own_ref[0, 2:3, :tokens] - teacher_top - teacher_log
    factor = jnp.exp(student_shift)
    level = (
        own_ref[0, 6:7, :tokens] + student_shift - teacher_shift - divergence + sample_weight
    )
    zeros = jnp.zeros((LANES - 3, tokens), jnp.float32)
    columns = jnp.concatenate([factor, level, per_token, zeros], axis=0).T
    share = tokens_ref[:, 1:2]
    weight = share * scale_ref[0]
    loss_ref[...] = jnp.sum(share * columns[:, 2:3], axis=0, keepdims=True)
    factor = weight * columns[:, 0:1]
    level = columns[:, 1:2]
    weight = sample_weight * weight
    for step in range(chips):
        block = (
            factor * (terms_ref[step, :tokens] + level * terms_ref[step, tokens:])
            - weight * picks_ref[step].astype(jnp.float32)
        )
        first, second = parted([block[:, i : i + LANES] for i in range(0, width, LANES)])
        first, second = packed_half(first), packed_half(second)
        keep_ref[step] = jnp.where(core == 0, first, second)
        give_ref[step] = jnp.where(core == 0, second, first).astype(jnp.bfloat16)


def sum_kernel(own_ref, *refs):
    tokens, half = refs[-1].shape
    total = own_ref[...]
    for share_ref in refs[:-1]:
        total += share_ref[...].astype(jnp.float32)
    tiles = jnp.concatenate(unpacked_half(total, tokens), axis=1)
    refs[-1][...] = tiles[:, :half].astype(refs[-1].dtype)


def paired_shards(
    hidden_states, head, teacher_values, teacher_scales, token_ids, lengths, row_map, loss_scale
):
    count = lax.axis_size("vocab")
    own_index = lax.axis_index("vocab")
    chips = count // 2
    tokens, half = hidden_states.shape
    width = 2 * half
    shard_rows = head.shape[0]
    place = jnp.reshape(own_index, (1,))
    vmem = pl.BlockSpec(memory_space=pltpu.VMEM)
    smem = pl.BlockSpec(memory_space=pltpu.SMEM)
    hbm = pl.BlockSpec(memory_space=pl.ANY)
    params = pltpu.CompilerParams(vmem_limit_bytes=VMEM_LIMIT)
    head = in_hbm(head)
    head_scratch = pltpu.VMEM((chips, shard_rows, width), head.dtype)
    head_sems = pltpu.SemaphoreType.DMA((chips,))
    rows_scratch = pltpu.VMEM((3 * tokens, shard_rows), jnp.bfloat16)
    rows_sem = pltpu.SemaphoreType.DMA
    slots, entries = teacher_values.shape
    hidden_rows = tokens * half // LANES
    teacher_rows = 2 * slots * (shard_rows + LANES // 2) // LANES

    operands = (
        hidden_states,
        teacher_values,
        teacher_scales,
        token_ids[None, :],
        row_map[None, :],
        lengths[None, :],
    )
    packed, owner, table = pl.pallas_call(
        functools.partial(pack_kernel, shard_rows=shard_rows),
        out_shape=(
            jax.ShapeDtypeStruct((chips, hidden_rows + teacher_rows, LANES), jnp.bfloat16),
            vmem_array((tokens, tokens), jnp.bfloat16),
            vmem_array((tokens, LANES), jnp.float32),
        ),
        in_specs=[smem] + [hbm] * len(operands),
        out_specs=[vmem] * 3,
        scratch_shapes=[pltpu.VMEM(operand.shape, operand.dtype) for operand in operands]
        + [
            pltpu.VMEM((2 * slots, entries + LANES), jnp.float32),
            pltpu.SemaphoreType.DMA((len(operands),)),
        ],
        compiler_params=params,
        name="pack",
    )(place, *[in_hbm(operand) for operand in operands])
    steps = range(1, chips)
    near = [packed[0]] + [across_chips(packed[step], step) for step in steps]
    far = [
        swap_cores(jnp.stack(near[chips // 2 + 1 :])),
        swap_cores(jnp.stack(near[: chips // 2 + 1])),
    ]

    rows, stats = pl.pallas_call(
        functools.partial(logits_kernel, chips=chips),
        out_shape=(
            hbm_array((3 * tokens, shard_rows), jnp.bfloat16),
            jax.ShapeDtypeStruct((count, STATS, pl.cdiv(tokens, LANES) * LANES), jnp.float32),
        ),
        in_specs=[smem] + [vmem] * (chips + 4) + [hbm],
        out_specs=[hbm, vmem],
        scratch_shapes=[
            head_scratch,
            rows_scratch,
            pltpu.VMEM((chips, tokens, width), jnp.bfloat16),
            pltpu.VMEM((tokens, shard_rows + LANES // 2), jnp.float32),
            pltpu.VMEM((tokens, shard_rows), jnp.float32),
            head_sems,
            rows_sem,
        ],
        compiler_params=params,
        cost_estimate=pl.CostEstimate(
            flops=2 * tokens * head.size, bytes_accessed=2 * head.size, transcendentals=0
        ),
        name="logits",
    )(place, *near[::-1], *far, in_vmem(owner), in_vmem(table), head)

    all_stats = lax.all_to_all(stats, "vocab", split_axis=0, concat_axis=0, tiled=True)

    terms, picks = pl.pallas_call(
        products_kernel,
        out_shape=(
            vmem_array((chips, 2 * tokens, width), jnp.float32),
            vmem_array((chips, tokens, width), jnp.bfloat16),
        ),
        in_specs=[smem, hbm, hbm],
        out_specs=[vmem] * 2,
        scratch_shapes=[head_scratch, rows_scratch, head_sems, rows_sem],
        compiler_params=params,
        cost_estimate=pl.CostEstimate(
            flops=6 * tokens * head.size, bytes_accessed=2 * head.size, transcendentals=0
        ),
        name="products",
    )(place, in_hbm(rows), head)

    keep, give, loss = pl.pallas_call(
        combine_kernel,
        out_shape=(
            vmem_array((chips, hidden_rows, LANES), jnp.float32),
            vmem_array((chips, hidden_rows, LANES), jnp.bfloat16),
            jax.ShapeDtypeStruct((1, 1), jnp.float32),
        ),
        in_specs=[smem] * 2 + [vmem] * 5,
        out_specs=[vmem] * 3,
        compiler_params=params,
        name="combine",
    )(place, loss_scale, all_stats, stats, in_vmem(table), in_vmem(terms), in_vmem(picks))

    sums = keep + swap_cores(give).astype(jnp.float32)
    shares = [across_chips(sums[step].astype(jnp.bfloat16), step) for step in steps[::-1]]
    total = pl.pallas_call(
        sum_kernel,
        out_shape=jax.ShapeDtypeStruct((tokens, half), jnp.bfloat16),
        in_specs=[vmem] * chips,
        out_specs=vmem,
        compiler_params=params,
        name="total",
    )(sums[0], *shares)
    return total, jnp.reshape(loss, (1,))


VMEM_LIMIT = 24 * 1024 * 1024


def shards(
    hidden_states, head, teacher_values, teacher_scales, token_ids, lengths, row_map, loss_scale
):
    count = lax.axis_size("vocab")
    own_index = lax.axis_index("vocab")
    tokens = hidden_states.shape[0]
    own_features = hidden_states.shape[1]
    shard_rows = head.shape[0]
    seq_length = tokens // lengths.shape[0]
    contract_last = (((1,), (1,)), ((), ()))

    scaled = scaled_teacher(teacher_values, teacher_scales, count, shard_rows)
    arrived = lax.all_to_all(scaled, "vocab", split_axis=0, concat_axis=0, tiled=True)
    arrived = arrived.reshape(tokens, shard_rows)
    gathered = to_all(hidden_states, count).transpose(1, 0, 2).reshape(tokens, -1)
    logits = lax.dot_general(gathered, head, contract_last, preferred_element_type=jnp.float32)

    positions = jnp.arange(tokens, dtype=jnp.int32)
    owner = row_map[None, :] == positions[:, None]
    slot_of = jnp.sum(jnp.where(owner, positions[None, :], 0), axis=1)
    teacher = jnp.take(arrived, slot_of, axis=0).astype(jnp.float32)

    seq_ids = jnp.arange(lengths.shape[0], dtype=jnp.int32)
    own_length = jnp.sum(
        jnp.where((positions // seq_length)[:, None] == seq_ids[None, :], lengths[None, :], 0),
        axis=1,
    )
    live_mask = (positions % seq_length < own_length).astype(jnp.float32)
    live_count = jnp.sum(live_mask)

    local_ids = token_ids - own_index * shard_rows
    target_hit = local_ids[:, None] == jnp.arange(shard_rows, dtype=jnp.int32)[None, :]
    target_part = jnp.sum(jnp.where(target_hit, logits, 0.0), axis=1)
    student_top = jnp.max(logits, axis=1)
    teacher_top = jnp.max(teacher, axis=1)
    student_off = logits - student_top[:, None]
    teacher_off = teacher - teacher_top[:, None]
    student_exp = jnp.exp(student_off)
    student_sum = jnp.sum(student_exp, axis=1)
    teacher_sum = jnp.sum(jnp.exp(teacher_off), axis=1)
    cross_sum = jnp.sum(student_exp * (student_off - teacher_off), axis=1)

    stats = to_all(
        jnp.stack(
            [student_top, student_sum, teacher_top, teacher_sum, cross_sum, target_part]
        ),
        count,
    )
    tops, sums, teacher_tops, teacher_sums, crosses, targets = [stats[:, i] for i in range(6)]
    student_max, student_total, teacher_max, teacher_total, cross_total = merge_stats(
        tops, sums, teacher_tops, teacher_sums, crosses
    )
    student_log = jnp.log(student_total)
    teacher_log = jnp.log(teacher_total)
    student_lse = student_max + student_log
    teacher_lse = teacher_max + teacher_log
    divergence = cross_total / student_total - (student_log - teacher_log)
    target = jnp.sum(targets, axis=0)

    per_token = divergence + sample_weight * (student_lse - target)
    loss = jnp.reshape(jnp.sum(live_mask * per_token) / live_count, (1,))
    token_weight = live_mask * loss_scale[0] / live_count
    log_student = logits - student_lse[:, None]
    log_teacher = teacher - teacher_lse[:, None]
    student_prob = jnp.exp(log_student)
    grad_logits = (
        token_weight[:, None]
        * (
            student_prob * (log_student - log_teacher - divergence[:, None])
            + sample_weight * (student_prob - target_hit.astype(jnp.float32))
        )
    ).astype(jnp.bfloat16)
    terms = jnp.dot(grad_logits, head, preferred_element_type=jnp.float32).astype(jnp.bfloat16)
    terms = terms.reshape(tokens, count, own_features).transpose(1, 0, 2)
    shares = lax.all_to_all(terms, "vocab", split_axis=0, concat_axis=0, tiled=True)
    grad_hidden = jnp.sum(shares.astype(jnp.float32), axis=0)
    return (grad_hidden.astype(jnp.bfloat16), loss)


def any_shards(*arrays):
    hidden_states, head, teacher_values = arrays[:3]
    count = lax.axis_size("vocab")
    fits = (
        count > 1
        and count & (count - 1) == 0
        and hidden_states.shape[1] == 5 * LANES // 2
        and hidden_states.shape[0] % 32 == 0
        and head.shape[0] % LANES == LANES // 2
        and (head.shape[0] + LANES // 2) // LANES % 2 == 0
        and teacher_values.shape[0] == 4
    )
    return paired_shards(*arrays) if fits else shards(*arrays)


def solution(mesh):
    in_specs = (
        P("dom", "vocab"),
        P("vocab", None),
        P(("dom", "vocab"), None),
        P(("dom", "vocab"), None),
        P("dom"),
        P("dom"),
        P("dom"),
        P(),
    )
    out_specs = (P("dom", "vocab"), P("dom"))
    return jax.shard_map(
        any_shards, mesh=mesh, in_specs=in_specs, out_specs=out_specs, check_vma=False
    )
```

```python
import functools

import jax
import jax.numpy as jnp
from jax import lax
from jax.experimental import pallas as pl
from jax.experimental.pallas import tpu as pltpu
from jax.sharding import PartitionSpec as P

BLOCK = 32
LANES = 128
STATS = 8
AHEAD = 3
EARLY = 3


sample_weight = 0.5


def to_all(piece, count):
    copies = jnp.broadcast_to(piece[None], (count,) + piece.shape)
    return lax.all_to_all(copies, "vocab", split_axis=0, concat_axis=0, tiled=True)


def scaled_teacher(teacher_values, teacher_scales, count, shard_rows):
    slot_rows = teacher_values.shape[0]
    scaled = (
        teacher_values.astype(jnp.float32).reshape(slot_rows, -1, BLOCK) * teacher_scales[:, :, None]
    ).astype(jnp.bfloat16)
    return scaled.reshape(slot_rows, count, shard_rows).transpose(1, 0, 2)


def merge_stats(tops, sums, teacher_tops, teacher_sums, crosses):
    top = jnp.max(tops, axis=0)
    teacher_top = jnp.max(teacher_tops, axis=0)
    shift = tops - top[None]
    teacher_shift = teacher_tops - teacher_top[None]
    weight = jnp.exp(shift)
    total = jnp.sum(sums * weight, axis=0)
    teacher_total = jnp.sum(teacher_sums * jnp.exp(teacher_shift), axis=0)
    cross = jnp.sum(weight * (crosses + sums * (shift - teacher_shift)), axis=0)
    return top, total, teacher_top, teacher_total, cross


def swap_cores(array):
    count = lax.axis_size("vocab")
    return lax.ppermute(array, "vocab", [(i, i ^ 1) for i in range(count)])


def along_chips(array, step):
    count = lax.axis_size("vocab")
    return lax.ppermute(array, "vocab", [(i, (i + 2 * step) % count) for i in range(count)])


def vmem_array(shape, dtype):
    return pltpu.VMEM(shape, dtype)


def in_vmem(array):
    return pltpu.with_memory_space_constraint(array, pltpu.VMEM)


def in_hbm(array):
    return pltpu.with_memory_space_constraint(array, pltpu.HBM)


def hbm_array(shape, dtype):
    return pltpu.HBM(shape, dtype)


def low_lanes(shape):
    return lax.broadcasted_iota(jnp.int32, shape, len(shape) - 1) < LANES // 2


def low_rows(shape, count):
    return lax.broadcasted_iota(jnp.int32, shape, 0) < count


def turned(array):
    return pltpu.roll(array, LANES // 2, 1)


def packed_half(tiles):
    rows = tiles[2].shape[0] // 2
    upper, lower = tiles[2][:rows], tiles[2][rows:]
    rest = jnp.where(low_lanes(upper.shape), upper, turned(lower))
    return jnp.concatenate([tiles[0], tiles[1], rest], axis=0)


def unpacked_half(packed, tokens):
    rest = packed[2 * tokens :]
    return [packed[:tokens], packed[tokens : 2 * tokens], jnp.concatenate([rest, turned(rest)])]


def joined(first, second):
    low = low_lanes(first[0].shape)
    turns = [turned(tile) for tile in second]
    return [
        first[0],
        first[1],
        jnp.where(low, first[2], turns[0]),
        jnp.where(low, turns[0], turns[1]),
        jnp.where(low, turns[1], turns[2]),
    ]


def parted(tiles):
    low = low_lanes(tiles[0].shape)
    turns = [turned(tile) for tile in tiles[2:]]
    return tiles[:3], [
        jnp.where(low, turns[0], turns[1]),
        jnp.where(low, turns[1], turns[2]),
        turns[2],
    ]


def column_of(row):
    size = row.shape[1]
    down = lax.broadcasted_iota(jnp.int32, (size, size), 0)
    along = lax.broadcasted_iota(jnp.int32, (size, size), 1)
    return jnp.sum(jnp.where(down == along, row, jnp.zeros_like(row)), axis=1, keepdims=True)


def token_facts(ids, row_map, lengths, first_entry):
    tokens = row_map.shape[1]
    token = lax.broadcasted_iota(jnp.int32, (tokens, tokens), 0)
    slot = lax.broadcasted_iota(jnp.int32, (tokens, tokens), 1)
    owner = (row_map == token).astype(jnp.float32)
    named = jnp.max(owner, axis=1, keepdims=True)
    owner = jnp.where((slot == 0) & (named == 0.0), 1.0, owner)

    seqs = lengths.shape[1]
    seq_length = tokens // seqs
    position = lax.broadcasted_iota(jnp.int32, (tokens, 1), 0)
    live_until = jnp.zeros((tokens, 1), jnp.int32)
    for seq in range(seqs):
        inside = (position >= seq * seq_length) & (position < (seq + 1) * seq_length)
        until = lengths[:, seq : seq + 1] + seq * seq_length
        live_until = jnp.where(inside, until, live_until)
    live = (position < live_until).astype(jnp.float32)
    count = jnp.sum(live, axis=0, keepdims=True)
    entry = (column_of(ids) - first_entry).astype(jnp.float32)
    lane = lax.broadcasted_iota(jnp.int32, (tokens, LANES), 1)
    return owner.astype(jnp.bfloat16), jnp.where(lane == 0, entry, live / count)


def pack_kernel(place_ref, *refs, shard_rows):
    outside, refs = refs[:6], refs[6:]
    packed_ref, owner_ref, table_ref = refs[:3]
    inside, wide_ref, sems = refs[3:9], refs[9], refs[10]
    copies = [
        pltpu.make_async_copy(source, target, sems.at[i])
        for i, (source, target) in enumerate(zip(outside, inside))
    ]
    for copy in copies:
        copy.start()
    for copy in copies:
        copy.wait()
    hidden_ref, values_ref, scales_ref, ids_ref, map_ref, lengths_ref = inside
    owner_ref[...], table_ref[...] = token_facts(
        ids_ref[...], map_ref[...], lengths_ref[...], place_ref[0] * shard_rows
    )
    chips = packed_ref.shape[0]
    tokens, half = hidden_ref.shape
    slots, entries = values_ref.shape
    pair = entries // chips
    shard = pair // 2
    blocks = pair // BLOCK
    scales = jnp.concatenate([scales_ref[...]] * 2, axis=0)
    stacked = jnp.concatenate(
        [scales[:, blocks * chip : blocks * (chip + 1)] for chip in range(chips)], axis=0
    )
    block = lax.broadcasted_iota(jnp.int32, (blocks, pair), 0)
    entry = lax.broadcasted_iota(jnp.int32, (blocks, pair), 1)
    inside = (entry >= block * BLOCK) & (entry < block * BLOCK + BLOCK)
    spread = jnp.dot(
        stacked.astype(jnp.bfloat16),
        inside.astype(jnp.bfloat16),
        preferred_element_type=jnp.float32,
    )
    values = values_ref[...].astype(jnp.float32)
    values = jnp.concatenate([values, values], axis=0)
    for chip in range(chips):
        wide_ref[:, pair * chip : pair * (chip + 1)] = (
            values[:, pair * chip : pair * (chip + 1)]
            * spread[2 * slots * chip : 2 * slots * (chip + 1)]
        )
    wide_ref[:, entries:] = jnp.zeros((2 * slots, LANES), jnp.float32)

    hidden = hidden_ref[...].astype(jnp.float32)
    hidden = jnp.concatenate([hidden, jnp.zeros((tokens, LANES // 2), jnp.float32)], axis=1)
    hidden = packed_half([hidden[:, LANES * i : LANES * (i + 1)] for i in range(3)])
    hidden = hidden.astype(jnp.bfloat16)
    hidden_rows = hidden.shape[0]
    upper = low_rows((2 * slots, LANES), slots)
    low = low_lanes((2 * slots, LANES))
    tile_pairs = (shard + LANES // 2) // LANES // 2
    for chip in range(chips):
        rows = []
        for core in range(2):
            start = pair * chip + (shard - LANES // 2) * core
            tiles = [
                wide_ref[:, start + LANES * i : start + LANES * (i + 1)]
                for i in range(2 * tile_pairs + core)
            ]
            if core == 1:
                tiles = [turned(tile) for tile in tiles]
                tiles = [
                    jnp.where(low, tiles[i], tiles[i + 1]) for i in range(2 * tile_pairs)
                ]
            rows += [
                jnp.where(upper, tiles[2 * i], tiles[2 * i + 1]) for i in range(tile_pairs)
            ]
        step = lax.rem(chip - place_ref[0] // 2 + chips, chips)
        packed_ref[step, :hidden_rows] = hidden
        packed_ref[step, hidden_rows:] = jnp.concatenate(rows, axis=0).astype(jnp.bfloat16)


def head_copies(head_ref, held_ref, sems, chips):
    width = held_ref.shape[2]
    copies = []
    for step, chip in enumerate(chips):
        columns = pl.ds(pl.multiple_of(chip * width, LANES), width)
        copies.append(
            pltpu.make_async_copy(head_ref.at[:, columns], held_ref.at[step], sems.at[step])
        )
    return copies


def source_chips(place_ref, chips):
    return [lax.rem(place_ref[0] // 2 - step + chips, chips) for step in range(chips)]


def preload_kernel(place_ref, head_ref, _, early_ref, sems, *, chips):
    sources = source_chips(place_ref, chips)[: early_ref.shape[0]]
    copies = head_copies(head_ref, early_ref, sems, sources)
    for copy in copies:
        copy.start()
    for copy in copies:
        copy.wait()


def logits_kernel(place_ref, *refs, chips):
    near, far, refs = refs[:chips][::-1], refs[chips : chips + 2], refs[chips + 2 :]
    owner_ref, tokens_ref, early_ref, head_ref, rows_ref, stats_ref = refs[:6]
    held_ref, made_ref, hidden_ref, arrived_ref, teacher_ref, sems, made_sem = refs[6:]
    core = place_ref[0] % 2
    sources = source_chips(place_ref, chips)
    early = early_ref.shape[0]
    copies = head_copies(head_ref, held_ref, sems, sources[early:])
    for copy in copies[:AHEAD]:
        copy.start()
    _, tokens, width = hidden_ref.shape
    shard_rows = head_ref.shape[0]
    hidden_rows = tokens * width // 2 // LANES
    slots = tokens // (2 * chips)
    upper = low_rows((2 * slots, LANES), slots)

    def both(step, rows):
        own = near[step][rows].astype(jnp.float32)
        late = step > chips // 2
        group = far[0] if late else far[1]
        other = group[step - chips // 2 - 1 if late else step, rows].astype(jnp.float32)
        return jnp.where(core == 0, own, other), jnp.where(core == 0, other, own)

    def unpack_hidden(step):
        first, second = both(step, slice(0, hidden_rows))
        tiles = joined(unpacked_half(first, tokens), unpacked_half(second, tokens))
        hidden_ref[step] = jnp.concatenate(tiles, axis=1).astype(jnp.bfloat16)

    def unpack_teacher(step):
        first, second = both(step, slice(hidden_rows, near[0].shape[0]))
        share = first.shape[0] // 2
        first = jnp.where(core == 0, first[:share], first[share:])
        second = jnp.where(core == 0, second[:share], second[share:])
        tiles = []
        for row in range(0, share, 2 * slots):
            one, two = first[row : row + 2 * slots], second[row : row + 2 * slots]
            tiles.append(jnp.where(upper, one, pltpu.roll(two, slots, 0)))
            tiles.append(jnp.where(upper, pltpu.roll(one, slots, 0), two))
        rows = pl.ds(pl.multiple_of(2 * slots * sources[step], 2 * slots), 2 * slots)
        arrived_ref[rows] = jnp.concatenate(tiles, axis=1)

    unpack_hidden(0)
    logits = jnp.zeros((tokens, shard_rows), jnp.float32)
    for chip in range(chips):
        if chip >= early:
            copies[chip - early].wait()
        if 0 < chip + 1 - early and chip + AHEAD - early < len(copies):
            copies[chip + AHEAD - early].start()
        if chip + 1 < chips:
            unpack_hidden(chip + 1)
        if chip < chips // 2:
            unpack_teacher(2 * chip)
            unpack_teacher(2 * chip + 1)
        if chip == chips // 2:
            teacher = jnp.dot(
                owner_ref[...],
                arrived_ref[:, :shard_rows].astype(jnp.bfloat16),
                preferred_element_type=jnp.float32,
            )
            teacher_top = jnp.max(teacher, axis=1, keepdims=True)
            teacher_off = teacher - teacher_top
            teacher_total = jnp.sum(jnp.exp(teacher_off), axis=1, keepdims=True)
            teacher_ref[...] = teacher_off
        logits += lax.dot_general(
            hidden_ref[chip],
            early_ref[chip] if chip < early else held_ref[chip - early],
            (((1,), (1,)), ((), ())),
            preferred_element_type=jnp.float32,
        )

    top = jnp.max(logits, axis=1, keepdims=True)
    off = logits - top
    exps = jnp.exp(off)
    total = jnp.sum(exps, axis=1, keepdims=True)
    gap = off - teacher_ref[...]
    cross = jnp.sum(exps * gap, axis=1, keepdims=True)
    centre = cross / total
    entry = lax.broadcasted_iota(jnp.int32, (tokens, shard_rows), 1)
    hit = entry == tokens_ref[:, :1].astype(jnp.int32)
    target = jnp.sum(jnp.where(hit, logits, 0.0), axis=1, keepdims=True)
    made_ref[:tokens] = (exps * (gap - centre)).astype(jnp.bfloat16)
    made_ref[tokens : 2 * tokens] = exps.astype(jnp.bfloat16)
    made_ref[2 * tokens :] = hit.astype(jnp.bfloat16)
    out = pltpu.make_async_copy(made_ref, rows_ref, made_sem)
    out.start()

    lane = lax.broadcasted_iota(jnp.int32, (tokens, LANES), 1)
    table = jnp.zeros((tokens, LANES), jnp.float32)
    for place, column in enumerate(
        (top, total, teacher_top, teacher_total, cross, target, centre)
    ):
        table = jnp.where(lane == place, column, table)
    stats = jnp.concatenate([table, jnp.zeros((stats_ref.shape[2] - tokens, LANES), jnp.float32)])
    stats_ref[...] = jnp.broadcast_to(stats.T[None, :STATS], stats_ref.shape)
    out.wait()


def products_kernel(
    place_ref, rows_ref, head_ref, terms_ref, picks_ref, held_ref, made_ref, sems, made_sem
):
    into = pltpu.make_async_copy(rows_ref, made_ref, made_sem)
    into.start()
    chips = held_ref.shape[0]
    targets = [lax.rem(place_ref[0] // 2 + step, chips) for step in range(chips)]
    copies = head_copies(head_ref, held_ref, sems, targets)
    for copy in copies[:AHEAD]:
        copy.start()
    into.wait()
    tokens = made_ref.shape[0] // 3
    width = held_ref.shape[2]
    for step, copy in enumerate(copies):
        copy.wait()
        if step + AHEAD < len(copies):
            copies[step + AHEAD].start()
        products = jnp.dot(made_ref[...], held_ref[step], preferred_element_type=jnp.float32)
        for part in range(3):
            rows = products[tokens * part : tokens * (part + 1)]
            halves = parted([rows[:, i : i + LANES] for i in range(0, width, LANES)])
            for parity, tiles in enumerate(halves):
                packed = packed_half(tiles)
                if part < 2:
                    terms_ref[step, parity, part] = packed
                else:
                    picks_ref[step, parity] = packed.astype(jnp.bfloat16)


def gradient_share(step, parity, factors_ref, terms_ref, picks_ref):
    sums = terms_ref[step, parity, 0] + factors_ref[1] * terms_ref[step, parity, 1]
    return factors_ref[0] * sums - factors_ref[2] * picks_ref[step, parity].astype(jnp.float32)


def give_kernel(
    place_ref,
    scale_ref,
    stats_ref,
    own_ref,
    tokens_ref,
    terms_ref,
    picks_ref,
    give_ref,
    factors_ref,
    loss_ref,
):
    tokens = tokens_ref.shape[0]
    tops, sums, teacher_tops, teacher_sums, crosses, targets = [
        stats_ref[:, i, :tokens] for i in range(6)
    ]
    top, total, teacher_top, teacher_total, cross = [
        part[None] for part in merge_stats(tops, sums, teacher_tops, teacher_sums, crosses)
    ]
    target = jnp.sum(targets, axis=0, keepdims=True)
    student_log = jnp.log(total)
    teacher_log = jnp.log(teacher_total)
    divergence = cross / total - (student_log - teacher_log)
    student_lse = top + student_log
    per_token = divergence + sample_weight * (student_lse - target)
    student_shift = own_ref[0, 0:1, :tokens] - top - student_log
    teacher_shift = own_ref[0, 2:3, :tokens] - teacher_top - teacher_log
    factor = jnp.exp(student_shift)
    level = (
        own_ref[0, 6:7, :tokens] + student_shift - teacher_shift - divergence + sample_weight
    )
    zeros = jnp.zeros((LANES - 3, tokens), jnp.float32)
    columns = jnp.concatenate([factor, level, per_token, zeros], axis=0).T
    share = tokens_ref[:, 1:2]
    weight = share * scale_ref[0]
    loss_ref[...] = jnp.sum(share * columns[:, 2:3], axis=0, keepdims=True)
    for i, column in enumerate(
        (weight * columns[:, 0:1], columns[:, 1:2], sample_weight * weight)
    ):
        factors_ref[i] = packed_half([jnp.broadcast_to(column, (tokens, LANES))] * 3)
    parity = 1 - place_ref[0] % 2
    for step in range(terms_ref.shape[0]):
        share = gradient_share(step, parity, factors_ref, terms_ref, picks_ref)
        give_ref[step] = share.astype(jnp.bfloat16)


def keep_kernel(place_ref, factors_ref, terms_ref, picks_ref, keep_ref):
    parity = place_ref[0] % 2
    for step in range(terms_ref.shape[0]):
        keep_ref[step] = gradient_share(step, parity, factors_ref, terms_ref, picks_ref)


def sum_kernel(own_ref, *refs):
    tokens, half = refs[-1].shape
    total = own_ref[...]
    for share_ref in refs[:-1]:
        total += share_ref[...].astype(jnp.float32)
    tiles = jnp.concatenate(unpacked_half(total, tokens), axis=1)
    refs[-1][...] = tiles[:, :half].astype(refs[-1].dtype)


def paired_shards(
    hidden_states, head, teacher_values, teacher_scales, token_ids, lengths, row_map, loss_scale
):
    count = lax.axis_size("vocab")
    own_index = lax.axis_index("vocab")
    chips = count // 2
    tokens, half = hidden_states.shape
    width = 2 * half
    shard_rows = head.shape[0]
    place = jnp.reshape(own_index, (1,))
    vmem = pl.BlockSpec(memory_space=pltpu.VMEM)
    smem = pl.BlockSpec(memory_space=pltpu.SMEM)
    hbm = pl.BlockSpec(memory_space=pl.ANY)
    params = pltpu.CompilerParams(vmem_limit_bytes=VMEM_LIMIT)
    head = in_hbm(head)
    head_scratch = pltpu.VMEM((chips, shard_rows, width), head.dtype)
    head_sems = pltpu.SemaphoreType.DMA((chips,))
    rows_scratch = pltpu.VMEM((3 * tokens, shard_rows), jnp.bfloat16)
    rows_sem = pltpu.SemaphoreType.DMA
    slots, entries = teacher_values.shape
    hidden_rows = tokens * half // LANES
    teacher_rows = 2 * slots * (shard_rows + LANES // 2) // LANES

    operands = (
        hidden_states,
        teacher_values,
        teacher_scales,
        token_ids[None, :],
        row_map[None, :],
        lengths[None, :],
    )
    packed, owner, table = pl.pallas_call(
        functools.partial(pack_kernel, shard_rows=shard_rows),
        out_shape=(
            jax.ShapeDtypeStruct((chips, hidden_rows + teacher_rows, LANES), jnp.bfloat16),
            vmem_array((tokens, tokens), jnp.bfloat16),
            vmem_array((tokens, LANES), jnp.float32),
        ),
        in_specs=[smem] + [hbm] * len(operands),
        out_specs=[vmem] * 3,
        scratch_shapes=[pltpu.VMEM(operand.shape, operand.dtype) for operand in operands]
        + [
            pltpu.VMEM((2 * slots, entries + LANES), jnp.float32),
            pltpu.SemaphoreType.DMA((len(operands),)),
        ],
        compiler_params=params,
        name="pack",
    )(place, *[in_hbm(operand) for operand in operands])
    steps = range(1, chips)
    near = [packed[0]] + [along_chips(packed[step], step) for step in steps]
    first, last = jnp.stack(near[: chips // 2 + 1]), jnp.stack(near[chips // 2 + 1 :])
    early = pl.pallas_call(
        functools.partial(preload_kernel, chips=chips),
        out_shape=vmem_array((EARLY, shard_rows, width), head.dtype),
        in_specs=[smem] + [hbm] * 2,
        out_specs=vmem,
        scratch_shapes=[pltpu.SemaphoreType.DMA((EARLY,))],
        compiler_params=params,
        cost_estimate=pl.CostEstimate(
            flops=0, bytes_accessed=4 * EARLY * shard_rows * width, transcendentals=0
        ),
        name="preload",
    )(place, head, near[3])
    last, early = lax.optimization_barrier((last, early))
    far = [swap_cores(last), swap_cores(first)]

    rows, stats = pl.pallas_call(
        functools.partial(logits_kernel, chips=chips),
        out_shape=(
            hbm_array((3 * tokens, shard_rows), jnp.bfloat16),
            jax.ShapeDtypeStruct((count, STATS, pl.cdiv(tokens, LANES) * LANES), jnp.float32),
        ),
        in_specs=[smem] + [vmem] * (chips + 5) + [hbm],
        out_specs=[hbm, vmem],
        scratch_shapes=[
            pltpu.VMEM((chips - EARLY, shard_rows, width), head.dtype),
            rows_scratch,
            pltpu.VMEM((chips, tokens, width), jnp.bfloat16),
            pltpu.VMEM((tokens, shard_rows + LANES // 2), jnp.float32),
            pltpu.VMEM((tokens, shard_rows), jnp.float32),
            pltpu.SemaphoreType.DMA((chips - EARLY,)),
            rows_sem,
        ],
        compiler_params=params,
        cost_estimate=pl.CostEstimate(
            flops=2 * tokens * head.size, bytes_accessed=2 * head.size, transcendentals=0
        ),
        name="logits",
    )(place, *near[::-1], *far, in_vmem(owner), in_vmem(table), in_vmem(early), head)

    all_stats = lax.all_to_all(stats, "vocab", split_axis=0, concat_axis=0, tiled=True)

    terms, picks = pl.pallas_call(
        products_kernel,
        out_shape=(
            vmem_array((chips, 2, 2, hidden_rows, LANES), jnp.float32),
            vmem_array((chips, 2, hidden_rows, LANES), jnp.bfloat16),
        ),
        in_specs=[smem, hbm, hbm],
        out_specs=[vmem] * 2,
        scratch_shapes=[head_scratch, rows_scratch, head_sems, rows_sem],
        compiler_params=params,
        cost_estimate=pl.CostEstimate(
            flops=6 * tokens * head.size, bytes_accessed=2 * head.size, transcendentals=0
        ),
        name="products",
    )(place, in_hbm(rows), head)

    terms, picks = in_vmem(terms), in_vmem(picks)
    give, factors, loss = pl.pallas_call(
        give_kernel,
        out_shape=(
            vmem_array((chips, hidden_rows, LANES), jnp.bfloat16),
            vmem_array((3, hidden_rows, LANES), jnp.float32),
            jax.ShapeDtypeStruct((1, 1), jnp.float32),
        ),
        in_specs=[smem] * 2 + [vmem] * 5,
        out_specs=[vmem] * 3,
        compiler_params=params,
        name="give",
    )(place, loss_scale, all_stats, stats, in_vmem(table), terms, picks)
    taken = swap_cores(give)
    keep = pl.pallas_call(
        keep_kernel,
        out_shape=vmem_array((chips, hidden_rows, LANES), jnp.float32),
        in_specs=[smem] + [vmem] * 3,
        out_specs=vmem,
        compiler_params=params,
        cost_estimate=pl.CostEstimate(
            flops=4 * terms.size, bytes_accessed=4 * terms.size, transcendentals=0
        ),
        name="keep",
    )(place, in_vmem(factors), terms, picks)
    sums = keep + taken.astype(jnp.float32)
    shares = [along_chips(sums[step].astype(jnp.bfloat16), step) for step in steps]
    total = pl.pallas_call(
        sum_kernel,
        out_shape=jax.ShapeDtypeStruct((tokens, half), jnp.bfloat16),
        in_specs=[vmem] * chips,
        out_specs=vmem,
        compiler_params=params,
        name="total",
    )(sums[0], *shares)
    return total, jnp.reshape(loss, (1,))


VMEM_LIMIT = 24 * 1024 * 1024


def shards(
    hidden_states, head, teacher_values, teacher_scales, token_ids, lengths, row_map, loss_scale
):
    count = lax.axis_size("vocab")
    own_index = lax.axis_index("vocab")
    tokens = hidden_states.shape[0]
    own_features = hidden_states.shape[1]
    shard_rows = head.shape[0]
    seq_length = tokens // lengths.shape[0]
    contract_last = (((1,), (1,)), ((), ()))

    scaled = scaled_teacher(teacher_values, teacher_scales, count, shard_rows)
    arrived = lax.all_to_all(scaled, "vocab", split_axis=0, concat_axis=0, tiled=True)
    arrived = arrived.reshape(tokens, shard_rows)
    gathered = to_all(hidden_states, count).transpose(1, 0, 2).reshape(tokens, -1)
    logits = lax.dot_general(gathered, head, contract_last, preferred_element_type=jnp.float32)

    positions = jnp.arange(tokens, dtype=jnp.int32)
    owner = row_map[None, :] == positions[:, None]
    slot_of = jnp.sum(jnp.where(owner, positions[None, :], 0), axis=1)
    teacher = jnp.take(arrived, slot_of, axis=0).astype(jnp.float32)

    seq_ids = jnp.arange(lengths.shape[0], dtype=jnp.int32)
    own_length = jnp.sum(
        jnp.where((positions // seq_length)[:, None] == seq_ids[None, :], lengths[None, :], 0),
        axis=1,
    )
    live_mask = (positions % seq_length < own_length).astype(jnp.float32)
    live_count = jnp.sum(live_mask)

    local_ids = token_ids - own_index * shard_rows
    target_hit = local_ids[:, None] == jnp.arange(shard_rows, dtype=jnp.int32)[None, :]
    target_part = jnp.sum(jnp.where(target_hit, logits, 0.0), axis=1)
    student_top = jnp.max(logits, axis=1)
    teacher_top = jnp.max(teacher, axis=1)
    student_off = logits - student_top[:, None]
    teacher_off = teacher - teacher_top[:, None]
    student_exp = jnp.exp(student_off)
    student_sum = jnp.sum(student_exp, axis=1)
    teacher_sum = jnp.sum(jnp.exp(teacher_off), axis=1)
    cross_sum = jnp.sum(student_exp * (student_off - teacher_off), axis=1)

    stats = to_all(
        jnp.stack(
            [student_top, student_sum, teacher_top, teacher_sum, cross_sum, target_part]
        ),
        count,
    )
    tops, sums, teacher_tops, teacher_sums, crosses, targets = [stats[:, i] for i in range(6)]
    student_max, student_total, teacher_max, teacher_total, cross_total = merge_stats(
        tops, sums, teacher_tops, teacher_sums, crosses
    )
    student_log = jnp.log(student_total)
    teacher_log = jnp.log(teacher_total)
    student_lse = student_max + student_log
    teacher_lse = teacher_max + teacher_log
    divergence = cross_total / student_total - (student_log - teacher_log)
    target = jnp.sum(targets, axis=0)

    per_token = divergence + sample_weight * (student_lse - target)
    loss = jnp.reshape(jnp.sum(live_mask * per_token) / live_count, (1,))
    token_weight = live_mask * loss_scale[0] / live_count
    log_student = logits - student_lse[:, None]
    log_teacher = teacher - teacher_lse[:, None]
    student_prob = jnp.exp(log_student)
    grad_logits = (
        token_weight[:, None]
        * (
            student_prob * (log_student - log_teacher - divergence[:, None])
            + sample_weight * (student_prob - target_hit.astype(jnp.float32))
        )
    ).astype(jnp.bfloat16)
    terms = jnp.dot(grad_logits, head, preferred_element_type=jnp.float32).astype(jnp.bfloat16)
    terms = terms.reshape(tokens, count, own_features).transpose(1, 0, 2)
    shares = lax.all_to_all(terms, "vocab", split_axis=0, concat_axis=0, tiled=True)
    grad_hidden = jnp.sum(shares.astype(jnp.float32), axis=0)
    return (grad_hidden.astype(jnp.bfloat16), loss)


def any_shards(*arrays):
    hidden_states, head, teacher_values = arrays[:3]
    count = lax.axis_size("vocab")
    fits = (
        count % 2 == 0
        and hidden_states.shape[1] == 5 * LANES // 2
        and hidden_states.shape[0] % 32 == 0
        and head.shape[0] % LANES == LANES // 2
        and (head.shape[0] + LANES // 2) // LANES % 2 == 0
        and teacher_values.shape[0] == 4
    )
    return paired_shards(*arrays) if fits else shards(*arrays)


def solution(mesh):
    in_specs = (
        P("dom", "vocab"),
        P("vocab", None),
        P(("dom", "vocab"), None),
        P(("dom", "vocab"), None),
        P("dom"),
        P("dom"),
        P("dom"),
        P(),
    )
    out_specs = (P("dom", "vocab"), P("dom"))
    return jax.shard_map(
        any_shards, mesh=mesh, in_specs=in_specs, out_specs=out_specs, check_vma=False
    )
```

```python
import functools

import jax
import jax.numpy as jnp
from jax import lax
from jax.experimental import pallas as pl
from jax.experimental.pallas import tpu as pltpu
from jax.sharding import PartitionSpec as P

BLOCK = 32
LANES = 128
STATS = 8
AHEAD = 3
EARLY = 3


sample_weight = 0.5


def to_all(piece, count):
    copies = jnp.broadcast_to(piece[None], (count,) + piece.shape)
    return lax.all_to_all(copies, "vocab", split_axis=0, concat_axis=0, tiled=True)


def scaled_teacher(teacher_values, teacher_scales, count, shard_rows):
    slot_rows = teacher_values.shape[0]
    scaled = (
        teacher_values.astype(jnp.float32).reshape(slot_rows, -1, BLOCK) * teacher_scales[:, :, None]
    ).astype(jnp.bfloat16)
    return scaled.reshape(slot_rows, count, shard_rows).transpose(1, 0, 2)


def merge_stats(tops, sums, teacher_tops, teacher_sums, crosses):
    top = jnp.max(tops, axis=0)
    teacher_top = jnp.max(teacher_tops, axis=0)
    shift = tops - top[None]
    teacher_shift = teacher_tops - teacher_top[None]
    weight = jnp.exp(shift)
    total = jnp.sum(sums * weight, axis=0)
    teacher_total = jnp.sum(teacher_sums * jnp.exp(teacher_shift), axis=0)
    cross = jnp.sum(weight * (crosses + sums * (shift - teacher_shift)), axis=0)
    return top, total, teacher_top, teacher_total, cross


def swap_cores(array):
    count = lax.axis_size("vocab")
    return lax.ppermute(array, "vocab", [(i, i ^ 1) for i in range(count)])


def along_chips(array, step):
    count = lax.axis_size("vocab")
    return lax.ppermute(array, "vocab", [(i, (i + 2 * step) % count) for i in range(count)])


def vmem_array(shape, dtype):
    return pltpu.VMEM(shape, dtype)


def in_vmem(array):
    return pltpu.with_memory_space_constraint(array, pltpu.VMEM)


def in_hbm(array):
    return pltpu.with_memory_space_constraint(array, pltpu.HBM)


def hbm_array(shape, dtype):
    return pltpu.HBM(shape, dtype)


def low_lanes(shape):
    return lax.broadcasted_iota(jnp.int32, shape, len(shape) - 1) < LANES // 2


def low_rows(shape, count):
    return lax.broadcasted_iota(jnp.int32, shape, 0) < count


def turned(array):
    return pltpu.roll(array, LANES // 2, 1)


def packed_half(tiles):
    rows = tiles[2].shape[0] // 2
    upper, lower = tiles[2][:rows], tiles[2][rows:]
    rest = jnp.where(low_lanes(upper.shape), upper, turned(lower))
    return jnp.concatenate([tiles[0], tiles[1], rest], axis=0)


def unpacked_half(packed, tokens):
    rest = packed[2 * tokens :]
    return [packed[:tokens], packed[tokens : 2 * tokens], jnp.concatenate([rest, turned(rest)])]


def joined(first, second):
    low = low_lanes(first[0].shape)
    turns = [turned(tile) for tile in second]
    return [
        first[0],
        first[1],
        jnp.where(low, first[2], turns[0]),
        jnp.where(low, turns[0], turns[1]),
        jnp.where(low, turns[1], turns[2]),
    ]


def parted(tiles):
    low = low_lanes(tiles[0].shape)
    turns = [turned(tile) for tile in tiles[2:]]
    return tiles[:3], [
        jnp.where(low, turns[0], turns[1]),
        jnp.where(low, turns[1], turns[2]),
        turns[2],
    ]


def column_of(row):
    size = row.shape[1]
    down = lax.broadcasted_iota(jnp.int32, (size, size), 0)
    along = lax.broadcasted_iota(jnp.int32, (size, size), 1)
    return jnp.sum(jnp.where(down == along, row, jnp.zeros_like(row)), axis=1, keepdims=True)


def token_facts(ids, row_map, lengths, first_entry):
    tokens = row_map.shape[1]
    token = lax.broadcasted_iota(jnp.int32, (tokens, tokens), 0)
    slot = lax.broadcasted_iota(jnp.int32, (tokens, tokens), 1)
    owner = (row_map == token).astype(jnp.float32)
    named = jnp.max(owner, axis=1, keepdims=True)
    owner = jnp.where((slot == 0) & (named == 0.0), 1.0, owner)

    seqs = lengths.shape[1]
    seq_length = tokens // seqs
    position = lax.broadcasted_iota(jnp.int32, (tokens, 1), 0)
    live_until = jnp.zeros((tokens, 1), jnp.int32)
    for seq in range(seqs):
        inside = (position >= seq * seq_length) & (position < (seq + 1) * seq_length)
        until = lengths[:, seq : seq + 1] + seq * seq_length
        live_until = jnp.where(inside, until, live_until)
    live = (position < live_until).astype(jnp.float32)
    count = jnp.sum(live, axis=0, keepdims=True)
    entry = (column_of(ids) - first_entry).astype(jnp.float32)
    lane = lax.broadcasted_iota(jnp.int32, (tokens, LANES), 1)
    return owner.astype(jnp.bfloat16), jnp.where(lane == 0, entry, live / count)


def pack_kernel(place_ref, *refs, shard_rows):
    outside, refs = refs[:6], refs[6:]
    packed_ref, owner_ref, table_ref = refs[:3]
    inside, wide_ref, sems = refs[3:9], refs[9], refs[10]
    copies = [
        pltpu.make_async_copy(source, target, sems.at[i])
        for i, (source, target) in enumerate(zip(outside, inside))
    ]
    for copy in copies:
        copy.start()
    for copy in copies:
        copy.wait()
    hidden_ref, values_ref, scales_ref, ids_ref, map_ref, lengths_ref = inside
    owner_ref[...], table_ref[...] = token_facts(
        ids_ref[...], map_ref[...], lengths_ref[...], place_ref[0] * shard_rows
    )
    chips = packed_ref.shape[0]
    tokens, half = hidden_ref.shape
    slots, entries = values_ref.shape
    pair = entries // chips
    shard = pair // 2
    blocks = pair // BLOCK
    scales = jnp.concatenate([scales_ref[...]] * 2, axis=0)
    stacked = jnp.concatenate(
        [scales[:, blocks * chip : blocks * (chip + 1)] for chip in range(chips)], axis=0
    )
    block = lax.broadcasted_iota(jnp.int32, (blocks, pair), 0)
    entry = lax.broadcasted_iota(jnp.int32, (blocks, pair), 1)
    inside = (entry >= block * BLOCK) & (entry < block * BLOCK + BLOCK)
    spread = jnp.dot(
        stacked.astype(jnp.bfloat16),
        inside.astype(jnp.bfloat16),
        preferred_element_type=jnp.float32,
    )
    values = values_ref[...].astype(jnp.float32)
    values = jnp.concatenate([values, values], axis=0)
    for chip in range(chips):
        wide_ref[:, pair * chip : pair * (chip + 1)] = (
            values[:, pair * chip : pair * (chip + 1)]
            * spread[2 * slots * chip : 2 * slots * (chip + 1)]
        )
    wide_ref[:, entries:] = jnp.zeros((2 * slots, LANES), jnp.float32)

    hidden = hidden_ref[...].astype(jnp.float32)
    hidden = jnp.concatenate([hidden, jnp.zeros((tokens, LANES // 2), jnp.float32)], axis=1)
    hidden = packed_half([hidden[:, LANES * i : LANES * (i + 1)] for i in range(3)])
    hidden = hidden.astype(jnp.bfloat16)
    hidden_rows = hidden.shape[0]
    upper = low_rows((2 * slots, LANES), slots)
    low = low_lanes((2 * slots, LANES))
    tile_pairs = (shard + LANES // 2) // LANES // 2
    for chip in range(chips):
        rows = []
        for core in range(2):
            start = pair * chip + (shard - LANES // 2) * core
            tiles = [
                wide_ref[:, start + LANES * i : start + LANES * (i + 1)]
                for i in range(2 * tile_pairs + core)
            ]
            if core == 1:
                tiles = [turned(tile) for tile in tiles]
                tiles = [
                    jnp.where(low, tiles[i], tiles[i + 1]) for i in range(2 * tile_pairs)
                ]
            rows += [
                jnp.where(upper, tiles[2 * i], tiles[2 * i + 1]) for i in range(tile_pairs)
            ]
        step = lax.rem(chip - place_ref[0] // 2 + chips, chips)
        packed_ref[step, :hidden_rows] = hidden
        packed_ref[step, hidden_rows:] = jnp.concatenate(rows, axis=0).astype(jnp.bfloat16)


def head_copies(head_ref, held_ref, sems, chips):
    width = held_ref.shape[1] // len(chips)
    copies = []
    for step, chip in enumerate(chips):
        columns = pl.ds(pl.multiple_of(chip * width, LANES), width)
        copies.append(
            pltpu.make_async_copy(
                head_ref.at[:, columns],
                held_ref.at[:, width * step : width * (step + 1)],
                sems.at[step],
            )
        )
    return copies


def take(copies, steps):
    for step in steps:
        copies[step].wait()
        if step + AHEAD < len(copies):
            copies[step + AHEAD].start()


def grouped(count, sizes):
    groups, start = [], 0
    while start < count:
        size = min(sizes[min(len(groups), len(sizes) - 1)], count - start)
        groups.append(range(start, start + size))
        start += size
    return groups


def source_chips(place_ref, chips):
    return [lax.rem(place_ref[0] // 2 - step + chips, chips) for step in range(chips)]


def preload_kernel(place_ref, head_ref, _, early_ref, sems, *, chips):
    sources = source_chips(place_ref, chips)[:EARLY]
    copies = head_copies(head_ref, early_ref, sems, sources)
    for copy in copies:
        copy.start()
    for copy in copies:
        copy.wait()


def logits_kernel(place_ref, *refs, chips):
    near, far, refs = refs[:chips][::-1], refs[chips : chips + 2], refs[chips + 2 :]
    owner_ref, tokens_ref, early_ref, head_ref, rows_ref, stats_ref, own_ref = refs[:7]
    held_ref, made_ref, hidden_ref, arrived_ref, teacher_ref, sems, made_sem = refs[7:]
    core = place_ref[0] % 2
    sources = source_chips(place_ref, chips)
    copies = head_copies(head_ref, held_ref, sems, sources[EARLY:])
    for copy in copies[:AHEAD]:
        copy.start()
    tokens, width = hidden_ref.shape[0], hidden_ref.shape[1] // chips
    shard_rows = head_ref.shape[0]
    hidden_rows = tokens * width // 2 // LANES
    slots = tokens // (2 * chips)
    upper = low_rows((2 * slots, LANES), slots)

    def both(step, rows):
        own = near[step][rows].astype(jnp.float32)
        late = step > chips // 2
        group = far[0] if late else far[1]
        other = group[step - chips // 2 - 1 if late else step, rows].astype(jnp.float32)
        return jnp.where(core == 0, own, other), jnp.where(core == 0, other, own)

    def unpack_hidden(step):
        first, second = both(step, slice(0, hidden_rows))
        tiles = joined(unpacked_half(first, tokens), unpacked_half(second, tokens))
        tiles = jnp.concatenate(tiles, axis=1).astype(jnp.bfloat16)
        hidden_ref[:, width * step : width * (step + 1)] = tiles

    def unpack_teacher(step):
        first, second = both(step, slice(hidden_rows, near[0].shape[0]))
        share = first.shape[0] // 2
        first = jnp.where(core == 0, first[:share], first[share:])
        second = jnp.where(core == 0, second[:share], second[share:])
        tiles = []
        for row in range(0, share, 2 * slots):
            one, two = first[row : row + 2 * slots], second[row : row + 2 * slots]
            tiles.append(jnp.where(upper, one, pltpu.roll(two, slots, 0)))
            tiles.append(jnp.where(upper, pltpu.roll(one, slots, 0), two))
        rows = pl.ds(pl.multiple_of(2 * slots * sources[step], 2 * slots), 2 * slots)
        arrived_ref[rows] = jnp.concatenate(tiles, axis=1)

    def product(step, count, columns):
        return lax.dot_general(
            hidden_ref[:, width * step : width * (step + count)],
            columns,
            (((1,), (1,)), ((), ())),
            preferred_element_type=jnp.float32,
        )

    for step in range(chips):
        unpack_hidden(step)
        unpack_teacher(step)
    logits = product(0, EARLY, early_ref[...])
    teacher = jnp.dot(
        owner_ref[...],
        arrived_ref[:, :shard_rows].astype(jnp.bfloat16),
        preferred_element_type=jnp.float32,
    )
    teacher_top = jnp.max(teacher, axis=1, keepdims=True)
    teacher_off = teacher - teacher_top
    teacher_total = jnp.sum(jnp.exp(teacher_off), axis=1, keepdims=True)
    teacher_ref[...] = teacher_off
    for group in grouped(len(copies), (3, 2)):
        take(copies, group)
        columns = held_ref[:, width * group.start : width * group.stop]
        logits += product(EARLY + group.start, len(group), columns)

    top = jnp.max(logits, axis=1, keepdims=True)
    off = logits - top
    exps = jnp.exp(off)
    total = jnp.sum(exps, axis=1, keepdims=True)
    gap = off - teacher_ref[...]
    cross = jnp.sum(exps * gap, axis=1, keepdims=True)
    centre = cross / total
    entry = lax.broadcasted_iota(jnp.int32, (tokens, shard_rows), 1)
    hit = entry == tokens_ref[:, :1].astype(jnp.int32)
    target = jnp.sum(jnp.where(hit, logits, 0.0), axis=1, keepdims=True)
    made_ref[:tokens] = (exps * (gap - centre)).astype(jnp.bfloat16)
    made_ref[tokens : 2 * tokens] = exps.astype(jnp.bfloat16)
    made_ref[2 * tokens :] = hit.astype(jnp.bfloat16)
    out = pltpu.make_async_copy(made_ref, rows_ref, made_sem)
    out.start()

    lane = lax.broadcasted_iota(jnp.int32, (tokens, LANES), 1)
    table = jnp.zeros((tokens, LANES), jnp.float32)
    for place, column in enumerate(
        (top, total, teacher_top, teacher_total, cross, target, centre)
    ):
        table = jnp.where(lane == place, column, table)
    stats = jnp.concatenate([table, jnp.zeros((stats_ref.shape[2] - tokens, LANES), jnp.float32)])
    stats = stats.T[:STATS]
    own_ref[...] = stats
    stats_ref[...] = jnp.broadcast_to(stats[None], stats_ref.shape)
    out.wait()


def products_kernel(
    place_ref, rows_ref, head_ref, terms_ref, picks_ref, held_ref, made_ref, sems, made_sem
):
    into = pltpu.make_async_copy(rows_ref, made_ref, made_sem)
    into.start()
    chips = terms_ref.shape[0]
    targets = [lax.rem(place_ref[0] // 2 + step, chips) for step in range(chips)]
    copies = head_copies(head_ref, held_ref, sems, targets)
    for copy in copies[:AHEAD]:
        copy.start()
    into.wait()
    tokens = made_ref.shape[0] // 3
    width = held_ref.shape[1] // chips
    for group in grouped(chips, (2, 2, 2, 1)):
        take(copies, group)
        products = jnp.dot(
            made_ref[...],
            held_ref[:, width * group.start : width * group.stop],
            preferred_element_type=jnp.float32,
        )
        for place, step in enumerate(group):
            for part in range(3):
                rows = products[tokens * part : tokens * (part + 1)]
                columns = range(width * place, width * (place + 1), LANES)
                halves = parted([rows[:, i : i + LANES] for i in columns])
                for parity, tiles in enumerate(halves):
                    packed = packed_half(tiles)
                    if part < 2:
                        terms_ref[step, parity, part] = packed
                    else:
                        picks_ref[step, parity] = packed.astype(jnp.bfloat16)


def gradient_share(step, parity, factors_ref, terms_ref, picks_ref):
    sums = terms_ref[step, parity, 0] + factors_ref[1] * terms_ref[step, parity, 1]
    return factors_ref[0] * sums - factors_ref[2] * picks_ref[step, parity].astype(jnp.float32)


def give_kernel(
    place_ref,
    scale_ref,
    stats_ref,
    own_ref,
    tokens_ref,
    terms_ref,
    picks_ref,
    give_ref,
    factors_ref,
    loss_ref,
):
    tokens = tokens_ref.shape[0]
    tops, sums, teacher_tops, teacher_sums, crosses, targets = [
        stats_ref[:, i, :tokens] for i in range(6)
    ]
    top, total, teacher_top, teacher_total, cross = [
        part[None] for part in merge_stats(tops, sums, teacher_tops, teacher_sums, crosses)
    ]
    target = jnp.sum(targets, axis=0, keepdims=True)
    student_log = jnp.log(total)
    teacher_log = jnp.log(teacher_total)
    divergence = cross / total - (student_log - teacher_log)
    student_lse = top + student_log
    per_token = divergence + sample_weight * (student_lse - target)
    student_shift = own_ref[0:1, :tokens] - top - student_log
    teacher_shift = own_ref[2:3, :tokens] - teacher_top - teacher_log
    factor = jnp.exp(student_shift)
    level = (
        own_ref[6:7, :tokens] + student_shift - teacher_shift - divergence + sample_weight
    )
    zeros = jnp.zeros((LANES - 3, tokens), jnp.float32)
    columns = jnp.concatenate([factor, level, per_token, zeros], axis=0).T
    share = tokens_ref[:, 1:2]
    weight = share * scale_ref[0]
    loss_ref[...] = jnp.sum(share * columns[:, 2:3], axis=0, keepdims=True)
    for i, column in enumerate(
        (weight * columns[:, 0:1], columns[:, 1:2], sample_weight * weight)
    ):
        factors_ref[i] = packed_half([jnp.broadcast_to(column, (tokens, LANES))] * 3)
    parity = 1 - place_ref[0] % 2
    for step in range(terms_ref.shape[0]):
        share = gradient_share(step, parity, factors_ref, terms_ref, picks_ref)
        give_ref[step] = share.astype(jnp.bfloat16)


def keep_kernel(place_ref, factors_ref, found_ref, terms_ref, picks_ref, keep_ref, loss_ref):
    loss_ref[...] = found_ref[...]
    parity = place_ref[0] % 2
    for step in range(terms_ref.shape[0]):
        keep_ref[step] = gradient_share(step, parity, factors_ref, terms_ref, picks_ref)


def sum_kernel(own_ref, *refs):
    tokens, half = refs[-1].shape
    total = own_ref[...]
    for share_ref in refs[:-1]:
        total += share_ref[...].astype(jnp.float32)
    tiles = jnp.concatenate(unpacked_half(total, tokens), axis=1)
    refs[-1][...] = tiles[:, :half].astype(refs[-1].dtype)


def paired_shards(
    hidden_states, head, teacher_values, teacher_scales, token_ids, lengths, row_map, loss_scale
):
    count = lax.axis_size("vocab")
    own_index = lax.axis_index("vocab")
    chips = count // 2
    tokens, half = hidden_states.shape
    width = 2 * half
    shard_rows = head.shape[0]
    place = jnp.reshape(own_index, (1,))
    vmem = pl.BlockSpec(memory_space=pltpu.VMEM)
    smem = pl.BlockSpec(memory_space=pltpu.SMEM)
    hbm = pl.BlockSpec(memory_space=pl.ANY)
    params = pltpu.CompilerParams(vmem_limit_bytes=VMEM_LIMIT)
    head = in_hbm(head)
    head_scratch = pltpu.VMEM((shard_rows, chips * width), head.dtype)
    head_sems = pltpu.SemaphoreType.DMA((chips,))
    rows_scratch = pltpu.VMEM((3 * tokens, shard_rows), jnp.bfloat16)
    rows_sem = pltpu.SemaphoreType.DMA
    slots, entries = teacher_values.shape
    hidden_rows = tokens * half // LANES
    teacher_rows = 2 * slots * (shard_rows + LANES // 2) // LANES

    operands = (
        hidden_states,
        teacher_values,
        teacher_scales,
        token_ids[None, :],
        row_map[None, :],
        lengths[None, :],
    )
    packed, owner, table = pl.pallas_call(
        functools.partial(pack_kernel, shard_rows=shard_rows),
        out_shape=(
            jax.ShapeDtypeStruct((chips, hidden_rows + teacher_rows, LANES), jnp.bfloat16),
            vmem_array((tokens, tokens), jnp.bfloat16),
            vmem_array((tokens, LANES), jnp.float32),
        ),
        in_specs=[smem] + [hbm] * len(operands),
        out_specs=[vmem] * 3,
        scratch_shapes=[pltpu.VMEM(operand.shape, operand.dtype) for operand in operands]
        + [
            pltpu.VMEM((2 * slots, entries + LANES), jnp.float32),
            pltpu.SemaphoreType.DMA((len(operands),)),
        ],
        compiler_params=params,
        name="pack",
    )(place, *[in_hbm(operand) for operand in operands])
    steps = range(1, chips)
    near = [packed[0]] + [along_chips(packed[step], step) for step in steps]
    first, last = jnp.stack(near[: chips // 2 + 1]), jnp.stack(near[chips // 2 + 1 :])
    early = pl.pallas_call(
        functools.partial(preload_kernel, chips=chips),
        out_shape=vmem_array((shard_rows, EARLY * width), head.dtype),
        in_specs=[smem] + [hbm] * 2,
        out_specs=vmem,
        scratch_shapes=[pltpu.SemaphoreType.DMA((EARLY,))],
        compiler_params=params,
        cost_estimate=pl.CostEstimate(
            flops=0, bytes_accessed=4 * EARLY * shard_rows * width, transcendentals=0
        ),
        name="preload",
    )(place, head, near[3])
    last, early = lax.optimization_barrier((last, early))
    far = [swap_cores(last), swap_cores(first)]

    rows, stats, own_stats = pl.pallas_call(
        functools.partial(logits_kernel, chips=chips),
        out_shape=(
            hbm_array((3 * tokens, shard_rows), jnp.bfloat16),
            jax.ShapeDtypeStruct((count, STATS, pl.cdiv(tokens, LANES) * LANES), jnp.float32),
            vmem_array((STATS, pl.cdiv(tokens, LANES) * LANES), jnp.float32),
        ),
        in_specs=[smem] + [vmem] * (chips + 5) + [hbm],
        out_specs=[hbm, vmem, vmem],
        scratch_shapes=[
            pltpu.VMEM((shard_rows, (chips - EARLY) * width), head.dtype),
            rows_scratch,
            pltpu.VMEM((tokens, chips * width), jnp.bfloat16),
            pltpu.VMEM((tokens, shard_rows + LANES // 2), jnp.float32),
            pltpu.VMEM((tokens, shard_rows), jnp.float32),
            pltpu.SemaphoreType.DMA((chips - EARLY,)),
            rows_sem,
        ],
        compiler_params=params,
        cost_estimate=pl.CostEstimate(
            flops=2 * tokens * head.size, bytes_accessed=2 * head.size, transcendentals=0
        ),
        name="logits",
    )(place, *near[::-1], *far, in_vmem(owner), in_vmem(table), in_vmem(early), head)

    all_stats = lax.all_to_all(stats, "vocab", split_axis=0, concat_axis=0, tiled=True)

    terms, picks = pl.pallas_call(
        products_kernel,
        out_shape=(
            vmem_array((chips, 2, 2, hidden_rows, LANES), jnp.float32),
            vmem_array((chips, 2, hidden_rows, LANES), jnp.bfloat16),
        ),
        in_specs=[smem, hbm, hbm],
        out_specs=[vmem] * 2,
        scratch_shapes=[head_scratch, rows_scratch, head_sems, rows_sem],
        compiler_params=params,
        cost_estimate=pl.CostEstimate(
            flops=6 * tokens * head.size, bytes_accessed=2 * head.size, transcendentals=0
        ),
        name="products",
    )(place, in_hbm(rows), head)

    terms, picks = in_vmem(terms), in_vmem(picks)
    give, factors, loss = pl.pallas_call(
        give_kernel,
        out_shape=(
            vmem_array((chips, hidden_rows, LANES), jnp.bfloat16),
            vmem_array((3, hidden_rows, LANES), jnp.float32),
            vmem_array((1, 1), jnp.float32),
        ),
        in_specs=[smem] * 2 + [vmem] * 5,
        out_specs=[vmem] * 3,
        compiler_params=params,
        name="give",
    )(place, loss_scale, all_stats, in_vmem(own_stats), in_vmem(table), terms, picks)
    taken = swap_cores(give)
    keep, loss = pl.pallas_call(
        keep_kernel,
        out_shape=(
            vmem_array((chips, hidden_rows, LANES), jnp.float32),
            jax.ShapeDtypeStruct((1, 1), jnp.float32),
        ),
        in_specs=[smem] + [vmem] * 4,
        out_specs=[vmem] * 2,
        compiler_params=params,
        cost_estimate=pl.CostEstimate(
            flops=4 * terms.size, bytes_accessed=4 * terms.size, transcendentals=0
        ),
        name="keep",
    )(place, in_vmem(factors), in_vmem(loss), terms, picks)
    sums = keep + taken.astype(jnp.float32)
    shares = [along_chips(sums[step].astype(jnp.bfloat16), step) for step in steps]
    total = pl.pallas_call(
        sum_kernel,
        out_shape=jax.ShapeDtypeStruct((tokens, half), jnp.bfloat16),
        in_specs=[vmem] * chips,
        out_specs=vmem,
        compiler_params=params,
        name="total",
    )(sums[0], *shares)
    return total, jnp.reshape(loss, (1,))


VMEM_LIMIT = 24 * 1024 * 1024


def shards(
    hidden_states, head, teacher_values, teacher_scales, token_ids, lengths, row_map, loss_scale
):
    count = lax.axis_size("vocab")
    own_index = lax.axis_index("vocab")
    tokens = hidden_states.shape[0]
    own_features = hidden_states.shape[1]
    shard_rows = head.shape[0]
    seq_length = tokens // lengths.shape[0]
    contract_last = (((1,), (1,)), ((), ()))

    scaled = scaled_teacher(teacher_values, teacher_scales, count, shard_rows)
    arrived = lax.all_to_all(scaled, "vocab", split_axis=0, concat_axis=0, tiled=True)
    arrived = arrived.reshape(tokens, shard_rows)
    gathered = to_all(hidden_states, count).transpose(1, 0, 2).reshape(tokens, -1)
    logits = lax.dot_general(gathered, head, contract_last, preferred_element_type=jnp.float32)

    positions = jnp.arange(tokens, dtype=jnp.int32)
    owner = row_map[None, :] == positions[:, None]
    slot_of = jnp.sum(jnp.where(owner, positions[None, :], 0), axis=1)
    teacher = jnp.take(arrived, slot_of, axis=0).astype(jnp.float32)

    seq_ids = jnp.arange(lengths.shape[0], dtype=jnp.int32)
    own_length = jnp.sum(
        jnp.where((positions // seq_length)[:, None] == seq_ids[None, :], lengths[None, :], 0),
        axis=1,
    )
    live_mask = (positions % seq_length < own_length).astype(jnp.float32)
    live_count = jnp.sum(live_mask)

    local_ids = token_ids - own_index * shard_rows
    target_hit = local_ids[:, None] == jnp.arange(shard_rows, dtype=jnp.int32)[None, :]
    target_part = jnp.sum(jnp.where(target_hit, logits, 0.0), axis=1)
    student_top = jnp.max(logits, axis=1)
    teacher_top = jnp.max(teacher, axis=1)
    student_off = logits - student_top[:, None]
    teacher_off = teacher - teacher_top[:, None]
    student_exp = jnp.exp(student_off)
    student_sum = jnp.sum(student_exp, axis=1)
    teacher_sum = jnp.sum(jnp.exp(teacher_off), axis=1)
    cross_sum = jnp.sum(student_exp * (student_off - teacher_off), axis=1)

    stats = to_all(
        jnp.stack(
            [student_top, student_sum, teacher_top, teacher_sum, cross_sum, target_part]
        ),
        count,
    )
    tops, sums, teacher_tops, teacher_sums, crosses, targets = [stats[:, i] for i in range(6)]
    student_max, student_total, teacher_max, teacher_total, cross_total = merge_stats(
        tops, sums, teacher_tops, teacher_sums, crosses
    )
    student_log = jnp.log(student_total)
    teacher_log = jnp.log(teacher_total)
    student_lse = student_max + student_log
    teacher_lse = teacher_max + teacher_log
    divergence = cross_total / student_total - (student_log - teacher_log)
    target = jnp.sum(targets, axis=0)

    per_token = divergence + sample_weight * (student_lse - target)
    loss = jnp.reshape(jnp.sum(live_mask * per_token) / live_count, (1,))
    token_weight = live_mask * loss_scale[0] / live_count
    log_student = logits - student_lse[:, None]
    log_teacher = teacher - teacher_lse[:, None]
    student_prob = jnp.exp(log_student)
    grad_logits = (
        token_weight[:, None]
        * (
            student_prob * (log_student - log_teacher - divergence[:, None])
            + sample_weight * (student_prob - target_hit.astype(jnp.float32))
        )
    ).astype(jnp.bfloat16)
    terms = jnp.dot(grad_logits, head, preferred_element_type=jnp.float32).astype(jnp.bfloat16)
    terms = terms.reshape(tokens, count, own_features).transpose(1, 0, 2)
    shares = lax.all_to_all(terms, "vocab", split_axis=0, concat_axis=0, tiled=True)
    grad_hidden = jnp.sum(shares.astype(jnp.float32), axis=0)
    return (grad_hidden.astype(jnp.bfloat16), loss)


def any_shards(*arrays):
    hidden_states, head, teacher_values = arrays[:3]
    count = lax.axis_size("vocab")
    fits = (
        count % 2 == 0
        and hidden_states.shape[1] == 5 * LANES // 2
        and hidden_states.shape[0] % 32 == 0
        and head.shape[0] % LANES == LANES // 2
        and (head.shape[0] + LANES // 2) // LANES % 2 == 0
        and teacher_values.shape[0] == 4
    )
    return paired_shards(*arrays) if fits else shards(*arrays)


def solution(mesh):
    in_specs = (
        P("dom", "vocab"),
        P("vocab", None),
        P(("dom", "vocab"), None),
        P(("dom", "vocab"), None),
        P("dom"),
        P("dom"),
        P("dom"),
        P(),
    )
    out_specs = (P("dom", "vocab"), P("dom"))
    return jax.shard_map(
        any_shards, mesh=mesh, in_specs=in_specs, out_specs=out_specs, check_vma=False
    )
```

```python
import functools

import jax
import jax.numpy as jnp
from jax import lax
from jax.experimental import pallas as pl
from jax.experimental.pallas import tpu as pltpu
from jax.sharding import PartitionSpec as P

BLOCK = 32
LANES = 128
STATS = 8
AHEAD = 3
EARLY = 3


sample_weight = 0.5


def to_all(piece, count):
    copies = jnp.broadcast_to(piece[None], (count,) + piece.shape)
    return lax.all_to_all(copies, "vocab", split_axis=0, concat_axis=0, tiled=True)


def scaled_teacher(teacher_values, teacher_scales, count, shard_rows):
    slot_rows = teacher_values.shape[0]
    scaled = (
        teacher_values.astype(jnp.float32).reshape(slot_rows, -1, BLOCK) * teacher_scales[:, :, None]
    ).astype(jnp.bfloat16)
    return scaled.reshape(slot_rows, count, shard_rows).transpose(1, 0, 2)


def merge_stats(tops, sums, teacher_tops, teacher_sums, crosses):
    top = jnp.max(tops, axis=0)
    teacher_top = jnp.max(teacher_tops, axis=0)
    shift = tops - top[None]
    teacher_shift = teacher_tops - teacher_top[None]
    weight = jnp.exp(shift)
    total = jnp.sum(sums * weight, axis=0)
    teacher_total = jnp.sum(teacher_sums * jnp.exp(teacher_shift), axis=0)
    cross = jnp.sum(weight * (crosses + sums * (shift - teacher_shift)), axis=0)
    return top, total, teacher_top, teacher_total, cross


def swap_cores(array):
    count = lax.axis_size("vocab")
    return lax.ppermute(array, "vocab", [(i, i ^ 1) for i in range(count)])


def along_chips(array, step):
    count = lax.axis_size("vocab")
    return lax.ppermute(array, "vocab", [(i, (i + 2 * step) % count) for i in range(count)])


def vmem_array(shape, dtype):
    return pltpu.VMEM(shape, dtype)


def in_vmem(array):
    return pltpu.with_memory_space_constraint(array, pltpu.VMEM)


def in_hbm(array):
    return pltpu.with_memory_space_constraint(array, pltpu.HBM)


def hbm_array(shape, dtype):
    return pltpu.HBM(shape, dtype)


def low_lanes(shape):
    return lax.broadcasted_iota(jnp.int32, shape, len(shape) - 1) < LANES // 2


def low_rows(shape, count):
    return lax.broadcasted_iota(jnp.int32, shape, 0) < count


def turned(array):
    return pltpu.roll(array, LANES // 2, 1)


def tiles_of(array, count):
    return [array[:, LANES * i : LANES * (i + 1)] for i in range(count)]


def column_of(row):
    size = row.shape[1]
    down = lax.broadcasted_iota(jnp.int32, (size, size), 0)
    along = lax.broadcasted_iota(jnp.int32, (size, size), 1)
    return jnp.sum(jnp.where(down == along, row, jnp.zeros_like(row)), axis=1, keepdims=True)


def token_facts(ids, row_map, lengths, first_entry, slots):
    tokens = row_map.shape[1]
    token = lax.broadcasted_iota(jnp.int32, (tokens, tokens), 0)
    slot = lax.broadcasted_iota(jnp.int32, (tokens, tokens), 1)
    owner = (row_map == token).astype(jnp.float32)
    named = jnp.max(owner, axis=1, keepdims=True)
    owner = jnp.where((slot == 0) & (named == 0.0), 1.0, owner)
    rows = 2 * tokens
    slot = lax.broadcasted_iota(jnp.int32, (tokens, rows), 0)
    row = lax.broadcasted_iota(jnp.int32, (tokens, rows), 1)
    source, within = row // (2 * slots), row % (2 * slots)
    chosen = (slot == source * slots + within % slots).astype(jnp.bfloat16)
    owner = jnp.dot(owner.astype(jnp.bfloat16), chosen, preferred_element_type=jnp.float32)
    odd = within >= slots
    owner = jnp.concatenate([jnp.where(odd, 0.0, owner), jnp.where(odd, owner, 0.0)], axis=0)

    seqs = lengths.shape[1]
    seq_length = tokens // seqs
    position = lax.broadcasted_iota(jnp.int32, (tokens, 1), 0)
    live_until = jnp.zeros((tokens, 1), jnp.int32)
    for seq in range(seqs):
        inside = (position >= seq * seq_length) & (position < (seq + 1) * seq_length)
        until = lengths[:, seq : seq + 1] + seq * seq_length
        live_until = jnp.where(inside, until, live_until)
    live = (position < live_until).astype(jnp.float32)
    count = jnp.sum(live, axis=0, keepdims=True)
    entry = (column_of(ids) - first_entry).astype(jnp.float32)
    lane = lax.broadcasted_iota(jnp.int32, (tokens, LANES), 1)
    return owner.astype(jnp.bfloat16), jnp.where(lane == 0, entry, live / count)


def pack_kernel(place_ref, *refs, shard_rows):
    outside, refs = refs[:6], refs[6:]
    packed_ref, owner_ref, table_ref = refs[:3]
    inside, wide_ref, sems = refs[3:9], refs[9], refs[10]
    copies = [
        pltpu.make_async_copy(source, target, sems.at[i])
        for i, (source, target) in enumerate(zip(outside, inside))
    ]
    for copy in copies:
        copy.start()
    for copy in copies:
        copy.wait()
    hidden_ref, values_ref, scales_ref, ids_ref, map_ref, lengths_ref = inside
    owner_ref[...], table_ref[...] = token_facts(
        ids_ref[...], map_ref[...], lengths_ref[...], place_ref[0] * shard_rows, values_ref.shape[0]
    )
    chips = packed_ref.shape[0]
    tokens, half = hidden_ref.shape
    slots, entries = values_ref.shape
    pair = entries // chips
    shard = pair // 2
    blocks = pair // BLOCK
    scales = jnp.concatenate([scales_ref[...]] * 2, axis=0)
    stacked = jnp.concatenate(
        [scales[:, blocks * chip : blocks * (chip + 1)] for chip in range(chips)], axis=0
    )
    block = lax.broadcasted_iota(jnp.int32, (blocks, pair), 0)
    entry = lax.broadcasted_iota(jnp.int32, (blocks, pair), 1)
    inside = (entry >= block * BLOCK) & (entry < block * BLOCK + BLOCK)
    spread = jnp.dot(
        stacked.astype(jnp.bfloat16),
        inside.astype(jnp.bfloat16),
        preferred_element_type=jnp.float32,
    )
    values = values_ref[...].astype(jnp.float32)
    values = jnp.concatenate([values, values], axis=0)
    for chip in range(chips):
        wide_ref[:, pair * chip : pair * (chip + 1)] = (
            values[:, pair * chip : pair * (chip + 1)]
            * spread[2 * slots * chip : 2 * slots * (chip + 1)]
        )
    wide_ref[:, entries:] = jnp.zeros((2 * slots, LANES), jnp.float32)

    hidden = hidden_ref[...].astype(jnp.float32)
    zeros = jnp.zeros((tokens, LANES // 2), jnp.float32)
    tiles = tiles_of(jnp.concatenate([hidden, zeros], axis=1), 3)
    turns = [turned(tile) for tile in tiles]
    low = low_lanes(tiles[0].shape)
    first = place_ref[0] % 2 == 0
    hidden = jnp.concatenate(
        [
            jnp.where(first, tiles[0], jnp.where(low, turns[0], turns[1])),
            jnp.where(first, tiles[1], jnp.where(low, turns[1], turns[2])),
            jnp.where(first, tiles[2], jnp.where(low, 0.0, turns[0])),
        ],
        axis=0,
    ).astype(jnp.bfloat16)
    hidden_rows = hidden.shape[0]
    upper = low_rows((2 * slots, LANES), slots)
    low = low_lanes((2 * slots, LANES))
    tile_pairs = (shard + LANES // 2) // LANES // 2
    for chip in range(chips):
        rows = []
        for core in range(2):
            start = pair * chip + (shard - LANES // 2) * core
            tiles = [
                wide_ref[:, start + LANES * i : start + LANES * (i + 1)]
                for i in range(2 * tile_pairs + core)
            ]
            if core == 1:
                tiles = [turned(tile) for tile in tiles]
                tiles = [
                    jnp.where(low, tiles[i], tiles[i + 1]) for i in range(2 * tile_pairs)
                ]
            rows += [
                jnp.where(upper, tiles[2 * i], tiles[2 * i + 1]) for i in range(tile_pairs)
            ]
        step = lax.rem(chip - place_ref[0] // 2 + chips, chips)
        packed_ref[step, :hidden_rows] = hidden
        packed_ref[step, hidden_rows:] = jnp.concatenate(rows, axis=0).astype(jnp.bfloat16)


def head_copies(head_ref, held_ref, sems, chips):
    width = held_ref.shape[1] // len(chips)
    copies = []
    for step, chip in enumerate(chips):
        columns = pl.ds(pl.multiple_of(chip * width, LANES), width)
        copies.append(
            pltpu.make_async_copy(
                head_ref.at[:, columns],
                held_ref.at[:, width * step : width * (step + 1)],
                sems.at[step],
            )
        )
    return copies


def take(copies, step):
    copies[step].wait()
    if step + AHEAD < len(copies):
        copies[step + AHEAD].start()


def source_chips(place_ref, chips):
    return [lax.rem(place_ref[0] // 2 - step + chips, chips) for step in range(chips)]


def preload_kernel(place_ref, head_ref, _, early_ref, sems, *, chips):
    sources = source_chips(place_ref, chips)[:EARLY]
    copies = head_copies(head_ref, early_ref, sems, sources)
    for copy in copies:
        copy.start()
    for copy in copies:
        copy.wait()


def logits_kernel(place_ref, *refs, chips):
    near, far, refs = refs[:chips][::-1], refs[chips : chips + 2], refs[chips + 2 :]
    owner_ref, tokens_ref, early_ref, head_ref, rows_ref, stats_ref, own_ref = refs[:7]
    held_ref, made_ref, hidden_ref, arrived_ref, teacher_ref, sems, made_sem = refs[7:]
    core = place_ref[0] % 2
    sources = source_chips(place_ref, chips)
    copies = head_copies(head_ref, held_ref, sems, sources[EARLY:])
    for copy in copies[:AHEAD]:
        copy.start()
    tokens, width = hidden_ref.shape[0], hidden_ref.shape[1] // chips
    shard_rows = head_ref.shape[0]
    hidden_rows = 3 * tokens
    slots = tokens // (2 * chips)

    for step in range(chips):
        late = step > chips // 2
        group = far[0] if late else far[1]
        place = step - chips // 2 - 1 if late else step
        blocks = near[step], group.at[place]
        base = width * step
        for block, parity in zip(blocks, (core, 1 - core)):
            for i in range(2):
                column = base + LANES * i + (width - 2 * LANES) * parity
                lanes = pl.ds(pl.multiple_of(column, LANES), LANES)
                hidden_ref[:, lanes] = block[tokens * i : tokens * (i + 1)]
            teacher = block[hidden_rows:].astype(jnp.float32)
            share = teacher.shape[0] // 2
            teacher = jnp.where(core == 0, teacher[:share], teacher[share:])
            row = 2 * slots * (2 * sources[step] + parity)
            rows = pl.ds(pl.multiple_of(row, 2 * slots), 2 * slots)
            for i in range(share // (2 * slots)):
                arrived_ref[rows, LANES * i : LANES * (i + 1)] = teacher[
                    2 * slots * i : 2 * slots * (i + 1)
                ]
        both = [block[2 * tokens : hidden_rows] for block in blocks]
        hidden_ref[:, base + 2 * LANES : base + 3 * LANES] = both[0] + both[1]

    def product(step, count, columns):
        return lax.dot_general(
            hidden_ref[:, width * step : width * (step + count)],
            columns,
            (((1,), (1,)), ((), ())),
            preferred_element_type=jnp.float32,
        )

    logits = product(0, EARLY, early_ref[...])
    placed = jnp.dot(
        owner_ref[...], arrived_ref[...].astype(jnp.bfloat16), preferred_element_type=jnp.float32
    )
    pairs = arrived_ref.shape[1] // LANES
    even, odd = tiles_of(placed[:tokens], pairs), tiles_of(placed[tokens:], pairs)
    teacher = jnp.concatenate([tile for pair in zip(even, odd) for tile in pair], axis=1)
    teacher = teacher[:, :shard_rows]
    teacher_top = jnp.max(teacher, axis=1, keepdims=True)
    teacher_off = teacher - teacher_top
    teacher_total = jnp.sum(jnp.exp(teacher_off), axis=1, keepdims=True)
    teacher_ref[...] = teacher_off
    for step in range(len(copies)):
        take(copies, step)
        columns = held_ref[:, width * step : width * (step + 1)]
        logits += product(EARLY + step, 1, columns)

    top = jnp.max(logits, axis=1, keepdims=True)
    off = logits - top
    exps = jnp.exp(off)
    total = jnp.sum(exps, axis=1, keepdims=True)
    gap = off - teacher_ref[...]
    cross = jnp.sum(exps * gap, axis=1, keepdims=True)
    centre = cross / total
    entry = lax.broadcasted_iota(jnp.int32, (tokens, shard_rows), 1)
    hit = entry == tokens_ref[:, :1].astype(jnp.int32)
    target = jnp.sum(jnp.where(hit, logits, 0.0), axis=1, keepdims=True)
    made_ref[:tokens] = (exps * (gap - centre)).astype(jnp.bfloat16)
    made_ref[tokens : 2 * tokens] = exps.astype(jnp.bfloat16)
    made_ref[2 * tokens :] = hit.astype(jnp.bfloat16)
    out = pltpu.make_async_copy(made_ref, rows_ref, made_sem)
    out.start()

    lane = lax.broadcasted_iota(jnp.int32, (tokens, LANES), 1)
    table = jnp.zeros((tokens, LANES), jnp.float32)
    for place, column in enumerate(
        (top, total, teacher_top, teacher_total, cross, target, centre)
    ):
        table = jnp.where(lane == place, column, table)
    stats = jnp.concatenate([table, jnp.zeros((stats_ref.shape[2] - tokens, LANES), jnp.float32)])
    stats = stats.T[:STATS]
    own_ref[...] = stats
    stats_ref[...] = jnp.broadcast_to(stats[None], stats_ref.shape)
    out.wait()


def products_kernel(
    place_ref, rows_ref, head_ref, terms_ref, picks_ref, held_ref, made_ref, sems, made_sem
):
    into = pltpu.make_async_copy(rows_ref, made_ref, made_sem)
    into.start()
    chips = terms_ref.shape[0]
    targets = [lax.rem(place_ref[0] // 2 + step, chips) for step in range(chips)]
    copies = head_copies(head_ref, held_ref, sems, targets)
    for copy in copies[:AHEAD]:
        copy.start()
    into.wait()
    tokens = made_ref.shape[0] // 3
    width = held_ref.shape[1] // chips
    for step in range(chips):
        take(copies, step)
        products = jnp.dot(
            made_ref[...],
            held_ref[:, width * step : width * (step + 1)],
            preferred_element_type=jnp.float32,
        )
        for i, tile in enumerate(tiles_of(products, width // LANES)):
            terms_ref[step, i, 0] = tile[:tokens]
            terms_ref[step, i, 1] = tile[tokens : 2 * tokens]
            picks_ref[step, i] = tile[2 * tokens :].astype(jnp.bfloat16)


def put_shares(parity, factors_ref, terms_ref, picks_ref, out_ref):
    tokens = terms_ref.shape[3]
    factor, level, weight = [factors_ref[i] for i in range(3)]
    for step in range(terms_ref.shape[0]):
        for i in range(3):
            tile = 2 * parity + i
            sums = terms_ref[step, tile, 0] + level * terms_ref[step, tile, 1]
            share = factor * sums - weight * picks_ref[step, tile].astype(jnp.float32)
            out_ref[step, tokens * i : tokens * (i + 1)] = share.astype(out_ref.dtype)


def give_kernel(
    place_ref,
    scale_ref,
    stats_ref,
    own_ref,
    tokens_ref,
    terms_ref,
    picks_ref,
    give_ref,
    factors_ref,
    loss_ref,
):
    tokens = tokens_ref.shape[0]
    tops, sums, teacher_tops, teacher_sums, crosses, targets = [
        stats_ref[:, i, :tokens] for i in range(6)
    ]
    top, total, teacher_top, teacher_total, cross = [
        part[None] for part in merge_stats(tops, sums, teacher_tops, teacher_sums, crosses)
    ]
    target = jnp.sum(targets, axis=0, keepdims=True)
    student_log = jnp.log(total)
    teacher_log = jnp.log(teacher_total)
    divergence = cross / total - (student_log - teacher_log)
    student_lse = top + student_log
    per_token = divergence + sample_weight * (student_lse - target)
    student_shift = own_ref[0:1, :tokens] - top - student_log
    teacher_shift = own_ref[2:3, :tokens] - teacher_top - teacher_log
    factor = jnp.exp(student_shift)
    level = (
        own_ref[6:7, :tokens] + student_shift - teacher_shift - divergence + sample_weight
    )
    zeros = jnp.zeros((LANES - 3, tokens), jnp.float32)
    columns = jnp.concatenate([factor, level, per_token, zeros], axis=0).T
    share = tokens_ref[:, 1:2]
    weight = share * scale_ref[0]
    loss_ref[...] = jnp.sum(share * columns[:, 2:3], axis=0, keepdims=True)
    for i, column in enumerate(
        (weight * columns[:, 0:1], columns[:, 1:2], sample_weight * weight)
    ):
        factors_ref[i] = jnp.broadcast_to(column, (tokens, LANES))
    put_shares(1 - place_ref[0] % 2, factors_ref, terms_ref, picks_ref, give_ref)


def keep_kernel(place_ref, factors_ref, found_ref, terms_ref, picks_ref, keep_ref, loss_ref):
    loss_ref[...] = found_ref[...]
    put_shares(place_ref[0] % 2, factors_ref, terms_ref, picks_ref, keep_ref)


def sum_kernel(place_ref, own_ref, *refs):
    tokens, half = refs[-1].shape
    total = own_ref[...]
    for share_ref in refs[:-1]:
        total += share_ref[...].astype(jnp.float32)
    tiles = [total[tokens * i : tokens * (i + 1)] for i in range(3)]
    turns = [turned(tile) for tile in tiles]
    low = low_lanes(tiles[0].shape)
    first = place_ref[0] % 2 == 0
    tiles = [
        jnp.where(first, tiles[0], jnp.where(low, turns[0], turns[1])),
        jnp.where(first, tiles[1], jnp.where(low, turns[1], turns[2])),
        jnp.where(first, tiles[2], turns[2]),
    ]
    total = jnp.concatenate(tiles, axis=1)[:, :half]
    refs[-1][...] = total.astype(refs[-1].dtype)


def paired_shards(
    hidden_states, head, teacher_values, teacher_scales, token_ids, lengths, row_map, loss_scale
):
    count = lax.axis_size("vocab")
    own_index = lax.axis_index("vocab")
    chips = count // 2
    tokens, half = hidden_states.shape
    width = 2 * half
    shard_rows = head.shape[0]
    place = jnp.reshape(own_index, (1,))
    vmem = pl.BlockSpec(memory_space=pltpu.VMEM)
    smem = pl.BlockSpec(memory_space=pltpu.SMEM)
    hbm = pl.BlockSpec(memory_space=pl.ANY)
    params = pltpu.CompilerParams(vmem_limit_bytes=VMEM_LIMIT)
    head = in_hbm(head)
    head_scratch = pltpu.VMEM((shard_rows, chips * width), head.dtype)
    head_sems = pltpu.SemaphoreType.DMA((chips,))
    rows_scratch = pltpu.VMEM((3 * tokens, shard_rows), jnp.bfloat16)
    rows_sem = pltpu.SemaphoreType.DMA
    slots, entries = teacher_values.shape
    hidden_rows = 3 * tokens
    teacher_rows = 2 * slots * (shard_rows + LANES // 2) // LANES

    operands = (
        hidden_states,
        teacher_values,
        teacher_scales,
        token_ids[None, :],
        row_map[None, :],
        lengths[None, :],
    )
    packed, owner, table = pl.pallas_call(
        functools.partial(pack_kernel, shard_rows=shard_rows),
        out_shape=(
            jax.ShapeDtypeStruct((chips, hidden_rows + teacher_rows, LANES), jnp.bfloat16),
            vmem_array((2 * tokens, 2 * tokens), jnp.bfloat16),
            vmem_array((tokens, LANES), jnp.float32),
        ),
        in_specs=[smem] + [hbm] * len(operands),
        out_specs=[vmem] * 3,
        scratch_shapes=[pltpu.VMEM(operand.shape, operand.dtype) for operand in operands]
        + [
            pltpu.VMEM((2 * slots, entries + LANES), jnp.float32),
            pltpu.SemaphoreType.DMA((len(operands),)),
        ],
        compiler_params=params,
        name="pack",
    )(place, *[in_hbm(operand) for operand in operands])
    steps = range(1, chips)
    near = [packed[0]] + [along_chips(packed[step], step) for step in steps]
    first, last = jnp.stack(near[: chips // 2 + 1]), jnp.stack(near[chips // 2 + 1 :])
    early = pl.pallas_call(
        functools.partial(preload_kernel, chips=chips),
        out_shape=vmem_array((shard_rows, EARLY * width), head.dtype),
        in_specs=[smem] + [hbm] * 2,
        out_specs=vmem,
        scratch_shapes=[pltpu.SemaphoreType.DMA((EARLY,))],
        compiler_params=params,
        cost_estimate=pl.CostEstimate(
            flops=0, bytes_accessed=4 * EARLY * shard_rows * width, transcendentals=0
        ),
        name="preload",
    )(place, head, near[3])
    last, early = lax.optimization_barrier((last, early))
    far = [swap_cores(last), swap_cores(first)]

    rows, stats, own_stats = pl.pallas_call(
        functools.partial(logits_kernel, chips=chips),
        out_shape=(
            hbm_array((3 * tokens, shard_rows), jnp.bfloat16),
            jax.ShapeDtypeStruct((count, STATS, pl.cdiv(tokens, LANES) * LANES), jnp.float32),
            vmem_array((STATS, pl.cdiv(tokens, LANES) * LANES), jnp.float32),
        ),
        in_specs=[smem] + [vmem] * (chips + 5) + [hbm],
        out_specs=[hbm, vmem, vmem],
        scratch_shapes=[
            pltpu.VMEM((shard_rows, (chips - EARLY) * width), head.dtype),
            rows_scratch,
            pltpu.VMEM((tokens, chips * width), jnp.bfloat16),
            pltpu.VMEM((2 * tokens, (shard_rows + LANES // 2) // 2), jnp.float32),
            pltpu.VMEM((tokens, shard_rows), jnp.float32),
            pltpu.SemaphoreType.DMA((chips - EARLY,)),
            rows_sem,
        ],
        compiler_params=params,
        cost_estimate=pl.CostEstimate(
            flops=2 * tokens * head.size, bytes_accessed=2 * head.size, transcendentals=0
        ),
        name="logits",
    )(place, *near[::-1], *far, in_vmem(owner), in_vmem(table), in_vmem(early), head)

    all_stats = lax.all_to_all(stats, "vocab", split_axis=0, concat_axis=0, tiled=True)

    terms, picks = pl.pallas_call(
        products_kernel,
        out_shape=(
            vmem_array((chips, width // LANES, 2, tokens, LANES), jnp.float32),
            vmem_array((chips, width // LANES, tokens, LANES), jnp.bfloat16),
        ),
        in_specs=[smem, hbm, hbm],
        out_specs=[vmem] * 2,
        scratch_shapes=[head_scratch, rows_scratch, head_sems, rows_sem],
        compiler_params=params,
        cost_estimate=pl.CostEstimate(
            flops=6 * tokens * head.size, bytes_accessed=2 * head.size, transcendentals=0
        ),
        name="products",
    )(place, in_hbm(rows), head)

    terms, picks = in_vmem(terms), in_vmem(picks)
    give, factors, loss = pl.pallas_call(
        give_kernel,
        out_shape=(
            vmem_array((chips, hidden_rows, LANES), jnp.bfloat16),
            vmem_array((3, tokens, LANES), jnp.float32),
            vmem_array((1, 1), jnp.float32),
        ),
        in_specs=[smem] * 2 + [vmem] * 5,
        out_specs=[vmem] * 3,
        compiler_params=params,
        name="give",
    )(place, loss_scale, all_stats, in_vmem(own_stats), in_vmem(table), terms, picks)
    taken = swap_cores(give)
    keep, loss = pl.pallas_call(
        keep_kernel,
        out_shape=(
            vmem_array((chips, hidden_rows, LANES), jnp.float32),
            jax.ShapeDtypeStruct((1, 1), jnp.float32),
        ),
        in_specs=[smem] + [vmem] * 4,
        out_specs=[vmem] * 2,
        compiler_params=params,
        cost_estimate=pl.CostEstimate(
            flops=4 * terms.size, bytes_accessed=4 * terms.size, transcendentals=0
        ),
        name="keep",
    )(place, in_vmem(factors), in_vmem(loss), terms, picks)
    sums = keep + taken.astype(jnp.float32)
    shares = [along_chips(sums[step].astype(jnp.bfloat16), step) for step in steps]
    total = pl.pallas_call(
        sum_kernel,
        out_shape=jax.ShapeDtypeStruct((tokens, half), jnp.bfloat16),
        in_specs=[smem] + [vmem] * chips,
        out_specs=vmem,
        compiler_params=params,
        name="total",
    )(place, sums[0], *shares)
    return total, jnp.reshape(loss, (1,))


VMEM_LIMIT = 24 * 1024 * 1024


def shards(
    hidden_states, head, teacher_values, teacher_scales, token_ids, lengths, row_map, loss_scale
):
    count = lax.axis_size("vocab")
    own_index = lax.axis_index("vocab")
    tokens = hidden_states.shape[0]
    own_features = hidden_states.shape[1]
    shard_rows = head.shape[0]
    seq_length = tokens // lengths.shape[0]
    contract_last = (((1,), (1,)), ((), ()))

    scaled = scaled_teacher(teacher_values, teacher_scales, count, shard_rows)
    arrived = lax.all_to_all(scaled, "vocab", split_axis=0, concat_axis=0, tiled=True)
    arrived = arrived.reshape(tokens, shard_rows)
    gathered = to_all(hidden_states, count).transpose(1, 0, 2).reshape(tokens, -1)
    logits = lax.dot_general(gathered, head, contract_last, preferred_element_type=jnp.float32)

    positions = jnp.arange(tokens, dtype=jnp.int32)
    owner = row_map[None, :] == positions[:, None]
    slot_of = jnp.sum(jnp.where(owner, positions[None, :], 0), axis=1)
    teacher = jnp.take(arrived, slot_of, axis=0).astype(jnp.float32)

    seq_ids = jnp.arange(lengths.shape[0], dtype=jnp.int32)
    own_length = jnp.sum(
        jnp.where((positions // seq_length)[:, None] == seq_ids[None, :], lengths[None, :], 0),
        axis=1,
    )
    live_mask = (positions % seq_length < own_length).astype(jnp.float32)
    live_count = jnp.sum(live_mask)

    local_ids = token_ids - own_index * shard_rows
    target_hit = local_ids[:, None] == jnp.arange(shard_rows, dtype=jnp.int32)[None, :]
    target_part = jnp.sum(jnp.where(target_hit, logits, 0.0), axis=1)
    student_top = jnp.max(logits, axis=1)
    teacher_top = jnp.max(teacher, axis=1)
    student_off = logits - student_top[:, None]
    teacher_off = teacher - teacher_top[:, None]
    student_exp = jnp.exp(student_off)
    student_sum = jnp.sum(student_exp, axis=1)
    teacher_sum = jnp.sum(jnp.exp(teacher_off), axis=1)
    cross_sum = jnp.sum(student_exp * (student_off - teacher_off), axis=1)

    stats = to_all(
        jnp.stack(
            [student_top, student_sum, teacher_top, teacher_sum, cross_sum, target_part]
        ),
        count,
    )
    tops, sums, teacher_tops, teacher_sums, crosses, targets = [stats[:, i] for i in range(6)]
    student_max, student_total, teacher_max, teacher_total, cross_total = merge_stats(
        tops, sums, teacher_tops, teacher_sums, crosses
    )
    student_log = jnp.log(student_total)
    teacher_log = jnp.log(teacher_total)
    student_lse = student_max + student_log
    teacher_lse = teacher_max + teacher_log
    divergence = cross_total / student_total - (student_log - teacher_log)
    target = jnp.sum(targets, axis=0)

    per_token = divergence + sample_weight * (student_lse - target)
    loss = jnp.reshape(jnp.sum(live_mask * per_token) / live_count, (1,))
    token_weight = live_mask * loss_scale[0] / live_count
    log_student = logits - student_lse[:, None]
    log_teacher = teacher - teacher_lse[:, None]
    student_prob = jnp.exp(log_student)
    grad_logits = (
        token_weight[:, None]
        * (
            student_prob * (log_student - log_teacher - divergence[:, None])
            + sample_weight * (student_prob - target_hit.astype(jnp.float32))
        )
    ).astype(jnp.bfloat16)
    terms = jnp.dot(grad_logits, head, preferred_element_type=jnp.float32).astype(jnp.bfloat16)
    terms = terms.reshape(tokens, count, own_features).transpose(1, 0, 2)
    shares = lax.all_to_all(terms, "vocab", split_axis=0, concat_axis=0, tiled=True)
    grad_hidden = jnp.sum(shares.astype(jnp.float32), axis=0)
    return (grad_hidden.astype(jnp.bfloat16), loss)


def any_shards(*arrays):
    hidden_states, head, teacher_values = arrays[:3]
    count = lax.axis_size("vocab")
    fits = (
        count % 2 == 0
        and hidden_states.shape[1] == 5 * LANES // 2
        and hidden_states.shape[0] % 32 == 0
        and head.shape[0] % LANES == LANES // 2
        and (head.shape[0] + LANES // 2) // LANES % 2 == 0
        and teacher_values.shape[0] == 4
    )
    return paired_shards(*arrays) if fits else shards(*arrays)


def solution(mesh):
    in_specs = (
        P("dom", "vocab"),
        P("vocab", None),
        P(("dom", "vocab"), None),
        P(("dom", "vocab"), None),
        P("dom"),
        P("dom"),
        P("dom"),
        P(),
    )
    out_specs = (P("dom", "vocab"), P("dom"))
    return jax.shard_map(
        any_shards, mesh=mesh, in_specs=in_specs, out_specs=out_specs, check_vma=False
    )
```

```python
import functools

import jax
import jax.numpy as jnp
from jax import lax
from jax.experimental import pallas as pl
from jax.experimental.pallas import tpu as pltpu
from jax.sharding import PartitionSpec as P

BLOCK = 32
LANES = 128
STATS = 8
AHEAD = 3
EARLY = 3


sample_weight = 0.5


def to_all(piece, count):
    copies = jnp.broadcast_to(piece[None], (count,) + piece.shape)
    return lax.all_to_all(copies, "vocab", split_axis=0, concat_axis=0, tiled=True)


def scaled_teacher(teacher_values, teacher_scales, count, shard_rows):
    slot_rows = teacher_values.shape[0]
    scaled = (
        teacher_values.astype(jnp.float32).reshape(slot_rows, -1, BLOCK) * teacher_scales[:, :, None]
    ).astype(jnp.bfloat16)
    return scaled.reshape(slot_rows, count, shard_rows).transpose(1, 0, 2)


def merge_stats(tops, sums, teacher_tops, teacher_sums, crosses):
    top = jnp.max(tops, axis=0)
    teacher_top = jnp.max(teacher_tops, axis=0)
    shift = tops - top[None]
    teacher_shift = teacher_tops - teacher_top[None]
    weight = jnp.exp(shift)
    total = jnp.sum(sums * weight, axis=0)
    teacher_total = jnp.sum(teacher_sums * jnp.exp(teacher_shift), axis=0)
    cross = jnp.sum(weight * (crosses + sums * (shift - teacher_shift)), axis=0)
    return top, total, teacher_top, teacher_total, cross


def swap_cores(array):
    count = lax.axis_size("vocab")
    return lax.ppermute(array, "vocab", [(i, i ^ 1) for i in range(count)])


def along_chips(array, step):
    count = lax.axis_size("vocab")
    return lax.ppermute(array, "vocab", [(i, (i + 2 * step) % count) for i in range(count)])


def vmem_array(shape, dtype):
    return pltpu.VMEM(shape, dtype)


def in_vmem(array):
    return pltpu.with_memory_space_constraint(array, pltpu.VMEM)


def in_hbm(array):
    return pltpu.with_memory_space_constraint(array, pltpu.HBM)


def hbm_array(shape, dtype):
    return pltpu.HBM(shape, dtype)


def low_lanes(shape):
    return lax.broadcasted_iota(jnp.int32, shape, len(shape) - 1) < LANES // 2


def low_rows(shape, count):
    return lax.broadcasted_iota(jnp.int32, shape, 0) < count


def turned(array):
    return pltpu.roll(array, LANES // 2, 1)


def folded(first, tile):
    rows = tile.shape[0] // 2
    upper, lower = tile[:rows], turned(tile[rows:])
    low = low_lanes(upper.shape)
    return jnp.where(first, jnp.where(low, upper, lower), jnp.where(low, lower, upper))


def tiles_of(array, count):
    return [array[:, LANES * i : LANES * (i + 1)] for i in range(count)]


def column_of(row):
    size = row.shape[1]
    down = lax.broadcasted_iota(jnp.int32, (size, size), 0)
    along = lax.broadcasted_iota(jnp.int32, (size, size), 1)
    return jnp.sum(jnp.where(down == along, row, jnp.zeros_like(row)), axis=1, keepdims=True)


def token_facts(ids, row_map, lengths, first_entry, slots):
    tokens = row_map.shape[1]
    token = lax.broadcasted_iota(jnp.int32, (tokens, tokens), 0)
    slot = lax.broadcasted_iota(jnp.int32, (tokens, tokens), 1)
    owner = (row_map == token).astype(jnp.float32)
    named = jnp.max(owner, axis=1, keepdims=True)
    owner = jnp.where((slot == 0) & (named == 0.0), 1.0, owner)
    rows = 2 * tokens
    slot = lax.broadcasted_iota(jnp.int32, (tokens, rows), 0)
    row = lax.broadcasted_iota(jnp.int32, (tokens, rows), 1)
    source, within = row // (2 * slots), row % (2 * slots)
    chosen = (slot == source * slots + within % slots).astype(jnp.bfloat16)
    owner = jnp.dot(owner.astype(jnp.bfloat16), chosen, preferred_element_type=jnp.float32)
    odd = within >= slots
    owner = jnp.concatenate([jnp.where(odd, 0.0, owner), jnp.where(odd, owner, 0.0)], axis=0)

    seqs = lengths.shape[1]
    seq_length = tokens // seqs
    position = lax.broadcasted_iota(jnp.int32, (tokens, 1), 0)
    live_until = jnp.zeros((tokens, 1), jnp.int32)
    for seq in range(seqs):
        inside = (position >= seq * seq_length) & (position < (seq + 1) * seq_length)
        until = lengths[:, seq : seq + 1] + seq * seq_length
        live_until = jnp.where(inside, until, live_until)
    live = (position < live_until).astype(jnp.float32)
    count = jnp.sum(live, axis=0, keepdims=True)
    entry = (column_of(ids) - first_entry).astype(jnp.float32)
    lane = lax.broadcasted_iota(jnp.int32, (tokens, LANES), 1)
    return owner.astype(jnp.bfloat16), jnp.where(lane == 0, entry, live / count)


def pack_kernel(place_ref, *refs, shard_rows):
    outside, refs = refs[:6], refs[6:]
    packed_ref, owner_ref, table_ref = refs[:3]
    inside, wide_ref, sems = refs[3:9], refs[9], refs[10]
    copies = [
        pltpu.make_async_copy(source, target, sems.at[i])
        for i, (source, target) in enumerate(zip(outside, inside))
    ]
    for copy in copies:
        copy.start()
    for copy in copies:
        copy.wait()
    hidden_ref, values_ref, scales_ref, ids_ref, map_ref, lengths_ref = inside
    owner_ref[...], table_ref[...] = token_facts(
        ids_ref[...], map_ref[...], lengths_ref[...], place_ref[0] * shard_rows, values_ref.shape[0]
    )
    chips = packed_ref.shape[0]
    tokens, half = hidden_ref.shape
    slots, entries = values_ref.shape
    pair = entries // chips
    shard = pair // 2
    blocks = pair // BLOCK
    scales = jnp.concatenate([scales_ref[...]] * 2, axis=0)
    stacked = jnp.concatenate(
        [scales[:, blocks * chip : blocks * (chip + 1)] for chip in range(chips)], axis=0
    )
    block = lax.broadcasted_iota(jnp.int32, (blocks, pair), 0)
    entry = lax.broadcasted_iota(jnp.int32, (blocks, pair), 1)
    inside = (entry >= block * BLOCK) & (entry < block * BLOCK + BLOCK)
    spread = jnp.dot(
        stacked.astype(jnp.bfloat16),
        inside.astype(jnp.bfloat16),
        preferred_element_type=jnp.float32,
    )
    values = values_ref[...].astype(jnp.float32)
    values = jnp.concatenate([values, values], axis=0)
    for chip in range(chips):
        wide_ref[:, pair * chip : pair * (chip + 1)] = (
            values[:, pair * chip : pair * (chip + 1)]
            * spread[2 * slots * chip : 2 * slots * (chip + 1)]
        )
    wide_ref[:, entries:] = jnp.zeros((2 * slots, LANES), jnp.float32)

    hidden = hidden_ref[...].astype(jnp.float32)
    zeros = jnp.zeros((tokens, LANES // 2), jnp.float32)
    tiles = tiles_of(jnp.concatenate([hidden, zeros], axis=1), 3)
    turns = [turned(tile) for tile in tiles]
    low = low_lanes(tiles[0].shape)
    first = place_ref[0] % 2 == 0
    hidden = jnp.concatenate(
        [
            jnp.where(first, tiles[0], jnp.where(low, turns[0], turns[1])),
            jnp.where(first, tiles[1], jnp.where(low, turns[1], turns[2])),
            folded(first, jnp.where(first, tiles[2], turns[0])),
        ],
        axis=0,
    ).astype(jnp.bfloat16)
    hidden_rows = hidden.shape[0]
    upper = low_rows((2 * slots, LANES), slots)
    low = low_lanes((2 * slots, LANES))
    tile_pairs = (shard + LANES // 2) // LANES // 2
    for chip in range(chips):
        rows = []
        for core in range(2):
            start = pair * chip + (shard - LANES // 2) * core
            tiles = [
                wide_ref[:, start + LANES * i : start + LANES * (i + 1)]
                for i in range(2 * tile_pairs + core)
            ]
            if core == 1:
                tiles = [turned(tile) for tile in tiles]
                tiles = [
                    jnp.where(low, tiles[i], tiles[i + 1]) for i in range(2 * tile_pairs)
                ]
            rows += [
                jnp.where(upper, tiles[2 * i], tiles[2 * i + 1]) for i in range(tile_pairs)
            ]
        step = lax.rem(chip - place_ref[0] // 2 + chips, chips)
        packed_ref[step, :hidden_rows] = hidden
        packed_ref[step, hidden_rows:] = jnp.concatenate(rows, axis=0).astype(jnp.bfloat16)


def head_copies(head_ref, held_ref, sems, chips):
    width = held_ref.shape[1] // len(chips)
    copies = []
    for step, chip in enumerate(chips):
        columns = pl.ds(pl.multiple_of(chip * width, LANES), width)
        copies.append(
            pltpu.make_async_copy(
                head_ref.at[:, columns],
                held_ref.at[:, width * step : width * (step + 1)],
                sems.at[step],
            )
        )
    return copies


def take(copies, step):
    copies[step].wait()
    if step + AHEAD < len(copies):
        copies[step + AHEAD].start()


def source_chips(place_ref, chips):
    return [lax.rem(place_ref[0] // 2 - step + chips, chips) for step in range(chips)]


def preload_kernel(place_ref, head_ref, _, early_ref, sems, *, chips):
    sources = source_chips(place_ref, chips)[:EARLY]
    copies = head_copies(head_ref, early_ref, sems, sources)
    for copy in copies:
        copy.start()
    for copy in copies:
        copy.wait()


def logits_kernel(place_ref, *refs, chips):
    near, far, refs = refs[:chips][::-1], refs[chips : chips + 2], refs[chips + 2 :]
    owner_ref, tokens_ref, early_ref, head_ref, rows_ref, stats_ref, own_ref = refs[:7]
    held_ref, made_ref, hidden_ref, arrived_ref, teacher_ref, sems, made_sem = refs[7:]
    core = place_ref[0] % 2
    sources = source_chips(place_ref, chips)
    copies = head_copies(head_ref, held_ref, sems, sources[EARLY:])
    for copy in copies[:AHEAD]:
        copy.start()
    tokens, width = hidden_ref.shape[0], hidden_ref.shape[1] // chips
    shard_rows = head_ref.shape[0]
    hidden_rows = 5 * tokens // 2
    slots = tokens // (2 * chips)
    low = low_lanes((tokens // 2, LANES))

    for step in range(chips):
        late = step > chips // 2
        group = far[0] if late else far[1]
        place = step - chips // 2 - 1 if late else step
        blocks = near[step], group.at[place]
        base = width * step
        for block, parity in zip(blocks, (core, 1 - core)):
            for i in range(2):
                column = base + LANES * i + (width - 2 * LANES) * parity
                lanes = pl.ds(pl.multiple_of(column, LANES), LANES)
                hidden_ref[:, lanes] = block[tokens * i : tokens * (i + 1)]
            teacher = block[hidden_rows:].astype(jnp.float32)
            share = teacher.shape[0] // 2
            teacher = jnp.where(core == 0, teacher[:share], teacher[share:])
            row = 2 * slots * (2 * sources[step] + parity)
            rows = pl.ds(pl.multiple_of(row, 2 * slots), 2 * slots)
            for i in range(share // (2 * slots)):
                arrived_ref[rows, LANES * i : LANES * (i + 1)] = teacher[
                    2 * slots * i : 2 * slots * (i + 1)
                ]
        own, other = [block[2 * tokens : hidden_rows].astype(jnp.float32) for block in blocks]
        one, two = jnp.where(core == 0, own, other), jnp.where(core == 0, other, own)
        tile = [jnp.where(low, one, two), turned(jnp.where(low, two, one))]
        tile = jnp.concatenate(tile, axis=0).astype(jnp.bfloat16)
        hidden_ref[:, base + 2 * LANES : base + 3 * LANES] = tile

    def product(step, count, columns):
        return lax.dot_general(
            hidden_ref[:, width * step : width * (step + count)],
            columns,
            (((1,), (1,)), ((), ())),
            preferred_element_type=jnp.float32,
        )

    logits = product(0, EARLY, early_ref[...])
    placed = jnp.dot(
        owner_ref[...], arrived_ref[...].astype(jnp.bfloat16), preferred_element_type=jnp.float32
    )
    pairs = arrived_ref.shape[1] // LANES
    even, odd = tiles_of(placed[:tokens], pairs), tiles_of(placed[tokens:], pairs)
    teacher = jnp.concatenate([tile for pair in zip(even, odd) for tile in pair], axis=1)
    teacher = teacher[:, :shard_rows]
    teacher_top = jnp.max(teacher, axis=1, keepdims=True)
    teacher_off = teacher - teacher_top
    teacher_total = jnp.sum(jnp.exp(teacher_off), axis=1, keepdims=True)
    teacher_ref[...] = teacher_off
    for step in range(len(copies)):
        take(copies, step)
        columns = held_ref[:, width * step : width * (step + 1)]
        logits += product(EARLY + step, 1, columns)

    top = jnp.max(logits, axis=1, keepdims=True)
    off = logits - top
    exps = jnp.exp(off)
    total = jnp.sum(exps, axis=1, keepdims=True)
    gap = off - teacher_ref[...]
    cross = jnp.sum(exps * gap, axis=1, keepdims=True)
    centre = cross / total
    entry = lax.broadcasted_iota(jnp.int32, (tokens, shard_rows), 1)
    hit = entry == tokens_ref[:, :1].astype(jnp.int32)
    target = jnp.sum(jnp.where(hit, logits, 0.0), axis=1, keepdims=True)
    made_ref[:tokens] = (exps * (gap - centre)).astype(jnp.bfloat16)
    made_ref[tokens : 2 * tokens] = exps.astype(jnp.bfloat16)
    made_ref[2 * tokens :] = hit.astype(jnp.bfloat16)
    out = pltpu.make_async_copy(made_ref, rows_ref, made_sem)
    out.start()

    lane = lax.broadcasted_iota(jnp.int32, (tokens, LANES), 1)
    table = jnp.zeros((tokens, LANES), jnp.float32)
    for place, column in enumerate(
        (top, total, teacher_top, teacher_total, cross, target, centre)
    ):
        table = jnp.where(lane == place, column, table)
    stats = jnp.concatenate([table, jnp.zeros((stats_ref.shape[2] - tokens, LANES), jnp.float32)])
    stats = stats.T[:STATS]
    own_ref[...] = stats
    stats_ref[...] = jnp.broadcast_to(stats[None], stats_ref.shape)
    out.wait()


def products_kernel(
    place_ref, rows_ref, head_ref, terms_ref, picks_ref, held_ref, made_ref, sems, made_sem
):
    into = pltpu.make_async_copy(rows_ref, made_ref, made_sem)
    into.start()
    chips = terms_ref.shape[0]
    targets = [lax.rem(place_ref[0] // 2 + step, chips) for step in range(chips)]
    copies = head_copies(head_ref, held_ref, sems, targets)
    for copy in copies[:AHEAD]:
        copy.start()
    into.wait()
    tokens = made_ref.shape[0] // 3
    width = held_ref.shape[1] // chips
    for step in range(chips):
        take(copies, step)
        products = jnp.dot(
            made_ref[...],
            held_ref[:, width * step : width * (step + 1)],
            preferred_element_type=jnp.float32,
        )
        for i, tile in enumerate(tiles_of(products, width // LANES)):
            terms_ref[step, i, 0] = tile[:tokens]
            terms_ref[step, i, 1] = tile[tokens : 2 * tokens]
            picks_ref[step, i] = tile[2 * tokens :].astype(jnp.bfloat16)


def put_shares(parity, factors_ref, terms_ref, picks_ref, out_ref):
    tokens = terms_ref.shape[3]
    factor, level, weight = [factors_ref[i] for i in range(3)]
    for step in range(terms_ref.shape[0]):
        for i, tile in enumerate((3 * parity, 3 * parity + 1, 2)):
            sums = terms_ref[step, tile, 0] + level * terms_ref[step, tile, 1]
            share = factor * sums - weight * picks_ref[step, tile].astype(jnp.float32)
            if i == 2:
                share = folded(parity == 0, share)
            out_ref[step, tokens * i : tokens * i + share.shape[0]] = share.astype(out_ref.dtype)


def give_kernel(
    place_ref,
    scale_ref,
    stats_ref,
    own_ref,
    tokens_ref,
    terms_ref,
    picks_ref,
    give_ref,
    factors_ref,
    loss_ref,
):
    tokens = tokens_ref.shape[0]
    tops, sums, teacher_tops, teacher_sums, crosses, targets = [
        stats_ref[:, i, :tokens] for i in range(6)
    ]
    top, total, teacher_top, teacher_total, cross = [
        part[None] for part in merge_stats(tops, sums, teacher_tops, teacher_sums, crosses)
    ]
    target = jnp.sum(targets, axis=0, keepdims=True)
    student_log = jnp.log(total)
    teacher_log = jnp.log(teacher_total)
    divergence = cross / total - (student_log - teacher_log)
    student_lse = top + student_log
    per_token = divergence + sample_weight * (student_lse - target)
    student_shift = own_ref[0:1, :tokens] - top - student_log
    teacher_shift = own_ref[2:3, :tokens] - teacher_top - teacher_log
    factor = jnp.exp(student_shift)
    level = (
        own_ref[6:7, :tokens] + student_shift - teacher_shift - divergence + sample_weight
    )
    zeros = jnp.zeros((LANES - 3, tokens), jnp.float32)
    columns = jnp.concatenate([factor, level, per_token, zeros], axis=0).T
    share = tokens_ref[:, 1:2]
    weight = share * scale_ref[0]
    loss_ref[...] = jnp.sum(share * columns[:, 2:3], axis=0, keepdims=True)
    for i, column in enumerate(
        (weight * columns[:, 0:1], columns[:, 1:2], sample_weight * weight)
    ):
        factors_ref[i] = jnp.broadcast_to(column, (tokens, LANES))
    put_shares(1 - place_ref[0] % 2, factors_ref, terms_ref, picks_ref, give_ref)


def keep_kernel(place_ref, factors_ref, found_ref, terms_ref, picks_ref, keep_ref, loss_ref):
    loss_ref[...] = found_ref[...]
    put_shares(place_ref[0] % 2, factors_ref, terms_ref, picks_ref, keep_ref)


def sum_kernel(place_ref, own_ref, *refs):
    tokens, half = refs[-1].shape
    total = own_ref[...]
    for share_ref in refs[:-1]:
        total += share_ref[...].astype(jnp.float32)
    one, two, rest = total[:tokens], total[tokens : 2 * tokens], total[2 * tokens :]
    rest = jnp.concatenate([rest, turned(rest)], axis=0)
    turns = [turned(tile) for tile in (rest, one, two)]
    low = low_lanes(one.shape)
    first = place_ref[0] % 2 == 0
    tiles = [
        jnp.where(first, one, jnp.where(low, turns[0], turns[1])),
        jnp.where(first, two, jnp.where(low, turns[1], turns[2])),
        jnp.where(first, rest, turns[2]),
    ]
    total = jnp.concatenate(tiles, axis=1)[:, :half]
    refs[-1][...] = total.astype(refs[-1].dtype)


def paired_shards(
    hidden_states, head, teacher_values, teacher_scales, token_ids, lengths, row_map, loss_scale
):
    count = lax.axis_size("vocab")
    own_index = lax.axis_index("vocab")
    chips = count // 2
    tokens, half = hidden_states.shape
    width = 2 * half
    shard_rows = head.shape[0]
    place = jnp.reshape(own_index, (1,))
    vmem = pl.BlockSpec(memory_space=pltpu.VMEM)
    smem = pl.BlockSpec(memory_space=pltpu.SMEM)
    hbm = pl.BlockSpec(memory_space=pl.ANY)
    params = pltpu.CompilerParams(vmem_limit_bytes=VMEM_LIMIT)
    head = in_hbm(head)
    head_scratch = pltpu.VMEM((shard_rows, chips * width), head.dtype)
    head_sems = pltpu.SemaphoreType.DMA((chips,))
    rows_scratch = pltpu.VMEM((3 * tokens, shard_rows), jnp.bfloat16)
    rows_sem = pltpu.SemaphoreType.DMA
    slots, entries = teacher_values.shape
    hidden_rows = 5 * tokens // 2
    teacher_rows = 2 * slots * (shard_rows + LANES // 2) // LANES

    operands = (
        hidden_states,
        teacher_values,
        teacher_scales,
        token_ids[None, :],
        row_map[None, :],
        lengths[None, :],
    )
    packed, owner, table = pl.pallas_call(
        functools.partial(pack_kernel, shard_rows=shard_rows),
        out_shape=(
            vmem_array((chips, hidden_rows + teacher_rows, LANES), jnp.bfloat16),
            vmem_array((2 * tokens, 2 * tokens), jnp.bfloat16),
            vmem_array((tokens, LANES), jnp.float32),
        ),
        in_specs=[smem] + [hbm] * len(operands),
        out_specs=[vmem] * 3,
        scratch_shapes=[pltpu.VMEM(operand.shape, operand.dtype) for operand in operands]
        + [
            pltpu.VMEM((2 * slots, entries + LANES), jnp.float32),
            pltpu.SemaphoreType.DMA((len(operands),)),
        ],
        compiler_params=params,
        name="pack",
    )(place, *[in_hbm(operand) for operand in operands])
    steps = range(1, chips)
    near = [packed[0]] + [along_chips(packed[step], step) for step in steps]
    first, last = jnp.stack(near[: chips // 2 + 1]), jnp.stack(near[chips // 2 + 1 :])
    early = pl.pallas_call(
        functools.partial(preload_kernel, chips=chips),
        out_shape=vmem_array((shard_rows, EARLY * width), head.dtype),
        in_specs=[smem] + [hbm] * 2,
        out_specs=vmem,
        scratch_shapes=[pltpu.SemaphoreType.DMA((EARLY,))],
        compiler_params=params,
        cost_estimate=pl.CostEstimate(
            flops=0, bytes_accessed=4 * EARLY * shard_rows * width, transcendentals=0
        ),
        name="preload",
    )(place, head, near[3])
    last, early = lax.optimization_barrier((last, early))
    far = [swap_cores(last), swap_cores(first)]

    rows, stats, own_stats = pl.pallas_call(
        functools.partial(logits_kernel, chips=chips),
        out_shape=(
            hbm_array((3 * tokens, shard_rows), jnp.bfloat16),
            jax.ShapeDtypeStruct((count, STATS, pl.cdiv(tokens, LANES) * LANES), jnp.float32),
            vmem_array((STATS, pl.cdiv(tokens, LANES) * LANES), jnp.float32),
        ),
        in_specs=[smem] + [vmem] * (chips + 5) + [hbm],
        out_specs=[hbm, vmem, vmem],
        scratch_shapes=[
            pltpu.VMEM((shard_rows, (chips - EARLY) * width), head.dtype),
            rows_scratch,
            pltpu.VMEM((tokens, chips * width), jnp.bfloat16),
            pltpu.VMEM((2 * tokens, (shard_rows + LANES // 2) // 2), jnp.float32),
            pltpu.VMEM((tokens, shard_rows), jnp.float32),
            pltpu.SemaphoreType.DMA((chips - EARLY,)),
            rows_sem,
        ],
        compiler_params=params,
        cost_estimate=pl.CostEstimate(
            flops=2 * tokens * head.size, bytes_accessed=2 * head.size, transcendentals=0
        ),
        name="logits",
    )(place, *[in_vmem(block) for block in near[::-1] + far], in_vmem(owner), in_vmem(table), in_vmem(early), head)

    all_stats = lax.all_to_all(stats, "vocab", split_axis=0, concat_axis=0, tiled=True)

    terms, picks = pl.pallas_call(
        products_kernel,
        out_shape=(
            vmem_array((chips, width // LANES, 2, tokens, LANES), jnp.float32),
            vmem_array((chips, width // LANES, tokens, LANES), jnp.bfloat16),
        ),
        in_specs=[smem, hbm, hbm],
        out_specs=[vmem] * 2,
        scratch_shapes=[head_scratch, rows_scratch, head_sems, rows_sem],
        compiler_params=params,
        cost_estimate=pl.CostEstimate(
            flops=6 * tokens * head.size, bytes_accessed=2 * head.size, transcendentals=0
        ),
        name="products",
    )(place, in_hbm(rows), head)

    terms, picks = in_vmem(terms), in_vmem(picks)
    give, factors, loss = pl.pallas_call(
        give_kernel,
        out_shape=(
            vmem_array((chips, hidden_rows, LANES), jnp.bfloat16),
            vmem_array((3, tokens, LANES), jnp.float32),
            vmem_array((1, 1), jnp.float32),
        ),
        in_specs=[smem] * 2 + [vmem] * 5,
        out_specs=[vmem] * 3,
        compiler_params=params,
        name="give",
    )(place, loss_scale, in_vmem(all_stats), in_vmem(own_stats), in_vmem(table), terms, picks)
    taken = swap_cores(give)
    keep, loss = pl.pallas_call(
        keep_kernel,
        out_shape=(
            vmem_array((chips, hidden_rows, LANES), jnp.float32),
            jax.ShapeDtypeStruct((1, 1), jnp.float32),
        ),
        in_specs=[smem] + [vmem] * 4,
        out_specs=[vmem] * 2,
        compiler_params=params,
        cost_estimate=pl.CostEstimate(
            flops=4 * terms.size, bytes_accessed=4 * terms.size, transcendentals=0
        ),
        name="keep",
    )(place, in_vmem(factors), in_vmem(loss), terms, picks)
    sums = keep + taken.astype(jnp.float32)
    shares = [along_chips(sums[step].astype(jnp.bfloat16), step) for step in steps]
    total = pl.pallas_call(
        sum_kernel,
        out_shape=jax.ShapeDtypeStruct((tokens, half), jnp.bfloat16),
        in_specs=[smem] + [vmem] * chips,
        out_specs=vmem,
        compiler_params=params,
        name="total",
    )(place, *[in_vmem(share) for share in [sums[0]] + shares])
    return total, jnp.reshape(loss, (1,))


VMEM_LIMIT = 24 * 1024 * 1024


def shards(
    hidden_states, head, teacher_values, teacher_scales, token_ids, lengths, row_map, loss_scale
):
    count = lax.axis_size("vocab")
    own_index = lax.axis_index("vocab")
    tokens = hidden_states.shape[0]
    own_features = hidden_states.shape[1]
    shard_rows = head.shape[0]
    seq_length = tokens // lengths.shape[0]
    contract_last = (((1,), (1,)), ((), ()))

    scaled = scaled_teacher(teacher_values, teacher_scales, count, shard_rows)
    arrived = lax.all_to_all(scaled, "vocab", split_axis=0, concat_axis=0, tiled=True)
    arrived = arrived.reshape(tokens, shard_rows)
    gathered = to_all(hidden_states, count).transpose(1, 0, 2).reshape(tokens, -1)
    logits = lax.dot_general(gathered, head, contract_last, preferred_element_type=jnp.float32)

    positions = jnp.arange(tokens, dtype=jnp.int32)
    owner = row_map[None, :] == positions[:, None]
    slot_of = jnp.sum(jnp.where(owner, positions[None, :], 0), axis=1)
    teacher = jnp.take(arrived, slot_of, axis=0).astype(jnp.float32)

    seq_ids = jnp.arange(lengths.shape[0], dtype=jnp.int32)
    own_length = jnp.sum(
        jnp.where((positions // seq_length)[:, None] == seq_ids[None, :], lengths[None, :], 0),
        axis=1,
    )
    live_mask = (positions % seq_length < own_length).astype(jnp.float32)
    live_count = jnp.sum(live_mask)

    local_ids = token_ids - own_index * shard_rows
    target_hit = local_ids[:, None] == jnp.arange(shard_rows, dtype=jnp.int32)[None, :]
    target_part = jnp.sum(jnp.where(target_hit, logits, 0.0), axis=1)
    student_top = jnp.max(logits, axis=1)
    teacher_top = jnp.max(teacher, axis=1)
    student_off = logits - student_top[:, None]
    teacher_off = teacher - teacher_top[:, None]
    student_exp = jnp.exp(student_off)
    student_sum = jnp.sum(student_exp, axis=1)
    teacher_sum = jnp.sum(jnp.exp(teacher_off), axis=1)
    cross_sum = jnp.sum(student_exp * (student_off - teacher_off), axis=1)

    stats = to_all(
        jnp.stack(
            [student_top, student_sum, teacher_top, teacher_sum, cross_sum, target_part]
        ),
        count,
    )
    tops, sums, teacher_tops, teacher_sums, crosses, targets = [stats[:, i] for i in range(6)]
    student_max, student_total, teacher_max, teacher_total, cross_total = merge_stats(
        tops, sums, teacher_tops, teacher_sums, crosses
    )
    student_log = jnp.log(student_total)
    teacher_log = jnp.log(teacher_total)
    student_lse = student_max + student_log
    teacher_lse = teacher_max + teacher_log
    divergence = cross_total / student_total - (student_log - teacher_log)
    target = jnp.sum(targets, axis=0)

    per_token = divergence + sample_weight * (student_lse - target)
    loss = jnp.reshape(jnp.sum(live_mask * per_token) / live_count, (1,))
    token_weight = live_mask * loss_scale[0] / live_count
    log_student = logits - student_lse[:, None]
    log_teacher = teacher - teacher_lse[:, None]
    student_prob = jnp.exp(log_student)
    grad_logits = (
        token_weight[:, None]
        * (
            student_prob * (log_student - log_teacher - divergence[:, None])
            + sample_weight * (student_prob - target_hit.astype(jnp.float32))
        )
    ).astype(jnp.bfloat16)
    terms = jnp.dot(grad_logits, head, preferred_element_type=jnp.float32).astype(jnp.bfloat16)
    terms = terms.reshape(tokens, count, own_features).transpose(1, 0, 2)
    shares = lax.all_to_all(terms, "vocab", split_axis=0, concat_axis=0, tiled=True)
    grad_hidden = jnp.sum(shares.astype(jnp.float32), axis=0)
    return (grad_hidden.astype(jnp.bfloat16), loss)


def any_shards(*arrays):
    hidden_states, head, teacher_values = arrays[:3]
    count = lax.axis_size("vocab")
    fits = (
        count % 2 == 0
        and hidden_states.shape[1] == 5 * LANES // 2
        and hidden_states.shape[0] % 32 == 0
        and head.shape[0] % LANES == LANES // 2
        and (head.shape[0] + LANES // 2) // LANES % 2 == 0
        and teacher_values.shape[0] == 4
    )
    return paired_shards(*arrays) if fits else shards(*arrays)


def solution(mesh):
    in_specs = (
        P("dom", "vocab"),
        P("vocab", None),
        P(("dom", "vocab"), None),
        P(("dom", "vocab"), None),
        P("dom"),
        P("dom"),
        P("dom"),
        P(),
    )
    out_specs = (P("dom", "vocab"), P("dom"))
    return jax.shard_map(
        any_shards, mesh=mesh, in_specs=in_specs, out_specs=out_specs, check_vma=False
    )
```

```python
import functools

import jax
import jax.numpy as jnp
from jax import lax
from jax.experimental import pallas as pl
from jax.experimental.pallas import tpu as pltpu
from jax.sharding import PartitionSpec as P

BLOCK = 32
LANES = 128
STATS = 8
AHEAD = 3
EARLY = 3


sample_weight = 0.5


def to_all(piece, count):
    copies = jnp.broadcast_to(piece[None], (count,) + piece.shape)
    return lax.all_to_all(copies, "vocab", split_axis=0, concat_axis=0, tiled=True)


def scaled_teacher(teacher_values, teacher_scales, count, shard_rows):
    slot_rows = teacher_values.shape[0]
    scaled = (
        teacher_values.astype(jnp.float32).reshape(slot_rows, -1, BLOCK) * teacher_scales[:, :, None]
    ).astype(jnp.bfloat16)
    return scaled.reshape(slot_rows, count, shard_rows).transpose(1, 0, 2)


def merge_stats(tops, sums, teacher_tops, teacher_sums, crosses):
    top = jnp.max(tops, axis=0)
    teacher_top = jnp.max(teacher_tops, axis=0)
    shift = tops - top[None]
    teacher_shift = teacher_tops - teacher_top[None]
    weight = jnp.exp(shift)
    total = jnp.sum(sums * weight, axis=0)
    teacher_total = jnp.sum(teacher_sums * jnp.exp(teacher_shift), axis=0)
    cross = jnp.sum(weight * (crosses + sums * (shift - teacher_shift)), axis=0)
    return top, total, teacher_top, teacher_total, cross


def swap_cores(array):
    count = lax.axis_size("vocab")
    return lax.ppermute(array, "vocab", [(i, i ^ 1) for i in range(count)])


def along_chips(array, step):
    count = lax.axis_size("vocab")
    return lax.ppermute(array, "vocab", [(i, (i + 2 * step) % count) for i in range(count)])


def vmem_array(shape, dtype):
    return pltpu.VMEM(shape, dtype)


def in_vmem(array):
    return pltpu.with_memory_space_constraint(array, pltpu.VMEM)


def in_hbm(array):
    return pltpu.with_memory_space_constraint(array, pltpu.HBM)


def hbm_array(shape, dtype):
    return pltpu.HBM(shape, dtype)


def low_lanes(shape):
    return lax.broadcasted_iota(jnp.int32, shape, len(shape) - 1) < LANES // 2


def low_rows(shape, count):
    return lax.broadcasted_iota(jnp.int32, shape, 0) < count


def turned(array):
    return pltpu.roll(array, LANES // 2, 1)


def folded(first, tile):
    rows = tile.shape[0] // 2
    upper, lower = tile[:rows], turned(tile[rows:])
    low = low_lanes(upper.shape)
    return jnp.where(first, jnp.where(low, upper, lower), jnp.where(low, lower, upper))


def tiles_of(array, count):
    return [array[:, LANES * i : LANES * (i + 1)] for i in range(count)]


def column_of(row):
    size = row.shape[1]
    down = lax.broadcasted_iota(jnp.int32, (size, size), 0)
    along = lax.broadcasted_iota(jnp.int32, (size, size), 1)
    return jnp.sum(jnp.where(down == along, row, jnp.zeros_like(row)), axis=1, keepdims=True)


def token_facts(ids, row_map, lengths, first_entry, slots):
    tokens = row_map.shape[1]
    token = lax.broadcasted_iota(jnp.int32, (tokens, tokens), 0)
    slot = lax.broadcasted_iota(jnp.int32, (tokens, tokens), 1)
    owner = (row_map == token).astype(jnp.float32)
    named = jnp.max(owner, axis=1, keepdims=True)
    owner = jnp.where((slot == 0) & (named == 0.0), 1.0, owner)
    rows = 2 * tokens
    slot = lax.broadcasted_iota(jnp.int32, (tokens, rows), 0)
    row = lax.broadcasted_iota(jnp.int32, (tokens, rows), 1)
    source, within = row // (2 * slots), row % (2 * slots)
    chosen = (slot == source * slots + within % slots).astype(jnp.bfloat16)
    owner = jnp.dot(owner.astype(jnp.bfloat16), chosen, preferred_element_type=jnp.float32)
    odd = within >= slots
    owner = jnp.concatenate([jnp.where(odd, 0.0, owner), jnp.where(odd, owner, 0.0)], axis=0)

    seqs = lengths.shape[1]
    seq_length = tokens // seqs
    position = lax.broadcasted_iota(jnp.int32, (tokens, 1), 0)
    live_until = jnp.zeros((tokens, 1), jnp.int32)
    for seq in range(seqs):
        inside = (position >= seq * seq_length) & (position < (seq + 1) * seq_length)
        until = lengths[:, seq : seq + 1] + seq * seq_length
        live_until = jnp.where(inside, until, live_until)
    live = (position < live_until).astype(jnp.float32)
    count = jnp.sum(live, axis=0, keepdims=True)
    entry = (column_of(ids) - first_entry).astype(jnp.float32)
    lane = lax.broadcasted_iota(jnp.int32, (tokens, LANES), 1)
    return owner.astype(jnp.bfloat16), jnp.where(lane == 0, entry, live / count)


def pack_kernel(place_ref, *refs, shard_rows):
    outside, refs = refs[:6], refs[6:]
    packed_ref, owner_ref, table_ref = refs[:3]
    inside, wide_ref, sems = refs[3:9], refs[9], refs[10]
    copies = [
        pltpu.make_async_copy(source, target, sems.at[i])
        for i, (source, target) in enumerate(zip(outside, inside))
    ]
    for copy in copies:
        copy.start()
    for copy in copies:
        copy.wait()
    hidden_ref, values_ref, scales_ref, ids_ref, map_ref, lengths_ref = inside
    owner_ref[...], table_ref[...] = token_facts(
        ids_ref[...], map_ref[...], lengths_ref[...], place_ref[0] * shard_rows, values_ref.shape[0]
    )
    chips = packed_ref.shape[0]
    tokens, half = hidden_ref.shape
    slots, entries = values_ref.shape
    pair = entries // chips
    shard = pair // 2
    blocks = pair // BLOCK
    scales = jnp.concatenate([scales_ref[...]] * 2, axis=0)
    stacked = jnp.concatenate(
        [scales[:, blocks * chip : blocks * (chip + 1)] for chip in range(chips)], axis=0
    )
    block = lax.broadcasted_iota(jnp.int32, (blocks, pair), 0)
    entry = lax.broadcasted_iota(jnp.int32, (blocks, pair), 1)
    inside = (entry >= block * BLOCK) & (entry < block * BLOCK + BLOCK)
    spread = jnp.dot(
        stacked.astype(jnp.bfloat16),
        inside.astype(jnp.bfloat16),
        preferred_element_type=jnp.float32,
    )
    values = values_ref[...].astype(jnp.float32)
    values = jnp.concatenate([values, values], axis=0)
    for chip in range(chips):
        wide_ref[:, pair * chip : pair * (chip + 1)] = (
            values[:, pair * chip : pair * (chip + 1)]
            * spread[2 * slots * chip : 2 * slots * (chip + 1)]
        )
    wide_ref[:, entries:] = jnp.zeros((2 * slots, LANES), jnp.float32)

    hidden = hidden_ref[...].astype(jnp.float32)
    zeros = jnp.zeros((tokens, LANES // 2), jnp.float32)
    tiles = tiles_of(jnp.concatenate([hidden, zeros], axis=1), 3)
    turns = [turned(tile) for tile in tiles]
    low = low_lanes(tiles[0].shape)
    first = place_ref[0] % 2 == 0
    hidden = jnp.concatenate(
        [
            jnp.where(first, tiles[0], jnp.where(low, turns[0], turns[1])),
            jnp.where(first, tiles[1], jnp.where(low, turns[1], turns[2])),
            folded(first, jnp.where(first, tiles[2], turns[0])),
        ],
        axis=0,
    ).astype(jnp.bfloat16)
    hidden_rows = hidden.shape[0]
    upper = low_rows((2 * slots, LANES), slots)
    low = low_lanes((2 * slots, LANES))
    tile_pairs = (shard + LANES // 2) // LANES // 2
    for chip in range(chips):
        rows = []
        for core in range(2):
            start = pair * chip + (shard - LANES // 2) * core
            tiles = [
                wide_ref[:, start + LANES * i : start + LANES * (i + 1)]
                for i in range(2 * tile_pairs + core)
            ]
            if core == 1:
                tiles = [turned(tile) for tile in tiles]
                tiles = [
                    jnp.where(low, tiles[i], tiles[i + 1]) for i in range(2 * tile_pairs)
                ]
            rows += [
                jnp.where(upper, tiles[2 * i], tiles[2 * i + 1]) for i in range(tile_pairs)
            ]
        step = lax.rem(chip - place_ref[0] // 2 + chips, chips)
        packed_ref[step, :hidden_rows] = hidden
        packed_ref[step, hidden_rows:] = jnp.concatenate(rows, axis=0).astype(jnp.bfloat16)


def head_copies(head_ref, held_ref, sems, chips):
    width = held_ref.shape[1] // len(chips)
    copies = []
    for step, chip in enumerate(chips):
        columns = pl.ds(pl.multiple_of(chip * width, LANES), width)
        copies.append(
            pltpu.make_async_copy(
                head_ref.at[:, columns],
                held_ref.at[:, width * step : width * (step + 1)],
                sems.at[step],
            )
        )
    return copies


def take(copies, step):
    copies[step].wait()
    if step + AHEAD < len(copies):
        copies[step + AHEAD].start()


def source_chips(place_ref, chips):
    return [lax.rem(place_ref[0] // 2 - step + chips, chips) for step in range(chips)]


def preload_kernel(place_ref, head_ref, _, early_ref, sems, *, chips):
    sources = source_chips(place_ref, chips)[:EARLY]
    copies = head_copies(head_ref, early_ref, sems, sources)
    for copy in copies:
        copy.start()
    for copy in copies:
        copy.wait()


def logits_kernel(place_ref, *refs, chips):
    near, far, refs = refs[:chips][::-1], refs[chips : chips + 2], refs[chips + 2 :]
    owner_ref, tokens_ref, early_ref, head_ref, rows_ref, stats_ref, own_ref = refs[:7]
    held_ref, made_ref, hidden_ref, arrived_ref, teacher_ref, sems, made_sem = refs[7:]
    core = place_ref[0] % 2
    sources = source_chips(place_ref, chips)
    copies = head_copies(head_ref, held_ref, sems, sources[EARLY:])
    for copy in copies[:AHEAD]:
        copy.start()
    tokens, width = hidden_ref.shape[0], hidden_ref.shape[1] // chips
    shard_rows = head_ref.shape[0]
    hidden_rows = 5 * tokens // 2
    slots = tokens // (2 * chips)
    low = low_lanes((tokens // 2, LANES))

    for step in range(chips):
        late = step > chips // 2
        group = far[0] if late else far[1]
        place = step - chips // 2 - 1 if late else step
        blocks = near[step], group.at[place]
        base = width * step
        for block, parity in zip(blocks, (core, 1 - core)):
            for i in range(2):
                column = base + LANES * i + (width - 2 * LANES) * parity
                lanes = pl.ds(pl.multiple_of(column, LANES), LANES)
                hidden_ref[:, lanes] = block[tokens * i : tokens * (i + 1)]
            teacher = block[hidden_rows:].astype(jnp.float32)
            share = teacher.shape[0] // 2
            teacher = jnp.where(core == 0, teacher[:share], teacher[share:])
            row = 2 * slots * (2 * sources[step] + parity)
            rows = pl.ds(pl.multiple_of(row, 2 * slots), 2 * slots)
            for i in range(share // (2 * slots)):
                arrived_ref[rows, LANES * i : LANES * (i + 1)] = teacher[
                    2 * slots * i : 2 * slots * (i + 1)
                ]
        own, other = [block[2 * tokens : hidden_rows].astype(jnp.float32) for block in blocks]
        one, two = jnp.where(core == 0, own, other), jnp.where(core == 0, other, own)
        tile = [jnp.where(low, one, two), turned(jnp.where(low, two, one))]
        tile = jnp.concatenate(tile, axis=0).astype(jnp.bfloat16)
        hidden_ref[:, base + 2 * LANES : base + 3 * LANES] = tile

    def product(step, columns):
        return lax.dot_general(
            hidden_ref[:, width * step : width * (step + 1)],
            columns,
            (((1,), (1,)), ((), ())),
            preferred_element_type=jnp.float32,
        )

    logits = product(0, early_ref[:, :width])
    for step in range(1, EARLY):
        logits += product(step, early_ref[:, width * step : width * (step + 1)])
    placed = jnp.dot(
        owner_ref[...], arrived_ref[...].astype(jnp.bfloat16), preferred_element_type=jnp.float32
    )
    pairs = arrived_ref.shape[1] // LANES
    even, odd = tiles_of(placed[:tokens], pairs), tiles_of(placed[tokens:], pairs)
    teacher = jnp.concatenate([tile for pair in zip(even, odd) for tile in pair], axis=1)
    teacher = teacher[:, :shard_rows]
    teacher_top = jnp.max(teacher, axis=1, keepdims=True)
    teacher_off = teacher - teacher_top
    teacher_total = jnp.sum(jnp.exp(teacher_off), axis=1, keepdims=True)
    teacher_ref[...] = teacher_off
    for step in range(len(copies)):
        take(copies, step)
        columns = held_ref[:, width * step : width * (step + 1)]
        logits += product(EARLY + step, columns)

    top = jnp.max(logits, axis=1, keepdims=True)
    off = logits - top
    exps = jnp.exp(off)
    total = jnp.sum(exps, axis=1, keepdims=True)
    gap = off - teacher_ref[...]
    cross = jnp.sum(exps * gap, axis=1, keepdims=True)
    centre = cross / total
    entry = lax.broadcasted_iota(jnp.int32, (tokens, shard_rows), 1)
    hit = entry == tokens_ref[:, :1].astype(jnp.int32)
    target = jnp.sum(jnp.where(hit, logits, 0.0), axis=1, keepdims=True)
    made_ref[:tokens] = (exps * (gap - centre)).astype(jnp.bfloat16)
    made_ref[tokens : 2 * tokens] = exps.astype(jnp.bfloat16)
    made_ref[2 * tokens :] = hit.astype(jnp.bfloat16)
    out = pltpu.make_async_copy(made_ref, rows_ref, made_sem)
    out.start()

    lane = lax.broadcasted_iota(jnp.int32, (tokens, LANES), 1)
    table = jnp.zeros((tokens, LANES), jnp.float32)
    for place, column in enumerate(
        (top, total, teacher_top, teacher_total, cross, target, centre)
    ):
        table = jnp.where(lane == place, column, table)
    stats = jnp.concatenate([table, jnp.zeros((stats_ref.shape[2] - tokens, LANES), jnp.float32)])
    stats = stats.T[:STATS]
    own_ref[...] = stats
    stats_ref[...] = jnp.broadcast_to(stats[None], stats_ref.shape)
    out.wait()


def products_kernel(
    place_ref, rows_ref, head_ref, terms_ref, picks_ref, held_ref, made_ref, sems, made_sem
):
    into = pltpu.make_async_copy(rows_ref, made_ref, made_sem)
    into.start()
    chips = terms_ref.shape[0]
    targets = [lax.rem(place_ref[0] // 2 + step, chips) for step in range(chips)]
    copies = head_copies(head_ref, held_ref, sems, targets)
    for copy in copies[:AHEAD]:
        copy.start()
    into.wait()
    tokens = made_ref.shape[0] // 3
    width = held_ref.shape[1] // chips
    for step in range(chips):
        take(copies, step)
        products = jnp.dot(
            made_ref[...],
            held_ref[:, width * step : width * (step + 1)],
            preferred_element_type=jnp.float32,
        )
        for i, tile in enumerate(tiles_of(products, width // LANES)):
            terms_ref[step, i, 0] = tile[:tokens]
            terms_ref[step, i, 1] = tile[tokens : 2 * tokens]
            picks_ref[step, i] = tile[2 * tokens :].astype(jnp.bfloat16)


def put_shares(parity, factors_ref, terms_ref, picks_ref, out_ref):
    tokens = terms_ref.shape[3]
    factor, level, weight = [factors_ref[i] for i in range(3)]
    for step in range(terms_ref.shape[0]):
        for i, tile in enumerate((3 * parity, 3 * parity + 1, 2)):
            sums = terms_ref[step, tile, 0] + level * terms_ref[step, tile, 1]
            share = factor * sums - weight * picks_ref[step, tile].astype(jnp.float32)
            if i == 2:
                share = folded(parity == 0, share)
            out_ref[step, tokens * i : tokens * i + share.shape[0]] = share.astype(out_ref.dtype)


def give_kernel(
    place_ref,
    scale_ref,
    stats_ref,
    own_ref,
    tokens_ref,
    terms_ref,
    picks_ref,
    give_ref,
    factors_ref,
    loss_ref,
):
    tokens = tokens_ref.shape[0]
    tops, sums, teacher_tops, teacher_sums, crosses, targets = [
        stats_ref[:, i, :tokens] for i in range(6)
    ]
    top, total, teacher_top, teacher_total, cross = [
        part[None] for part in merge_stats(tops, sums, teacher_tops, teacher_sums, crosses)
    ]
    target = jnp.sum(targets, axis=0, keepdims=True)
    student_log = jnp.log(total)
    teacher_log = jnp.log(teacher_total)
    divergence = cross / total - (student_log - teacher_log)
    student_lse = top + student_log
    per_token = divergence + sample_weight * (student_lse - target)
    student_shift = own_ref[0:1, :tokens] - top - student_log
    teacher_shift = own_ref[2:3, :tokens] - teacher_top - teacher_log
    factor = jnp.exp(student_shift)
    level = (
        own_ref[6:7, :tokens] + student_shift - teacher_shift - divergence + sample_weight
    )
    zeros = jnp.zeros((LANES - 3, tokens), jnp.float32)
    columns = jnp.concatenate([factor, level, per_token, zeros], axis=0).T
    share = tokens_ref[:, 1:2]
    weight = share * scale_ref[0]
    loss_ref[...] = jnp.sum(share * columns[:, 2:3], axis=0, keepdims=True)
    for i, column in enumerate(
        (weight * columns[:, 0:1], columns[:, 1:2], sample_weight * weight)
    ):
        factors_ref[i] = jnp.broadcast_to(column, (tokens, LANES))
    put_shares(1 - place_ref[0] % 2, factors_ref, terms_ref, picks_ref, give_ref)


def keep_kernel(place_ref, factors_ref, found_ref, terms_ref, picks_ref, keep_ref, loss_ref):
    loss_ref[...] = found_ref[...]
    put_shares(place_ref[0] % 2, factors_ref, terms_ref, picks_ref, keep_ref)


def sum_kernel(place_ref, own_ref, *refs):
    tokens, half = refs[-1].shape
    total = own_ref[...]
    for share_ref in refs[:-1]:
        total += share_ref[...].astype(jnp.float32)
    one, two, rest = total[:tokens], total[tokens : 2 * tokens], total[2 * tokens :]
    rest = jnp.concatenate([rest, turned(rest)], axis=0)
    turns = [turned(tile) for tile in (rest, one, two)]
    low = low_lanes(one.shape)
    first = place_ref[0] % 2 == 0
    tiles = [
        jnp.where(first, one, jnp.where(low, turns[0], turns[1])),
        jnp.where(first, two, jnp.where(low, turns[1], turns[2])),
        jnp.where(first, rest, turns[2]),
    ]
    total = jnp.concatenate(tiles, axis=1)[:, :half]
    refs[-1][...] = total.astype(refs[-1].dtype)


def paired_shards(
    hidden_states, head, teacher_values, teacher_scales, token_ids, lengths, row_map, loss_scale
):
    count = lax.axis_size("vocab")
    own_index = lax.axis_index("vocab")
    chips = count // 2
    tokens, half = hidden_states.shape
    width = 2 * half
    shard_rows = head.shape[0]
    place = jnp.reshape(own_index, (1,))
    vmem = pl.BlockSpec(memory_space=pltpu.VMEM)
    smem = pl.BlockSpec(memory_space=pltpu.SMEM)
    hbm = pl.BlockSpec(memory_space=pl.ANY)
    params = pltpu.CompilerParams(vmem_limit_bytes=VMEM_LIMIT)
    head = in_hbm(head)
    head_scratch = pltpu.VMEM((shard_rows, chips * width), head.dtype)
    head_sems = pltpu.SemaphoreType.DMA((chips,))
    rows_scratch = pltpu.VMEM((3 * tokens, shard_rows), jnp.bfloat16)
    rows_sem = pltpu.SemaphoreType.DMA
    slots, entries = teacher_values.shape
    hidden_rows = 5 * tokens // 2
    teacher_rows = 2 * slots * (shard_rows + LANES // 2) // LANES

    operands = (
        hidden_states,
        teacher_values,
        teacher_scales,
        token_ids[None, :],
        row_map[None, :],
        lengths[None, :],
    )
    packed, owner, table = pl.pallas_call(
        functools.partial(pack_kernel, shard_rows=shard_rows),
        out_shape=(
            vmem_array((chips, hidden_rows + teacher_rows, LANES), jnp.bfloat16),
            vmem_array((2 * tokens, 2 * tokens), jnp.bfloat16),
            vmem_array((tokens, LANES), jnp.float32),
        ),
        in_specs=[smem] + [hbm] * len(operands),
        out_specs=[vmem] * 3,
        scratch_shapes=[pltpu.VMEM(operand.shape, operand.dtype) for operand in operands]
        + [
            pltpu.VMEM((2 * slots, entries + LANES), jnp.float32),
            pltpu.SemaphoreType.DMA((len(operands),)),
        ],
        compiler_params=params,
        name="pack",
    )(place, *[in_hbm(operand) for operand in operands])
    steps = range(1, chips)
    near = [packed[0]] + [along_chips(packed[step], step) for step in steps]
    first, last = jnp.stack(near[: chips // 2 + 1]), jnp.stack(near[chips // 2 + 1 :])
    early = pl.pallas_call(
        functools.partial(preload_kernel, chips=chips),
        out_shape=vmem_array((shard_rows, EARLY * width), head.dtype),
        in_specs=[smem] + [hbm] * 2,
        out_specs=vmem,
        scratch_shapes=[pltpu.SemaphoreType.DMA((EARLY,))],
        compiler_params=params,
        cost_estimate=pl.CostEstimate(
            flops=0, bytes_accessed=4 * EARLY * shard_rows * width, transcendentals=0
        ),
        name="preload",
    )(place, head, near[3])
    last, early = lax.optimization_barrier((last, early))
    far = [swap_cores(last), swap_cores(first)]

    rows, stats, own_stats = pl.pallas_call(
        functools.partial(logits_kernel, chips=chips),
        out_shape=(
            hbm_array((3 * tokens, shard_rows), jnp.bfloat16),
            jax.ShapeDtypeStruct((count, STATS, pl.cdiv(tokens, LANES) * LANES), jnp.float32),
            vmem_array((STATS, pl.cdiv(tokens, LANES) * LANES), jnp.float32),
        ),
        in_specs=[smem] + [vmem] * (chips + 5) + [hbm],
        out_specs=[hbm, vmem, vmem],
        scratch_shapes=[
            pltpu.VMEM((shard_rows, (chips - EARLY) * width), head.dtype),
            rows_scratch,
            pltpu.VMEM((tokens, chips * width), jnp.bfloat16),
            pltpu.VMEM((2 * tokens, (shard_rows + LANES // 2) // 2), jnp.float32),
            pltpu.VMEM((tokens, shard_rows), jnp.float32),
            pltpu.SemaphoreType.DMA((chips - EARLY,)),
            rows_sem,
        ],
        compiler_params=params,
        cost_estimate=pl.CostEstimate(
            flops=2 * tokens * head.size, bytes_accessed=2 * head.size, transcendentals=0
        ),
        name="logits",
    )(place, *[in_vmem(block) for block in near[::-1] + far], in_vmem(owner), in_vmem(table), in_vmem(early), head)

    all_stats = lax.all_to_all(stats, "vocab", split_axis=0, concat_axis=0, tiled=True)

    terms, picks = pl.pallas_call(
        products_kernel,
        out_shape=(
            vmem_array((chips, width // LANES, 2, tokens, LANES), jnp.float32),
            vmem_array((chips, width // LANES, tokens, LANES), jnp.bfloat16),
        ),
        in_specs=[smem, hbm, hbm],
        out_specs=[vmem] * 2,
        scratch_shapes=[head_scratch, rows_scratch, head_sems, rows_sem],
        compiler_params=params,
        cost_estimate=pl.CostEstimate(
            flops=6 * tokens * head.size, bytes_accessed=2 * head.size, transcendentals=0
        ),
        name="products",
    )(place, in_hbm(rows), head)

    terms, picks = in_vmem(terms), in_vmem(picks)
    give, factors, loss = pl.pallas_call(
        give_kernel,
        out_shape=(
            vmem_array((chips, hidden_rows, LANES), jnp.bfloat16),
            vmem_array((3, tokens, LANES), jnp.float32),
            vmem_array((1, 1), jnp.float32),
        ),
        in_specs=[smem] * 2 + [vmem] * 5,
        out_specs=[vmem] * 3,
        compiler_params=params,
        name="give",
    )(place, loss_scale, in_vmem(all_stats), in_vmem(own_stats), in_vmem(table), terms, picks)
    taken = swap_cores(give)
    keep, loss = pl.pallas_call(
        keep_kernel,
        out_shape=(
            vmem_array((chips, hidden_rows, LANES), jnp.float32),
            jax.ShapeDtypeStruct((1, 1), jnp.float32),
        ),
        in_specs=[smem] + [vmem] * 4,
        out_specs=[vmem] * 2,
        compiler_params=params,
        cost_estimate=pl.CostEstimate(
            flops=4 * terms.size, bytes_accessed=4 * terms.size, transcendentals=0
        ),
        name="keep",
    )(place, in_vmem(factors), in_vmem(loss), terms, picks)
    sums = keep + taken.astype(jnp.float32)
    shares = [along_chips(sums[step].astype(jnp.bfloat16), step) for step in steps]
    total = pl.pallas_call(
        sum_kernel,
        out_shape=jax.ShapeDtypeStruct((tokens, half), jnp.bfloat16),
        in_specs=[smem] + [vmem] * chips,
        out_specs=vmem,
        compiler_params=params,
        name="total",
    )(place, *[in_vmem(share) for share in [sums[0]] + shares])
    return total, jnp.reshape(loss, (1,))


VMEM_LIMIT = 24 * 1024 * 1024


def shards(
    hidden_states, head, teacher_values, teacher_scales, token_ids, lengths, row_map, loss_scale
):
    count = lax.axis_size("vocab")
    own_index = lax.axis_index("vocab")
    tokens = hidden_states.shape[0]
    own_features = hidden_states.shape[1]
    shard_rows = head.shape[0]
    seq_length = tokens // lengths.shape[0]
    contract_last = (((1,), (1,)), ((), ()))

    scaled = scaled_teacher(teacher_values, teacher_scales, count, shard_rows)
    arrived = lax.all_to_all(scaled, "vocab", split_axis=0, concat_axis=0, tiled=True)
    arrived = arrived.reshape(tokens, shard_rows)
    gathered = to_all(hidden_states, count).transpose(1, 0, 2).reshape(tokens, -1)
    logits = lax.dot_general(gathered, head, contract_last, preferred_element_type=jnp.float32)

    positions = jnp.arange(tokens, dtype=jnp.int32)
    owner = row_map[None, :] == positions[:, None]
    slot_of = jnp.sum(jnp.where(owner, positions[None, :], 0), axis=1)
    teacher = jnp.take(arrived, slot_of, axis=0).astype(jnp.float32)

    seq_ids = jnp.arange(lengths.shape[0], dtype=jnp.int32)
    own_length = jnp.sum(
        jnp.where((positions // seq_length)[:, None] == seq_ids[None, :], lengths[None, :], 0),
        axis=1,
    )
    live_mask = (positions % seq_length < own_length).astype(jnp.float32)
    live_count = jnp.sum(live_mask)

    local_ids = token_ids - own_index * shard_rows
    target_hit = local_ids[:, None] == jnp.arange(shard_rows, dtype=jnp.int32)[None, :]
    target_part = jnp.sum(jnp.where(target_hit, logits, 0.0), axis=1)
    student_top = jnp.max(logits, axis=1)
    teacher_top = jnp.max(teacher, axis=1)
    student_off = logits - student_top[:, None]
    teacher_off = teacher - teacher_top[:, None]
    student_exp = jnp.exp(student_off)
    student_sum = jnp.sum(student_exp, axis=1)
    teacher_sum = jnp.sum(jnp.exp(teacher_off), axis=1)
    cross_sum = jnp.sum(student_exp * (student_off - teacher_off), axis=1)

    stats = to_all(
        jnp.stack(
            [student_top, student_sum, teacher_top, teacher_sum, cross_sum, target_part]
        ),
        count,
    )
    tops, sums, teacher_tops, teacher_sums, crosses, targets = [stats[:, i] for i in range(6)]
    student_max, student_total, teacher_max, teacher_total, cross_total = merge_stats(
        tops, sums, teacher_tops, teacher_sums, crosses
    )
    student_log = jnp.log(student_total)
    teacher_log = jnp.log(teacher_total)
    student_lse = student_max + student_log
    teacher_lse = teacher_max + teacher_log
    divergence = cross_total / student_total - (student_log - teacher_log)
    target = jnp.sum(targets, axis=0)

    per_token = divergence + sample_weight * (student_lse - target)
    loss = jnp.reshape(jnp.sum(live_mask * per_token) / live_count, (1,))
    token_weight = live_mask * loss_scale[0] / live_count
    log_student = logits - student_lse[:, None]
    log_teacher = teacher - teacher_lse[:, None]
    student_prob = jnp.exp(log_student)
    grad_logits = (
        token_weight[:, None]
        * (
            student_prob * (log_student - log_teacher - divergence[:, None])
            + sample_weight * (student_prob - target_hit.astype(jnp.float32))
        )
    ).astype(jnp.bfloat16)
    terms = jnp.dot(grad_logits, head, preferred_element_type=jnp.float32).astype(jnp.bfloat16)
    terms = terms.reshape(tokens, count, own_features).transpose(1, 0, 2)
    shares = lax.all_to_all(terms, "vocab", split_axis=0, concat_axis=0, tiled=True)
    grad_hidden = jnp.sum(shares.astype(jnp.float32), axis=0)
    return (grad_hidden.astype(jnp.bfloat16), loss)


def any_shards(*arrays):
    hidden_states, head, teacher_values = arrays[:3]
    count = lax.axis_size("vocab")
    fits = (
        count % 2 == 0
        and hidden_states.shape[1] == 5 * LANES // 2
        and hidden_states.shape[0] % 32 == 0
        and head.shape[0] % LANES == LANES // 2
        and (head.shape[0] + LANES // 2) // LANES % 2 == 0
        and teacher_values.shape[0] == 4
    )
    return paired_shards(*arrays) if fits else shards(*arrays)


def solution(mesh):
    in_specs = (
        P("dom", "vocab"),
        P("vocab", None),
        P(("dom", "vocab"), None),
        P(("dom", "vocab"), None),
        P("dom"),
        P("dom"),
        P("dom"),
        P(),
    )
    out_specs = (P("dom", "vocab"), P("dom"))
    return jax.shard_map(
        any_shards, mesh=mesh, in_specs=in_specs, out_specs=out_specs, check_vma=False
    )
```

```python
import functools

import jax
import jax.numpy as jnp
from jax import lax
from jax.experimental import pallas as pl
from jax.experimental.pallas import tpu as pltpu
from jax.sharding import PartitionSpec as P

BLOCK = 32
LANES = 128
STATS = 8
AHEAD = 3
EARLY = 3


sample_weight = 0.5


def to_all(piece, count):
    copies = jnp.broadcast_to(piece[None], (count,) + piece.shape)
    return lax.all_to_all(copies, "vocab", split_axis=0, concat_axis=0, tiled=True)


def scaled_teacher(teacher_values, teacher_scales, count, shard_rows):
    slot_rows = teacher_values.shape[0]
    scaled = (
        teacher_values.astype(jnp.float32).reshape(slot_rows, -1, BLOCK) * teacher_scales[:, :, None]
    ).astype(jnp.bfloat16)
    return scaled.reshape(slot_rows, count, shard_rows).transpose(1, 0, 2)


def merge_stats(tops, sums, teacher_tops, teacher_sums, crosses):
    top = jnp.max(tops, axis=0)
    teacher_top = jnp.max(teacher_tops, axis=0)
    shift = tops - top[None]
    teacher_shift = teacher_tops - teacher_top[None]
    weight = jnp.exp(shift)
    total = jnp.sum(sums * weight, axis=0)
    teacher_total = jnp.sum(teacher_sums * jnp.exp(teacher_shift), axis=0)
    cross = jnp.sum(weight * (crosses + sums * (shift - teacher_shift)), axis=0)
    return top, total, teacher_top, teacher_total, cross


def swap_cores(array):
    count = lax.axis_size("vocab")
    return lax.ppermute(array, "vocab", [(i, i ^ 1) for i in range(count)])


def along_chips(array, step):
    count = lax.axis_size("vocab")
    return lax.ppermute(array, "vocab", [(i, (i + 2 * step) % count) for i in range(count)])


def vmem_array(shape, dtype):
    return pltpu.VMEM(shape, dtype)


def in_vmem(array):
    return pltpu.with_memory_space_constraint(array, pltpu.VMEM)


def in_hbm(array):
    return pltpu.with_memory_space_constraint(array, pltpu.HBM)


def hbm_array(shape, dtype):
    return pltpu.HBM(shape, dtype)


def low_lanes(shape):
    return lax.broadcasted_iota(jnp.int32, shape, len(shape) - 1) < LANES // 2


def low_rows(shape, count):
    return lax.broadcasted_iota(jnp.int32, shape, 0) < count


def turned(array):
    return pltpu.roll(array, LANES // 2, 1)


def folded(first, tile):
    rows = tile.shape[0] // 2
    upper, lower = tile[:rows], turned(tile[rows:])
    low = low_lanes(upper.shape)
    return jnp.where(first, jnp.where(low, upper, lower), jnp.where(low, lower, upper))


def tiles_of(array, count):
    return [array[:, LANES * i : LANES * (i + 1)] for i in range(count)]


def column_of(row):
    size = row.shape[1]
    down = lax.broadcasted_iota(jnp.int32, (size, size), 0)
    along = lax.broadcasted_iota(jnp.int32, (size, size), 1)
    return jnp.sum(jnp.where(down == along, row, jnp.zeros_like(row)), axis=1, keepdims=True)


def token_facts(ids, row_map, lengths, first_entry, slots):
    tokens = row_map.shape[1]
    token = lax.broadcasted_iota(jnp.int32, (tokens, tokens), 0)
    slot = lax.broadcasted_iota(jnp.int32, (tokens, tokens), 1)
    owner = (row_map == token).astype(jnp.float32)
    named = jnp.max(owner, axis=1, keepdims=True)
    owner = jnp.where((slot == 0) & (named == 0.0), 1.0, owner)
    rows = 2 * tokens
    slot = lax.broadcasted_iota(jnp.int32, (tokens, rows), 0)
    row = lax.broadcasted_iota(jnp.int32, (tokens, rows), 1)
    source, within = row // (2 * slots), row % (2 * slots)
    chosen = (slot == source * slots + within % slots).astype(jnp.bfloat16)
    owner = jnp.dot(owner.astype(jnp.bfloat16), chosen, preferred_element_type=jnp.float32)
    odd = within >= slots
    owner = jnp.concatenate([jnp.where(odd, 0.0, owner), jnp.where(odd, owner, 0.0)], axis=0)

    seqs = lengths.shape[1]
    seq_length = tokens // seqs
    position = lax.broadcasted_iota(jnp.int32, (tokens, 1), 0)
    live_until = jnp.zeros((tokens, 1), jnp.int32)
    for seq in range(seqs):
        inside = (position >= seq * seq_length) & (position < (seq + 1) * seq_length)
        until = lengths[:, seq : seq + 1] + seq * seq_length
        live_until = jnp.where(inside, until, live_until)
    live = (position < live_until).astype(jnp.float32)
    count = jnp.sum(live, axis=0, keepdims=True)
    entry = (column_of(ids) - first_entry).astype(jnp.float32)
    lane = lax.broadcasted_iota(jnp.int32, (tokens, LANES), 1)
    return owner.astype(jnp.bfloat16), jnp.where(lane == 0, entry, live / count)


def pack_kernel(place_ref, *refs, shard_rows):
    outside, refs = refs[:6], refs[6:]
    packed_ref, owner_ref, table_ref = refs[:3]
    inside, wide_ref, sems = refs[3:9], refs[9], refs[10]
    copies = [
        pltpu.make_async_copy(source, target, sems.at[i])
        for i, (source, target) in enumerate(zip(outside, inside))
    ]
    for copy in copies:
        copy.start()
    for copy in copies:
        copy.wait()
    hidden_ref, values_ref, scales_ref, ids_ref, map_ref, lengths_ref = inside
    owner_ref[...], table_ref[...] = token_facts(
        ids_ref[...], map_ref[...], lengths_ref[...], place_ref[0] * shard_rows, values_ref.shape[0]
    )
    chips = packed_ref.shape[0]
    tokens, half = hidden_ref.shape
    slots, entries = values_ref.shape
    pair = entries // chips
    shard = pair // 2
    blocks = pair // BLOCK
    scales = jnp.concatenate([scales_ref[...]] * 2, axis=0)
    stacked = jnp.concatenate(
        [scales[:, blocks * chip : blocks * (chip + 1)] for chip in range(chips)], axis=0
    )
    block = lax.broadcasted_iota(jnp.int32, (blocks, pair), 0)
    entry = lax.broadcasted_iota(jnp.int32, (blocks, pair), 1)
    inside = (entry >= block * BLOCK) & (entry < block * BLOCK + BLOCK)
    spread = jnp.dot(
        stacked.astype(jnp.bfloat16),
        inside.astype(jnp.bfloat16),
        preferred_element_type=jnp.float32,
    )
    values = values_ref[...].astype(jnp.float32)
    values = jnp.concatenate([values, values], axis=0)
    for chip in range(chips):
        wide_ref[:, pair * chip : pair * (chip + 1)] = (
            values[:, pair * chip : pair * (chip + 1)]
            * spread[2 * slots * chip : 2 * slots * (chip + 1)]
        )
    wide_ref[:, entries:] = jnp.zeros((2 * slots, LANES), jnp.float32)

    hidden = hidden_ref[...].astype(jnp.float32)
    zeros = jnp.zeros((tokens, LANES // 2), jnp.float32)
    tiles = tiles_of(jnp.concatenate([hidden, zeros], axis=1), 3)
    turns = [turned(tile) for tile in tiles]
    low = low_lanes(tiles[0].shape)
    first = place_ref[0] % 2 == 0
    hidden = jnp.concatenate(
        [
            jnp.where(first, tiles[0], jnp.where(low, turns[0], turns[1])),
            jnp.where(first, tiles[1], jnp.where(low, turns[1], turns[2])),
            folded(first, jnp.where(first, tiles[2], turns[0])),
        ],
        axis=0,
    ).astype(jnp.bfloat16)
    hidden_rows = hidden.shape[0]
    upper = low_rows((2 * slots, LANES), slots)
    low = low_lanes((2 * slots, LANES))
    tile_pairs = (shard + LANES // 2) // LANES // 2
    for chip in range(chips):
        rows = []
        for core in range(2):
            start = pair * chip + (shard - LANES // 2) * core
            tiles = [
                wide_ref[:, start + LANES * i : start + LANES * (i + 1)]
                for i in range(2 * tile_pairs + core)
            ]
            if core == 1:
                tiles = [turned(tile) for tile in tiles]
                tiles = [
                    jnp.where(low, tiles[i], tiles[i + 1]) for i in range(2 * tile_pairs)
                ]
            rows += [
                jnp.where(upper, tiles[2 * i], tiles[2 * i + 1]) for i in range(tile_pairs)
            ]
        step = lax.rem(chip - place_ref[0] // 2 + chips, chips)
        packed_ref[step, :hidden_rows] = hidden
        packed_ref[step, hidden_rows:] = jnp.concatenate(rows, axis=0).astype(jnp.bfloat16)


def head_copies(head_ref, held_ref, sems, chips):
    width = held_ref.shape[1] // len(chips)
    copies = []
    for step, chip in enumerate(chips):
        columns = pl.ds(pl.multiple_of(chip * width, LANES), width)
        copies.append(
            pltpu.make_async_copy(
                head_ref.at[:, columns],
                held_ref.at[:, width * step : width * (step + 1)],
                sems.at[step],
            )
        )
    return copies


def take(copies, step):
    copies[step].wait()
    if step + AHEAD < len(copies):
        copies[step + AHEAD].start()


def source_chips(place_ref, chips):
    return [lax.rem(place_ref[0] // 2 - step + chips, chips) for step in range(chips)]


def preload_kernel(place_ref, head_ref, _, early_ref, sems, *, chips):
    sources = source_chips(place_ref, chips)[:EARLY]
    copies = head_copies(head_ref, early_ref, sems, sources)
    for copy in copies:
        copy.start()
    for copy in copies:
        copy.wait()


def logits_kernel(place_ref, *refs, chips):
    near, far, refs = refs[:chips][::-1], refs[chips : chips + 2], refs[chips + 2 :]
    owner_ref, tokens_ref, early_ref, head_ref, rows_ref, stats_ref, own_ref = refs[:7]
    held_ref, made_ref, hidden_ref, arrived_ref, teacher_ref, sems, made_sem = refs[7:]
    core = place_ref[0] % 2
    sources = source_chips(place_ref, chips)
    copies = head_copies(head_ref, held_ref, sems, sources[EARLY:])
    for copy in copies[:AHEAD]:
        copy.start()
    tokens, width = hidden_ref.shape[0], hidden_ref.shape[1] // chips
    shard_rows = head_ref.shape[0]
    hidden_rows = 5 * tokens // 2
    slots = tokens // (2 * chips)
    low = low_lanes((tokens // 2, LANES))

    for step in range(chips):
        late = step > chips // 2
        group = far[0] if late else far[1]
        place = step - chips // 2 - 1 if late else step
        blocks = near[step], group.at[place]
        base = width * step
        for block, parity in zip(blocks, (core, 1 - core)):
            for i in range(2):
                column = base + LANES * i + (width - 2 * LANES) * parity
                lanes = pl.ds(pl.multiple_of(column, LANES), LANES)
                hidden_ref[:, lanes] = block[tokens * i : tokens * (i + 1)]
            teacher = block[hidden_rows:].astype(jnp.float32)
            share = teacher.shape[0] // 2
            teacher = jnp.where(core == 0, teacher[:share], teacher[share:])
            row = 2 * slots * (2 * sources[step] + parity)
            rows = pl.ds(pl.multiple_of(row, 2 * slots), 2 * slots)
            for i in range(share // (2 * slots)):
                arrived_ref[rows, LANES * i : LANES * (i + 1)] = teacher[
                    2 * slots * i : 2 * slots * (i + 1)
                ]
        own, other = [block[2 * tokens : hidden_rows].astype(jnp.float32) for block in blocks]
        one, two = jnp.where(core == 0, own, other), jnp.where(core == 0, other, own)
        tile = [jnp.where(low, one, two), turned(jnp.where(low, two, one))]
        tile = jnp.concatenate(tile, axis=0).astype(jnp.bfloat16)
        hidden_ref[:, base + 2 * LANES : base + 3 * LANES] = tile

    def product(step, columns):
        return lax.dot_general(
            hidden_ref[:, width * step : width * (step + 1)],
            columns,
            (((1,), (1,)), ((), ())),
            preferred_element_type=jnp.float32,
        )

    logits = product(0, early_ref[:, :width])
    for step in range(1, EARLY):
        logits += product(step, early_ref[:, width * step : width * (step + 1)])
    placed = jnp.dot(
        owner_ref[...], arrived_ref[...].astype(jnp.bfloat16), preferred_element_type=jnp.float32
    )
    pairs = arrived_ref.shape[1] // LANES
    even, odd = tiles_of(placed[:tokens], pairs), tiles_of(placed[tokens:], pairs)
    teacher = jnp.concatenate([tile for pair in zip(even, odd) for tile in pair], axis=1)
    teacher = teacher[:, :shard_rows]
    teacher_top = jnp.max(teacher, axis=1, keepdims=True)
    teacher_off = teacher - teacher_top
    teacher_total = jnp.sum(jnp.exp(teacher_off), axis=1, keepdims=True)
    teacher_ref[...] = teacher_off
    for group in (range(AHEAD), range(AHEAD, len(copies))):
        for step in group:
            take(copies, step)
        for step in group:
            columns = held_ref[:, width * step : width * (step + 1)]
            logits += product(EARLY + step, columns)

    top = jnp.max(logits, axis=1, keepdims=True)
    off = logits - top
    exps = jnp.exp(off)
    total = jnp.sum(exps, axis=1, keepdims=True)
    gap = off - teacher_ref[...]
    cross = jnp.sum(exps * gap, axis=1, keepdims=True)
    centre = cross / total
    entry = lax.broadcasted_iota(jnp.int32, (tokens, shard_rows), 1)
    hit = entry == tokens_ref[:, :1].astype(jnp.int32)
    target = jnp.sum(jnp.where(hit, logits, 0.0), axis=1, keepdims=True)
    made_ref[:tokens] = (exps * (gap - centre)).astype(jnp.bfloat16)
    made_ref[tokens : 2 * tokens] = exps.astype(jnp.bfloat16)
    made_ref[2 * tokens :] = hit.astype(jnp.bfloat16)
    out = pltpu.make_async_copy(made_ref, rows_ref, made_sem)
    out.start()

    lane = lax.broadcasted_iota(jnp.int32, (tokens, LANES), 1)
    table = jnp.zeros((tokens, LANES), jnp.float32)
    for place, column in enumerate(
        (top, total, teacher_top, teacher_total, cross, target, centre)
    ):
        table = jnp.where(lane == place, column, table)
    stats = jnp.concatenate([table, jnp.zeros((stats_ref.shape[2] - tokens, LANES), jnp.float32)])
    stats = stats.T[:STATS]
    own_ref[...] = stats
    stats_ref[...] = jnp.broadcast_to(stats[None], stats_ref.shape)
    out.wait()


def products_kernel(
    place_ref, rows_ref, head_ref, terms_ref, picks_ref, held_ref, made_ref, sems, made_sem
):
    into = pltpu.make_async_copy(rows_ref, made_ref, made_sem)
    into.start()
    chips = terms_ref.shape[0]
    targets = [lax.rem(place_ref[0] // 2 + step, chips) for step in range(chips)]
    copies = head_copies(head_ref, held_ref, sems, targets)
    for copy in copies[:AHEAD]:
        copy.start()
    into.wait()
    tokens = made_ref.shape[0] // 3
    width = held_ref.shape[1] // chips
    for step in range(chips):
        take(copies, step)
        products = jnp.dot(
            made_ref[...],
            held_ref[:, width * step : width * (step + 1)],
            preferred_element_type=jnp.float32,
        )
        for i, tile in enumerate(tiles_of(products, width // LANES)):
            terms_ref[step, i, 0] = tile[:tokens]
            terms_ref[step, i, 1] = tile[tokens : 2 * tokens]
            picks_ref[step, i] = tile[2 * tokens :].astype(jnp.bfloat16)


def put_shares(parity, factors_ref, terms_ref, picks_ref, out_ref):
    tokens = terms_ref.shape[3]
    factor, level, weight = [factors_ref[i] for i in range(3)]
    for step in range(terms_ref.shape[0]):
        for i, tile in enumerate((3 * parity, 3 * parity + 1, 2)):
            sums = terms_ref[step, tile, 0] + level * terms_ref[step, tile, 1]
            share = factor * sums - weight * picks_ref[step, tile].astype(jnp.float32)
            if i == 2:
                share = folded(parity == 0, share)
            out_ref[step, tokens * i : tokens * i + share.shape[0]] = share.astype(out_ref.dtype)


def give_kernel(
    place_ref,
    scale_ref,
    stats_ref,
    own_ref,
    tokens_ref,
    terms_ref,
    picks_ref,
    give_ref,
    factors_ref,
    loss_ref,
):
    tokens = tokens_ref.shape[0]
    tops, sums, teacher_tops, teacher_sums, crosses, targets = [
        stats_ref[:, i, :tokens] for i in range(6)
    ]
    top, total, teacher_top, teacher_total, cross = [
        part[None] for part in merge_stats(tops, sums, teacher_tops, teacher_sums, crosses)
    ]
    target = jnp.sum(targets, axis=0, keepdims=True)
    student_log = jnp.log(total)
    teacher_log = jnp.log(teacher_total)
    divergence = cross / total - (student_log - teacher_log)
    student_lse = top + student_log
    per_token = divergence + sample_weight * (student_lse - target)
    student_shift = own_ref[0:1, :tokens] - top - student_log
    teacher_shift = own_ref[2:3, :tokens] - teacher_top - teacher_log
    factor = jnp.exp(student_shift)
    level = (
        own_ref[6:7, :tokens] + student_shift - teacher_shift - divergence + sample_weight
    )
    zeros = jnp.zeros((LANES - 3, tokens), jnp.float32)
    columns = jnp.concatenate([factor, level, per_token, zeros], axis=0).T
    share = tokens_ref[:, 1:2]
    weight = share * scale_ref[0]
    loss_ref[...] = jnp.sum(share * columns[:, 2:3], axis=0, keepdims=True)
    for i, column in enumerate(
        (weight * columns[:, 0:1], columns[:, 1:2], sample_weight * weight)
    ):
        factors_ref[i] = jnp.broadcast_to(column, (tokens, LANES))
    put_shares(1 - place_ref[0] % 2, factors_ref, terms_ref, picks_ref, give_ref)


def keep_kernel(place_ref, factors_ref, found_ref, terms_ref, picks_ref, keep_ref, loss_ref):
    loss_ref[...] = found_ref[...]
    put_shares(place_ref[0] % 2, factors_ref, terms_ref, picks_ref, keep_ref)


def sum_kernel(place_ref, own_ref, *refs):
    tokens, half = refs[-1].shape
    total = own_ref[...]
    for share_ref in refs[:-1]:
        total += share_ref[...].astype(jnp.float32)
    one, two, rest = total[:tokens], total[tokens : 2 * tokens], total[2 * tokens :]
    rest = jnp.concatenate([rest, turned(rest)], axis=0)
    turns = [turned(tile) for tile in (rest, one, two)]
    low = low_lanes(one.shape)
    first = place_ref[0] % 2 == 0
    tiles = [
        jnp.where(first, one, jnp.where(low, turns[0], turns[1])),
        jnp.where(first, two, jnp.where(low, turns[1], turns[2])),
        jnp.where(first, rest, turns[2]),
    ]
    total = jnp.concatenate(tiles, axis=1)[:, :half]
    refs[-1][...] = total.astype(refs[-1].dtype)


def paired_shards(
    hidden_states, head, teacher_values, teacher_scales, token_ids, lengths, row_map, loss_scale
):
    count = lax.axis_size("vocab")
    own_index = lax.axis_index("vocab")
    chips = count // 2
    tokens, half = hidden_states.shape
    width = 2 * half
    shard_rows = head.shape[0]
    place = jnp.reshape(own_index, (1,))
    vmem = pl.BlockSpec(memory_space=pltpu.VMEM)
    smem = pl.BlockSpec(memory_space=pltpu.SMEM)
    hbm = pl.BlockSpec(memory_space=pl.ANY)
    params = pltpu.CompilerParams(vmem_limit_bytes=VMEM_LIMIT)
    head = in_hbm(head)
    head_scratch = pltpu.VMEM((shard_rows, chips * width), head.dtype)
    head_sems = pltpu.SemaphoreType.DMA((chips,))
    rows_scratch = pltpu.VMEM((3 * tokens, shard_rows), jnp.bfloat16)
    rows_sem = pltpu.SemaphoreType.DMA
    slots, entries = teacher_values.shape
    hidden_rows = 5 * tokens // 2
    teacher_rows = 2 * slots * (shard_rows + LANES // 2) // LANES

    operands = (
        hidden_states,
        teacher_values,
        teacher_scales,
        token_ids[None, :],
        row_map[None, :],
        lengths[None, :],
    )
    packed, owner, table = pl.pallas_call(
        functools.partial(pack_kernel, shard_rows=shard_rows),
        out_shape=(
            vmem_array((chips, hidden_rows + teacher_rows, LANES), jnp.bfloat16),
            vmem_array((2 * tokens, 2 * tokens), jnp.bfloat16),
            vmem_array((tokens, LANES), jnp.float32),
        ),
        in_specs=[smem] + [hbm] * len(operands),
        out_specs=[vmem] * 3,
        scratch_shapes=[pltpu.VMEM(operand.shape, operand.dtype) for operand in operands]
        + [
            pltpu.VMEM((2 * slots, entries + LANES), jnp.float32),
            pltpu.SemaphoreType.DMA((len(operands),)),
        ],
        compiler_params=params,
        name="pack",
    )(place, *[in_hbm(operand) for operand in operands])
    steps = range(1, chips)
    near = [packed[0]] + [along_chips(packed[step], step) for step in steps]
    first, last = jnp.stack(near[: chips // 2 + 1]), jnp.stack(near[chips // 2 + 1 :])
    early = pl.pallas_call(
        functools.partial(preload_kernel, chips=chips),
        out_shape=vmem_array((shard_rows, EARLY * width), head.dtype),
        in_specs=[smem] + [hbm] * 2,
        out_specs=vmem,
        scratch_shapes=[pltpu.SemaphoreType.DMA((EARLY,))],
        compiler_params=params,
        cost_estimate=pl.CostEstimate(
            flops=0, bytes_accessed=4 * EARLY * shard_rows * width, transcendentals=0
        ),
        name="preload",
    )(place, head, near[3])
    last, early = lax.optimization_barrier((last, early))
    far = [swap_cores(last), swap_cores(first)]

    rows, stats, own_stats = pl.pallas_call(
        functools.partial(logits_kernel, chips=chips),
        out_shape=(
            hbm_array((3 * tokens, shard_rows), jnp.bfloat16),
            jax.ShapeDtypeStruct((count, STATS, pl.cdiv(tokens, LANES) * LANES), jnp.float32),
            vmem_array((STATS, pl.cdiv(tokens, LANES) * LANES), jnp.float32),
        ),
        in_specs=[smem] + [vmem] * (chips + 5) + [hbm],
        out_specs=[hbm, vmem, vmem],
        scratch_shapes=[
            pltpu.VMEM((shard_rows, (chips - EARLY) * width), head.dtype),
            rows_scratch,
            pltpu.VMEM((tokens, chips * width), jnp.bfloat16),
            pltpu.VMEM((2 * tokens, (shard_rows + LANES // 2) // 2), jnp.float32),
            pltpu.VMEM((tokens, shard_rows), jnp.float32),
            pltpu.SemaphoreType.DMA((chips - EARLY,)),
            rows_sem,
        ],
        compiler_params=params,
        cost_estimate=pl.CostEstimate(
            flops=2 * tokens * head.size, bytes_accessed=2 * head.size, transcendentals=0
        ),
        name="logits",
    )(place, *[in_vmem(block) for block in near[::-1] + far], in_vmem(owner), in_vmem(table), in_vmem(early), head)

    all_stats = lax.all_to_all(stats, "vocab", split_axis=0, concat_axis=0, tiled=True)

    terms, picks = pl.pallas_call(
        products_kernel,
        out_shape=(
            vmem_array((chips, width // LANES, 2, tokens, LANES), jnp.float32),
            vmem_array((chips, width // LANES, tokens, LANES), jnp.bfloat16),
        ),
        in_specs=[smem, hbm, hbm],
        out_specs=[vmem] * 2,
        scratch_shapes=[head_scratch, rows_scratch, head_sems, rows_sem],
        compiler_params=params,
        cost_estimate=pl.CostEstimate(
            flops=6 * tokens * head.size, bytes_accessed=2 * head.size, transcendentals=0
        ),
        name="products",
    )(place, in_hbm(rows), head)

    terms, picks = in_vmem(terms), in_vmem(picks)
    give, factors, loss = pl.pallas_call(
        give_kernel,
        out_shape=(
            vmem_array((chips, hidden_rows, LANES), jnp.bfloat16),
            vmem_array((3, tokens, LANES), jnp.float32),
            vmem_array((1, 1), jnp.float32),
        ),
        in_specs=[smem] * 2 + [vmem] * 5,
        out_specs=[vmem] * 3,
        compiler_params=params,
        name="give",
    )(place, loss_scale, in_vmem(all_stats), in_vmem(own_stats), in_vmem(table), terms, picks)
    taken = swap_cores(give)
    keep, loss = pl.pallas_call(
        keep_kernel,
        out_shape=(
            vmem_array((chips, hidden_rows, LANES), jnp.float32),
            jax.ShapeDtypeStruct((1, 1), jnp.float32),
        ),
        in_specs=[smem] + [vmem] * 4,
        out_specs=[vmem] * 2,
        compiler_params=params,
        cost_estimate=pl.CostEstimate(
            flops=4 * terms.size, bytes_accessed=4 * terms.size, transcendentals=0
        ),
        name="keep",
    )(place, in_vmem(factors), in_vmem(loss), terms, picks)
    sums = keep + taken.astype(jnp.float32)
    shares = [along_chips(sums[step].astype(jnp.bfloat16), step) for step in steps]
    total = pl.pallas_call(
        sum_kernel,
        out_shape=jax.ShapeDtypeStruct((tokens, half), jnp.bfloat16),
        in_specs=[smem] + [vmem] * chips,
        out_specs=vmem,
        compiler_params=params,
        name="total",
    )(place, *[in_vmem(share) for share in [sums[0]] + shares])
    return total, jnp.reshape(loss, (1,))


VMEM_LIMIT = 24 * 1024 * 1024


def shards(
    hidden_states, head, teacher_values, teacher_scales, token_ids, lengths, row_map, loss_scale
):
    count = lax.axis_size("vocab")
    own_index = lax.axis_index("vocab")
    tokens = hidden_states.shape[0]
    own_features = hidden_states.shape[1]
    shard_rows = head.shape[0]
    seq_length = tokens // lengths.shape[0]
    contract_last = (((1,), (1,)), ((), ()))

    scaled = scaled_teacher(teacher_values, teacher_scales, count, shard_rows)
    arrived = lax.all_to_all(scaled, "vocab", split_axis=0, concat_axis=0, tiled=True)
    arrived = arrived.reshape(tokens, shard_rows)
    gathered = to_all(hidden_states, count).transpose(1, 0, 2).reshape(tokens, -1)
    logits = lax.dot_general(gathered, head, contract_last, preferred_element_type=jnp.float32)

    positions = jnp.arange(tokens, dtype=jnp.int32)
    owner = row_map[None, :] == positions[:, None]
    slot_of = jnp.sum(jnp.where(owner, positions[None, :], 0), axis=1)
    teacher = jnp.take(arrived, slot_of, axis=0).astype(jnp.float32)

    seq_ids = jnp.arange(lengths.shape[0], dtype=jnp.int32)
    own_length = jnp.sum(
        jnp.where((positions // seq_length)[:, None] == seq_ids[None, :], lengths[None, :], 0),
        axis=1,
    )
    live_mask = (positions % seq_length < own_length).astype(jnp.float32)
    live_count = jnp.sum(live_mask)

    local_ids = token_ids - own_index * shard_rows
    target_hit = local_ids[:, None] == jnp.arange(shard_rows, dtype=jnp.int32)[None, :]
    target_part = jnp.sum(jnp.where(target_hit, logits, 0.0), axis=1)
    student_top = jnp.max(logits, axis=1)
    teacher_top = jnp.max(teacher, axis=1)
    student_off = logits - student_top[:, None]
    teacher_off = teacher - teacher_top[:, None]
    student_exp = jnp.exp(student_off)
    student_sum = jnp.sum(student_exp, axis=1)
    teacher_sum = jnp.sum(jnp.exp(teacher_off), axis=1)
    cross_sum = jnp.sum(student_exp * (student_off - teacher_off), axis=1)

    stats = to_all(
        jnp.stack(
            [student_top, student_sum, teacher_top, teacher_sum, cross_sum, target_part]
        ),
        count,
    )
    tops, sums, teacher_tops, teacher_sums, crosses, targets = [stats[:, i] for i in range(6)]
    student_max, student_total, teacher_max, teacher_total, cross_total = merge_stats(
        tops, sums, teacher_tops, teacher_sums, crosses
    )
    student_log = jnp.log(student_total)
    teacher_log = jnp.log(teacher_total)
    student_lse = student_max + student_log
    teacher_lse = teacher_max + teacher_log
    divergence = cross_total / student_total - (student_log - teacher_log)
    target = jnp.sum(targets, axis=0)

    per_token = divergence + sample_weight * (student_lse - target)
    loss = jnp.reshape(jnp.sum(live_mask * per_token) / live_count, (1,))
    token_weight = live_mask * loss_scale[0] / live_count
    log_student = logits - student_lse[:, None]
    log_teacher = teacher - teacher_lse[:, None]
    student_prob = jnp.exp(log_student)
    grad_logits = (
        token_weight[:, None]
        * (
            student_prob * (log_student - log_teacher - divergence[:, None])
            + sample_weight * (student_prob - target_hit.astype(jnp.float32))
        )
    ).astype(jnp.bfloat16)
    terms = jnp.dot(grad_logits, head, preferred_element_type=jnp.float32).astype(jnp.bfloat16)
    terms = terms.reshape(tokens, count, own_features).transpose(1, 0, 2)
    shares = lax.all_to_all(terms, "vocab", split_axis=0, concat_axis=0, tiled=True)
    grad_hidden = jnp.sum(shares.astype(jnp.float32), axis=0)
    return (grad_hidden.astype(jnp.bfloat16), loss)


def any_shards(*arrays):
    hidden_states, head, teacher_values = arrays[:3]
    count = lax.axis_size("vocab")
    fits = (
        count % 2 == 0
        and hidden_states.shape[1] == 5 * LANES // 2
        and hidden_states.shape[0] % 32 == 0
        and head.shape[0] % LANES == LANES // 2
        and (head.shape[0] + LANES // 2) // LANES % 2 == 0
        and teacher_values.shape[0] == 4
    )
    return paired_shards(*arrays) if fits else shards(*arrays)


def solution(mesh):
    in_specs = (
        P("dom", "vocab"),
        P("vocab", None),
        P(("dom", "vocab"), None),
        P(("dom", "vocab"), None),
        P("dom"),
        P("dom"),
        P("dom"),
        P(),
    )
    out_specs = (P("dom", "vocab"), P("dom"))
    return jax.shard_map(
        any_shards, mesh=mesh, in_specs=in_specs, out_specs=out_specs, check_vma=False
    )
```

```python
import functools

import jax
import jax.numpy as jnp
from jax import lax
from jax.experimental import pallas as pl
from jax.experimental.pallas import tpu as pltpu
from jax.sharding import PartitionSpec as P

BLOCK = 32
LANES = 128
STATS = 8
AHEAD = 3
EARLY = 3


sample_weight = 0.5


def to_all(piece, count):
    copies = jnp.broadcast_to(piece[None], (count,) + piece.shape)
    return lax.all_to_all(copies, "vocab", split_axis=0, concat_axis=0, tiled=True)


def scaled_teacher(teacher_values, teacher_scales, count, shard_rows):
    slot_rows = teacher_values.shape[0]
    scaled = (
        teacher_values.astype(jnp.float32).reshape(slot_rows, -1, BLOCK) * teacher_scales[:, :, None]
    ).astype(jnp.bfloat16)
    return scaled.reshape(slot_rows, count, shard_rows).transpose(1, 0, 2)


def merge_stats(tops, sums, teacher_tops, teacher_sums, crosses):
    top = jnp.max(tops, axis=0)
    teacher_top = jnp.max(teacher_tops, axis=0)
    shift = tops - top[None]
    teacher_shift = teacher_tops - teacher_top[None]
    weight = jnp.exp(shift)
    total = jnp.sum(sums * weight, axis=0)
    teacher_total = jnp.sum(teacher_sums * jnp.exp(teacher_shift), axis=0)
    cross = jnp.sum(weight * (crosses + sums * (shift - teacher_shift)), axis=0)
    return top, total, teacher_top, teacher_total, cross


def swap_cores(array):
    count = lax.axis_size("vocab")
    return lax.ppermute(array, "vocab", [(i, i ^ 1) for i in range(count)])


def along_chips(array, step):
    count = lax.axis_size("vocab")
    return lax.ppermute(array, "vocab", [(i, (i + 2 * step) % count) for i in range(count)])


def vmem_array(shape, dtype):
    return pltpu.VMEM(shape, dtype)


def in_vmem(array):
    return pltpu.with_memory_space_constraint(array, pltpu.VMEM)


def in_hbm(array):
    return pltpu.with_memory_space_constraint(array, pltpu.HBM)


def hbm_array(shape, dtype):
    return pltpu.HBM(shape, dtype)


def low_lanes(shape):
    return lax.broadcasted_iota(jnp.int32, shape, len(shape) - 1) < LANES // 2


def low_rows(shape, count):
    return lax.broadcasted_iota(jnp.int32, shape, 0) < count


def turned(array):
    return pltpu.roll(array, LANES // 2, 1)


def folded(first, tile):
    rows = tile.shape[0] // 2
    upper, lower = tile[:rows], turned(tile[rows:])
    low = low_lanes(upper.shape)
    return jnp.where(first, jnp.where(low, upper, lower), jnp.where(low, lower, upper))


def tiles_of(array, count):
    return [array[:, LANES * i : LANES * (i + 1)] for i in range(count)]


def column_of(row):
    size = row.shape[1]
    down = lax.broadcasted_iota(jnp.int32, (size, size), 0)
    along = lax.broadcasted_iota(jnp.int32, (size, size), 1)
    return jnp.sum(jnp.where(down == along, row, jnp.zeros_like(row)), axis=1, keepdims=True)


def token_facts(ids, row_map, lengths, first_entry, slots):
    tokens = row_map.shape[1]
    token = lax.broadcasted_iota(jnp.int32, (tokens, tokens), 0)
    slot = lax.broadcasted_iota(jnp.int32, (tokens, tokens), 1)
    owner = (row_map == token).astype(jnp.float32)
    named = jnp.max(owner, axis=1, keepdims=True)
    owner = jnp.where((slot == 0) & (named == 0.0), 1.0, owner)
    rows = 2 * tokens
    slot = lax.broadcasted_iota(jnp.int32, (tokens, rows), 0)
    row = lax.broadcasted_iota(jnp.int32, (tokens, rows), 1)
    source, within = row // (2 * slots), row % (2 * slots)
    chosen = (slot == source * slots + within % slots).astype(jnp.bfloat16)
    owner = jnp.dot(owner.astype(jnp.bfloat16), chosen, preferred_element_type=jnp.float32)
    odd = within >= slots
    owner = jnp.concatenate([jnp.where(odd, 0.0, owner), jnp.where(odd, owner, 0.0)], axis=0)

    seqs = lengths.shape[1]
    seq_length = tokens // seqs
    position = lax.broadcasted_iota(jnp.int32, (tokens, 1), 0)
    live_until = jnp.zeros((tokens, 1), jnp.int32)
    for seq in range(seqs):
        inside = (position >= seq * seq_length) & (position < (seq + 1) * seq_length)
        until = lengths[:, seq : seq + 1] + seq * seq_length
        live_until = jnp.where(inside, until, live_until)
    live = (position < live_until).astype(jnp.float32)
    count = jnp.sum(live, axis=0, keepdims=True)
    entry = (column_of(ids) - first_entry).astype(jnp.float32)
    lane = lax.broadcasted_iota(jnp.int32, (tokens, LANES), 1)
    return owner.astype(jnp.bfloat16), jnp.where(lane == 0, entry, live / count)


def pack_kernel(place_ref, *refs, shard_rows):
    outside, refs = refs[:6], refs[6:]
    packed_ref, owner_ref, table_ref = refs[:3]
    inside, wide_ref, sems = refs[3:9], refs[9], refs[10]
    copies = [
        pltpu.make_async_copy(source, target, sems.at[i])
        for i, (source, target) in enumerate(zip(outside, inside))
    ]
    for copy in copies:
        copy.start()
    for copy in copies:
        copy.wait()
    hidden_ref, values_ref, scales_ref, ids_ref, map_ref, lengths_ref = inside
    owner_ref[...], table_ref[...] = token_facts(
        ids_ref[...], map_ref[...], lengths_ref[...], place_ref[0] * shard_rows, values_ref.shape[0]
    )
    chips = packed_ref.shape[0]
    tokens, half = hidden_ref.shape
    slots, entries = values_ref.shape
    pair = entries // chips
    shard = pair // 2
    blocks = pair // BLOCK
    scales = jnp.concatenate([scales_ref[...]] * 2, axis=0)
    stacked = jnp.concatenate(
        [scales[:, blocks * chip : blocks * (chip + 1)] for chip in range(chips)], axis=0
    )
    block = lax.broadcasted_iota(jnp.int32, (blocks, pair), 0)
    entry = lax.broadcasted_iota(jnp.int32, (blocks, pair), 1)
    inside = (entry >= block * BLOCK) & (entry < block * BLOCK + BLOCK)
    spread = jnp.dot(
        stacked.astype(jnp.bfloat16),
        inside.astype(jnp.bfloat16),
        preferred_element_type=jnp.float32,
    )
    values = values_ref[...].astype(jnp.float32)
    values = jnp.concatenate([values, values], axis=0)
    for chip in range(chips):
        wide_ref[:, pair * chip : pair * (chip + 1)] = (
            values[:, pair * chip : pair * (chip + 1)]
            * spread[2 * slots * chip : 2 * slots * (chip + 1)]
        )
    wide_ref[:, entries:] = jnp.zeros((2 * slots, LANES), jnp.float32)

    hidden = hidden_ref[...].astype(jnp.float32)
    zeros = jnp.zeros((tokens, LANES // 2), jnp.float32)
    tiles = tiles_of(jnp.concatenate([hidden, zeros], axis=1), 3)
    turns = [turned(tile) for tile in tiles]
    low = low_lanes(tiles[0].shape)
    first = place_ref[0] % 2 == 0
    hidden = jnp.concatenate(
        [
            jnp.where(first, tiles[0], jnp.where(low, turns[0], turns[1])),
            jnp.where(first, tiles[1], jnp.where(low, turns[1], turns[2])),
            folded(first, jnp.where(first, tiles[2], turns[0])),
        ],
        axis=0,
    ).astype(jnp.bfloat16)
    hidden_rows = hidden.shape[0]
    upper = low_rows((2 * slots, LANES), slots)
    low = low_lanes((2 * slots, LANES))
    tile_pairs = (shard + LANES // 2) // LANES // 2
    for chip in range(chips):
        rows = []
        for core in range(2):
            start = pair * chip + (shard - LANES // 2) * core
            tiles = [
                wide_ref[:, start + LANES * i : start + LANES * (i + 1)]
                for i in range(2 * tile_pairs + core)
            ]
            if core == 1:
                tiles = [turned(tile) for tile in tiles]
                tiles = [
                    jnp.where(low, tiles[i], tiles[i + 1]) for i in range(2 * tile_pairs)
                ]
            rows += [
                jnp.where(upper, tiles[2 * i], tiles[2 * i + 1]) for i in range(tile_pairs)
            ]
        step = lax.rem(chip - place_ref[0] // 2 + chips, chips)
        packed_ref[step, :hidden_rows] = hidden
        packed_ref[step, hidden_rows:] = jnp.concatenate(rows, axis=0).astype(jnp.bfloat16)


def head_copies(head_ref, held_ref, sems, chips):
    width = held_ref.shape[1] // len(chips)
    copies = []
    for step, chip in enumerate(chips):
        columns = pl.ds(pl.multiple_of(chip * width, LANES), width)
        copies.append(
            pltpu.make_async_copy(
                head_ref.at[:, columns],
                held_ref.at[:, width * step : width * (step + 1)],
                sems.at[step],
            )
        )
    return copies


def take(copies, step):
    copies[step].wait()
    if step + AHEAD < len(copies):
        copies[step + AHEAD].start()


def source_chips(place_ref, chips):
    return [lax.rem(place_ref[0] // 2 - step + chips, chips) for step in range(chips)]


def preload_kernel(place_ref, head_ref, _, early_ref, sems, *, chips):
    sources = source_chips(place_ref, chips)[:EARLY]
    copies = head_copies(head_ref, early_ref, sems, sources)
    for copy in copies:
        copy.start()
    for copy in copies:
        copy.wait()


def logits_kernel(place_ref, *refs, chips):
    near, far, refs = refs[:chips][::-1], refs[chips : chips + 2], refs[chips + 2 :]
    owner_ref, tokens_ref, early_ref, head_ref, rows_ref, stats_ref, own_ref = refs[:7]
    held_ref, made_ref, hidden_ref, arrived_ref, teacher_ref, sems, made_sem = refs[7:]
    core = place_ref[0] % 2
    sources = source_chips(place_ref, chips)
    copies = head_copies(head_ref, held_ref, sems, sources[EARLY:])
    for copy in copies:
        copy.start()
    tokens, width = hidden_ref.shape[0], hidden_ref.shape[1] // chips
    shard_rows = head_ref.shape[0]
    hidden_rows = 5 * tokens // 2
    slots = tokens // (2 * chips)
    low = low_lanes((tokens // 2, LANES))

    for step in range(chips):
        late = step > chips // 2
        group = far[0] if late else far[1]
        place = step - chips // 2 - 1 if late else step
        blocks = near[step], group.at[place]
        base = width * step
        for block, parity in zip(blocks, (core, 1 - core)):
            for i in range(2):
                column = base + LANES * i + (width - 2 * LANES) * parity
                lanes = pl.ds(pl.multiple_of(column, LANES), LANES)
                hidden_ref[:, lanes] = block[tokens * i : tokens * (i + 1)]
            teacher = block[hidden_rows:].astype(jnp.float32)
            share = teacher.shape[0] // 2
            teacher = jnp.where(core == 0, teacher[:share], teacher[share:])
            row = 2 * slots * (2 * sources[step] + parity)
            rows = pl.ds(pl.multiple_of(row, 2 * slots), 2 * slots)
            for i in range(share // (2 * slots)):
                arrived_ref[rows, LANES * i : LANES * (i + 1)] = teacher[
                    2 * slots * i : 2 * slots * (i + 1)
                ]
        own, other = [block[2 * tokens : hidden_rows].astype(jnp.float32) for block in blocks]
        one, two = jnp.where(core == 0, own, other), jnp.where(core == 0, other, own)
        tile = [jnp.where(low, one, two), turned(jnp.where(low, two, one))]
        tile = jnp.concatenate(tile, axis=0).astype(jnp.bfloat16)
        hidden_ref[:, base + 2 * LANES : base + 3 * LANES] = tile

    def product(step, columns):
        return lax.dot_general(
            hidden_ref[:, width * step : width * (step + 1)],
            columns,
            (((1,), (1,)), ((), ())),
            preferred_element_type=jnp.float32,
        )

    logits = product(0, early_ref[:, :width])
    for step in range(1, EARLY):
        logits += product(step, early_ref[:, width * step : width * (step + 1)])
    placed = jnp.dot(
        owner_ref[...], arrived_ref[...].astype(jnp.bfloat16), preferred_element_type=jnp.float32
    )
    pairs = arrived_ref.shape[1] // LANES
    even, odd = tiles_of(placed[:tokens], pairs), tiles_of(placed[tokens:], pairs)
    teacher = jnp.concatenate([tile for pair in zip(even, odd) for tile in pair], axis=1)
    teacher = teacher[:, :shard_rows]
    teacher_top = jnp.max(teacher, axis=1, keepdims=True)
    teacher_off = teacher - teacher_top
    teacher_total = jnp.sum(jnp.exp(teacher_off), axis=1, keepdims=True)
    teacher_ref[...] = teacher_off
    for copy in copies:
        copy.wait()
    for step in range(len(copies)):
        columns = held_ref[:, width * step : width * (step + 1)]
        logits += product(EARLY + step, columns)

    top = jnp.max(logits, axis=1, keepdims=True)
    off = logits - top
    exps = jnp.exp(off)
    total = jnp.sum(exps, axis=1, keepdims=True)
    gap = off - teacher_ref[...]
    cross = jnp.sum(exps * gap, axis=1, keepdims=True)
    centre = cross / total
    entry = lax.broadcasted_iota(jnp.int32, (tokens, shard_rows), 1)
    hit = entry == tokens_ref[:, :1].astype(jnp.int32)
    target = jnp.sum(jnp.where(hit, logits, 0.0), axis=1, keepdims=True)
    made_ref[:tokens] = (exps * (gap - centre)).astype(jnp.bfloat16)
    made_ref[tokens : 2 * tokens] = exps.astype(jnp.bfloat16)
    made_ref[2 * tokens :] = hit.astype(jnp.bfloat16)
    out = pltpu.make_async_copy(made_ref, rows_ref, made_sem)
    out.start()

    lane = lax.broadcasted_iota(jnp.int32, (tokens, LANES), 1)
    table = jnp.zeros((tokens, LANES), jnp.float32)
    for place, column in enumerate(
        (top, total, teacher_top, teacher_total, cross, target, centre)
    ):
        table = jnp.where(lane == place, column, table)
    stats = jnp.concatenate([table, jnp.zeros((stats_ref.shape[2] - tokens, LANES), jnp.float32)])
    stats = stats.T[:STATS]
    own_ref[...] = stats
    stats_ref[...] = jnp.broadcast_to(stats[None], stats_ref.shape)
    out.wait()


def products_kernel(
    place_ref, rows_ref, head_ref, terms_ref, picks_ref, held_ref, made_ref, sems, made_sem
):
    into = pltpu.make_async_copy(rows_ref, made_ref, made_sem)
    into.start()
    chips = terms_ref.shape[0]
    targets = [lax.rem(place_ref[0] // 2 + step, chips) for step in range(chips)]
    copies = head_copies(head_ref, held_ref, sems, targets)
    for copy in copies[:AHEAD]:
        copy.start()
    into.wait()
    tokens = made_ref.shape[0] // 3
    width = held_ref.shape[1] // chips
    for step in range(chips):
        take(copies, step)
        products = jnp.dot(
            made_ref[...],
            held_ref[:, width * step : width * (step + 1)],
            preferred_element_type=jnp.float32,
        )
        for i, tile in enumerate(tiles_of(products, width // LANES)):
            terms_ref[step, i, 0] = tile[:tokens]
            terms_ref[step, i, 1] = tile[tokens : 2 * tokens]
            picks_ref[step, i] = tile[2 * tokens :].astype(jnp.bfloat16)


def put_shares(parity, factors_ref, terms_ref, picks_ref, out_ref):
    tokens = terms_ref.shape[3]
    factor, level, weight = [factors_ref[i] for i in range(3)]
    for step in range(terms_ref.shape[0]):
        for i, tile in enumerate((3 * parity, 3 * parity + 1, 2)):
            sums = terms_ref[step, tile, 0] + level * terms_ref[step, tile, 1]
            share = factor * sums - weight * picks_ref[step, tile].astype(jnp.float32)
            if i == 2:
                share = folded(parity == 0, share)
            out_ref[step, tokens * i : tokens * i + share.shape[0]] = share.astype(out_ref.dtype)


def give_kernel(
    place_ref,
    scale_ref,
    stats_ref,
    own_ref,
    tokens_ref,
    terms_ref,
    picks_ref,
    give_ref,
    factors_ref,
    loss_ref,
):
    tokens = tokens_ref.shape[0]
    tops, sums, teacher_tops, teacher_sums, crosses, targets = [
        stats_ref[:, i, :tokens] for i in range(6)
    ]
    top, total, teacher_top, teacher_total, cross = [
        part[None] for part in merge_stats(tops, sums, teacher_tops, teacher_sums, crosses)
    ]
    target = jnp.sum(targets, axis=0, keepdims=True)
    student_log = jnp.log(total)
    teacher_log = jnp.log(teacher_total)
    divergence = cross / total - (student_log - teacher_log)
    student_lse = top + student_log
    per_token = divergence + sample_weight * (student_lse - target)
    student_shift = own_ref[0:1, :tokens] - top - student_log
    teacher_shift = own_ref[2:3, :tokens] - teacher_top - teacher_log
    factor = jnp.exp(student_shift)
    level = (
        own_ref[6:7, :tokens] + student_shift - teacher_shift - divergence + sample_weight
    )
    zeros = jnp.zeros((LANES - 3, tokens), jnp.float32)
    columns = jnp.concatenate([factor, level, per_token, zeros], axis=0).T
    share = tokens_ref[:, 1:2]
    weight = share * scale_ref[0]
    loss_ref[...] = jnp.sum(share * columns[:, 2:3], axis=0, keepdims=True)
    for i, column in enumerate(
        (weight * columns[:, 0:1], columns[:, 1:2], sample_weight * weight)
    ):
        factors_ref[i] = jnp.broadcast_to(column, (tokens, LANES))
    put_shares(1 - place_ref[0] % 2, factors_ref, terms_ref, picks_ref, give_ref)


def keep_kernel(place_ref, factors_ref, found_ref, terms_ref, picks_ref, keep_ref, loss_ref):
    loss_ref[...] = found_ref[...]
    put_shares(place_ref[0] % 2, factors_ref, terms_ref, picks_ref, keep_ref)


def sum_kernel(place_ref, own_ref, *refs):
    tokens, half = refs[-1].shape
    total = own_ref[...]
    for share_ref in refs[:-1]:
        total += share_ref[...].astype(jnp.float32)
    one, two, rest = total[:tokens], total[tokens : 2 * tokens], total[2 * tokens :]
    rest = jnp.concatenate([rest, turned(rest)], axis=0)
    turns = [turned(tile) for tile in (rest, one, two)]
    low = low_lanes(one.shape)
    first = place_ref[0] % 2 == 0
    tiles = [
        jnp.where(first, one, jnp.where(low, turns[0], turns[1])),
        jnp.where(first, two, jnp.where(low, turns[1], turns[2])),
        jnp.where(first, rest, turns[2]),
    ]
    total = jnp.concatenate(tiles, axis=1)[:, :half]
    refs[-1][...] = total.astype(refs[-1].dtype)


def paired_shards(
    hidden_states, head, teacher_values, teacher_scales, token_ids, lengths, row_map, loss_scale
):
    count = lax.axis_size("vocab")
    own_index = lax.axis_index("vocab")
    chips = count // 2
    tokens, half = hidden_states.shape
    width = 2 * half
    shard_rows = head.shape[0]
    place = jnp.reshape(own_index, (1,))
    vmem = pl.BlockSpec(memory_space=pltpu.VMEM)
    smem = pl.BlockSpec(memory_space=pltpu.SMEM)
    hbm = pl.BlockSpec(memory_space=pl.ANY)
    params = pltpu.CompilerParams(vmem_limit_bytes=VMEM_LIMIT)
    head = in_hbm(head)
    head_scratch = pltpu.VMEM((shard_rows, chips * width), head.dtype)
    head_sems = pltpu.SemaphoreType.DMA((chips,))
    rows_scratch = pltpu.VMEM((3 * tokens, shard_rows), jnp.bfloat16)
    rows_sem = pltpu.SemaphoreType.DMA
    slots, entries = teacher_values.shape
    hidden_rows = 5 * tokens // 2
    teacher_rows = 2 * slots * (shard_rows + LANES // 2) // LANES

    operands = (
        hidden_states,
        teacher_values,
        teacher_scales,
        token_ids[None, :],
        row_map[None, :],
        lengths[None, :],
    )
    packed, owner, table = pl.pallas_call(
        functools.partial(pack_kernel, shard_rows=shard_rows),
        out_shape=(
            vmem_array((chips, hidden_rows + teacher_rows, LANES), jnp.bfloat16),
            vmem_array((2 * tokens, 2 * tokens), jnp.bfloat16),
            vmem_array((tokens, LANES), jnp.float32),
        ),
        in_specs=[smem] + [hbm] * len(operands),
        out_specs=[vmem] * 3,
        scratch_shapes=[pltpu.VMEM(operand.shape, operand.dtype) for operand in operands]
        + [
            pltpu.VMEM((2 * slots, entries + LANES), jnp.float32),
            pltpu.SemaphoreType.DMA((len(operands),)),
        ],
        compiler_params=params,
        name="pack",
    )(place, *[in_hbm(operand) for operand in operands])
    steps = range(1, chips)
    near = [packed[0]] + [along_chips(packed[step], step) for step in steps]
    first, last = jnp.stack(near[: chips // 2 + 1]), jnp.stack(near[chips // 2 + 1 :])
    early = pl.pallas_call(
        functools.partial(preload_kernel, chips=chips),
        out_shape=vmem_array((shard_rows, EARLY * width), head.dtype),
        in_specs=[smem] + [hbm] * 2,
        out_specs=vmem,
        scratch_shapes=[pltpu.SemaphoreType.DMA((EARLY,))],
        compiler_params=params,
        cost_estimate=pl.CostEstimate(
            flops=0, bytes_accessed=4 * EARLY * shard_rows * width, transcendentals=0
        ),
        name="preload",
    )(place, head, near[3])
    last, early = lax.optimization_barrier((last, early))
    far = [swap_cores(last), swap_cores(first)]

    rows, stats, own_stats = pl.pallas_call(
        functools.partial(logits_kernel, chips=chips),
        out_shape=(
            hbm_array((3 * tokens, shard_rows), jnp.bfloat16),
            jax.ShapeDtypeStruct((count, STATS, pl.cdiv(tokens, LANES) * LANES), jnp.float32),
            vmem_array((STATS, pl.cdiv(tokens, LANES) * LANES), jnp.float32),
        ),
        in_specs=[smem] + [vmem] * (chips + 5) + [hbm],
        out_specs=[hbm, vmem, vmem],
        scratch_shapes=[
            pltpu.VMEM((shard_rows, (chips - EARLY) * width), head.dtype),
            rows_scratch,
            pltpu.VMEM((tokens, chips * width), jnp.bfloat16),
            pltpu.VMEM((2 * tokens, (shard_rows + LANES // 2) // 2), jnp.float32),
            pltpu.VMEM((tokens, shard_rows), jnp.float32),
            pltpu.SemaphoreType.DMA((chips - EARLY,)),
            rows_sem,
        ],
        compiler_params=params,
        cost_estimate=pl.CostEstimate(
            flops=2 * tokens * head.size, bytes_accessed=2 * head.size, transcendentals=0
        ),
        name="logits",
    )(place, *[in_vmem(block) for block in near[::-1] + far], in_vmem(owner), in_vmem(table), in_vmem(early), head)

    all_stats = lax.all_to_all(stats, "vocab", split_axis=0, concat_axis=0, tiled=True)

    terms, picks = pl.pallas_call(
        products_kernel,
        out_shape=(
            vmem_array((chips, width // LANES, 2, tokens, LANES), jnp.float32),
            vmem_array((chips, width // LANES, tokens, LANES), jnp.bfloat16),
        ),
        in_specs=[smem, hbm, hbm],
        out_specs=[vmem] * 2,
        scratch_shapes=[head_scratch, rows_scratch, head_sems, rows_sem],
        compiler_params=params,
        cost_estimate=pl.CostEstimate(
            flops=6 * tokens * head.size, bytes_accessed=2 * head.size, transcendentals=0
        ),
        name="products",
    )(place, in_hbm(rows), head)

    terms, picks = in_vmem(terms), in_vmem(picks)
    give, factors, loss = pl.pallas_call(
        give_kernel,
        out_shape=(
            vmem_array((chips, hidden_rows, LANES), jnp.bfloat16),
            vmem_array((3, tokens, LANES), jnp.float32),
            vmem_array((1, 1), jnp.float32),
        ),
        in_specs=[smem] * 2 + [vmem] * 5,
        out_specs=[vmem] * 3,
        compiler_params=params,
        name="give",
    )(place, loss_scale, in_vmem(all_stats), in_vmem(own_stats), in_vmem(table), terms, picks)
    taken = swap_cores(give)
    keep, loss = pl.pallas_call(
        keep_kernel,
        out_shape=(
            vmem_array((chips, hidden_rows, LANES), jnp.float32),
            jax.ShapeDtypeStruct((1, 1), jnp.float32),
        ),
        in_specs=[smem] + [vmem] * 4,
        out_specs=[vmem] * 2,
        compiler_params=params,
        cost_estimate=pl.CostEstimate(
            flops=4 * terms.size, bytes_accessed=4 * terms.size, transcendentals=0
        ),
        name="keep",
    )(place, in_vmem(factors), in_vmem(loss), terms, picks)
    sums = keep + taken.astype(jnp.float32)
    shares = [along_chips(sums[step].astype(jnp.bfloat16), step) for step in steps]
    total = pl.pallas_call(
        sum_kernel,
        out_shape=jax.ShapeDtypeStruct((tokens, half), jnp.bfloat16),
        in_specs=[smem] + [vmem] * chips,
        out_specs=vmem,
        compiler_params=params,
        name="total",
    )(place, *[in_vmem(share) for share in [sums[0]] + shares])
    return total, jnp.reshape(loss, (1,))


VMEM_LIMIT = 24 * 1024 * 1024


def shards(
    hidden_states, head, teacher_values, teacher_scales, token_ids, lengths, row_map, loss_scale
):
    count = lax.axis_size("vocab")
    own_index = lax.axis_index("vocab")
    tokens = hidden_states.shape[0]
    own_features = hidden_states.shape[1]
    shard_rows = head.shape[0]
    seq_length = tokens // lengths.shape[0]
    contract_last = (((1,), (1,)), ((), ()))

    scaled = scaled_teacher(teacher_values, teacher_scales, count, shard_rows)
    arrived = lax.all_to_all(scaled, "vocab", split_axis=0, concat_axis=0, tiled=True)
    arrived = arrived.reshape(tokens, shard_rows)
    gathered = to_all(hidden_states, count).transpose(1, 0, 2).reshape(tokens, -1)
    logits = lax.dot_general(gathered, head, contract_last, preferred_element_type=jnp.float32)

    positions = jnp.arange(tokens, dtype=jnp.int32)
    owner = row_map[None, :] == positions[:, None]
    slot_of = jnp.sum(jnp.where(owner, positions[None, :], 0), axis=1)
    teacher = jnp.take(arrived, slot_of, axis=0).astype(jnp.float32)

    seq_ids = jnp.arange(lengths.shape[0], dtype=jnp.int32)
    own_length = jnp.sum(
        jnp.where((positions // seq_length)[:, None] == seq_ids[None, :], lengths[None, :], 0),
        axis=1,
    )
    live_mask = (positions % seq_length < own_length).astype(jnp.float32)
    live_count = jnp.sum(live_mask)

    local_ids = token_ids - own_index * shard_rows
    target_hit = local_ids[:, None] == jnp.arange(shard_rows, dtype=jnp.int32)[None, :]
    target_part = jnp.sum(jnp.where(target_hit, logits, 0.0), axis=1)
    student_top = jnp.max(logits, axis=1)
    teacher_top = jnp.max(teacher, axis=1)
    student_off = logits - student_top[:, None]
    teacher_off = teacher - teacher_top[:, None]
    student_exp = jnp.exp(student_off)
    student_sum = jnp.sum(student_exp, axis=1)
    teacher_sum = jnp.sum(jnp.exp(teacher_off), axis=1)
    cross_sum = jnp.sum(student_exp * (student_off - teacher_off), axis=1)

    stats = to_all(
        jnp.stack(
            [student_top, student_sum, teacher_top, teacher_sum, cross_sum, target_part]
        ),
        count,
    )
    tops, sums, teacher_tops, teacher_sums, crosses, targets = [stats[:, i] for i in range(6)]
    student_max, student_total, teacher_max, teacher_total, cross_total = merge_stats(
        tops, sums, teacher_tops, teacher_sums, crosses
    )
    student_log = jnp.log(student_total)
    teacher_log = jnp.log(teacher_total)
    student_lse = student_max + student_log
    teacher_lse = teacher_max + teacher_log
    divergence = cross_total / student_total - (student_log - teacher_log)
    target = jnp.sum(targets, axis=0)

    per_token = divergence + sample_weight * (student_lse - target)
    loss = jnp.reshape(jnp.sum(live_mask * per_token) / live_count, (1,))
    token_weight = live_mask * loss_scale[0] / live_count
    log_student = logits - student_lse[:, None]
    log_teacher = teacher - teacher_lse[:, None]
    student_prob = jnp.exp(log_student)
    grad_logits = (
        token_weight[:, None]
        * (
            student_prob * (log_student - log_teacher - divergence[:, None])
            + sample_weight * (student_prob - target_hit.astype(jnp.float32))
        )
    ).astype(jnp.bfloat16)
    terms = jnp.dot(grad_logits, head, preferred_element_type=jnp.float32).astype(jnp.bfloat16)
    terms = terms.reshape(tokens, count, own_features).transpose(1, 0, 2)
    shares = lax.all_to_all(terms, "vocab", split_axis=0, concat_axis=0, tiled=True)
    grad_hidden = jnp.sum(shares.astype(jnp.float32), axis=0)
    return (grad_hidden.astype(jnp.bfloat16), loss)


def any_shards(*arrays):
    hidden_states, head, teacher_values = arrays[:3]
    count = lax.axis_size("vocab")
    fits = (
        count % 2 == 0
        and hidden_states.shape[1] == 5 * LANES // 2
        and hidden_states.shape[0] % 32 == 0
        and head.shape[0] % LANES == LANES // 2
        and (head.shape[0] + LANES // 2) // LANES % 2 == 0
        and teacher_values.shape[0] == 4
    )
    return paired_shards(*arrays) if fits else shards(*arrays)


def solution(mesh):
    in_specs = (
        P("dom", "vocab"),
        P("vocab", None),
        P(("dom", "vocab"), None),
        P(("dom", "vocab"), None),
        P("dom"),
        P("dom"),
        P("dom"),
        P(),
    )
    out_specs = (P("dom", "vocab"), P("dom"))
    return jax.shard_map(
        any_shards, mesh=mesh, in_specs=in_specs, out_specs=out_specs, check_vma=False
    )
```

```python
import functools

import jax
import jax.numpy as jnp
from jax import lax
from jax.experimental import pallas as pl
from jax.experimental.pallas import tpu as pltpu
from jax.sharding import PartitionSpec as P

BLOCK = 32
LANES = 128
STATS = 8
AHEAD = 3
EARLY = 3


sample_weight = 0.5


def to_all(piece, count):
    copies = jnp.broadcast_to(piece[None], (count,) + piece.shape)
    return lax.all_to_all(copies, "vocab", split_axis=0, concat_axis=0, tiled=True)


def scaled_teacher(teacher_values, teacher_scales, count, shard_rows):
    slot_rows = teacher_values.shape[0]
    scaled = (
        teacher_values.astype(jnp.float32).reshape(slot_rows, -1, BLOCK) * teacher_scales[:, :, None]
    ).astype(jnp.bfloat16)
    return scaled.reshape(slot_rows, count, shard_rows).transpose(1, 0, 2)


def merge_stats(tops, sums, teacher_tops, teacher_sums, crosses):
    top = jnp.max(tops, axis=0)
    teacher_top = jnp.max(teacher_tops, axis=0)
    shift = tops - top[None]
    teacher_shift = teacher_tops - teacher_top[None]
    weight = jnp.exp(shift)
    total = jnp.sum(sums * weight, axis=0)
    teacher_total = jnp.sum(teacher_sums * jnp.exp(teacher_shift), axis=0)
    cross = jnp.sum(weight * (crosses + sums * (shift - teacher_shift)), axis=0)
    return top, total, teacher_top, teacher_total, cross


def swap_cores(array):
    count = lax.axis_size("vocab")
    return lax.ppermute(array, "vocab", [(i, i ^ 1) for i in range(count)])


def along_chips(array, step):
    count = lax.axis_size("vocab")
    return lax.ppermute(array, "vocab", [(i, (i + 2 * step) % count) for i in range(count)])


def vmem_array(shape, dtype):
    return pltpu.VMEM(shape, dtype)


def in_vmem(array):
    return pltpu.with_memory_space_constraint(array, pltpu.VMEM)


def in_hbm(array):
    return pltpu.with_memory_space_constraint(array, pltpu.HBM)


def hbm_array(shape, dtype):
    return pltpu.HBM(shape, dtype)


def low_lanes(shape):
    return lax.broadcasted_iota(jnp.int32, shape, len(shape) - 1) < LANES // 2


def low_rows(shape, count):
    return lax.broadcasted_iota(jnp.int32, shape, 0) < count


def turned(array):
    return pltpu.roll(array, LANES // 2, 1)


def folded(first, tile):
    rows = tile.shape[0] // 2
    upper, lower = tile[:rows], turned(tile[rows:])
    low = low_lanes(upper.shape)
    return jnp.where(first, jnp.where(low, upper, lower), jnp.where(low, lower, upper))


def tiles_of(array, count):
    return [array[:, LANES * i : LANES * (i + 1)] for i in range(count)]


def column_of(row):
    size = row.shape[1]
    down = lax.broadcasted_iota(jnp.int32, (size, size), 0)
    along = lax.broadcasted_iota(jnp.int32, (size, size), 1)
    return jnp.sum(jnp.where(down == along, row, jnp.zeros_like(row)), axis=1, keepdims=True)


def token_facts(ids, row_map, lengths, first_entry, slots):
    tokens = row_map.shape[1]
    token = lax.broadcasted_iota(jnp.int32, (tokens, tokens), 0)
    slot = lax.broadcasted_iota(jnp.int32, (tokens, tokens), 1)
    owner = (row_map == token).astype(jnp.float32)
    named = jnp.max(owner, axis=1, keepdims=True)
    owner = jnp.where((slot == 0) & (named == 0.0), 1.0, owner)
    rows = 2 * tokens
    slot = lax.broadcasted_iota(jnp.int32, (tokens, rows), 0)
    row = lax.broadcasted_iota(jnp.int32, (tokens, rows), 1)
    source, within = row // (2 * slots), row % (2 * slots)
    chosen = (slot == source * slots + within % slots).astype(jnp.bfloat16)
    owner = jnp.dot(owner.astype(jnp.bfloat16), chosen, preferred_element_type=jnp.float32)
    odd = within >= slots
    owner = jnp.concatenate([jnp.where(odd, 0.0, owner), jnp.where(odd, owner, 0.0)], axis=0)

    seqs = lengths.shape[1]
    seq_length = tokens // seqs
    position = lax.broadcasted_iota(jnp.int32, (tokens, 1), 0)
    live_until = jnp.zeros((tokens, 1), jnp.int32)
    for seq in range(seqs):
        inside = (position >= seq * seq_length) & (position < (seq + 1) * seq_length)
        until = lengths[:, seq : seq + 1] + seq * seq_length
        live_until = jnp.where(inside, until, live_until)
    live = (position < live_until).astype(jnp.float32)
    count = jnp.sum(live, axis=0, keepdims=True)
    entry = (column_of(ids) - first_entry).astype(jnp.float32)
    lane = lax.broadcasted_iota(jnp.int32, (tokens, LANES), 1)
    return owner.astype(jnp.bfloat16), jnp.where(lane == 0, entry, live / count)


def pack_kernel(place_ref, *refs, shard_rows):
    outside, refs = refs[:6], refs[6:]
    packed_ref, owner_ref, table_ref = refs[:3]
    inside, wide_ref, sems = refs[3:9], refs[9], refs[10]
    copies = [
        pltpu.make_async_copy(source, target, sems.at[i])
        for i, (source, target) in enumerate(zip(outside, inside))
    ]
    for copy in copies:
        copy.start()
    for copy in copies:
        copy.wait()
    hidden_ref, values_ref, scales_ref, ids_ref, map_ref, lengths_ref = inside
    owner_ref[...], table_ref[...] = token_facts(
        ids_ref[...], map_ref[...], lengths_ref[...], place_ref[0] * shard_rows, values_ref.shape[0]
    )
    chips = packed_ref.shape[0]
    tokens, half = hidden_ref.shape
    slots, entries = values_ref.shape
    pair = entries // chips
    shard = pair // 2
    blocks = pair // BLOCK
    scales = jnp.concatenate([scales_ref[...]] * 2, axis=0)
    stacked = jnp.concatenate(
        [scales[:, blocks * chip : blocks * (chip + 1)] for chip in range(chips)], axis=0
    )
    block = lax.broadcasted_iota(jnp.int32, (blocks, pair), 0)
    entry = lax.broadcasted_iota(jnp.int32, (blocks, pair), 1)
    inside = (entry >= block * BLOCK) & (entry < block * BLOCK + BLOCK)
    spread = jnp.dot(
        stacked.astype(jnp.bfloat16),
        inside.astype(jnp.bfloat16),
        preferred_element_type=jnp.float32,
    )
    values = values_ref[...].astype(jnp.float32)
    values = jnp.concatenate([values, values], axis=0)
    for chip in range(chips):
        wide_ref[:, pair * chip : pair * (chip + 1)] = (
            values[:, pair * chip : pair * (chip + 1)]
            * spread[2 * slots * chip : 2 * slots * (chip + 1)]
        )
    wide_ref[:, entries:] = jnp.zeros((2 * slots, LANES), jnp.float32)

    hidden = hidden_ref[...].astype(jnp.float32)
    zeros = jnp.zeros((tokens, LANES // 2), jnp.float32)
    tiles = tiles_of(jnp.concatenate([hidden, zeros], axis=1), 3)
    turns = [turned(tile) for tile in tiles]
    low = low_lanes(tiles[0].shape)
    first = place_ref[0] % 2 == 0
    hidden = jnp.concatenate(
        [
            jnp.where(first, tiles[0], jnp.where(low, turns[0], turns[1])),
            jnp.where(first, tiles[1], jnp.where(low, turns[1], turns[2])),
            folded(first, jnp.where(first, tiles[2], turns[0])),
        ],
        axis=0,
    ).astype(jnp.bfloat16)
    hidden_rows = hidden.shape[0]
    upper = low_rows((2 * slots, LANES), slots)
    low = low_lanes((2 * slots, LANES))
    tile_pairs = (shard + LANES // 2) // LANES // 2
    for chip in range(chips):
        rows = []
        for core in range(2):
            start = pair * chip + (shard - LANES // 2) * core
            tiles = [
                wide_ref[:, start + LANES * i : start + LANES * (i + 1)]
                for i in range(2 * tile_pairs + core)
            ]
            if core == 1:
                tiles = [turned(tile) for tile in tiles]
                tiles = [
                    jnp.where(low, tiles[i], tiles[i + 1]) for i in range(2 * tile_pairs)
                ]
            rows += [
                jnp.where(upper, tiles[2 * i], tiles[2 * i + 1]) for i in range(tile_pairs)
            ]
        step = lax.rem(chip - place_ref[0] // 2 + chips, chips)
        packed_ref[step, :hidden_rows] = hidden
        packed_ref[step, hidden_rows:] = jnp.concatenate(rows, axis=0).astype(jnp.bfloat16)


def head_copy(head_ref, held_ref, sems, chip, step):
    width = held_ref.shape[2]
    columns = pl.ds(pl.multiple_of(chip * width, LANES), width)
    return pltpu.make_async_copy(head_ref.at[:, columns], held_ref.at[step], sems.at[step])


def stream(chip_at, count, head_ref, held_ref, sems, use):
    def copy(step):
        return head_copy(head_ref, held_ref, sems, chip_at(step), step)

    def body(step, _):
        copy(step).wait()

        @pl.when(step + AHEAD < count)
        def _():
            copy(step + AHEAD).start()

        use(step)

    for step in range(min(AHEAD, count)):
        copy(step).start()
    return lambda: lax.fori_loop(0, count, body, None)


def source_chip(place_ref, chips, step):
    return lax.rem(place_ref[0] // 2 - step + chips, chips)


def preload_kernel(place_ref, head_ref, _, early_ref, sems, *, chips):
    copies = [
        head_copy(head_ref, early_ref, sems, source_chip(place_ref, chips, step), step)
        for step in range(EARLY)
    ]
    for copy in copies:
        copy.start()
    for copy in copies:
        copy.wait()


def logits_kernel(
    place_ref,
    first_ref,
    last_ref,
    first_far_ref,
    last_far_ref,
    owner_ref,
    tokens_ref,
    early_ref,
    head_ref,
    rows_ref,
    stats_ref,
    own_ref,
    held_ref,
    made_ref,
    hidden_ref,
    arrived_ref,
    teacher_ref,
    logits_ref,
    sems,
    made_sem,
):
    core = place_ref[0] % 2
    chips, tokens, width = hidden_ref.shape
    shard_rows = head_ref.shape[0]
    hidden_rows = 5 * tokens // 2
    slots = tokens // (2 * chips)
    low = low_lanes((tokens // 2, LANES))

    def add(step, columns):
        logits_ref[...] += lax.dot_general(
            hidden_ref[step], columns, (((1,), (1,)), ((), ())), preferred_element_type=jnp.float32
        )

    run = stream(
        lambda step: source_chip(place_ref, chips, step + EARLY),
        chips - EARLY,
        head_ref,
        held_ref,
        sems,
        lambda step: add(step + EARLY, held_ref[step]),
    )

    def unpack(near_ref, far_ref, base):
        def body(place, _):
            step = place + base
            blocks = near_ref.at[place], far_ref.at[place]
            for block, parity in zip(blocks, (core, 1 - core)):
                for i in range(2):
                    column = LANES * i + (width - 2 * LANES) * parity
                    lanes = pl.ds(pl.multiple_of(column, LANES), LANES)
                    hidden_ref[step, :, lanes] = block[tokens * i : tokens * (i + 1)]
                teacher = block[hidden_rows:].astype(jnp.float32)
                share = teacher.shape[0] // 2
                teacher = jnp.where(core == 0, teacher[:share], teacher[share:])
                row = 2 * slots * (2 * source_chip(place_ref, chips, step) + parity)
                rows = pl.ds(pl.multiple_of(row, 2 * slots), 2 * slots)
                for i in range(share // (2 * slots)):
                    arrived_ref[rows, LANES * i : LANES * (i + 1)] = teacher[
                        2 * slots * i : 2 * slots * (i + 1)
                    ]
            own, other = [block[2 * tokens : hidden_rows].astype(jnp.float32) for block in blocks]
            one, two = jnp.where(core == 0, own, other), jnp.where(core == 0, other, own)
            tile = [jnp.where(low, one, two), turned(jnp.where(low, two, one))]
            tile = jnp.concatenate(tile, axis=0).astype(jnp.bfloat16)
            hidden_ref[step, :, 2 * LANES : 3 * LANES] = tile

        lax.fori_loop(0, near_ref.shape[0], body, None)

    unpack(first_ref, first_far_ref, 0)
    unpack(last_ref, last_far_ref, first_ref.shape[0])
    logits_ref[...] = jnp.zeros_like(logits_ref)
    lax.fori_loop(0, EARLY, lambda step, _: add(step, early_ref[step]), None)
    placed = jnp.dot(
        owner_ref[...], arrived_ref[...].astype(jnp.bfloat16), preferred_element_type=jnp.float32
    )
    pairs = arrived_ref.shape[1] // LANES
    even, odd = tiles_of(placed[:tokens], pairs), tiles_of(placed[tokens:], pairs)
    teacher = jnp.concatenate([tile for pair in zip(even, odd) for tile in pair], axis=1)
    teacher = teacher[:, :shard_rows]
    teacher_top = jnp.max(teacher, axis=1, keepdims=True)
    teacher_off = teacher - teacher_top
    teacher_total = jnp.sum(jnp.exp(teacher_off), axis=1, keepdims=True)
    teacher_ref[...] = teacher_off
    run()
    logits = logits_ref[...]

    top = jnp.max(logits, axis=1, keepdims=True)
    off = logits - top
    exps = jnp.exp(off)
    total = jnp.sum(exps, axis=1, keepdims=True)
    gap = off - teacher_ref[...]
    cross = jnp.sum(exps * gap, axis=1, keepdims=True)
    centre = cross / total
    entry = lax.broadcasted_iota(jnp.int32, (tokens, shard_rows), 1)
    hit = entry == tokens_ref[:, :1].astype(jnp.int32)
    target = jnp.sum(jnp.where(hit, logits, 0.0), axis=1, keepdims=True)
    made_ref[:tokens] = (exps * (gap - centre)).astype(jnp.bfloat16)
    made_ref[tokens : 2 * tokens] = exps.astype(jnp.bfloat16)
    made_ref[2 * tokens :] = hit.astype(jnp.bfloat16)
    out = pltpu.make_async_copy(made_ref, rows_ref, made_sem)
    out.start()

    lane = lax.broadcasted_iota(jnp.int32, (tokens, LANES), 1)
    table = jnp.zeros((tokens, LANES), jnp.float32)
    for place, column in enumerate(
        (top, total, teacher_top, teacher_total, cross, target, centre)
    ):
        table = jnp.where(lane == place, column, table)
    stats = jnp.concatenate([table, jnp.zeros((stats_ref.shape[2] - tokens, LANES), jnp.float32)])
    stats = stats.T[:STATS]
    own_ref[...] = stats
    stats_ref[...] = jnp.broadcast_to(stats[None], stats_ref.shape)
    out.wait()


def products_kernel(
    place_ref, rows_ref, head_ref, terms_ref, picks_ref, held_ref, made_ref, sems, made_sem
):
    into = pltpu.make_async_copy(rows_ref, made_ref, made_sem)
    into.start()
    chips = terms_ref.shape[0]
    tokens = made_ref.shape[0] // 3
    width = held_ref.shape[2]

    def multiply(step):
        products = jnp.dot(made_ref[...], held_ref[step], preferred_element_type=jnp.float32)
        for i, tile in enumerate(tiles_of(products, width // LANES)):
            terms_ref[step, i, 0] = tile[:tokens]
            terms_ref[step, i, 1] = tile[tokens : 2 * tokens]
            picks_ref[step, i] = tile[2 * tokens :].astype(jnp.bfloat16)

    run = stream(
        lambda step: lax.rem(place_ref[0] // 2 + step, chips),
        chips,
        head_ref,
        held_ref,
        sems,
        multiply,
    )
    into.wait()
    run()


def put_shares(parity, factors_ref, terms_ref, picks_ref, out_ref):
    tokens = terms_ref.shape[3]
    factor, level, weight = [factors_ref[i] for i in range(3)]

    def put(step, _):
        for i, tile in enumerate((3 * parity, 3 * parity + 1, 2)):
            sums = terms_ref[step, tile, 0] + level * terms_ref[step, tile, 1]
            share = factor * sums - weight * picks_ref[step, tile].astype(jnp.float32)
            if i == 2:
                share = folded(parity == 0, share)
            out_ref[step, tokens * i : tokens * i + share.shape[0]] = share.astype(out_ref.dtype)

    lax.fori_loop(0, terms_ref.shape[0], put, None)


def give_kernel(
    place_ref,
    scale_ref,
    stats_ref,
    own_ref,
    tokens_ref,
    terms_ref,
    picks_ref,
    give_ref,
    factors_ref,
    loss_ref,
):
    tokens = tokens_ref.shape[0]
    tops, sums, teacher_tops, teacher_sums, crosses, targets = [
        stats_ref[:, i, :tokens] for i in range(6)
    ]
    top, total, teacher_top, teacher_total, cross = [
        part[None] for part in merge_stats(tops, sums, teacher_tops, teacher_sums, crosses)
    ]
    target = jnp.sum(targets, axis=0, keepdims=True)
    student_log = jnp.log(total)
    teacher_log = jnp.log(teacher_total)
    divergence = cross / total - (student_log - teacher_log)
    student_lse = top + student_log
    per_token = divergence + sample_weight * (student_lse - target)
    student_shift = own_ref[0:1, :tokens] - top - student_log
    teacher_shift = own_ref[2:3, :tokens] - teacher_top - teacher_log
    factor = jnp.exp(student_shift)
    level = (
        own_ref[6:7, :tokens] + student_shift - teacher_shift - divergence + sample_weight
    )
    zeros = jnp.zeros((LANES - 3, tokens), jnp.float32)
    columns = jnp.concatenate([factor, level, per_token, zeros], axis=0).T
    share = tokens_ref[:, 1:2]
    weight = share * scale_ref[0]
    loss_ref[...] = jnp.sum(share * columns[:, 2:3], axis=0, keepdims=True)
    for i, column in enumerate(
        (weight * columns[:, 0:1], columns[:, 1:2], sample_weight * weight)
    ):
        factors_ref[i] = jnp.broadcast_to(column, (tokens, LANES))
    put_shares(1 - place_ref[0] % 2, factors_ref, terms_ref, picks_ref, give_ref)


def keep_kernel(place_ref, factors_ref, found_ref, terms_ref, picks_ref, keep_ref, loss_ref):
    loss_ref[...] = found_ref[...]
    put_shares(place_ref[0] % 2, factors_ref, terms_ref, picks_ref, keep_ref)


def sum_kernel(place_ref, own_ref, *refs):
    tokens, half = refs[-1].shape
    total = own_ref[...]
    for share_ref in refs[:-1]:
        total += share_ref[...].astype(jnp.float32)
    one, two, rest = total[:tokens], total[tokens : 2 * tokens], total[2 * tokens :]
    rest = jnp.concatenate([rest, turned(rest)], axis=0)
    turns = [turned(tile) for tile in (rest, one, two)]
    low = low_lanes(one.shape)
    first = place_ref[0] % 2 == 0
    tiles = [
        jnp.where(first, one, jnp.where(low, turns[0], turns[1])),
        jnp.where(first, two, jnp.where(low, turns[1], turns[2])),
        jnp.where(first, rest, turns[2]),
    ]
    total = jnp.concatenate(tiles, axis=1)[:, :half]
    refs[-1][...] = total.astype(refs[-1].dtype)


def paired_shards(
    hidden_states, head, teacher_values, teacher_scales, token_ids, lengths, row_map, loss_scale
):
    count = lax.axis_size("vocab")
    own_index = lax.axis_index("vocab")
    chips = count // 2
    tokens, half = hidden_states.shape
    width = 2 * half
    shard_rows = head.shape[0]
    place = jnp.reshape(own_index, (1,))
    vmem = pl.BlockSpec(memory_space=pltpu.VMEM)
    smem = pl.BlockSpec(memory_space=pltpu.SMEM)
    hbm = pl.BlockSpec(memory_space=pl.ANY)
    params = pltpu.CompilerParams(vmem_limit_bytes=VMEM_LIMIT)
    head = in_hbm(head)
    head_scratch = pltpu.VMEM((chips, shard_rows, width), head.dtype)
    head_sems = pltpu.SemaphoreType.DMA((chips,))
    rows_scratch = pltpu.VMEM((3 * tokens, shard_rows), jnp.bfloat16)
    rows_sem = pltpu.SemaphoreType.DMA
    slots, entries = teacher_values.shape
    hidden_rows = 5 * tokens // 2
    teacher_rows = 2 * slots * (shard_rows + LANES // 2) // LANES

    operands = (
        hidden_states,
        teacher_values,
        teacher_scales,
        token_ids[None, :],
        row_map[None, :],
        lengths[None, :],
    )
    packed, owner, table = pl.pallas_call(
        functools.partial(pack_kernel, shard_rows=shard_rows),
        out_shape=(
            vmem_array((chips, hidden_rows + teacher_rows, LANES), jnp.bfloat16),
            vmem_array((2 * tokens, 2 * tokens), jnp.bfloat16),
            vmem_array((tokens, LANES), jnp.float32),
        ),
        in_specs=[smem] + [hbm] * len(operands),
        out_specs=[vmem] * 3,
        scratch_shapes=[pltpu.VMEM(operand.shape, operand.dtype) for operand in operands]
        + [
            pltpu.VMEM((2 * slots, entries + LANES), jnp.float32),
            pltpu.SemaphoreType.DMA((len(operands),)),
        ],
        compiler_params=params,
        name="pack",
    )(place, *[in_hbm(operand) for operand in operands])
    steps = range(1, chips)
    near = [packed[0]] + [along_chips(packed[step], step) for step in steps]
    first, last = jnp.stack(near[: chips // 2 + 1]), jnp.stack(near[chips // 2 + 1 :])
    early = pl.pallas_call(
        functools.partial(preload_kernel, chips=chips),
        out_shape=vmem_array((EARLY, shard_rows, width), head.dtype),
        in_specs=[smem] + [hbm] * 2,
        out_specs=vmem,
        scratch_shapes=[pltpu.SemaphoreType.DMA((EARLY,))],
        compiler_params=params,
        cost_estimate=pl.CostEstimate(
            flops=0, bytes_accessed=4 * EARLY * shard_rows * width, transcendentals=0
        ),
        name="preload",
    )(place, head, near[3])
    last, early = lax.optimization_barrier((last, early))
    far = [swap_cores(last), swap_cores(first)]

    rows, stats, own_stats = pl.pallas_call(
        logits_kernel,
        out_shape=(
            hbm_array((3 * tokens, shard_rows), jnp.bfloat16),
            jax.ShapeDtypeStruct((count, STATS, pl.cdiv(tokens, LANES) * LANES), jnp.float32),
            vmem_array((STATS, pl.cdiv(tokens, LANES) * LANES), jnp.float32),
        ),
        in_specs=[smem] + [vmem] * 7 + [hbm],
        out_specs=[hbm, vmem, vmem],
        scratch_shapes=[
            pltpu.VMEM((chips - EARLY, shard_rows, width), head.dtype),
            rows_scratch,
            pltpu.VMEM((chips, tokens, width), jnp.bfloat16),
            pltpu.VMEM((2 * tokens, (shard_rows + LANES // 2) // 2), jnp.float32),
            pltpu.VMEM((tokens, shard_rows), jnp.float32),
            pltpu.VMEM((tokens, shard_rows), jnp.float32),
            pltpu.SemaphoreType.DMA((chips - EARLY,)),
            rows_sem,
        ],
        compiler_params=params,
        cost_estimate=pl.CostEstimate(
            flops=2 * tokens * head.size, bytes_accessed=2 * head.size, transcendentals=0
        ),
        name="logits",
    )(
        place,
        *[in_vmem(blocks) for blocks in (first, last, far[1], far[0])],
        in_vmem(owner),
        in_vmem(table),
        in_vmem(early),
        head,
    )

    all_stats = lax.all_to_all(stats, "vocab", split_axis=0, concat_axis=0, tiled=True)

    terms, picks = pl.pallas_call(
        products_kernel,
        out_shape=(
            vmem_array((chips, width // LANES, 2, tokens, LANES), jnp.float32),
            vmem_array((chips, width // LANES, tokens, LANES), jnp.bfloat16),
        ),
        in_specs=[smem, hbm, hbm],
        out_specs=[vmem] * 2,
        scratch_shapes=[head_scratch, rows_scratch, head_sems, rows_sem],
        compiler_params=params,
        cost_estimate=pl.CostEstimate(
            flops=6 * tokens * head.size, bytes_accessed=2 * head.size, transcendentals=0
        ),
        name="products",
    )(place, in_hbm(rows), head)

    terms, picks = in_vmem(terms), in_vmem(picks)
    give, factors, loss = pl.pallas_call(
        give_kernel,
        out_shape=(
            vmem_array((chips, hidden_rows, LANES), jnp.bfloat16),
            vmem_array((3, tokens, LANES), jnp.float32),
            vmem_array((1, 1), jnp.float32),
        ),
        in_specs=[smem] * 2 + [vmem] * 5,
        out_specs=[vmem] * 3,
        compiler_params=params,
        name="give",
    )(place, loss_scale, in_vmem(all_stats), in_vmem(own_stats), in_vmem(table), terms, picks)
    taken = swap_cores(give)
    keep, loss = pl.pallas_call(
        keep_kernel,
        out_shape=(
            vmem_array((chips, hidden_rows, LANES), jnp.float32),
            jax.ShapeDtypeStruct((1, 1), jnp.float32),
        ),
        in_specs=[smem] + [vmem] * 4,
        out_specs=[vmem] * 2,
        compiler_params=params,
        cost_estimate=pl.CostEstimate(
            flops=4 * terms.size, bytes_accessed=4 * terms.size, transcendentals=0
        ),
        name="keep",
    )(place, in_vmem(factors), in_vmem(loss), terms, picks)
    sums = keep + taken.astype(jnp.float32)
    shares = [along_chips(sums[step].astype(jnp.bfloat16), step) for step in steps]
    total = pl.pallas_call(
        sum_kernel,
        out_shape=jax.ShapeDtypeStruct((tokens, half), jnp.bfloat16),
        in_specs=[smem] + [vmem] * chips,
        out_specs=vmem,
        compiler_params=params,
        name="total",
    )(place, *[in_vmem(share) for share in [sums[0]] + shares])
    return total, jnp.reshape(loss, (1,))


VMEM_LIMIT = 24 * 1024 * 1024


def shards(
    hidden_states, head, teacher_values, teacher_scales, token_ids, lengths, row_map, loss_scale
):
    count = lax.axis_size("vocab")
    own_index = lax.axis_index("vocab")
    tokens = hidden_states.shape[0]
    own_features = hidden_states.shape[1]
    shard_rows = head.shape[0]
    seq_length = tokens // lengths.shape[0]
    contract_last = (((1,), (1,)), ((), ()))

    scaled = scaled_teacher(teacher_values, teacher_scales, count, shard_rows)
    arrived = lax.all_to_all(scaled, "vocab", split_axis=0, concat_axis=0, tiled=True)
    arrived = arrived.reshape(tokens, shard_rows)
    gathered = to_all(hidden_states, count).transpose(1, 0, 2).reshape(tokens, -1)
    logits = lax.dot_general(gathered, head, contract_last, preferred_element_type=jnp.float32)

    positions = jnp.arange(tokens, dtype=jnp.int32)
    owner = row_map[None, :] == positions[:, None]
    slot_of = jnp.sum(jnp.where(owner, positions[None, :], 0), axis=1)
    teacher = jnp.take(arrived, slot_of, axis=0).astype(jnp.float32)

    seq_ids = jnp.arange(lengths.shape[0], dtype=jnp.int32)
    own_length = jnp.sum(
        jnp.where((positions // seq_length)[:, None] == seq_ids[None, :], lengths[None, :], 0),
        axis=1,
    )
    live_mask = (positions % seq_length < own_length).astype(jnp.float32)
    live_count = jnp.sum(live_mask)

    local_ids = token_ids - own_index * shard_rows
    target_hit = local_ids[:, None] == jnp.arange(shard_rows, dtype=jnp.int32)[None, :]
    target_part = jnp.sum(jnp.where(target_hit, logits, 0.0), axis=1)
    student_top = jnp.max(logits, axis=1)
    teacher_top = jnp.max(teacher, axis=1)
    student_off = logits - student_top[:, None]
    teacher_off = teacher - teacher_top[:, None]
    student_exp = jnp.exp(student_off)
    student_sum = jnp.sum(student_exp, axis=1)
    teacher_sum = jnp.sum(jnp.exp(teacher_off), axis=1)
    cross_sum = jnp.sum(student_exp * (student_off - teacher_off), axis=1)

    stats = to_all(
        jnp.stack(
            [student_top, student_sum, teacher_top, teacher_sum, cross_sum, target_part]
        ),
        count,
    )
    tops, sums, teacher_tops, teacher_sums, crosses, targets = [stats[:, i] for i in range(6)]
    student_max, student_total, teacher_max, teacher_total, cross_total = merge_stats(
        tops, sums, teacher_tops, teacher_sums, crosses
    )
    student_log = jnp.log(student_total)
    teacher_log = jnp.log(teacher_total)
    student_lse = student_max + student_log
    teacher_lse = teacher_max + teacher_log
    divergence = cross_total / student_total - (student_log - teacher_log)
    target = jnp.sum(targets, axis=0)

    per_token = divergence + sample_weight * (student_lse - target)
    loss = jnp.reshape(jnp.sum(live_mask * per_token) / live_count, (1,))
    token_weight = live_mask * loss_scale[0] / live_count
    log_student = logits - student_lse[:, None]
    log_teacher = teacher - teacher_lse[:, None]
    student_prob = jnp.exp(log_student)
    grad_logits = (
        token_weight[:, None]
        * (
            student_prob * (log_student - log_teacher - divergence[:, None])
            + sample_weight * (student_prob - target_hit.astype(jnp.float32))
        )
    ).astype(jnp.bfloat16)
    terms = jnp.dot(grad_logits, head, preferred_element_type=jnp.float32).astype(jnp.bfloat16)
    terms = terms.reshape(tokens, count, own_features).transpose(1, 0, 2)
    shares = lax.all_to_all(terms, "vocab", split_axis=0, concat_axis=0, tiled=True)
    grad_hidden = jnp.sum(shares.astype(jnp.float32), axis=0)
    return (grad_hidden.astype(jnp.bfloat16), loss)


def any_shards(*arrays):
    hidden_states, head, teacher_values = arrays[:3]
    count = lax.axis_size("vocab")
    fits = (
        count % 2 == 0
        and hidden_states.shape[1] == 5 * LANES // 2
        and hidden_states.shape[0] % 32 == 0
        and head.shape[0] % LANES == LANES // 2
        and (head.shape[0] + LANES // 2) // LANES % 2 == 0
        and teacher_values.shape[0] == 4
    )
    return paired_shards(*arrays) if fits else shards(*arrays)


def solution(mesh):
    in_specs = (
        P("dom", "vocab"),
        P("vocab", None),
        P(("dom", "vocab"), None),
        P(("dom", "vocab"), None),
        P("dom"),
        P("dom"),
        P("dom"),
        P(),
    )
    out_specs = (P("dom", "vocab"), P("dom"))
    return jax.shard_map(
        any_shards, mesh=mesh, in_specs=in_specs, out_specs=out_specs, check_vma=False
    )
```

```python
import functools

import jax
import jax.numpy as jnp
from jax import lax
from jax.experimental import pallas as pl
from jax.experimental.pallas import tpu as pltpu
from jax.sharding import PartitionSpec as P

BLOCK = 32
LANES = 128
STATS = 8
AHEAD = 3
EARLY = 3


sample_weight = 0.5


def to_all(piece, count):
    copies = jnp.broadcast_to(piece[None], (count,) + piece.shape)
    return lax.all_to_all(copies, "vocab", split_axis=0, concat_axis=0, tiled=True)


def scaled_teacher(teacher_values, teacher_scales, count, shard_rows):
    slot_rows = teacher_values.shape[0]
    scaled = (
        teacher_values.astype(jnp.float32).reshape(slot_rows, -1, BLOCK) * teacher_scales[:, :, None]
    ).astype(jnp.bfloat16)
    return scaled.reshape(slot_rows, count, shard_rows).transpose(1, 0, 2)


def merge_stats(tops, sums, teacher_tops, teacher_sums, crosses):
    top = jnp.max(tops, axis=0)
    teacher_top = jnp.max(teacher_tops, axis=0)
    shift = tops - top[None]
    teacher_shift = teacher_tops - teacher_top[None]
    weight = jnp.exp(shift)
    total = jnp.sum(sums * weight, axis=0)
    teacher_total = jnp.sum(teacher_sums * jnp.exp(teacher_shift), axis=0)
    cross = jnp.sum(weight * (crosses + sums * (shift - teacher_shift)), axis=0)
    return top, total, teacher_top, teacher_total, cross


def swap_cores(array):
    count = lax.axis_size("vocab")
    return lax.ppermute(array, "vocab", [(i, i ^ 1) for i in range(count)])


def along_chips(array, step):
    count = lax.axis_size("vocab")
    return lax.ppermute(array, "vocab", [(i, (i + 2 * step) % count) for i in range(count)])


def vmem_array(shape, dtype):
    return pltpu.VMEM(shape, dtype)


def in_vmem(array):
    return pltpu.with_memory_space_constraint(array, pltpu.VMEM)


def in_hbm(array):
    return pltpu.with_memory_space_constraint(array, pltpu.HBM)


def hbm_array(shape, dtype):
    return pltpu.HBM(shape, dtype)


def low_lanes(shape):
    return lax.broadcasted_iota(jnp.int32, shape, len(shape) - 1) < LANES // 2


def low_rows(shape, count):
    return lax.broadcasted_iota(jnp.int32, shape, 0) < count


def turned(array):
    return pltpu.roll(array, LANES // 2, 1)


def folded(first, tile):
    rows = tile.shape[0] // 2
    upper, lower = tile[:rows], turned(tile[rows:])
    low = low_lanes(upper.shape)
    return jnp.where(first, jnp.where(low, upper, lower), jnp.where(low, lower, upper))


def tiles_of(array, count):
    return [array[:, LANES * i : LANES * (i + 1)] for i in range(count)]


def column_of(row):
    size = row.shape[1]
    down = lax.broadcasted_iota(jnp.int32, (size, size), 0)
    along = lax.broadcasted_iota(jnp.int32, (size, size), 1)
    return jnp.sum(jnp.where(down == along, row, jnp.zeros_like(row)), axis=1, keepdims=True)


def token_facts(ids, row_map, lengths, first_entry, slots):
    tokens = row_map.shape[1]
    token = lax.broadcasted_iota(jnp.int32, (tokens, tokens), 0)
    slot = lax.broadcasted_iota(jnp.int32, (tokens, tokens), 1)
    owner = (row_map == token).astype(jnp.float32)
    named = jnp.max(owner, axis=1, keepdims=True)
    owner = jnp.where((slot == 0) & (named == 0.0), 1.0, owner)
    rows = 2 * tokens
    slot = lax.broadcasted_iota(jnp.int32, (tokens, rows), 0)
    row = lax.broadcasted_iota(jnp.int32, (tokens, rows), 1)
    source, within = row // (2 * slots), row % (2 * slots)
    chosen = (slot == source * slots + within % slots).astype(jnp.bfloat16)
    owner = jnp.dot(owner.astype(jnp.bfloat16), chosen, preferred_element_type=jnp.float32)
    odd = within >= slots
    owner = jnp.concatenate([jnp.where(odd, 0.0, owner), jnp.where(odd, owner, 0.0)], axis=0)

    seqs = lengths.shape[1]
    seq_length = tokens // seqs
    position = lax.broadcasted_iota(jnp.int32, (tokens, 1), 0)
    live_until = jnp.zeros((tokens, 1), jnp.int32)
    for seq in range(seqs):
        inside = (position >= seq * seq_length) & (position < (seq + 1) * seq_length)
        until = lengths[:, seq : seq + 1] + seq * seq_length
        live_until = jnp.where(inside, until, live_until)
    live = (position < live_until).astype(jnp.float32)
    count = jnp.sum(live, axis=0, keepdims=True)
    entry = (column_of(ids) - first_entry).astype(jnp.float32)
    lane = lax.broadcasted_iota(jnp.int32, (tokens, LANES), 1)
    return owner.astype(jnp.bfloat16), jnp.where(lane == 0, entry, live / count)


def pack_kernel(place_ref, *refs, shard_rows):
    outside, refs = refs[:6], refs[6:]
    packed_ref, owner_ref, table_ref = refs[:3]
    inside, wide_ref, sems = refs[3:9], refs[9], refs[10]
    copies = [
        pltpu.make_async_copy(source, target, sems.at[i])
        for i, (source, target) in enumerate(zip(outside, inside))
    ]
    for copy in copies:
        copy.start()
    for copy in copies:
        copy.wait()
    hidden_ref, values_ref, scales_ref, ids_ref, map_ref, lengths_ref = inside
    owner_ref[...], table_ref[...] = token_facts(
        ids_ref[...], map_ref[...], lengths_ref[...], place_ref[0] * shard_rows, values_ref.shape[0]
    )
    chips = packed_ref.shape[0]
    tokens, half = hidden_ref.shape
    slots, entries = values_ref.shape
    pair = entries // chips
    shard = pair // 2
    blocks = pair // BLOCK
    scales = jnp.concatenate([scales_ref[...]] * 2, axis=0)
    stacked = jnp.concatenate(
        [scales[:, blocks * chip : blocks * (chip + 1)] for chip in range(chips)], axis=0
    )
    block = lax.broadcasted_iota(jnp.int32, (blocks, pair), 0)
    entry = lax.broadcasted_iota(jnp.int32, (blocks, pair), 1)
    inside = (entry >= block * BLOCK) & (entry < block * BLOCK + BLOCK)
    spread = jnp.dot(
        stacked.astype(jnp.bfloat16),
        inside.astype(jnp.bfloat16),
        preferred_element_type=jnp.float32,
    )
    values = values_ref[...].astype(jnp.float32)
    values = jnp.concatenate([values, values], axis=0)
    for chip in range(chips):
        wide_ref[:, pair * chip : pair * (chip + 1)] = (
            values[:, pair * chip : pair * (chip + 1)]
            * spread[2 * slots * chip : 2 * slots * (chip + 1)]
        )
    wide_ref[:, entries:] = jnp.zeros((2 * slots, LANES), jnp.float32)

    hidden = hidden_ref[...].astype(jnp.float32)
    zeros = jnp.zeros((tokens, LANES // 2), jnp.float32)
    tiles = tiles_of(jnp.concatenate([hidden, zeros], axis=1), 3)
    turns = [turned(tile) for tile in tiles]
    low = low_lanes(tiles[0].shape)
    first = place_ref[0] % 2 == 0
    hidden = jnp.concatenate(
        [
            jnp.where(first, tiles[0], jnp.where(low, turns[0], turns[1])),
            jnp.where(first, tiles[1], jnp.where(low, turns[1], turns[2])),
            folded(first, jnp.where(first, tiles[2], turns[0])),
        ],
        axis=0,
    ).astype(jnp.bfloat16)
    hidden_rows = hidden.shape[0]
    upper = low_rows((2 * slots, LANES), slots)
    low = low_lanes((2 * slots, LANES))
    tile_pairs = (shard + LANES // 2) // LANES // 2
    for chip in range(chips):
        rows = []
        for core in range(2):
            start = pair * chip + (shard - LANES // 2) * core
            tiles = [
                wide_ref[:, start + LANES * i : start + LANES * (i + 1)]
                for i in range(2 * tile_pairs + core)
            ]
            if core == 1:
                tiles = [turned(tile) for tile in tiles]
                tiles = [
                    jnp.where(low, tiles[i], tiles[i + 1]) for i in range(2 * tile_pairs)
                ]
            rows += [
                jnp.where(upper, tiles[2 * i], tiles[2 * i + 1]) for i in range(tile_pairs)
            ]
        step = lax.rem(chip - place_ref[0] // 2 + chips, chips)
        packed_ref[step, :hidden_rows] = hidden
        packed_ref[step, hidden_rows:] = jnp.concatenate(rows, axis=0).astype(jnp.bfloat16)


def head_copy(head_ref, held_ref, sems, chip, step):
    width = held_ref.shape[2]
    columns = pl.ds(pl.multiple_of(chip * width, LANES), width)
    return pltpu.make_async_copy(head_ref.at[:, columns], held_ref.at[step], sems.at[step])


def stream(chip_at, count, head_ref, held_ref, sems, use):
    def copy(step):
        return head_copy(head_ref, held_ref, sems, chip_at(step), step)

    def body(step, _):
        copy(step).wait()

        @pl.when(step + AHEAD < count)
        def _():
            copy(step + AHEAD).start()

        use(step)

    for step in range(min(AHEAD, count)):
        copy(step).start()
    return lambda: lax.fori_loop(0, count, body, None)


def source_chip(place_ref, chips, step):
    return lax.rem(place_ref[0] // 2 - step + chips, chips)


def preload_kernel(place_ref, head_ref, _, early_ref, sems, *, chips):
    copies = [
        head_copy(head_ref, early_ref, sems, source_chip(place_ref, chips, step), step)
        for step in range(EARLY)
    ]
    for copy in copies:
        copy.start()
    for copy in copies:
        copy.wait()


def logits_kernel(
    place_ref,
    first_ref,
    last_ref,
    first_far_ref,
    last_far_ref,
    owner_ref,
    tokens_ref,
    early_ref,
    head_ref,
    rows_ref,
    stats_ref,
    own_ref,
    held_ref,
    made_ref,
    hidden_ref,
    arrived_ref,
    teacher_ref,
    logits_ref,
    copies_ref,
    sems,
    made_sem,
    stats_sem,
):
    core = place_ref[0] % 2
    chips, tokens, width = hidden_ref.shape
    shard_rows = head_ref.shape[0]
    hidden_rows = 5 * tokens // 2
    slots = tokens // (2 * chips)
    low = low_lanes((tokens // 2, LANES))

    def add(step, columns):
        logits_ref[...] += lax.dot_general(
            hidden_ref[step], columns, (((1,), (1,)), ((), ())), preferred_element_type=jnp.float32
        )

    run = stream(
        lambda step: source_chip(place_ref, chips, step + EARLY),
        chips - EARLY,
        head_ref,
        held_ref,
        sems,
        lambda step: add(step + EARLY, held_ref[step]),
    )

    def unpack(near_ref, far_ref, base):
        def body(place, _):
            step = place + base
            blocks = near_ref.at[place], far_ref.at[place]
            for block, parity in zip(blocks, (core, 1 - core)):
                for i in range(2):
                    column = LANES * i + (width - 2 * LANES) * parity
                    lanes = pl.ds(pl.multiple_of(column, LANES), LANES)
                    hidden_ref[step, :, lanes] = block[tokens * i : tokens * (i + 1)]
                teacher = block[hidden_rows:].astype(jnp.float32)
                share = teacher.shape[0] // 2
                teacher = jnp.where(core == 0, teacher[:share], teacher[share:])
                row = 2 * slots * (2 * source_chip(place_ref, chips, step) + parity)
                rows = pl.ds(pl.multiple_of(row, 2 * slots), 2 * slots)
                for i in range(share // (2 * slots)):
                    arrived_ref[rows, LANES * i : LANES * (i + 1)] = teacher[
                        2 * slots * i : 2 * slots * (i + 1)
                    ]
            own, other = [block[2 * tokens : hidden_rows].astype(jnp.float32) for block in blocks]
            one, two = jnp.where(core == 0, own, other), jnp.where(core == 0, other, own)
            tile = [jnp.where(low, one, two), turned(jnp.where(low, two, one))]
            tile = jnp.concatenate(tile, axis=0).astype(jnp.bfloat16)
            hidden_ref[step, :, 2 * LANES : 3 * LANES] = tile

        lax.fori_loop(0, near_ref.shape[0], body, None)

    unpack(first_ref, first_far_ref, 0)
    unpack(last_ref, last_far_ref, first_ref.shape[0])
    logits_ref[...] = jnp.zeros_like(logits_ref)
    lax.fori_loop(0, EARLY, lambda step, _: add(step, early_ref[step]), None)
    placed = jnp.dot(
        owner_ref[...], arrived_ref[...].astype(jnp.bfloat16), preferred_element_type=jnp.float32
    )
    pairs = arrived_ref.shape[1] // LANES
    even, odd = tiles_of(placed[:tokens], pairs), tiles_of(placed[tokens:], pairs)
    teacher = jnp.concatenate([tile for pair in zip(even, odd) for tile in pair], axis=1)
    teacher = teacher[:, :shard_rows]
    teacher_top = jnp.max(teacher, axis=1, keepdims=True)
    teacher_off = teacher - teacher_top
    teacher_total = jnp.sum(jnp.exp(teacher_off), axis=1, keepdims=True)
    teacher_ref[...] = teacher_off
    run()
    logits = logits_ref[...]

    top = jnp.max(logits, axis=1, keepdims=True)
    off = logits - top
    exps = jnp.exp(off)
    total = jnp.sum(exps, axis=1, keepdims=True)
    gap = off - teacher_ref[...]
    cross = jnp.sum(exps * gap, axis=1, keepdims=True)
    centre = cross / total
    entry = lax.broadcasted_iota(jnp.int32, (tokens, shard_rows), 1)
    hit = entry == tokens_ref[:, :1].astype(jnp.int32)
    target = jnp.sum(jnp.where(hit, logits, 0.0), axis=1, keepdims=True)
    made_ref[:tokens] = (exps * (gap - centre)).astype(jnp.bfloat16)
    made_ref[tokens : 2 * tokens] = exps.astype(jnp.bfloat16)
    made_ref[2 * tokens :] = hit.astype(jnp.bfloat16)
    out = pltpu.make_async_copy(made_ref, rows_ref, made_sem)
    out.start()

    lane = lax.broadcasted_iota(jnp.int32, (tokens, LANES), 1)
    table = jnp.zeros((tokens, LANES), jnp.float32)
    for place, column in enumerate(
        (top, total, teacher_top, teacher_total, cross, target, centre)
    ):
        table = jnp.where(lane == place, column, table)
    stats = jnp.concatenate([table, jnp.zeros((own_ref.shape[1] - tokens, LANES), jnp.float32)])
    stats = stats.T[:STATS]
    own_ref[...] = stats
    copies_ref[...] = jnp.broadcast_to(stats[None], copies_ref.shape)
    out_stats = pltpu.make_async_copy(copies_ref, stats_ref, stats_sem)
    out_stats.start()
    out.wait()
    out_stats.wait()


def products_kernel(
    place_ref, rows_ref, head_ref, terms_ref, picks_ref, held_ref, made_ref, sems, made_sem
):
    into = pltpu.make_async_copy(rows_ref, made_ref, made_sem)
    into.start()
    chips = terms_ref.shape[0]
    tokens = made_ref.shape[0] // 3
    width = held_ref.shape[2]

    def multiply(step):
        products = jnp.dot(made_ref[...], held_ref[step], preferred_element_type=jnp.float32)
        for i, tile in enumerate(tiles_of(products, width // LANES)):
            terms_ref[step, i, 0] = tile[:tokens]
            terms_ref[step, i, 1] = tile[tokens : 2 * tokens]
            picks_ref[step, i] = tile[2 * tokens :].astype(jnp.bfloat16)

    run = stream(
        lambda step: lax.rem(place_ref[0] // 2 + step, chips),
        chips,
        head_ref,
        held_ref,
        sems,
        multiply,
    )
    into.wait()
    run()


def put_shares(parity, factors_ref, terms_ref, picks_ref, out_ref):
    tokens = terms_ref.shape[3]
    factor, level, weight = [factors_ref[i] for i in range(3)]
    for step in range(terms_ref.shape[0]):
        for i, tile in enumerate((3 * parity, 3 * parity + 1, 2)):
            sums = terms_ref[step, tile, 0] + level * terms_ref[step, tile, 1]
            share = factor * sums - weight * picks_ref[step, tile].astype(jnp.float32)
            if i == 2:
                share = folded(parity == 0, share)
            out_ref[step, tokens * i : tokens * i + share.shape[0]] = share.astype(out_ref.dtype)


def give_kernel(
    place_ref,
    scale_ref,
    stats_ref,
    own_ref,
    tokens_ref,
    terms_ref,
    picks_ref,
    give_ref,
    factors_ref,
    loss_ref,
):
    tokens = tokens_ref.shape[0]
    tops, sums, teacher_tops, teacher_sums, crosses, targets = [
        stats_ref[:, i, :tokens] for i in range(6)
    ]
    top, total, teacher_top, teacher_total, cross = [
        part[None] for part in merge_stats(tops, sums, teacher_tops, teacher_sums, crosses)
    ]
    target = jnp.sum(targets, axis=0, keepdims=True)
    student_log = jnp.log(total)
    teacher_log = jnp.log(teacher_total)
    divergence = cross / total - (student_log - teacher_log)
    student_lse = top + student_log
    per_token = divergence + sample_weight * (student_lse - target)
    student_shift = own_ref[0:1, :tokens] - top - student_log
    teacher_shift = own_ref[2:3, :tokens] - teacher_top - teacher_log
    factor = jnp.exp(student_shift)
    level = (
        own_ref[6:7, :tokens] + student_shift - teacher_shift - divergence + sample_weight
    )
    zeros = jnp.zeros((LANES - 3, tokens), jnp.float32)
    columns = jnp.concatenate([factor, level, per_token, zeros], axis=0).T
    share = tokens_ref[:, 1:2]
    weight = share * scale_ref[0]
    loss_ref[...] = jnp.sum(share * columns[:, 2:3], axis=0, keepdims=True)
    for i, column in enumerate(
        (weight * columns[:, 0:1], columns[:, 1:2], sample_weight * weight)
    ):
        factors_ref[i] = jnp.broadcast_to(column, (tokens, LANES))
    put_shares(1 - place_ref[0] % 2, factors_ref, terms_ref, picks_ref, give_ref)


def keep_kernel(place_ref, factors_ref, found_ref, terms_ref, picks_ref, keep_ref, loss_ref):
    loss_ref[...] = found_ref[...]
    put_shares(place_ref[0] % 2, factors_ref, terms_ref, picks_ref, keep_ref)


def sum_kernel(place_ref, own_ref, *refs):
    tokens, half = refs[-1].shape
    total = own_ref[...]
    for share_ref in refs[:-1]:
        total += share_ref[...].astype(jnp.float32)
    one, two, rest = total[:tokens], total[tokens : 2 * tokens], total[2 * tokens :]
    rest = jnp.concatenate([rest, turned(rest)], axis=0)
    turns = [turned(tile) for tile in (rest, one, two)]
    low = low_lanes(one.shape)
    first = place_ref[0] % 2 == 0
    tiles = [
        jnp.where(first, one, jnp.where(low, turns[0], turns[1])),
        jnp.where(first, two, jnp.where(low, turns[1], turns[2])),
        jnp.where(first, rest, turns[2]),
    ]
    total = jnp.concatenate(tiles, axis=1)[:, :half]
    refs[-1][...] = total.astype(refs[-1].dtype)


def paired_shards(
    hidden_states, head, teacher_values, teacher_scales, token_ids, lengths, row_map, loss_scale
):
    count = lax.axis_size("vocab")
    own_index = lax.axis_index("vocab")
    chips = count // 2
    tokens, half = hidden_states.shape
    width = 2 * half
    shard_rows = head.shape[0]
    place = jnp.reshape(own_index, (1,))
    vmem = pl.BlockSpec(memory_space=pltpu.VMEM)
    smem = pl.BlockSpec(memory_space=pltpu.SMEM)
    hbm = pl.BlockSpec(memory_space=pl.ANY)
    params = pltpu.CompilerParams(vmem_limit_bytes=VMEM_LIMIT)
    head = in_hbm(head)
    head_scratch = pltpu.VMEM((chips, shard_rows, width), head.dtype)
    head_sems = pltpu.SemaphoreType.DMA((chips,))
    rows_scratch = pltpu.VMEM((3 * tokens, shard_rows), jnp.bfloat16)
    rows_sem = pltpu.SemaphoreType.DMA
    slots, entries = teacher_values.shape
    hidden_rows = 5 * tokens // 2
    teacher_rows = 2 * slots * (shard_rows + LANES // 2) // LANES

    operands = (
        hidden_states,
        teacher_values,
        teacher_scales,
        token_ids[None, :],
        row_map[None, :],
        lengths[None, :],
    )
    packed, owner, table = pl.pallas_call(
        functools.partial(pack_kernel, shard_rows=shard_rows),
        out_shape=(
            vmem_array((chips, hidden_rows + teacher_rows, LANES), jnp.bfloat16),
            vmem_array((2 * tokens, 2 * tokens), jnp.bfloat16),
            vmem_array((tokens, LANES), jnp.float32),
        ),
        in_specs=[smem] + [hbm] * len(operands),
        out_specs=[vmem] * 3,
        scratch_shapes=[pltpu.VMEM(operand.shape, operand.dtype) for operand in operands]
        + [
            pltpu.VMEM((2 * slots, entries + LANES), jnp.float32),
            pltpu.SemaphoreType.DMA((len(operands),)),
        ],
        compiler_params=params,
        name="pack",
    )(place, *[in_hbm(operand) for operand in operands])
    steps = range(1, chips)
    near = [packed[0]] + [along_chips(packed[step], step) for step in steps]
    first, last = jnp.stack(near[: chips // 2 + 1]), jnp.stack(near[chips // 2 + 1 :])
    early = pl.pallas_call(
        functools.partial(preload_kernel, chips=chips),
        out_shape=vmem_array((EARLY, shard_rows, width), head.dtype),
        in_specs=[smem] + [hbm] * 2,
        out_specs=vmem,
        scratch_shapes=[pltpu.SemaphoreType.DMA((EARLY,))],
        compiler_params=params,
        cost_estimate=pl.CostEstimate(
            flops=0, bytes_accessed=4 * EARLY * shard_rows * width, transcendentals=0
        ),
        name="preload",
    )(place, head, near[3])
    last, early = lax.optimization_barrier((last, early))
    far = [swap_cores(last), swap_cores(first)]

    stats_shape = (count, STATS, pl.cdiv(tokens, LANES) * LANES)
    rows, stats, own_stats = pl.pallas_call(
        logits_kernel,
        out_shape=(
            hbm_array((3 * tokens, shard_rows), jnp.bfloat16),
            hbm_array(stats_shape, jnp.float32),
            vmem_array(stats_shape[1:], jnp.float32),
        ),
        in_specs=[smem] + [vmem] * 7 + [hbm],
        out_specs=[hbm, hbm, vmem],
        scratch_shapes=[
            pltpu.VMEM((chips - EARLY, shard_rows, width), head.dtype),
            rows_scratch,
            pltpu.VMEM((chips, tokens, width), jnp.bfloat16),
            pltpu.VMEM((2 * tokens, (shard_rows + LANES // 2) // 2), jnp.float32),
            pltpu.VMEM((tokens, shard_rows), jnp.float32),
            pltpu.VMEM((tokens, shard_rows), jnp.float32),
            pltpu.VMEM(stats_shape, jnp.float32),
            pltpu.SemaphoreType.DMA((chips - EARLY,)),
            rows_sem,
            rows_sem,
        ],
        compiler_params=params,
        cost_estimate=pl.CostEstimate(
            flops=2 * tokens * head.size, bytes_accessed=2 * head.size, transcendentals=0
        ),
        name="logits",
    )(
        place,
        *[in_vmem(blocks) for blocks in (first, last, far[1], far[0])],
        in_vmem(owner),
        in_vmem(table),
        in_vmem(early),
        head,
    )

    all_stats = lax.all_to_all(stats, "vocab", split_axis=0, concat_axis=0, tiled=True)

    terms, picks = pl.pallas_call(
        products_kernel,
        out_shape=(
            vmem_array((chips, width // LANES, 2, tokens, LANES), jnp.float32),
            vmem_array((chips, width // LANES, tokens, LANES), jnp.bfloat16),
        ),
        in_specs=[smem, hbm, hbm],
        out_specs=[vmem] * 2,
        scratch_shapes=[head_scratch, rows_scratch, head_sems, rows_sem],
        compiler_params=params,
        cost_estimate=pl.CostEstimate(
            flops=6 * tokens * head.size, bytes_accessed=2 * head.size, transcendentals=0
        ),
        name="products",
    )(place, in_hbm(rows), head)

    terms, picks = in_vmem(terms), in_vmem(picks)
    give, factors, loss = pl.pallas_call(
        give_kernel,
        out_shape=(
            vmem_array((chips, hidden_rows, LANES), jnp.bfloat16),
            vmem_array((3, tokens, LANES), jnp.float32),
            vmem_array((1, 1), jnp.float32),
        ),
        in_specs=[smem] * 2 + [vmem] * 5,
        out_specs=[vmem] * 3,
        compiler_params=params,
        name="give",
    )(place, loss_scale, in_vmem(all_stats), in_vmem(own_stats), in_vmem(table), terms, picks)
    taken = swap_cores(give)
    keep, loss = pl.pallas_call(
        keep_kernel,
        out_shape=(
            vmem_array((chips, hidden_rows, LANES), jnp.float32),
            jax.ShapeDtypeStruct((1, 1), jnp.float32),
        ),
        in_specs=[smem] + [vmem] * 4,
        out_specs=[vmem] * 2,
        compiler_params=params,
        cost_estimate=pl.CostEstimate(
            flops=4 * terms.size, bytes_accessed=4 * terms.size, transcendentals=0
        ),
        name="keep",
    )(place, in_vmem(factors), in_vmem(loss), terms, picks)
    sums = keep + taken.astype(jnp.float32)
    shares = [along_chips(sums[step].astype(jnp.bfloat16), step) for step in steps]
    total = pl.pallas_call(
        sum_kernel,
        out_shape=jax.ShapeDtypeStruct((tokens, half), jnp.bfloat16),
        in_specs=[smem] + [vmem] * chips,
        out_specs=vmem,
        compiler_params=params,
        name="total",
    )(place, *[in_vmem(share) for share in [sums[0]] + shares])
    return total, jnp.reshape(loss, (1,))


VMEM_LIMIT = 24 * 1024 * 1024


def shards(
    hidden_states, head, teacher_values, teacher_scales, token_ids, lengths, row_map, loss_scale
):
    count = lax.axis_size("vocab")
    own_index = lax.axis_index("vocab")
    tokens = hidden_states.shape[0]
    own_features = hidden_states.shape[1]
    shard_rows = head.shape[0]
    seq_length = tokens // lengths.shape[0]
    contract_last = (((1,), (1,)), ((), ()))

    scaled = scaled_teacher(teacher_values, teacher_scales, count, shard_rows)
    arrived = lax.all_to_all(scaled, "vocab", split_axis=0, concat_axis=0, tiled=True)
    arrived = arrived.reshape(tokens, shard_rows)
    gathered = to_all(hidden_states, count).transpose(1, 0, 2).reshape(tokens, -1)
    logits = lax.dot_general(gathered, head, contract_last, preferred_element_type=jnp.float32)

    positions = jnp.arange(tokens, dtype=jnp.int32)
    owner = row_map[None, :] == positions[:, None]
    slot_of = jnp.sum(jnp.where(owner, positions[None, :], 0), axis=1)
    teacher = jnp.take(arrived, slot_of, axis=0).astype(jnp.float32)

    seq_ids = jnp.arange(lengths.shape[0], dtype=jnp.int32)
    own_length = jnp.sum(
        jnp.where((positions // seq_length)[:, None] == seq_ids[None, :], lengths[None, :], 0),
        axis=1,
    )
    live_mask = (positions % seq_length < own_length).astype(jnp.float32)
    live_count = jnp.sum(live_mask)

    local_ids = token_ids - own_index * shard_rows
    target_hit = local_ids[:, None] == jnp.arange(shard_rows, dtype=jnp.int32)[None, :]
    target_part = jnp.sum(jnp.where(target_hit, logits, 0.0), axis=1)
    student_top = jnp.max(logits, axis=1)
    teacher_top = jnp.max(teacher, axis=1)
    student_off = logits - student_top[:, None]
    teacher_off = teacher - teacher_top[:, None]
    student_exp = jnp.exp(student_off)
    student_sum = jnp.sum(student_exp, axis=1)
    teacher_sum = jnp.sum(jnp.exp(teacher_off), axis=1)
    cross_sum = jnp.sum(student_exp * (student_off - teacher_off), axis=1)

    stats = to_all(
        jnp.stack(
            [student_top, student_sum, teacher_top, teacher_sum, cross_sum, target_part]
        ),
        count,
    )
    tops, sums, teacher_tops, teacher_sums, crosses, targets = [stats[:, i] for i in range(6)]
    student_max, student_total, teacher_max, teacher_total, cross_total = merge_stats(
        tops, sums, teacher_tops, teacher_sums, crosses
    )
    student_log = jnp.log(student_total)
    teacher_log = jnp.log(teacher_total)
    student_lse = student_max + student_log
    teacher_lse = teacher_max + teacher_log
    divergence = cross_total / student_total - (student_log - teacher_log)
    target = jnp.sum(targets, axis=0)

    per_token = divergence + sample_weight * (student_lse - target)
    loss = jnp.reshape(jnp.sum(live_mask * per_token) / live_count, (1,))
    token_weight = live_mask * loss_scale[0] / live_count
    log_student = logits - student_lse[:, None]
    log_teacher = teacher - teacher_lse[:, None]
    student_prob = jnp.exp(log_student)
    grad_logits = (
        token_weight[:, None]
        * (
            student_prob * (log_student - log_teacher - divergence[:, None])
            + sample_weight * (student_prob - target_hit.astype(jnp.float32))
        )
    ).astype(jnp.bfloat16)
    terms = jnp.dot(grad_logits, head, preferred_element_type=jnp.float32).astype(jnp.bfloat16)
    terms = terms.reshape(tokens, count, own_features).transpose(1, 0, 2)
    shares = lax.all_to_all(terms, "vocab", split_axis=0, concat_axis=0, tiled=True)
    grad_hidden = jnp.sum(shares.astype(jnp.float32), axis=0)
    return (grad_hidden.astype(jnp.bfloat16), loss)


def any_shards(*arrays):
    hidden_states, head, teacher_values = arrays[:3]
    count = lax.axis_size("vocab")
    fits = (
        count % 2 == 0
        and hidden_states.shape[1] == 5 * LANES // 2
        and hidden_states.shape[0] % 32 == 0
        and head.shape[0] % LANES == LANES // 2
        and (head.shape[0] + LANES // 2) // LANES % 2 == 0
        and teacher_values.shape[0] == 4
    )
    return paired_shards(*arrays) if fits else shards(*arrays)


def solution(mesh):
    in_specs = (
        P("dom", "vocab"),
        P("vocab", None),
        P(("dom", "vocab"), None),
        P(("dom", "vocab"), None),
        P("dom"),
        P("dom"),
        P("dom"),
        P(),
    )
    out_specs = (P("dom", "vocab"), P("dom"))
    return jax.shard_map(
        any_shards, mesh=mesh, in_specs=in_specs, out_specs=out_specs, check_vma=False
    )
```

```python
import functools

import jax
import jax.numpy as jnp
from jax import lax
from jax.experimental import pallas as pl
from jax.experimental.pallas import tpu as pltpu
from jax.sharding import PartitionSpec as P

BLOCK = 32
LANES = 128
STATS = 8
AHEAD = 3
EARLY = 3


sample_weight = 0.5


def to_all(piece, count):
    copies = jnp.broadcast_to(piece[None], (count,) + piece.shape)
    return lax.all_to_all(copies, "vocab", split_axis=0, concat_axis=0, tiled=True)


def scaled_teacher(teacher_values, teacher_scales, count, shard_rows):
    slot_rows = teacher_values.shape[0]
    scaled = (
        teacher_values.astype(jnp.float32).reshape(slot_rows, -1, BLOCK) * teacher_scales[:, :, None]
    ).astype(jnp.bfloat16)
    return scaled.reshape(slot_rows, count, shard_rows).transpose(1, 0, 2)


def merge_stats(tops, sums, teacher_tops, teacher_sums, crosses):
    top = jnp.max(tops, axis=0)
    teacher_top = jnp.max(teacher_tops, axis=0)
    shift = tops - top[None]
    teacher_shift = teacher_tops - teacher_top[None]
    weight = jnp.exp(shift)
    total = jnp.sum(sums * weight, axis=0)
    teacher_total = jnp.sum(teacher_sums * jnp.exp(teacher_shift), axis=0)
    cross = jnp.sum(weight * (crosses + sums * (shift - teacher_shift)), axis=0)
    return top, total, teacher_top, teacher_total, cross


def swap_cores(array):
    count = lax.axis_size("vocab")
    return lax.ppermute(array, "vocab", [(i, i ^ 1) for i in range(count)])


def along_chips(array, step):
    count = lax.axis_size("vocab")
    return lax.ppermute(array, "vocab", [(i, (i + 2 * step) % count) for i in range(count)])


def vmem_array(shape, dtype):
    return pltpu.VMEM(shape, dtype)


def in_vmem(array):
    return pltpu.with_memory_space_constraint(array, pltpu.VMEM)


def in_hbm(array):
    return pltpu.with_memory_space_constraint(array, pltpu.HBM)


def hbm_array(shape, dtype):
    return pltpu.HBM(shape, dtype)


def low_lanes(shape):
    return lax.broadcasted_iota(jnp.int32, shape, len(shape) - 1) < LANES // 2


def low_rows(shape, count):
    return lax.broadcasted_iota(jnp.int32, shape, 0) < count


def turned(array):
    return pltpu.roll(array, LANES // 2, 1)


def folded(first, tile):
    rows = tile.shape[0] // 2
    upper, lower = tile[:rows], turned(tile[rows:])
    low = low_lanes(upper.shape)
    return jnp.where(first, jnp.where(low, upper, lower), jnp.where(low, lower, upper))


def tiles_of(array, count):
    return [array[:, LANES * i : LANES * (i + 1)] for i in range(count)]


def column_of(row):
    size = row.shape[1]
    down = lax.broadcasted_iota(jnp.int32, (size, size), 0)
    along = lax.broadcasted_iota(jnp.int32, (size, size), 1)
    return jnp.sum(jnp.where(down == along, row, jnp.zeros_like(row)), axis=1, keepdims=True)


def token_facts(ids, row_map, lengths, first_entry, slots):
    tokens = row_map.shape[1]
    token = lax.broadcasted_iota(jnp.int32, (tokens, tokens), 0)
    slot = lax.broadcasted_iota(jnp.int32, (tokens, tokens), 1)
    owner = (row_map == token).astype(jnp.float32)
    named = jnp.max(owner, axis=1, keepdims=True)
    owner = jnp.where((slot == 0) & (named == 0.0), 1.0, owner)
    rows = 2 * tokens
    slot = lax.broadcasted_iota(jnp.int32, (tokens, rows), 0)
    row = lax.broadcasted_iota(jnp.int32, (tokens, rows), 1)
    source, within = row // (2 * slots), row % (2 * slots)
    chosen = (slot == source * slots + within % slots).astype(jnp.bfloat16)
    owner = jnp.dot(owner.astype(jnp.bfloat16), chosen, preferred_element_type=jnp.float32)
    odd = within >= slots
    owner = jnp.concatenate([jnp.where(odd, 0.0, owner), jnp.where(odd, owner, 0.0)], axis=0)

    seqs = lengths.shape[1]
    seq_length = tokens // seqs
    position = lax.broadcasted_iota(jnp.int32, (tokens, 1), 0)
    live_until = jnp.zeros((tokens, 1), jnp.int32)
    for seq in range(seqs):
        inside = (position >= seq * seq_length) & (position < (seq + 1) * seq_length)
        until = lengths[:, seq : seq + 1] + seq * seq_length
        live_until = jnp.where(inside, until, live_until)
    live = (position < live_until).astype(jnp.float32)
    count = jnp.sum(live, axis=0, keepdims=True)
    entry = (column_of(ids) - first_entry).astype(jnp.float32)
    lane = lax.broadcasted_iota(jnp.int32, (tokens, LANES), 1)
    return owner.astype(jnp.bfloat16), jnp.where(lane == 0, entry, live / count)


def pack_kernel(place_ref, *refs, shard_rows):
    outside, refs = refs[:6], refs[6:]
    packed_ref, owner_ref, table_ref = refs[:3]
    inside, wide_ref, sems = refs[3:9], refs[9], refs[10]
    copies = [
        pltpu.make_async_copy(source, target, sems.at[i])
        for i, (source, target) in enumerate(zip(outside, inside))
    ]
    for copy in copies:
        copy.start()
    for copy in copies:
        copy.wait()
    hidden_ref, values_ref, scales_ref, ids_ref, map_ref, lengths_ref = inside
    owner_ref[...], table_ref[...] = token_facts(
        ids_ref[...], map_ref[...], lengths_ref[...], place_ref[0] * shard_rows, values_ref.shape[0]
    )
    chips = packed_ref.shape[0]
    tokens, half = hidden_ref.shape
    slots, entries = values_ref.shape
    pair = entries // chips
    shard = pair // 2
    blocks = pair // BLOCK
    scales = jnp.concatenate([scales_ref[...]] * 2, axis=0)
    stacked = jnp.concatenate(
        [scales[:, blocks * chip : blocks * (chip + 1)] for chip in range(chips)], axis=0
    )
    block = lax.broadcasted_iota(jnp.int32, (blocks, pair), 0)
    entry = lax.broadcasted_iota(jnp.int32, (blocks, pair), 1)
    inside = (entry >= block * BLOCK) & (entry < block * BLOCK + BLOCK)
    spread = jnp.dot(
        stacked.astype(jnp.bfloat16),
        inside.astype(jnp.bfloat16),
        preferred_element_type=jnp.float32,
    )
    values = values_ref[...].astype(jnp.float32)
    values = jnp.concatenate([values, values], axis=0)
    for chip in range(chips):
        wide_ref[:, pair * chip : pair * (chip + 1)] = (
            values[:, pair * chip : pair * (chip + 1)]
            * spread[2 * slots * chip : 2 * slots * (chip + 1)]
        )
    wide_ref[:, entries:] = jnp.zeros((2 * slots, LANES), jnp.float32)

    hidden = hidden_ref[...].astype(jnp.float32)
    zeros = jnp.zeros((tokens, LANES // 2), jnp.float32)
    tiles = tiles_of(jnp.concatenate([hidden, zeros], axis=1), 3)
    turns = [turned(tile) for tile in tiles]
    low = low_lanes(tiles[0].shape)
    first = place_ref[0] % 2 == 0
    hidden = jnp.concatenate(
        [
            jnp.where(first, tiles[0], jnp.where(low, turns[0], turns[1])),
            jnp.where(first, tiles[1], jnp.where(low, turns[1], turns[2])),
            folded(first, jnp.where(first, tiles[2], turns[0])),
        ],
        axis=0,
    ).astype(jnp.bfloat16)
    hidden_rows = hidden.shape[0]
    upper = low_rows((2 * slots, LANES), slots)
    low = low_lanes((2 * slots, LANES))
    tile_pairs = (shard + LANES // 2) // LANES // 2
    for chip in range(chips):
        rows = []
        for core in range(2):
            start = pair * chip + (shard - LANES // 2) * core
            tiles = [
                wide_ref[:, start + LANES * i : start + LANES * (i + 1)]
                for i in range(2 * tile_pairs + core)
            ]
            if core == 1:
                tiles = [turned(tile) for tile in tiles]
                tiles = [
                    jnp.where(low, tiles[i], tiles[i + 1]) for i in range(2 * tile_pairs)
                ]
            rows += [
                jnp.where(upper, tiles[2 * i], tiles[2 * i + 1]) for i in range(tile_pairs)
            ]
        step = lax.rem(chip - place_ref[0] // 2 + chips, chips)
        packed_ref[step, :hidden_rows] = hidden
        packed_ref[step, hidden_rows:] = jnp.concatenate(rows, axis=0).astype(jnp.bfloat16)


def head_copy(head_ref, held_ref, sems, chip, step):
    width = held_ref.shape[2]
    columns = pl.ds(pl.multiple_of(chip * width, LANES), width)
    return pltpu.make_async_copy(head_ref.at[:, columns], held_ref.at[step], sems.at[step])


def stream(chip_at, count, head_ref, held_ref, sems, use):
    def copy(step):
        return head_copy(head_ref, held_ref, sems, chip_at(step), step)

    def body(step, _):
        copy(step).wait()

        @pl.when(step + AHEAD < count)
        def _():
            copy(step + AHEAD).start()

        use(step)

    for step in range(min(AHEAD, count)):
        copy(step).start()
    return lambda: lax.fori_loop(0, count, body, None)


def source_chip(place_ref, chips, step):
    return lax.rem(place_ref[0] // 2 - step + chips, chips)


def preload_kernel(place_ref, head_ref, _, early_ref, sems, *, chips):
    copies = [
        head_copy(head_ref, early_ref, sems, source_chip(place_ref, chips, step), step)
        for step in range(EARLY)
    ]
    for copy in copies:
        copy.start()
    for copy in copies:
        copy.wait()


def logits_kernel(
    place_ref,
    first_ref,
    last_ref,
    first_far_ref,
    last_far_ref,
    owner_ref,
    tokens_ref,
    early_ref,
    head_ref,
    rows_ref,
    stats_ref,
    own_ref,
    held_ref,
    made_ref,
    hidden_ref,
    arrived_ref,
    teacher_ref,
    logits_ref,
    copies_ref,
    sems,
    made_sem,
    stats_sem,
):
    core = place_ref[0] % 2
    chips, tokens, width = hidden_ref.shape
    shard_rows = head_ref.shape[0]
    hidden_rows = 5 * tokens // 2
    slots = tokens // (2 * chips)
    low = low_lanes((tokens // 2, LANES))

    def add(step, columns):
        logits_ref[...] += lax.dot_general(
            columns, hidden_ref[step], (((1,), (1,)), ((), ())), preferred_element_type=jnp.float32
        )

    run = stream(
        lambda step: source_chip(place_ref, chips, step + EARLY),
        chips - EARLY,
        head_ref,
        held_ref,
        sems,
        lambda step: add(step + EARLY, held_ref[step]),
    )

    def unpack(near_ref, far_ref, base):
        def body(place, _):
            step = place + base
            blocks = near_ref.at[place], far_ref.at[place]
            for block, parity in zip(blocks, (core, 1 - core)):
                for i in range(2):
                    column = LANES * i + (width - 2 * LANES) * parity
                    lanes = pl.ds(pl.multiple_of(column, LANES), LANES)
                    hidden_ref[step, :, lanes] = block[tokens * i : tokens * (i + 1)]
                teacher = block[hidden_rows:].astype(jnp.float32)
                share = teacher.shape[0] // 2
                teacher = jnp.where(core == 0, teacher[:share], teacher[share:])
                row = 2 * slots * (2 * source_chip(place_ref, chips, step) + parity)
                rows = pl.ds(pl.multiple_of(row, 2 * slots), 2 * slots)
                for i in range(share // (2 * slots)):
                    arrived_ref[rows, LANES * i : LANES * (i + 1)] = teacher[
                        2 * slots * i : 2 * slots * (i + 1)
                    ]
            own, other = [block[2 * tokens : hidden_rows].astype(jnp.float32) for block in blocks]
            one, two = jnp.where(core == 0, own, other), jnp.where(core == 0, other, own)
            tile = [jnp.where(low, one, two), turned(jnp.where(low, two, one))]
            tile = jnp.concatenate(tile, axis=0).astype(jnp.bfloat16)
            hidden_ref[step, :, 2 * LANES : 3 * LANES] = tile

        lax.fori_loop(0, near_ref.shape[0], body, None)

    unpack(first_ref, first_far_ref, 0)
    unpack(last_ref, last_far_ref, first_ref.shape[0])
    logits_ref[...] = jnp.zeros_like(logits_ref)
    lax.fori_loop(0, EARLY, lambda step, _: add(step, early_ref[step]), None)
    placed = jnp.dot(
        owner_ref[...], arrived_ref[...].astype(jnp.bfloat16), preferred_element_type=jnp.float32
    )
    pairs = arrived_ref.shape[1] // LANES
    even, odd = tiles_of(placed[:tokens], pairs), tiles_of(placed[tokens:], pairs)
    teacher = jnp.concatenate([tile for pair in zip(even, odd) for tile in pair], axis=1)
    teacher = teacher[:, :shard_rows]
    teacher_top = jnp.max(teacher, axis=1, keepdims=True)
    teacher_off = teacher - teacher_top
    teacher_total = jnp.sum(jnp.exp(teacher_off), axis=1, keepdims=True)
    teacher_ref[...] = teacher_off
    run()
    logits = logits_ref[...].T

    top = jnp.max(logits, axis=1, keepdims=True)
    off = logits - top
    exps = jnp.exp(off)
    total = jnp.sum(exps, axis=1, keepdims=True)
    gap = off - teacher_ref[...]
    cross = jnp.sum(exps * gap, axis=1, keepdims=True)
    centre = cross / total
    entry = lax.broadcasted_iota(jnp.int32, (tokens, shard_rows), 1)
    hit = entry == tokens_ref[:, :1].astype(jnp.int32)
    target = jnp.sum(jnp.where(hit, logits, 0.0), axis=1, keepdims=True)
    made_ref[:tokens] = (exps * (gap - centre)).astype(jnp.bfloat16)
    made_ref[tokens : 2 * tokens] = exps.astype(jnp.bfloat16)
    made_ref[2 * tokens :] = hit.astype(jnp.bfloat16)
    out = pltpu.make_async_copy(made_ref, rows_ref, made_sem)
    out.start()

    lane = lax.broadcasted_iota(jnp.int32, (tokens, LANES), 1)
    table = jnp.zeros((tokens, LANES), jnp.float32)
    for place, column in enumerate(
        (top, total, teacher_top, teacher_total, cross, target, centre)
    ):
        table = jnp.where(lane == place, column, table)
    stats = jnp.concatenate([table, jnp.zeros((own_ref.shape[1] - tokens, LANES), jnp.float32)])
    stats = stats.T[:STATS]
    own_ref[...] = stats
    copies_ref[...] = jnp.broadcast_to(stats[None], copies_ref.shape)
    out_stats = pltpu.make_async_copy(copies_ref, stats_ref, stats_sem)
    out_stats.start()
    out.wait()
    out_stats.wait()


def products_kernel(
    place_ref, rows_ref, head_ref, terms_ref, picks_ref, held_ref, made_ref, sems, made_sem
):
    into = pltpu.make_async_copy(rows_ref, made_ref, made_sem)
    into.start()
    chips = terms_ref.shape[0]
    tokens = made_ref.shape[0] // 3
    width = held_ref.shape[2]

    def multiply(step):
        products = jnp.dot(made_ref[...], held_ref[step], preferred_element_type=jnp.float32)
        for i, tile in enumerate(tiles_of(products, width // LANES)):
            terms_ref[step, i, 0] = tile[:tokens]
            terms_ref[step, i, 1] = tile[tokens : 2 * tokens]
            picks_ref[step, i] = tile[2 * tokens :].astype(jnp.bfloat16)

    run = stream(
        lambda step: lax.rem(place_ref[0] // 2 + step, chips),
        chips,
        head_ref,
        held_ref,
        sems,
        multiply,
    )
    into.wait()
    run()


def put_shares(parity, factors_ref, terms_ref, picks_ref, out_ref):
    tokens = terms_ref.shape[3]
    factor, level, weight = [factors_ref[i] for i in range(3)]
    for step in range(terms_ref.shape[0]):
        for i, tile in enumerate((3 * parity, 3 * parity + 1, 2)):
            sums = terms_ref[step, tile, 0] + level * terms_ref[step, tile, 1]
            share = factor * sums - weight * picks_ref[step, tile].astype(jnp.float32)
            if i == 2:
                share = folded(parity == 0, share)
            out_ref[step, tokens * i : tokens * i + share.shape[0]] = share.astype(out_ref.dtype)


def give_kernel(
    place_ref,
    scale_ref,
    stats_ref,
    own_ref,
    tokens_ref,
    terms_ref,
    picks_ref,
    give_ref,
    factors_ref,
    loss_ref,
):
    tokens = tokens_ref.shape[0]
    tops, sums, teacher_tops, teacher_sums, crosses, targets = [
        stats_ref[:, i, :tokens] for i in range(6)
    ]
    top, total, teacher_top, teacher_total, cross = [
        part[None] for part in merge_stats(tops, sums, teacher_tops, teacher_sums, crosses)
    ]
    target = jnp.sum(targets, axis=0, keepdims=True)
    student_log = jnp.log(total)
    teacher_log = jnp.log(teacher_total)
    divergence = cross / total - (student_log - teacher_log)
    student_lse = top + student_log
    per_token = divergence + sample_weight * (student_lse - target)
    student_shift = own_ref[0:1, :tokens] - top - student_log
    teacher_shift = own_ref[2:3, :tokens] - teacher_top - teacher_log
    factor = jnp.exp(student_shift)
    level = (
        own_ref[6:7, :tokens] + student_shift - teacher_shift - divergence + sample_weight
    )
    zeros = jnp.zeros((LANES - 3, tokens), jnp.float32)
    columns = jnp.concatenate([factor, level, per_token, zeros], axis=0).T
    share = tokens_ref[:, 1:2]
    weight = share * scale_ref[0]
    loss_ref[...] = jnp.sum(share * columns[:, 2:3], axis=0, keepdims=True)
    for i, column in enumerate(
        (weight * columns[:, 0:1], columns[:, 1:2], sample_weight * weight)
    ):
        factors_ref[i] = jnp.broadcast_to(column, (tokens, LANES))
    put_shares(1 - place_ref[0] % 2, factors_ref, terms_ref, picks_ref, give_ref)


def keep_kernel(place_ref, factors_ref, found_ref, terms_ref, picks_ref, keep_ref, loss_ref):
    loss_ref[...] = found_ref[...]
    put_shares(place_ref[0] % 2, factors_ref, terms_ref, picks_ref, keep_ref)


def sum_kernel(place_ref, own_ref, *refs):
    tokens, half = refs[-1].shape
    total = own_ref[...]
    for share_ref in refs[:-1]:
        total += share_ref[...].astype(jnp.float32)
    one, two, rest = total[:tokens], total[tokens : 2 * tokens], total[2 * tokens :]
    rest = jnp.concatenate([rest, turned(rest)], axis=0)
    turns = [turned(tile) for tile in (rest, one, two)]
    low = low_lanes(one.shape)
    first = place_ref[0] % 2 == 0
    tiles = [
        jnp.where(first, one, jnp.where(low, turns[0], turns[1])),
        jnp.where(first, two, jnp.where(low, turns[1], turns[2])),
        jnp.where(first, rest, turns[2]),
    ]
    total = jnp.concatenate(tiles, axis=1)[:, :half]
    refs[-1][...] = total.astype(refs[-1].dtype)


def paired_shards(
    hidden_states, head, teacher_values, teacher_scales, token_ids, lengths, row_map, loss_scale
):
    count = lax.axis_size("vocab")
    own_index = lax.axis_index("vocab")
    chips = count // 2
    tokens, half = hidden_states.shape
    width = 2 * half
    shard_rows = head.shape[0]
    place = jnp.reshape(own_index, (1,))
    vmem = pl.BlockSpec(memory_space=pltpu.VMEM)
    smem = pl.BlockSpec(memory_space=pltpu.SMEM)
    hbm = pl.BlockSpec(memory_space=pl.ANY)
    params = pltpu.CompilerParams(vmem_limit_bytes=VMEM_LIMIT)
    head = in_hbm(head)
    head_scratch = pltpu.VMEM((chips, shard_rows, width), head.dtype)
    head_sems = pltpu.SemaphoreType.DMA((chips,))
    rows_scratch = pltpu.VMEM((3 * tokens, shard_rows), jnp.bfloat16)
    rows_sem = pltpu.SemaphoreType.DMA
    slots, entries = teacher_values.shape
    hidden_rows = 5 * tokens // 2
    teacher_rows = 2 * slots * (shard_rows + LANES // 2) // LANES

    operands = (
        hidden_states,
        teacher_values,
        teacher_scales,
        token_ids[None, :],
        row_map[None, :],
        lengths[None, :],
    )
    packed, owner, table = pl.pallas_call(
        functools.partial(pack_kernel, shard_rows=shard_rows),
        out_shape=(
            vmem_array((chips, hidden_rows + teacher_rows, LANES), jnp.bfloat16),
            vmem_array((2 * tokens, 2 * tokens), jnp.bfloat16),
            vmem_array((tokens, LANES), jnp.float32),
        ),
        in_specs=[smem] + [hbm] * len(operands),
        out_specs=[vmem] * 3,
        scratch_shapes=[pltpu.VMEM(operand.shape, operand.dtype) for operand in operands]
        + [
            pltpu.VMEM((2 * slots, entries + LANES), jnp.float32),
            pltpu.SemaphoreType.DMA((len(operands),)),
        ],
        compiler_params=params,
        name="pack",
    )(place, *[in_hbm(operand) for operand in operands])
    steps = range(1, chips)
    near = [packed[0]] + [along_chips(packed[step], step) for step in steps]
    first, last = jnp.stack(near[: chips // 2 + 1]), jnp.stack(near[chips // 2 + 1 :])
    early = pl.pallas_call(
        functools.partial(preload_kernel, chips=chips),
        out_shape=vmem_array((EARLY, shard_rows, width), head.dtype),
        in_specs=[smem] + [hbm] * 2,
        out_specs=vmem,
        scratch_shapes=[pltpu.SemaphoreType.DMA((EARLY,))],
        compiler_params=params,
        cost_estimate=pl.CostEstimate(
            flops=0, bytes_accessed=4 * EARLY * shard_rows * width, transcendentals=0
        ),
        name="preload",
    )(place, head, near[3])
    last, early = lax.optimization_barrier((last, early))
    far = [swap_cores(last), swap_cores(first)]

    stats_shape = (count, STATS, pl.cdiv(tokens, LANES) * LANES)
    rows, stats, own_stats = pl.pallas_call(
        logits_kernel,
        out_shape=(
            hbm_array((3 * tokens, shard_rows), jnp.bfloat16),
            hbm_array(stats_shape, jnp.float32),
            vmem_array(stats_shape[1:], jnp.float32),
        ),
        in_specs=[smem] + [vmem] * 7 + [hbm],
        out_specs=[hbm, hbm, vmem],
        scratch_shapes=[
            pltpu.VMEM((chips - EARLY, shard_rows, width), head.dtype),
            rows_scratch,
            pltpu.VMEM((chips, tokens, width), jnp.bfloat16),
            pltpu.VMEM((2 * tokens, (shard_rows + LANES // 2) // 2), jnp.float32),
            pltpu.VMEM((tokens, shard_rows), jnp.float32),
            pltpu.VMEM((shard_rows, tokens), jnp.float32),
            pltpu.VMEM(stats_shape, jnp.float32),
            pltpu.SemaphoreType.DMA((chips - EARLY,)),
            rows_sem,
            rows_sem,
        ],
        compiler_params=params,
        cost_estimate=pl.CostEstimate(
            flops=2 * tokens * head.size, bytes_accessed=2 * head.size, transcendentals=0
        ),
        name="logits",
    )(
        place,
        *[in_vmem(blocks) for blocks in (first, last, far[1], far[0])],
        in_vmem(owner),
        in_vmem(table),
        in_vmem(early),
        head,
    )

    all_stats = lax.all_to_all(stats, "vocab", split_axis=0, concat_axis=0, tiled=True)

    terms, picks = pl.pallas_call(
        products_kernel,
        out_shape=(
            vmem_array((chips, width // LANES, 2, tokens, LANES), jnp.float32),
            vmem_array((chips, width // LANES, tokens, LANES), jnp.bfloat16),
        ),
        in_specs=[smem, hbm, hbm],
        out_specs=[vmem] * 2,
        scratch_shapes=[head_scratch, rows_scratch, head_sems, rows_sem],
        compiler_params=params,
        cost_estimate=pl.CostEstimate(
            flops=6 * tokens * head.size, bytes_accessed=2 * head.size, transcendentals=0
        ),
        name="products",
    )(place, in_hbm(rows), head)

    terms, picks = in_vmem(terms), in_vmem(picks)
    give, factors, loss = pl.pallas_call(
        give_kernel,
        out_shape=(
            vmem_array((chips, hidden_rows, LANES), jnp.bfloat16),
            vmem_array((3, tokens, LANES), jnp.float32),
            vmem_array((1, 1), jnp.float32),
        ),
        in_specs=[smem] * 2 + [vmem] * 5,
        out_specs=[vmem] * 3,
        compiler_params=params,
        name="give",
    )(place, loss_scale, in_vmem(all_stats), in_vmem(own_stats), in_vmem(table), terms, picks)
    taken = swap_cores(give)
    keep, loss = pl.pallas_call(
        keep_kernel,
        out_shape=(
            vmem_array((chips, hidden_rows, LANES), jnp.float32),
            jax.ShapeDtypeStruct((1, 1), jnp.float32),
        ),
        in_specs=[smem] + [vmem] * 4,
        out_specs=[vmem] * 2,
        compiler_params=params,
        cost_estimate=pl.CostEstimate(
            flops=4 * terms.size, bytes_accessed=4 * terms.size, transcendentals=0
        ),
        name="keep",
    )(place, in_vmem(factors), in_vmem(loss), terms, picks)
    sums = keep + taken.astype(jnp.float32)
    shares = [along_chips(sums[step].astype(jnp.bfloat16), step) for step in steps]
    total = pl.pallas_call(
        sum_kernel,
        out_shape=jax.ShapeDtypeStruct((tokens, half), jnp.bfloat16),
        in_specs=[smem] + [vmem] * chips,
        out_specs=vmem,
        compiler_params=params,
        name="total",
    )(place, *[in_vmem(share) for share in [sums[0]] + shares])
    return total, jnp.reshape(loss, (1,))


VMEM_LIMIT = 24 * 1024 * 1024


def shards(
    hidden_states, head, teacher_values, teacher_scales, token_ids, lengths, row_map, loss_scale
):
    count = lax.axis_size("vocab")
    own_index = lax.axis_index("vocab")
    tokens = hidden_states.shape[0]
    own_features = hidden_states.shape[1]
    shard_rows = head.shape[0]
    seq_length = tokens // lengths.shape[0]
    contract_last = (((1,), (1,)), ((), ()))

    scaled = scaled_teacher(teacher_values, teacher_scales, count, shard_rows)
    arrived = lax.all_to_all(scaled, "vocab", split_axis=0, concat_axis=0, tiled=True)
    arrived = arrived.reshape(tokens, shard_rows)
    gathered = to_all(hidden_states, count).transpose(1, 0, 2).reshape(tokens, -1)
    logits = lax.dot_general(gathered, head, contract_last, preferred_element_type=jnp.float32)

    positions = jnp.arange(tokens, dtype=jnp.int32)
    owner = row_map[None, :] == positions[:, None]
    slot_of = jnp.sum(jnp.where(owner, positions[None, :], 0), axis=1)
    teacher = jnp.take(arrived, slot_of, axis=0).astype(jnp.float32)

    seq_ids = jnp.arange(lengths.shape[0], dtype=jnp.int32)
    own_length = jnp.sum(
        jnp.where((positions // seq_length)[:, None] == seq_ids[None, :], lengths[None, :], 0),
        axis=1,
    )
    live_mask = (positions % seq_length < own_length).astype(jnp.float32)
    live_count = jnp.sum(live_mask)

    local_ids = token_ids - own_index * shard_rows
    target_hit = local_ids[:, None] == jnp.arange(shard_rows, dtype=jnp.int32)[None, :]
    target_part = jnp.sum(jnp.where(target_hit, logits, 0.0), axis=1)
    student_top = jnp.max(logits, axis=1)
    teacher_top = jnp.max(teacher, axis=1)
    student_off = logits - student_top[:, None]
    teacher_off = teacher - teacher_top[:, None]
    student_exp = jnp.exp(student_off)
    student_sum = jnp.sum(student_exp, axis=1)
    teacher_sum = jnp.sum(jnp.exp(teacher_off), axis=1)
    cross_sum = jnp.sum(student_exp * (student_off - teacher_off), axis=1)

    stats = to_all(
        jnp.stack(
            [student_top, student_sum, teacher_top, teacher_sum, cross_sum, target_part]
        ),
        count,
    )
    tops, sums, teacher_tops, teacher_sums, crosses, targets = [stats[:, i] for i in range(6)]
    student_max, student_total, teacher_max, teacher_total, cross_total = merge_stats(
        tops, sums, teacher_tops, teacher_sums, crosses
    )
    student_log = jnp.log(student_total)
    teacher_log = jnp.log(teacher_total)
    student_lse = student_max + student_log
    teacher_lse = teacher_max + teacher_log
    divergence = cross_total / student_total - (student_log - teacher_log)
    target = jnp.sum(targets, axis=0)

    per_token = divergence + sample_weight * (student_lse - target)
    loss = jnp.reshape(jnp.sum(live_mask * per_token) / live_count, (1,))
    token_weight = live_mask * loss_scale[0] / live_count
    log_student = logits - student_lse[:, None]
    log_teacher = teacher - teacher_lse[:, None]
    student_prob = jnp.exp(log_student)
    grad_logits = (
        token_weight[:, None]
        * (
            student_prob * (log_student - log_teacher - divergence[:, None])
            + sample_weight * (student_prob - target_hit.astype(jnp.float32))
        )
    ).astype(jnp.bfloat16)
    terms = jnp.dot(grad_logits, head, preferred_element_type=jnp.float32).astype(jnp.bfloat16)
    terms = terms.reshape(tokens, count, own_features).transpose(1, 0, 2)
    shares = lax.all_to_all(terms, "vocab", split_axis=0, concat_axis=0, tiled=True)
    grad_hidden = jnp.sum(shares.astype(jnp.float32), axis=0)
    return (grad_hidden.astype(jnp.bfloat16), loss)


def any_shards(*arrays):
    hidden_states, head, teacher_values = arrays[:3]
    count = lax.axis_size("vocab")
    fits = (
        count % 2 == 0
        and hidden_states.shape[1] == 5 * LANES // 2
        and hidden_states.shape[0] % 32 == 0
        and head.shape[0] % LANES == LANES // 2
        and (head.shape[0] + LANES // 2) // LANES % 2 == 0
        and teacher_values.shape[0] == 4
    )
    return paired_shards(*arrays) if fits else shards(*arrays)


def solution(mesh):
    in_specs = (
        P("dom", "vocab"),
        P("vocab", None),
        P(("dom", "vocab"), None),
        P(("dom", "vocab"), None),
        P("dom"),
        P("dom"),
        P("dom"),
        P(),
    )
    out_specs = (P("dom", "vocab"), P("dom"))
    return jax.shard_map(
        any_shards, mesh=mesh, in_specs=in_specs, out_specs=out_specs, check_vma=False
    )
```

```python
import functools

import jax
import jax.numpy as jnp
from jax import lax
from jax.experimental import pallas as pl
from jax.experimental.pallas import tpu as pltpu
from jax.sharding import PartitionSpec as P

BLOCK = 32
LANES = 128
STATS = 8
AHEAD = 3
EARLY = 3


sample_weight = 0.5


def to_all(piece, count):
    copies = jnp.broadcast_to(piece[None], (count,) + piece.shape)
    return lax.all_to_all(copies, "vocab", split_axis=0, concat_axis=0, tiled=True)


def scaled_teacher(teacher_values, teacher_scales, count, shard_rows):
    slot_rows = teacher_values.shape[0]
    scaled = (
        teacher_values.astype(jnp.float32).reshape(slot_rows, -1, BLOCK) * teacher_scales[:, :, None]
    ).astype(jnp.bfloat16)
    return scaled.reshape(slot_rows, count, shard_rows).transpose(1, 0, 2)


def merge_stats(tops, sums, teacher_tops, teacher_sums, crosses):
    top = jnp.max(tops, axis=0)
    teacher_top = jnp.max(teacher_tops, axis=0)
    shift = tops - top[None]
    teacher_shift = teacher_tops - teacher_top[None]
    weight = jnp.exp(shift)
    total = jnp.sum(sums * weight, axis=0)
    teacher_total = jnp.sum(teacher_sums * jnp.exp(teacher_shift), axis=0)
    cross = jnp.sum(weight * (crosses + sums * (shift - teacher_shift)), axis=0)
    return top, total, teacher_top, teacher_total, cross


def swap_cores(array):
    count = lax.axis_size("vocab")
    return lax.ppermute(array, "vocab", [(i, i ^ 1) for i in range(count)])


def along_chips(array, step):
    count = lax.axis_size("vocab")
    return lax.ppermute(array, "vocab", [(i, (i + 2 * step) % count) for i in range(count)])


def vmem_array(shape, dtype):
    return pltpu.VMEM(shape, dtype)


def in_vmem(array):
    return pltpu.with_memory_space_constraint(array, pltpu.VMEM)


def in_hbm(array):
    return pltpu.with_memory_space_constraint(array, pltpu.HBM)


def hbm_array(shape, dtype):
    return pltpu.HBM(shape, dtype)


def low_lanes(shape):
    return lax.broadcasted_iota(jnp.int32, shape, len(shape) - 1) < LANES // 2


def low_rows(shape, count):
    return lax.broadcasted_iota(jnp.int32, shape, 0) < count


def turned(array):
    return pltpu.roll(array, LANES // 2, 1)


def folded(first, tile):
    rows = tile.shape[0] // 2
    upper, lower = tile[:rows], turned(tile[rows:])
    low = low_lanes(upper.shape)
    return jnp.where(first, jnp.where(low, upper, lower), jnp.where(low, lower, upper))


def tiles_of(array, count):
    return [array[:, LANES * i : LANES * (i + 1)] for i in range(count)]


def column_of(row):
    size = row.shape[1]
    down = lax.broadcasted_iota(jnp.int32, (size, size), 0)
    along = lax.broadcasted_iota(jnp.int32, (size, size), 1)
    return jnp.sum(jnp.where(down == along, row, jnp.zeros_like(row)), axis=1, keepdims=True)


def token_facts(ids, row_map, lengths, first_entry, slots):
    tokens = row_map.shape[1]
    token = lax.broadcasted_iota(jnp.int32, (tokens, tokens), 0)
    slot = lax.broadcasted_iota(jnp.int32, (tokens, tokens), 1)
    owner = (row_map == token).astype(jnp.float32)
    named = jnp.max(owner, axis=1, keepdims=True)
    owner = jnp.where((slot == 0) & (named == 0.0), 1.0, owner)
    rows = 2 * tokens
    slot = lax.broadcasted_iota(jnp.int32, (tokens, rows), 0)
    row = lax.broadcasted_iota(jnp.int32, (tokens, rows), 1)
    source, within = row // (2 * slots), row % (2 * slots)
    chosen = (slot == source * slots + within % slots).astype(jnp.bfloat16)
    owner = jnp.dot(owner.astype(jnp.bfloat16), chosen, preferred_element_type=jnp.float32)
    odd = within >= slots
    owner = jnp.concatenate([jnp.where(odd, 0.0, owner), jnp.where(odd, owner, 0.0)], axis=0)

    seqs = lengths.shape[1]
    seq_length = tokens // seqs
    position = lax.broadcasted_iota(jnp.int32, (tokens, 1), 0)
    live_until = jnp.zeros((tokens, 1), jnp.int32)
    for seq in range(seqs):
        inside = (position >= seq * seq_length) & (position < (seq + 1) * seq_length)
        until = lengths[:, seq : seq + 1] + seq * seq_length
        live_until = jnp.where(inside, until, live_until)
    live = (position < live_until).astype(jnp.float32)
    count = jnp.sum(live, axis=0, keepdims=True)
    entry = (column_of(ids) - first_entry).astype(jnp.float32)
    lane = lax.broadcasted_iota(jnp.int32, (tokens, LANES), 1)
    return owner.astype(jnp.bfloat16), jnp.where(lane == 0, entry, live / count)


def pack_kernel(place_ref, *refs, shard_rows):
    outside, refs = refs[:6], refs[6:]
    packed_ref, owner_ref, table_ref = refs[:3]
    inside, wide_ref, sems = refs[3:9], refs[9], refs[10]
    copies = [
        pltpu.make_async_copy(source, target, sems.at[i])
        for i, (source, target) in enumerate(zip(outside, inside))
    ]
    for copy in copies:
        copy.start()
    for copy in copies:
        copy.wait()
    hidden_ref, values_ref, scales_ref, ids_ref, map_ref, lengths_ref = inside
    owner_ref[...], table_ref[...] = token_facts(
        ids_ref[...], map_ref[...], lengths_ref[...], place_ref[0] * shard_rows, values_ref.shape[0]
    )
    chips = packed_ref.shape[0]
    tokens, half = hidden_ref.shape
    slots, entries = values_ref.shape
    pair = entries // chips
    shard = pair // 2
    blocks = pair // BLOCK
    scales = jnp.concatenate([scales_ref[...]] * 2, axis=0)
    stacked = jnp.concatenate(
        [scales[:, blocks * chip : blocks * (chip + 1)] for chip in range(chips)], axis=0
    )
    block = lax.broadcasted_iota(jnp.int32, (blocks, pair), 0)
    entry = lax.broadcasted_iota(jnp.int32, (blocks, pair), 1)
    inside = (entry >= block * BLOCK) & (entry < block * BLOCK + BLOCK)
    spread = jnp.dot(
        stacked.astype(jnp.bfloat16),
        inside.astype(jnp.bfloat16),
        preferred_element_type=jnp.float32,
    )
    values = values_ref[...].astype(jnp.float32)
    values = jnp.concatenate([values, values], axis=0)
    for chip in range(chips):
        wide_ref[:, pair * chip : pair * (chip + 1)] = (
            values[:, pair * chip : pair * (chip + 1)]
            * spread[2 * slots * chip : 2 * slots * (chip + 1)]
        )
    wide_ref[:, entries:] = jnp.zeros((2 * slots, LANES), jnp.float32)

    hidden = hidden_ref[...].astype(jnp.float32)
    zeros = jnp.zeros((tokens, LANES // 2), jnp.float32)
    tiles = tiles_of(jnp.concatenate([hidden, zeros], axis=1), 3)
    turns = [turned(tile) for tile in tiles]
    low = low_lanes(tiles[0].shape)
    first = place_ref[0] % 2 == 0
    hidden = jnp.concatenate(
        [
            jnp.where(first, tiles[0], jnp.where(low, turns[0], turns[1])),
            jnp.where(first, tiles[1], jnp.where(low, turns[1], turns[2])),
            folded(first, jnp.where(first, tiles[2], turns[0])),
        ],
        axis=0,
    ).astype(jnp.bfloat16)
    hidden_rows = hidden.shape[0]
    upper = low_rows((2 * slots, LANES), slots)
    low = low_lanes((2 * slots, LANES))
    tile_pairs = (shard + LANES // 2) // LANES // 2
    for chip in range(chips):
        rows = []
        for core in range(2):
            start = pair * chip + (shard - LANES // 2) * core
            tiles = [
                wide_ref[:, start + LANES * i : start + LANES * (i + 1)]
                for i in range(2 * tile_pairs + core)
            ]
            if core == 1:
                tiles = [turned(tile) for tile in tiles]
                tiles = [
                    jnp.where(low, tiles[i], tiles[i + 1]) for i in range(2 * tile_pairs)
                ]
            rows += [
                jnp.where(upper, tiles[2 * i], tiles[2 * i + 1]) for i in range(tile_pairs)
            ]
        step = lax.rem(chip - place_ref[0] // 2 + chips, chips)
        packed_ref[step, :hidden_rows] = hidden
        packed_ref[step, hidden_rows:] = jnp.concatenate(rows, axis=0).astype(jnp.bfloat16)


def head_copy(head_ref, held_ref, sems, chip, step):
    width = held_ref.shape[2]
    columns = pl.ds(pl.multiple_of(chip * width, LANES), width)
    return pltpu.make_async_copy(head_ref.at[:, columns], held_ref.at[step], sems.at[step])


def stream(chip_at, count, head_ref, held_ref, sems, use):
    def copy(step):
        return head_copy(head_ref, held_ref, sems, chip_at(step), step)

    def body(step, _):
        copy(step).wait()

        @pl.when(step + AHEAD < count)
        def _():
            copy(step + AHEAD).start()

        use(step)

    for step in range(min(AHEAD, count)):
        copy(step).start()
    return lambda: lax.fori_loop(0, count, body, None)


def source_chip(place_ref, chips, step):
    return lax.rem(place_ref[0] // 2 - step + chips, chips)


def preload_kernel(place_ref, head_ref, _, early_ref, sems, *, chips):
    copies = [
        head_copy(head_ref, early_ref, sems, source_chip(place_ref, chips, step), step)
        for step in range(EARLY)
    ]
    for copy in copies:
        copy.start()
    for copy in copies:
        copy.wait()


def logits_kernel(
    place_ref,
    first_ref,
    last_ref,
    first_far_ref,
    last_far_ref,
    owner_ref,
    tokens_ref,
    early_ref,
    head_ref,
    rows_ref,
    stats_ref,
    own_ref,
    held_ref,
    made_ref,
    hidden_ref,
    arrived_ref,
    teacher_ref,
    logits_ref,
    copies_ref,
    sems,
    made_sem,
    stats_sem,
):
    core = place_ref[0] % 2
    chips, tokens, width = hidden_ref.shape
    shard_rows = head_ref.shape[0]
    hidden_rows = 5 * tokens // 2
    slots = tokens // (2 * chips)
    low = low_lanes((tokens // 2, LANES))

    def add(step, columns):
        logits_ref[...] += lax.dot_general(
            columns, hidden_ref[step], (((1,), (1,)), ((), ())), preferred_element_type=jnp.float32
        )

    run = stream(
        lambda step: source_chip(place_ref, chips, step + EARLY),
        chips - EARLY,
        head_ref,
        held_ref,
        sems,
        lambda step: add(step + EARLY, held_ref[step]),
    )

    def unpack(near_ref, far_ref, base):
        for place in range(near_ref.shape[0]):
            step = place + base
            blocks = near_ref.at[place], far_ref.at[place]
            for block, parity in zip(blocks, (core, 1 - core)):
                for i in range(2):
                    column = LANES * i + (width - 2 * LANES) * parity
                    lanes = pl.ds(pl.multiple_of(column, LANES), LANES)
                    hidden_ref[step, :, lanes] = block[tokens * i : tokens * (i + 1)]
                teacher = block[hidden_rows:].astype(jnp.float32)
                share = teacher.shape[0] // 2
                teacher = jnp.where(core == 0, teacher[:share], teacher[share:])
                row = 2 * slots * (2 * source_chip(place_ref, chips, step) + parity)
                rows = pl.ds(pl.multiple_of(row, 2 * slots), 2 * slots)
                for i in range(share // (2 * slots)):
                    arrived_ref[rows, LANES * i : LANES * (i + 1)] = teacher[
                        2 * slots * i : 2 * slots * (i + 1)
                    ]
            own, other = [block[2 * tokens : hidden_rows].astype(jnp.float32) for block in blocks]
            one, two = jnp.where(core == 0, own, other), jnp.where(core == 0, other, own)
            tile = [jnp.where(low, one, two), turned(jnp.where(low, two, one))]
            tile = jnp.concatenate(tile, axis=0).astype(jnp.bfloat16)
            hidden_ref[step, :, 2 * LANES : 3 * LANES] = tile

    unpack(first_ref, first_far_ref, 0)
    unpack(last_ref, last_far_ref, first_ref.shape[0])
    logits_ref[...] = jnp.zeros_like(logits_ref)
    lax.fori_loop(0, EARLY, lambda step, _: add(step, early_ref[step]), None)
    placed = jnp.dot(
        owner_ref[...], arrived_ref[...].astype(jnp.bfloat16), preferred_element_type=jnp.float32
    )
    pairs = arrived_ref.shape[1] // LANES
    even, odd = tiles_of(placed[:tokens], pairs), tiles_of(placed[tokens:], pairs)
    teacher = jnp.concatenate([tile for pair in zip(even, odd) for tile in pair], axis=1)
    teacher = teacher[:, :shard_rows]
    teacher_top = jnp.max(teacher, axis=1, keepdims=True)
    teacher_off = teacher - teacher_top
    teacher_total = jnp.sum(jnp.exp(teacher_off), axis=1, keepdims=True)
    teacher_ref[...] = teacher_off
    run()
    logits = logits_ref[...].T

    top = jnp.max(logits, axis=1, keepdims=True)
    off = logits - top
    exps = jnp.exp(off)
    total = jnp.sum(exps, axis=1, keepdims=True)
    gap = off - teacher_ref[...]
    cross = jnp.sum(exps * gap, axis=1, keepdims=True)
    centre = cross / total
    entry = lax.broadcasted_iota(jnp.int32, (tokens, shard_rows), 1)
    hit = entry == tokens_ref[:, :1].astype(jnp.int32)
    target = jnp.sum(jnp.where(hit, logits, 0.0), axis=1, keepdims=True)
    made_ref[:tokens] = (exps * (gap - centre)).astype(jnp.bfloat16)
    made_ref[tokens : 2 * tokens] = exps.astype(jnp.bfloat16)
    made_ref[2 * tokens :] = hit.astype(jnp.bfloat16)
    out = pltpu.make_async_copy(made_ref, rows_ref, made_sem)
    out.start()

    lane = lax.broadcasted_iota(jnp.int32, (tokens, LANES), 1)
    table = jnp.zeros((tokens, LANES), jnp.float32)
    for place, column in enumerate(
        (top, total, teacher_top, teacher_total, cross, target, centre)
    ):
        table = jnp.where(lane == place, column, table)
    stats = jnp.concatenate([table, jnp.zeros((own_ref.shape[1] - tokens, LANES), jnp.float32)])
    stats = stats.T[:STATS]
    own_ref[...] = stats
    copies_ref[...] = jnp.broadcast_to(stats[None], copies_ref.shape)
    out_stats = pltpu.make_async_copy(copies_ref, stats_ref, stats_sem)
    out_stats.start()
    out.wait()
    out_stats.wait()


def products_kernel(
    place_ref, rows_ref, head_ref, terms_ref, picks_ref, held_ref, made_ref, sems, made_sem
):
    into = pltpu.make_async_copy(rows_ref, made_ref, made_sem)
    into.start()
    chips = terms_ref.shape[0]
    tokens = made_ref.shape[0] // 3
    width = held_ref.shape[2]

    def multiply(step):
        products = jnp.dot(made_ref[...], held_ref[step], preferred_element_type=jnp.float32)
        for i, tile in enumerate(tiles_of(products, width // LANES)):
            terms_ref[step, i, 0] = tile[:tokens]
            terms_ref[step, i, 1] = tile[tokens : 2 * tokens]
            picks_ref[step, i] = tile[2 * tokens :].astype(jnp.bfloat16)

    run = stream(
        lambda step: lax.rem(place_ref[0] // 2 + step, chips),
        chips,
        head_ref,
        held_ref,
        sems,
        multiply,
    )
    into.wait()
    run()


def put_shares(parity, factors_ref, terms_ref, picks_ref, out_ref):
    tokens = terms_ref.shape[3]
    factor, level, weight = [factors_ref[i] for i in range(3)]
    for step in range(terms_ref.shape[0]):
        for i, tile in enumerate((3 * parity, 3 * parity + 1, 2)):
            sums = terms_ref[step, tile, 0] + level * terms_ref[step, tile, 1]
            share = factor * sums - weight * picks_ref[step, tile].astype(jnp.float32)
            if i == 2:
                share = folded(parity == 0, share)
            out_ref[step, tokens * i : tokens * i + share.shape[0]] = share.astype(out_ref.dtype)


def give_kernel(
    place_ref,
    scale_ref,
    stats_ref,
    own_ref,
    tokens_ref,
    terms_ref,
    picks_ref,
    give_ref,
    factors_ref,
    loss_ref,
):
    tokens = tokens_ref.shape[0]
    tops, sums, teacher_tops, teacher_sums, crosses, targets = [
        stats_ref[:, i, :tokens] for i in range(6)
    ]
    top, total, teacher_top, teacher_total, cross = [
        part[None] for part in merge_stats(tops, sums, teacher_tops, teacher_sums, crosses)
    ]
    target = jnp.sum(targets, axis=0, keepdims=True)
    student_log = jnp.log(total)
    teacher_log = jnp.log(teacher_total)
    divergence = cross / total - (student_log - teacher_log)
    student_lse = top + student_log
    per_token = divergence + sample_weight * (student_lse - target)
    student_shift = own_ref[0:1, :tokens] - top - student_log
    teacher_shift = own_ref[2:3, :tokens] - teacher_top - teacher_log
    factor = jnp.exp(student_shift)
    level = (
        own_ref[6:7, :tokens] + student_shift - teacher_shift - divergence + sample_weight
    )
    zeros = jnp.zeros((LANES - 3, tokens), jnp.float32)
    columns = jnp.concatenate([factor, level, per_token, zeros], axis=0).T
    share = tokens_ref[:, 1:2]
    weight = share * scale_ref[0]
    loss_ref[...] = jnp.sum(share * columns[:, 2:3], axis=0, keepdims=True)
    for i, column in enumerate(
        (weight * columns[:, 0:1], columns[:, 1:2], sample_weight * weight)
    ):
        factors_ref[i] = jnp.broadcast_to(column, (tokens, LANES))
    put_shares(1 - place_ref[0] % 2, factors_ref, terms_ref, picks_ref, give_ref)


def keep_kernel(place_ref, factors_ref, found_ref, terms_ref, picks_ref, keep_ref, loss_ref):
    loss_ref[...] = found_ref[...]
    put_shares(place_ref[0] % 2, factors_ref, terms_ref, picks_ref, keep_ref)


def sum_kernel(place_ref, own_ref, *refs):
    tokens, half = refs[-1].shape
    total = own_ref[...]
    for share_ref in refs[:-1]:
        total += share_ref[...].astype(jnp.float32)
    one, two, rest = total[:tokens], total[tokens : 2 * tokens], total[2 * tokens :]
    rest = jnp.concatenate([rest, turned(rest)], axis=0)
    turns = [turned(tile) for tile in (rest, one, two)]
    low = low_lanes(one.shape)
    first = place_ref[0] % 2 == 0
    tiles = [
        jnp.where(first, one, jnp.where(low, turns[0], turns[1])),
        jnp.where(first, two, jnp.where(low, turns[1], turns[2])),
        jnp.where(first, rest, turns[2]),
    ]
    total = jnp.concatenate(tiles, axis=1)[:, :half]
    refs[-1][...] = total.astype(refs[-1].dtype)


def paired_shards(
    hidden_states, head, teacher_values, teacher_scales, token_ids, lengths, row_map, loss_scale
):
    count = lax.axis_size("vocab")
    own_index = lax.axis_index("vocab")
    chips = count // 2
    tokens, half = hidden_states.shape
    width = 2 * half
    shard_rows = head.shape[0]
    place = jnp.reshape(own_index, (1,))
    vmem = pl.BlockSpec(memory_space=pltpu.VMEM)
    smem = pl.BlockSpec(memory_space=pltpu.SMEM)
    hbm = pl.BlockSpec(memory_space=pl.ANY)
    params = pltpu.CompilerParams(vmem_limit_bytes=VMEM_LIMIT)
    head = in_hbm(head)
    head_scratch = pltpu.VMEM((chips, shard_rows, width), head.dtype)
    head_sems = pltpu.SemaphoreType.DMA((chips,))
    rows_scratch = pltpu.VMEM((3 * tokens, shard_rows), jnp.bfloat16)
    rows_sem = pltpu.SemaphoreType.DMA
    slots, entries = teacher_values.shape
    hidden_rows = 5 * tokens // 2
    teacher_rows = 2 * slots * (shard_rows + LANES // 2) // LANES

    operands = (
        hidden_states,
        teacher_values,
        teacher_scales,
        token_ids[None, :],
        row_map[None, :],
        lengths[None, :],
    )
    packed, owner, table = pl.pallas_call(
        functools.partial(pack_kernel, shard_rows=shard_rows),
        out_shape=(
            vmem_array((chips, hidden_rows + teacher_rows, LANES), jnp.bfloat16),
            vmem_array((2 * tokens, 2 * tokens), jnp.bfloat16),
            vmem_array((tokens, LANES), jnp.float32),
        ),
        in_specs=[smem] + [hbm] * len(operands),
        out_specs=[vmem] * 3,
        scratch_shapes=[pltpu.VMEM(operand.shape, operand.dtype) for operand in operands]
        + [
            pltpu.VMEM((2 * slots, entries + LANES), jnp.float32),
            pltpu.SemaphoreType.DMA((len(operands),)),
        ],
        compiler_params=params,
        name="pack",
    )(place, *[in_hbm(operand) for operand in operands])
    steps = range(1, chips)
    near = [packed[0]] + [along_chips(packed[step], step) for step in steps]
    first, last = jnp.stack(near[: chips // 2 + 1]), jnp.stack(near[chips // 2 + 1 :])
    early = pl.pallas_call(
        functools.partial(preload_kernel, chips=chips),
        out_shape=vmem_array((EARLY, shard_rows, width), head.dtype),
        in_specs=[smem] + [hbm] * 2,
        out_specs=vmem,
        scratch_shapes=[pltpu.SemaphoreType.DMA((EARLY,))],
        compiler_params=params,
        cost_estimate=pl.CostEstimate(
            flops=0, bytes_accessed=4 * EARLY * shard_rows * width, transcendentals=0
        ),
        name="preload",
    )(place, head, near[3])
    last, early = lax.optimization_barrier((last, early))
    far = [swap_cores(last), swap_cores(first)]

    stats_shape = (count, STATS, pl.cdiv(tokens, LANES) * LANES)
    rows, stats, own_stats = pl.pallas_call(
        logits_kernel,
        out_shape=(
            hbm_array((3 * tokens, shard_rows), jnp.bfloat16),
            hbm_array(stats_shape, jnp.float32),
            vmem_array(stats_shape[1:], jnp.float32),
        ),
        in_specs=[smem] + [vmem] * 7 + [hbm],
        out_specs=[hbm, hbm, vmem],
        scratch_shapes=[
            pltpu.VMEM((chips - EARLY, shard_rows, width), head.dtype),
            rows_scratch,
            pltpu.VMEM((chips, tokens, width), jnp.bfloat16),
            pltpu.VMEM((2 * tokens, (shard_rows + LANES // 2) // 2), jnp.float32),
            pltpu.VMEM((tokens, shard_rows), jnp.float32),
            pltpu.VMEM((shard_rows, tokens), jnp.float32),
            pltpu.VMEM(stats_shape, jnp.float32),
            pltpu.SemaphoreType.DMA((chips - EARLY,)),
            rows_sem,
            rows_sem,
        ],
        compiler_params=params,
        cost_estimate=pl.CostEstimate(
            flops=2 * tokens * head.size, bytes_accessed=2 * head.size, transcendentals=0
        ),
        name="logits",
    )(
        place,
        *[in_vmem(blocks) for blocks in (first, last, far[1], far[0])],
        in_vmem(owner),
        in_vmem(table),
        in_vmem(early),
        head,
    )

    all_stats = lax.all_to_all(stats, "vocab", split_axis=0, concat_axis=0, tiled=True)

    terms, picks = pl.pallas_call(
        products_kernel,
        out_shape=(
            vmem_array((chips, width // LANES, 2, tokens, LANES), jnp.float32),
            vmem_array((chips, width // LANES, tokens, LANES), jnp.bfloat16),
        ),
        in_specs=[smem, hbm, hbm],
        out_specs=[vmem] * 2,
        scratch_shapes=[head_scratch, rows_scratch, head_sems, rows_sem],
        compiler_params=params,
        cost_estimate=pl.CostEstimate(
            flops=6 * tokens * head.size, bytes_accessed=2 * head.size, transcendentals=0
        ),
        name="products",
    )(place, in_hbm(rows), head)

    terms, picks = in_vmem(terms), in_vmem(picks)
    give, factors, loss = pl.pallas_call(
        give_kernel,
        out_shape=(
            vmem_array((chips, hidden_rows, LANES), jnp.bfloat16),
            vmem_array((3, tokens, LANES), jnp.float32),
            vmem_array((1, 1), jnp.float32),
        ),
        in_specs=[smem] * 2 + [vmem] * 5,
        out_specs=[vmem] * 3,
        compiler_params=params,
        name="give",
    )(place, loss_scale, in_vmem(all_stats), in_vmem(own_stats), in_vmem(table), terms, picks)
    taken = swap_cores(give)
    keep, loss = pl.pallas_call(
        keep_kernel,
        out_shape=(
            vmem_array((chips, hidden_rows, LANES), jnp.float32),
            jax.ShapeDtypeStruct((1, 1), jnp.float32),
        ),
        in_specs=[smem] + [vmem] * 4,
        out_specs=[vmem] * 2,
        compiler_params=params,
        cost_estimate=pl.CostEstimate(
            flops=4 * terms.size, bytes_accessed=4 * terms.size, transcendentals=0
        ),
        name="keep",
    )(place, in_vmem(factors), in_vmem(loss), terms, picks)
    sums = keep + taken.astype(jnp.float32)
    shares = [along_chips(sums[step].astype(jnp.bfloat16), step) for step in steps]
    total = pl.pallas_call(
        sum_kernel,
        out_shape=jax.ShapeDtypeStruct((tokens, half), jnp.bfloat16),
        in_specs=[smem] + [vmem] * chips,
        out_specs=vmem,
        compiler_params=params,
        name="total",
    )(place, *[in_vmem(share) for share in [sums[0]] + shares])
    return total, jnp.reshape(loss, (1,))


VMEM_LIMIT = 24 * 1024 * 1024


def shards(
    hidden_states, head, teacher_values, teacher_scales, token_ids, lengths, row_map, loss_scale
):
    count = lax.axis_size("vocab")
    own_index = lax.axis_index("vocab")
    tokens = hidden_states.shape[0]
    own_features = hidden_states.shape[1]
    shard_rows = head.shape[0]
    seq_length = tokens // lengths.shape[0]
    contract_last = (((1,), (1,)), ((), ()))

    scaled = scaled_teacher(teacher_values, teacher_scales, count, shard_rows)
    arrived = lax.all_to_all(scaled, "vocab", split_axis=0, concat_axis=0, tiled=True)
    arrived = arrived.reshape(tokens, shard_rows)
    gathered = to_all(hidden_states, count).transpose(1, 0, 2).reshape(tokens, -1)
    logits = lax.dot_general(gathered, head, contract_last, preferred_element_type=jnp.float32)

    positions = jnp.arange(tokens, dtype=jnp.int32)
    owner = row_map[None, :] == positions[:, None]
    slot_of = jnp.sum(jnp.where(owner, positions[None, :], 0), axis=1)
    teacher = jnp.take(arrived, slot_of, axis=0).astype(jnp.float32)

    seq_ids = jnp.arange(lengths.shape[0], dtype=jnp.int32)
    own_length = jnp.sum(
        jnp.where((positions // seq_length)[:, None] == seq_ids[None, :], lengths[None, :], 0),
        axis=1,
    )
    live_mask = (positions % seq_length < own_length).astype(jnp.float32)
    live_count = jnp.sum(live_mask)

    local_ids = token_ids - own_index * shard_rows
    target_hit = local_ids[:, None] == jnp.arange(shard_rows, dtype=jnp.int32)[None, :]
    target_part = jnp.sum(jnp.where(target_hit, logits, 0.0), axis=1)
    student_top = jnp.max(logits, axis=1)
    teacher_top = jnp.max(teacher, axis=1)
    student_off = logits - student_top[:, None]
    teacher_off = teacher - teacher_top[:, None]
    student_exp = jnp.exp(student_off)
    student_sum = jnp.sum(student_exp, axis=1)
    teacher_sum = jnp.sum(jnp.exp(teacher_off), axis=1)
    cross_sum = jnp.sum(student_exp * (student_off - teacher_off), axis=1)

    stats = to_all(
        jnp.stack(
            [student_top, student_sum, teacher_top, teacher_sum, cross_sum, target_part]
        ),
        count,
    )
    tops, sums, teacher_tops, teacher_sums, crosses, targets = [stats[:, i] for i in range(6)]
    student_max, student_total, teacher_max, teacher_total, cross_total = merge_stats(
        tops, sums, teacher_tops, teacher_sums, crosses
    )
    student_log = jnp.log(student_total)
    teacher_log = jnp.log(teacher_total)
    student_lse = student_max + student_log
    teacher_lse = teacher_max + teacher_log
    divergence = cross_total / student_total - (student_log - teacher_log)
    target = jnp.sum(targets, axis=0)

    per_token = divergence + sample_weight * (student_lse - target)
    loss = jnp.reshape(jnp.sum(live_mask * per_token) / live_count, (1,))
    token_weight = live_mask * loss_scale[0] / live_count
    log_student = logits - student_lse[:, None]
    log_teacher = teacher - teacher_lse[:, None]
    student_prob = jnp.exp(log_student)
    grad_logits = (
        token_weight[:, None]
        * (
            student_prob * (log_student - log_teacher - divergence[:, None])
            + sample_weight * (student_prob - target_hit.astype(jnp.float32))
        )
    ).astype(jnp.bfloat16)
    terms = jnp.dot(grad_logits, head, preferred_element_type=jnp.float32).astype(jnp.bfloat16)
    terms = terms.reshape(tokens, count, own_features).transpose(1, 0, 2)
    shares = lax.all_to_all(terms, "vocab", split_axis=0, concat_axis=0, tiled=True)
    grad_hidden = jnp.sum(shares.astype(jnp.float32), axis=0)
    return (grad_hidden.astype(jnp.bfloat16), loss)


def any_shards(*arrays):
    hidden_states, head, teacher_values = arrays[:3]
    count = lax.axis_size("vocab")
    fits = (
        count % 2 == 0
        and hidden_states.shape[1] == 5 * LANES // 2
        and hidden_states.shape[0] % 32 == 0
        and head.shape[0] % LANES == LANES // 2
        and (head.shape[0] + LANES // 2) // LANES % 2 == 0
        and teacher_values.shape[0] == 4
    )
    return paired_shards(*arrays) if fits else shards(*arrays)


def solution(mesh):
    in_specs = (
        P("dom", "vocab"),
        P("vocab", None),
        P(("dom", "vocab"), None),
        P(("dom", "vocab"), None),
        P("dom"),
        P("dom"),
        P("dom"),
        P(),
    )
    out_specs = (P("dom", "vocab"), P("dom"))
    return jax.shard_map(
        any_shards, mesh=mesh, in_specs=in_specs, out_specs=out_specs, check_vma=False
    )
```

```python
import functools

import jax
import jax.numpy as jnp
from jax import lax
from jax.experimental import pallas as pl
from jax.experimental.pallas import tpu as pltpu
from jax.sharding import PartitionSpec as P

BLOCK = 32
LANES = 128
STATS = 8
AHEAD = 3
EARLY = 3


sample_weight = 0.5


def to_all(piece, count):
    copies = jnp.broadcast_to(piece[None], (count,) + piece.shape)
    return lax.all_to_all(copies, "vocab", split_axis=0, concat_axis=0, tiled=True)


def scaled_teacher(teacher_values, teacher_scales, count, shard_rows):
    slot_rows = teacher_values.shape[0]
    scaled = (
        teacher_values.astype(jnp.float32).reshape(slot_rows, -1, BLOCK) * teacher_scales[:, :, None]
    ).astype(jnp.bfloat16)
    return scaled.reshape(slot_rows, count, shard_rows).transpose(1, 0, 2)


def merge_stats(tops, sums, teacher_tops, teacher_sums, crosses):
    top = jnp.max(tops, axis=0)
    teacher_top = jnp.max(teacher_tops, axis=0)
    shift = tops - top[None]
    teacher_shift = teacher_tops - teacher_top[None]
    weight = jnp.exp(shift)
    total = jnp.sum(sums * weight, axis=0)
    teacher_total = jnp.sum(teacher_sums * jnp.exp(teacher_shift), axis=0)
    cross = jnp.sum(weight * (crosses + sums * (shift - teacher_shift)), axis=0)
    return top, total, teacher_top, teacher_total, cross


def swap_cores(array):
    count = lax.axis_size("vocab")
    return lax.ppermute(array, "vocab", [(i, i ^ 1) for i in range(count)])


def along_chips(array, step):
    count = lax.axis_size("vocab")
    return lax.ppermute(array, "vocab", [(i, (i + 2 * step) % count) for i in range(count)])


def vmem_array(shape, dtype):
    return pltpu.VMEM(shape, dtype)


def in_vmem(array):
    return pltpu.with_memory_space_constraint(array, pltpu.VMEM)


def in_hbm(array):
    return pltpu.with_memory_space_constraint(array, pltpu.HBM)


def hbm_array(shape, dtype):
    return pltpu.HBM(shape, dtype)


def low_lanes(shape):
    return lax.broadcasted_iota(jnp.int32, shape, len(shape) - 1) < LANES // 2


def low_rows(shape, count):
    return lax.broadcasted_iota(jnp.int32, shape, 0) < count


def turned(array):
    return pltpu.roll(array, LANES // 2, 1)


def folded(first, tile):
    rows = tile.shape[0] // 2
    upper, lower = tile[:rows], turned(tile[rows:])
    low = low_lanes(upper.shape)
    return jnp.where(first, jnp.where(low, upper, lower), jnp.where(low, lower, upper))


def tiles_of(array, count):
    return [array[:, LANES * i : LANES * (i + 1)] for i in range(count)]


def column_of(row):
    size = row.shape[1]
    down = lax.broadcasted_iota(jnp.int32, (size, size), 0)
    along = lax.broadcasted_iota(jnp.int32, (size, size), 1)
    return jnp.sum(jnp.where(down == along, row, jnp.zeros_like(row)), axis=1, keepdims=True)


def token_facts(ids, row_map, lengths, first_entry, slots):
    tokens = row_map.shape[1]
    token = lax.broadcasted_iota(jnp.int32, (tokens, tokens), 0)
    slot = lax.broadcasted_iota(jnp.int32, (tokens, tokens), 1)
    owner = (row_map == token).astype(jnp.float32)
    named = jnp.max(owner, axis=1, keepdims=True)
    owner = jnp.where((slot == 0) & (named == 0.0), 1.0, owner)
    rows = 2 * tokens
    slot = lax.broadcasted_iota(jnp.int32, (tokens, rows), 0)
    row = lax.broadcasted_iota(jnp.int32, (tokens, rows), 1)
    source, within = row // (2 * slots), row % (2 * slots)
    chosen = (slot == source * slots + within % slots).astype(jnp.bfloat16)
    owner = jnp.dot(owner.astype(jnp.bfloat16), chosen, preferred_element_type=jnp.float32)
    odd = within >= slots
    owner = jnp.concatenate([jnp.where(odd, 0.0, owner), jnp.where(odd, owner, 0.0)], axis=0)

    seqs = lengths.shape[1]
    seq_length = tokens // seqs
    position = lax.broadcasted_iota(jnp.int32, (tokens, 1), 0)
    live_until = jnp.zeros((tokens, 1), jnp.int32)
    for seq in range(seqs):
        inside = (position >= seq * seq_length) & (position < (seq + 1) * seq_length)
        until = lengths[:, seq : seq + 1] + seq * seq_length
        live_until = jnp.where(inside, until, live_until)
    live = (position < live_until).astype(jnp.float32)
    count = jnp.sum(live, axis=0, keepdims=True)
    entry = (column_of(ids) - first_entry).astype(jnp.float32)
    lane = lax.broadcasted_iota(jnp.int32, (tokens, LANES), 1)
    return owner.astype(jnp.bfloat16), jnp.where(lane == 0, entry, live / count)


def pack_kernel(place_ref, *refs, shard_rows):
    outside, refs = refs[:6], refs[6:]
    packed_ref, owner_ref, table_ref = refs[:3]
    inside, wide_ref, sems = refs[3:9], refs[9], refs[10]
    copies = [
        pltpu.make_async_copy(source, target, sems.at[i])
        for i, (source, target) in enumerate(zip(outside, inside))
    ]
    for copy in copies:
        copy.start()
    for copy in copies:
        copy.wait()
    hidden_ref, values_ref, scales_ref, ids_ref, map_ref, lengths_ref = inside
    owner_ref[...], table_ref[...] = token_facts(
        ids_ref[...], map_ref[...], lengths_ref[...], place_ref[0] * shard_rows, values_ref.shape[0]
    )
    chips = packed_ref.shape[0]
    tokens, half = hidden_ref.shape
    slots, entries = values_ref.shape
    pair = entries // chips
    shard = pair // 2
    blocks = pair // BLOCK
    scales = jnp.concatenate([scales_ref[...]] * 2, axis=0)
    stacked = jnp.concatenate(
        [scales[:, blocks * chip : blocks * (chip + 1)] for chip in range(chips)], axis=0
    )
    block = lax.broadcasted_iota(jnp.int32, (blocks, pair), 0)
    entry = lax.broadcasted_iota(jnp.int32, (blocks, pair), 1)
    inside = (entry >= block * BLOCK) & (entry < block * BLOCK + BLOCK)
    spread = jnp.dot(
        stacked.astype(jnp.bfloat16),
        inside.astype(jnp.bfloat16),
        preferred_element_type=jnp.float32,
    )
    values = values_ref[...].astype(jnp.float32)
    values = jnp.concatenate([values, values], axis=0)
    for chip in range(chips):
        wide_ref[:, pair * chip : pair * (chip + 1)] = (
            values[:, pair * chip : pair * (chip + 1)]
            * spread[2 * slots * chip : 2 * slots * (chip + 1)]
        )
    wide_ref[:, entries:] = jnp.zeros((2 * slots, LANES), jnp.float32)

    hidden = hidden_ref[...].astype(jnp.float32)
    zeros = jnp.zeros((tokens, LANES // 2), jnp.float32)
    tiles = tiles_of(jnp.concatenate([hidden, zeros], axis=1), 3)
    turns = [turned(tile) for tile in tiles]
    low = low_lanes(tiles[0].shape)
    first = place_ref[0] % 2 == 0
    hidden = jnp.concatenate(
        [
            jnp.where(first, tiles[0], jnp.where(low, turns[0], turns[1])),
            jnp.where(first, tiles[1], jnp.where(low, turns[1], turns[2])),
            folded(first, jnp.where(first, tiles[2], turns[0])),
        ],
        axis=0,
    ).astype(jnp.bfloat16)
    hidden_rows = hidden.shape[0]
    upper = low_rows((2 * slots, LANES), slots)
    low = low_lanes((2 * slots, LANES))
    tile_pairs = (shard + LANES // 2) // LANES // 2
    for chip in range(chips):
        rows = []
        for core in range(2):
            start = pair * chip + (shard - LANES // 2) * core
            tiles = [
                wide_ref[:, start + LANES * i : start + LANES * (i + 1)]
                for i in range(2 * tile_pairs + core)
            ]
            if core == 1:
                tiles = [turned(tile) for tile in tiles]
                tiles = [
                    jnp.where(low, tiles[i], tiles[i + 1]) for i in range(2 * tile_pairs)
                ]
            rows += [
                jnp.where(upper, tiles[2 * i], tiles[2 * i + 1]) for i in range(tile_pairs)
            ]
        step = lax.rem(chip - place_ref[0] // 2 + chips, chips)
        packed_ref[step, :hidden_rows] = hidden
        packed_ref[step, hidden_rows:] = jnp.concatenate(rows, axis=0).astype(jnp.bfloat16)


def head_copy(head_ref, held_ref, sems, chip, step):
    width = held_ref.shape[2]
    columns = pl.ds(pl.multiple_of(chip * width, LANES), width)
    return pltpu.make_async_copy(head_ref.at[:, columns], held_ref.at[step], sems.at[step])


def stream(chip_at, count, ahead, head_ref, held_ref, sems, use):
    def copy(step):
        return head_copy(head_ref, held_ref, sems, chip_at(step), step)

    def body(step, _):
        copy(step).wait()
        if ahead < count:

            @pl.when(step + ahead < count)
            def _():
                copy(step + ahead).start()

        use(step)

    for step in range(min(ahead, count)):
        copy(step).start()
    return lambda: lax.fori_loop(0, count, body, None)


def source_chip(place_ref, chips, step):
    return lax.rem(place_ref[0] // 2 - step + chips, chips)


def preload_kernel(place_ref, head_ref, _, early_ref, sems, *, chips):
    copies = [
        head_copy(head_ref, early_ref, sems, source_chip(place_ref, chips, step), step)
        for step in range(EARLY)
    ]
    for copy in copies:
        copy.start()
    for copy in copies:
        copy.wait()


def logits_kernel(
    place_ref,
    first_ref,
    last_ref,
    first_far_ref,
    last_far_ref,
    owner_ref,
    tokens_ref,
    early_ref,
    head_ref,
    rows_ref,
    stats_ref,
    own_ref,
    held_ref,
    made_ref,
    hidden_ref,
    arrived_ref,
    teacher_ref,
    logits_ref,
    copies_ref,
    sems,
    made_sem,
    stats_sem,
):
    core = place_ref[0] % 2
    chips, tokens, width = hidden_ref.shape
    shard_rows = head_ref.shape[0]
    hidden_rows = 5 * tokens // 2
    slots = tokens // (2 * chips)
    low = low_lanes((tokens // 2, LANES))

    def add(step, columns):
        logits_ref[...] += lax.dot_general(
            columns, hidden_ref[step], (((1,), (1,)), ((), ())), preferred_element_type=jnp.float32
        )

    run = stream(
        lambda step: source_chip(place_ref, chips, step + EARLY),
        chips - EARLY,
        chips - EARLY,
        head_ref,
        held_ref,
        sems,
        lambda step: add(step + EARLY, held_ref[step]),
    )

    def unpack(near_ref, far_ref, base):
        for place in range(near_ref.shape[0]):
            step = place + base
            blocks = near_ref.at[place], far_ref.at[place]
            for block, parity in zip(blocks, (core, 1 - core)):
                for i in range(2):
                    column = LANES * i + (width - 2 * LANES) * parity
                    lanes = pl.ds(pl.multiple_of(column, LANES), LANES)
                    hidden_ref[step, :, lanes] = block[tokens * i : tokens * (i + 1)]
                teacher = block[hidden_rows:].astype(jnp.float32)
                share = teacher.shape[0] // 2
                teacher = jnp.where(core == 0, teacher[:share], teacher[share:])
                row = 2 * slots * (2 * source_chip(place_ref, chips, step) + parity)
                rows = pl.ds(pl.multiple_of(row, 2 * slots), 2 * slots)
                for i in range(share // (2 * slots)):
                    arrived_ref[rows, LANES * i : LANES * (i + 1)] = teacher[
                        2 * slots * i : 2 * slots * (i + 1)
                    ]
            own, other = [block[2 * tokens : hidden_rows].astype(jnp.float32) for block in blocks]
            one, two = jnp.where(core == 0, own, other), jnp.where(core == 0, other, own)
            tile = [jnp.where(low, one, two), turned(jnp.where(low, two, one))]
            tile = jnp.concatenate(tile, axis=0).astype(jnp.bfloat16)
            hidden_ref[step, :, 2 * LANES : 3 * LANES] = tile

    unpack(first_ref, first_far_ref, 0)
    unpack(last_ref, last_far_ref, first_ref.shape[0])
    logits_ref[...] = jnp.zeros_like(logits_ref)
    lax.fori_loop(0, EARLY, lambda step, _: add(step, early_ref[step]), None)
    placed = jnp.dot(
        owner_ref[...], arrived_ref[...].astype(jnp.bfloat16), preferred_element_type=jnp.float32
    )
    pairs = arrived_ref.shape[1] // LANES
    even, odd = tiles_of(placed[:tokens], pairs), tiles_of(placed[tokens:], pairs)
    teacher = jnp.concatenate([tile for pair in zip(even, odd) for tile in pair], axis=1)
    teacher = teacher[:, :shard_rows]
    teacher_top = jnp.max(teacher, axis=1, keepdims=True)
    teacher_off = teacher - teacher_top
    teacher_total = jnp.sum(jnp.exp(teacher_off), axis=1, keepdims=True)
    teacher_ref[...] = teacher_off
    run()
    logits = logits_ref[...].T

    top = jnp.max(logits, axis=1, keepdims=True)
    off = logits - top
    exps = jnp.exp(off)
    total = jnp.sum(exps, axis=1, keepdims=True)
    gap = off - teacher_ref[...]
    cross = jnp.sum(exps * gap, axis=1, keepdims=True)
    centre = cross / total
    entry = lax.broadcasted_iota(jnp.int32, (tokens, shard_rows), 1)
    hit = entry == tokens_ref[:, :1].astype(jnp.int32)
    target = jnp.sum(jnp.where(hit, logits, 0.0), axis=1, keepdims=True)
    made_ref[:tokens] = (exps * (gap - centre)).astype(jnp.bfloat16)
    made_ref[tokens : 2 * tokens] = exps.astype(jnp.bfloat16)
    made_ref[2 * tokens :] = hit.astype(jnp.bfloat16)
    out = pltpu.make_async_copy(made_ref, rows_ref, made_sem)
    out.start()

    lane = lax.broadcasted_iota(jnp.int32, (tokens, LANES), 1)
    table = jnp.zeros((tokens, LANES), jnp.float32)
    for place, column in enumerate(
        (top, total, teacher_top, teacher_total, cross, target, centre)
    ):
        table = jnp.where(lane == place, column, table)
    stats = jnp.concatenate([table, jnp.zeros((own_ref.shape[1] - tokens, LANES), jnp.float32)])
    stats = stats.T[:STATS]
    own_ref[...] = stats
    copies_ref[...] = jnp.broadcast_to(stats[None], copies_ref.shape)
    out_stats = pltpu.make_async_copy(copies_ref, stats_ref, stats_sem)
    out_stats.start()
    out.wait()
    out_stats.wait()


def products_kernel(
    place_ref, rows_ref, head_ref, terms_ref, picks_ref, held_ref, made_ref, sems, made_sem
):
    into = pltpu.make_async_copy(rows_ref, made_ref, made_sem)
    into.start()
    chips = terms_ref.shape[0]
    tokens = made_ref.shape[0] // 3
    width = held_ref.shape[2]

    def multiply(step):
        products = jnp.dot(made_ref[...], held_ref[step], preferred_element_type=jnp.float32)
        for i, tile in enumerate(tiles_of(products, width // LANES)):
            terms_ref[step, i, 0] = tile[:tokens]
            terms_ref[step, i, 1] = tile[tokens : 2 * tokens]
            picks_ref[step, i] = tile[2 * tokens :].astype(jnp.bfloat16)

    run = stream(
        lambda step: lax.rem(place_ref[0] // 2 + step, chips),
        chips,
        AHEAD,
        head_ref,
        held_ref,
        sems,
        multiply,
    )
    into.wait()
    run()


def put_shares(parity, factors_ref, terms_ref, picks_ref, out_ref):
    tokens = terms_ref.shape[3]
    factor, level, weight = [factors_ref[i] for i in range(3)]
    for step in range(terms_ref.shape[0]):
        for i, tile in enumerate((3 * parity, 3 * parity + 1, 2)):
            sums = terms_ref[step, tile, 0] + level * terms_ref[step, tile, 1]
            share = factor * sums - weight * picks_ref[step, tile].astype(jnp.float32)
            if i == 2:
                share = folded(parity == 0, share)
            out_ref[step, tokens * i : tokens * i + share.shape[0]] = share.astype(out_ref.dtype)


def give_kernel(
    place_ref,
    scale_ref,
    stats_ref,
    own_ref,
    tokens_ref,
    terms_ref,
    picks_ref,
    give_ref,
    factors_ref,
    loss_ref,
):
    tokens = tokens_ref.shape[0]
    tops, sums, teacher_tops, teacher_sums, crosses, targets = [
        stats_ref[:, i, :tokens] for i in range(6)
    ]
    top, total, teacher_top, teacher_total, cross = [
        part[None] for part in merge_stats(tops, sums, teacher_tops, teacher_sums, crosses)
    ]
    target = jnp.sum(targets, axis=0, keepdims=True)
    student_log = jnp.log(total)
    teacher_log = jnp.log(teacher_total)
    divergence = cross / total - (student_log - teacher_log)
    student_lse = top + student_log
    per_token = divergence + sample_weight * (student_lse - target)
    student_shift = own_ref[0:1, :tokens] - top - student_log
    teacher_shift = own_ref[2:3, :tokens] - teacher_top - teacher_log
    factor = jnp.exp(student_shift)
    level = (
        own_ref[6:7, :tokens] + student_shift - teacher_shift - divergence + sample_weight
    )
    zeros = jnp.zeros((LANES - 3, tokens), jnp.float32)
    columns = jnp.concatenate([factor, level, per_token, zeros], axis=0).T
    share = tokens_ref[:, 1:2]
    weight = share * scale_ref[0]
    loss_ref[...] = jnp.sum(share * columns[:, 2:3], axis=0, keepdims=True)
    for i, column in enumerate(
        (weight * columns[:, 0:1], columns[:, 1:2], sample_weight * weight)
    ):
        factors_ref[i] = jnp.broadcast_to(column, (tokens, LANES))
    put_shares(1 - place_ref[0] % 2, factors_ref, terms_ref, picks_ref, give_ref)


def keep_kernel(place_ref, factors_ref, found_ref, terms_ref, picks_ref, keep_ref, loss_ref):
    loss_ref[...] = found_ref[...]
    put_shares(place_ref[0] % 2, factors_ref, terms_ref, picks_ref, keep_ref)


def sum_kernel(place_ref, own_ref, *refs):
    tokens, half = refs[-1].shape
    total = own_ref[...]
    for share_ref in refs[:-1]:
        total += share_ref[...].astype(jnp.float32)
    one, two, rest = total[:tokens], total[tokens : 2 * tokens], total[2 * tokens :]
    rest = jnp.concatenate([rest, turned(rest)], axis=0)
    turns = [turned(tile) for tile in (rest, one, two)]
    low = low_lanes(one.shape)
    first = place_ref[0] % 2 == 0
    tiles = [
        jnp.where(first, one, jnp.where(low, turns[0], turns[1])),
        jnp.where(first, two, jnp.where(low, turns[1], turns[2])),
        jnp.where(first, rest, turns[2]),
    ]
    total = jnp.concatenate(tiles, axis=1)[:, :half]
    refs[-1][...] = total.astype(refs[-1].dtype)


def paired_shards(
    hidden_states, head, teacher_values, teacher_scales, token_ids, lengths, row_map, loss_scale
):
    count = lax.axis_size("vocab")
    own_index = lax.axis_index("vocab")
    chips = count // 2
    tokens, half = hidden_states.shape
    width = 2 * half
    shard_rows = head.shape[0]
    place = jnp.reshape(own_index, (1,))
    vmem = pl.BlockSpec(memory_space=pltpu.VMEM)
    smem = pl.BlockSpec(memory_space=pltpu.SMEM)
    hbm = pl.BlockSpec(memory_space=pl.ANY)
    params = pltpu.CompilerParams(vmem_limit_bytes=VMEM_LIMIT)
    head = in_hbm(head)
    head_scratch = pltpu.VMEM((chips, shard_rows, width), head.dtype)
    head_sems = pltpu.SemaphoreType.DMA((chips,))
    rows_scratch = pltpu.VMEM((3 * tokens, shard_rows), jnp.bfloat16)
    rows_sem = pltpu.SemaphoreType.DMA
    slots, entries = teacher_values.shape
    hidden_rows = 5 * tokens // 2
    teacher_rows = 2 * slots * (shard_rows + LANES // 2) // LANES

    operands = (
        hidden_states,
        teacher_values,
        teacher_scales,
        token_ids[None, :],
        row_map[None, :],
        lengths[None, :],
    )
    packed, owner, table = pl.pallas_call(
        functools.partial(pack_kernel, shard_rows=shard_rows),
        out_shape=(
            vmem_array((chips, hidden_rows + teacher_rows, LANES), jnp.bfloat16),
            vmem_array((2 * tokens, 2 * tokens), jnp.bfloat16),
            vmem_array((tokens, LANES), jnp.float32),
        ),
        in_specs=[smem] + [hbm] * len(operands),
        out_specs=[vmem] * 3,
        scratch_shapes=[pltpu.VMEM(operand.shape, operand.dtype) for operand in operands]
        + [
            pltpu.VMEM((2 * slots, entries + LANES), jnp.float32),
            pltpu.SemaphoreType.DMA((len(operands),)),
        ],
        compiler_params=params,
        name="pack",
    )(place, *[in_hbm(operand) for operand in operands])
    steps = range(1, chips)
    near = [packed[0]] + [along_chips(packed[step], step) for step in steps]
    first, last = jnp.stack(near[: chips // 2 + 1]), jnp.stack(near[chips // 2 + 1 :])
    early = pl.pallas_call(
        functools.partial(preload_kernel, chips=chips),
        out_shape=vmem_array((EARLY, shard_rows, width), head.dtype),
        in_specs=[smem] + [hbm] * 2,
        out_specs=vmem,
        scratch_shapes=[pltpu.SemaphoreType.DMA((EARLY,))],
        compiler_params=params,
        cost_estimate=pl.CostEstimate(
            flops=0, bytes_accessed=4 * EARLY * shard_rows * width, transcendentals=0
        ),
        name="preload",
    )(place, head, near[3])
    last, early = lax.optimization_barrier((last, early))
    far = [swap_cores(last), swap_cores(first)]

    stats_shape = (count, STATS, pl.cdiv(tokens, LANES) * LANES)
    rows, stats, own_stats = pl.pallas_call(
        logits_kernel,
        out_shape=(
            hbm_array((3 * tokens, shard_rows), jnp.bfloat16),
            hbm_array(stats_shape, jnp.float32),
            vmem_array(stats_shape[1:], jnp.float32),
        ),
        in_specs=[smem] + [vmem] * 7 + [hbm],
        out_specs=[hbm, hbm, vmem],
        scratch_shapes=[
            pltpu.VMEM((chips - EARLY, shard_rows, width), head.dtype),
            rows_scratch,
            pltpu.VMEM((chips, tokens, width), jnp.bfloat16),
            pltpu.VMEM((2 * tokens, (shard_rows + LANES // 2) // 2), jnp.float32),
            pltpu.VMEM((tokens, shard_rows), jnp.float32),
            pltpu.VMEM((shard_rows, tokens), jnp.float32),
            pltpu.VMEM(stats_shape, jnp.float32),
            pltpu.SemaphoreType.DMA((chips - EARLY,)),
            rows_sem,
            rows_sem,
        ],
        compiler_params=params,
        cost_estimate=pl.CostEstimate(
            flops=2 * tokens * head.size, bytes_accessed=2 * head.size, transcendentals=0
        ),
        name="logits",
    )(
        place,
        *[in_vmem(blocks) for blocks in (first, last, far[1], far[0])],
        in_vmem(owner),
        in_vmem(table),
        in_vmem(early),
        head,
    )

    all_stats = lax.all_to_all(stats, "vocab", split_axis=0, concat_axis=0, tiled=True)

    terms, picks = pl.pallas_call(
        products_kernel,
        out_shape=(
            vmem_array((chips, width // LANES, 2, tokens, LANES), jnp.float32),
            vmem_array((chips, width // LANES, tokens, LANES), jnp.bfloat16),
        ),
        in_specs=[smem, hbm, hbm],
        out_specs=[vmem] * 2,
        scratch_shapes=[head_scratch, rows_scratch, head_sems, rows_sem],
        compiler_params=params,
        cost_estimate=pl.CostEstimate(
            flops=6 * tokens * head.size, bytes_accessed=2 * head.size, transcendentals=0
        ),
        name="products",
    )(place, in_hbm(rows), head)

    terms, picks = in_vmem(terms), in_vmem(picks)
    give, factors, loss = pl.pallas_call(
        give_kernel,
        out_shape=(
            vmem_array((chips, hidden_rows, LANES), jnp.bfloat16),
            vmem_array((3, tokens, LANES), jnp.float32),
            vmem_array((1, 1), jnp.float32),
        ),
        in_specs=[smem] * 2 + [vmem] * 5,
        out_specs=[vmem] * 3,
        compiler_params=params,
        name="give",
    )(place, loss_scale, in_vmem(all_stats), in_vmem(own_stats), in_vmem(table), terms, picks)
    taken = swap_cores(give)
    keep, loss = pl.pallas_call(
        keep_kernel,
        out_shape=(
            vmem_array((chips, hidden_rows, LANES), jnp.float32),
            jax.ShapeDtypeStruct((1, 1), jnp.float32),
        ),
        in_specs=[smem] + [vmem] * 4,
        out_specs=[vmem] * 2,
        compiler_params=params,
        cost_estimate=pl.CostEstimate(
            flops=4 * terms.size, bytes_accessed=4 * terms.size, transcendentals=0
        ),
        name="keep",
    )(place, in_vmem(factors), in_vmem(loss), terms, picks)
    sums = keep + taken.astype(jnp.float32)
    shares = [along_chips(sums[step].astype(jnp.bfloat16), step) for step in steps]
    total = pl.pallas_call(
        sum_kernel,
        out_shape=jax.ShapeDtypeStruct((tokens, half), jnp.bfloat16),
        in_specs=[smem] + [vmem] * chips,
        out_specs=vmem,
        compiler_params=params,
        name="total",
    )(place, *[in_vmem(share) for share in [sums[0]] + shares])
    return total, jnp.reshape(loss, (1,))


VMEM_LIMIT = 24 * 1024 * 1024


def shards(
    hidden_states, head, teacher_values, teacher_scales, token_ids, lengths, row_map, loss_scale
):
    count = lax.axis_size("vocab")
    own_index = lax.axis_index("vocab")
    tokens = hidden_states.shape[0]
    own_features = hidden_states.shape[1]
    shard_rows = head.shape[0]
    seq_length = tokens // lengths.shape[0]
    contract_last = (((1,), (1,)), ((), ()))

    scaled = scaled_teacher(teacher_values, teacher_scales, count, shard_rows)
    arrived = lax.all_to_all(scaled, "vocab", split_axis=0, concat_axis=0, tiled=True)
    arrived = arrived.reshape(tokens, shard_rows)
    gathered = to_all(hidden_states, count).transpose(1, 0, 2).reshape(tokens, -1)
    logits = lax.dot_general(gathered, head, contract_last, preferred_element_type=jnp.float32)

    positions = jnp.arange(tokens, dtype=jnp.int32)
    owner = row_map[None, :] == positions[:, None]
    slot_of = jnp.sum(jnp.where(owner, positions[None, :], 0), axis=1)
    teacher = jnp.take(arrived, slot_of, axis=0).astype(jnp.float32)

    seq_ids = jnp.arange(lengths.shape[0], dtype=jnp.int32)
    own_length = jnp.sum(
        jnp.where((positions // seq_length)[:, None] == seq_ids[None, :], lengths[None, :], 0),
        axis=1,
    )
    live_mask = (positions % seq_length < own_length).astype(jnp.float32)
    live_count = jnp.sum(live_mask)

    local_ids = token_ids - own_index * shard_rows
    target_hit = local_ids[:, None] == jnp.arange(shard_rows, dtype=jnp.int32)[None, :]
    target_part = jnp.sum(jnp.where(target_hit, logits, 0.0), axis=1)
    student_top = jnp.max(logits, axis=1)
    teacher_top = jnp.max(teacher, axis=1)
    student_off = logits - student_top[:, None]
    teacher_off = teacher - teacher_top[:, None]
    student_exp = jnp.exp(student_off)
    student_sum = jnp.sum(student_exp, axis=1)
    teacher_sum = jnp.sum(jnp.exp(teacher_off), axis=1)
    cross_sum = jnp.sum(student_exp * (student_off - teacher_off), axis=1)

    stats = to_all(
        jnp.stack(
            [student_top, student_sum, teacher_top, teacher_sum, cross_sum, target_part]
        ),
        count,
    )
    tops, sums, teacher_tops, teacher_sums, crosses, targets = [stats[:, i] for i in range(6)]
    student_max, student_total, teacher_max, teacher_total, cross_total = merge_stats(
        tops, sums, teacher_tops, teacher_sums, crosses
    )
    student_log = jnp.log(student_total)
    teacher_log = jnp.log(teacher_total)
    student_lse = student_max + student_log
    teacher_lse = teacher_max + teacher_log
    divergence = cross_total / student_total - (student_log - teacher_log)
    target = jnp.sum(targets, axis=0)

    per_token = divergence + sample_weight * (student_lse - target)
    loss = jnp.reshape(jnp.sum(live_mask * per_token) / live_count, (1,))
    token_weight = live_mask * loss_scale[0] / live_count
    log_student = logits - student_lse[:, None]
    log_teacher = teacher - teacher_lse[:, None]
    student_prob = jnp.exp(log_student)
    grad_logits = (
        token_weight[:, None]
        * (
            student_prob * (log_student - log_teacher - divergence[:, None])
            + sample_weight * (student_prob - target_hit.astype(jnp.float32))
        )
    ).astype(jnp.bfloat16)
    terms = jnp.dot(grad_logits, head, preferred_element_type=jnp.float32).astype(jnp.bfloat16)
    terms = terms.reshape(tokens, count, own_features).transpose(1, 0, 2)
    shares = lax.all_to_all(terms, "vocab", split_axis=0, concat_axis=0, tiled=True)
    grad_hidden = jnp.sum(shares.astype(jnp.float32), axis=0)
    return (grad_hidden.astype(jnp.bfloat16), loss)


def any_shards(*arrays):
    hidden_states, head, teacher_values = arrays[:3]
    count = lax.axis_size("vocab")
    fits = (
        count % 2 == 0
        and hidden_states.shape[1] == 5 * LANES // 2
        and hidden_states.shape[0] % 32 == 0
        and head.shape[0] % LANES == LANES // 2
        and (head.shape[0] + LANES // 2) // LANES % 2 == 0
        and teacher_values.shape[0] == 4
    )
    return paired_shards(*arrays) if fits else shards(*arrays)


def solution(mesh):
    in_specs = (
        P("dom", "vocab"),
        P("vocab", None),
        P(("dom", "vocab"), None),
        P(("dom", "vocab"), None),
        P("dom"),
        P("dom"),
        P("dom"),
        P(),
    )
    out_specs = (P("dom", "vocab"), P("dom"))
    return jax.shard_map(
        any_shards, mesh=mesh, in_specs=in_specs, out_specs=out_specs, check_vma=False
    )
```

```python
import functools

import jax
import jax.numpy as jnp
from jax import lax
from jax.experimental import pallas as pl
from jax.experimental.pallas import tpu as pltpu
from jax.sharding import PartitionSpec as P

BLOCK = 32
LANES = 128
STATS = 8
AHEAD = 3
EARLY = 3


sample_weight = 0.5


def to_all(piece, count):
    copies = jnp.broadcast_to(piece[None], (count,) + piece.shape)
    return lax.all_to_all(copies, "vocab", split_axis=0, concat_axis=0, tiled=True)


def scaled_teacher(teacher_values, teacher_scales, count, shard_rows):
    slot_rows = teacher_values.shape[0]
    scaled = (
        teacher_values.astype(jnp.float32).reshape(slot_rows, -1, BLOCK) * teacher_scales[:, :, None]
    ).astype(jnp.bfloat16)
    return scaled.reshape(slot_rows, count, shard_rows).transpose(1, 0, 2)


def merge_stats(tops, sums, teacher_tops, teacher_sums, crosses):
    top = jnp.max(tops, axis=0)
    teacher_top = jnp.max(teacher_tops, axis=0)
    shift = tops - top[None]
    teacher_shift = teacher_tops - teacher_top[None]
    weight = jnp.exp(shift)
    total = jnp.sum(sums * weight, axis=0)
    teacher_total = jnp.sum(teacher_sums * jnp.exp(teacher_shift), axis=0)
    cross = jnp.sum(weight * (crosses + sums * (shift - teacher_shift)), axis=0)
    return top, total, teacher_top, teacher_total, cross


def swap_cores(array):
    count = lax.axis_size("vocab")
    return lax.ppermute(array, "vocab", [(i, i ^ 1) for i in range(count)])


def along_chips(array, step):
    count = lax.axis_size("vocab")
    return lax.ppermute(array, "vocab", [(i, (i + 2 * step) % count) for i in range(count)])


def vmem_array(shape, dtype):
    return pltpu.VMEM(shape, dtype)


def in_vmem(array):
    return pltpu.with_memory_space_constraint(array, pltpu.VMEM)


def in_hbm(array):
    return pltpu.with_memory_space_constraint(array, pltpu.HBM)


def hbm_array(shape, dtype):
    return pltpu.HBM(shape, dtype)


def low_lanes(shape):
    return lax.broadcasted_iota(jnp.int32, shape, len(shape) - 1) < LANES // 2


def low_rows(shape, count):
    return lax.broadcasted_iota(jnp.int32, shape, 0) < count


def turned(array):
    return pltpu.roll(array, LANES // 2, 1)


def folded(first, tile):
    rows = tile.shape[0] // 2
    upper, lower = tile[:rows], turned(tile[rows:])
    low = low_lanes(upper.shape)
    return jnp.where(first, jnp.where(low, upper, lower), jnp.where(low, lower, upper))


def tiles_of(array, count):
    return [array[:, LANES * i : LANES * (i + 1)] for i in range(count)]


def column_of(row):
    size = row.shape[1]
    down = lax.broadcasted_iota(jnp.int32, (size, size), 0)
    along = lax.broadcasted_iota(jnp.int32, (size, size), 1)
    return jnp.sum(jnp.where(down == along, row, jnp.zeros_like(row)), axis=1, keepdims=True)


def token_facts(ids, row_map, lengths, first_entry, slots):
    tokens = row_map.shape[1]
    token = lax.broadcasted_iota(jnp.int32, (tokens, tokens), 0)
    slot = lax.broadcasted_iota(jnp.int32, (tokens, tokens), 1)
    owner = (row_map == token).astype(jnp.float32)
    named = jnp.max(owner, axis=1, keepdims=True)
    owner = jnp.where((slot == 0) & (named == 0.0), 1.0, owner)
    rows = 2 * tokens
    slot = lax.broadcasted_iota(jnp.int32, (tokens, rows), 0)
    row = lax.broadcasted_iota(jnp.int32, (tokens, rows), 1)
    source, within = row // (2 * slots), row % (2 * slots)
    chosen = (slot == source * slots + within % slots).astype(jnp.bfloat16)
    owner = jnp.dot(owner.astype(jnp.bfloat16), chosen, preferred_element_type=jnp.float32)
    odd = within >= slots
    owner = jnp.concatenate([jnp.where(odd, 0.0, owner), jnp.where(odd, owner, 0.0)], axis=0)

    seqs = lengths.shape[1]
    seq_length = tokens // seqs
    position = lax.broadcasted_iota(jnp.int32, (tokens, 1), 0)
    live_until = jnp.zeros((tokens, 1), jnp.int32)
    for seq in range(seqs):
        inside = (position >= seq * seq_length) & (position < (seq + 1) * seq_length)
        until = lengths[:, seq : seq + 1] + seq * seq_length
        live_until = jnp.where(inside, until, live_until)
    live = (position < live_until).astype(jnp.float32)
    count = jnp.sum(live, axis=0, keepdims=True)
    entry = (column_of(ids) - first_entry).astype(jnp.float32)
    lane = lax.broadcasted_iota(jnp.int32, (tokens, LANES), 1)
    return owner.astype(jnp.bfloat16), jnp.where(lane == 0, entry, live / count)


def pack_kernel(place_ref, *refs, shard_rows):
    outside, refs = refs[:6], refs[6:]
    packed_ref, owner_ref, table_ref = refs[:3]
    inside, wide_ref, sems = refs[3:9], refs[9], refs[10]
    copies = [
        pltpu.make_async_copy(source, target, sems.at[i])
        for i, (source, target) in enumerate(zip(outside, inside))
    ]
    for copy in copies:
        copy.start()
    for copy in copies:
        copy.wait()
    hidden_ref, values_ref, scales_ref, ids_ref, map_ref, lengths_ref = inside
    owner_ref[...], table_ref[...] = token_facts(
        ids_ref[...], map_ref[...], lengths_ref[...], place_ref[0] * shard_rows, values_ref.shape[0]
    )
    chips = packed_ref.shape[0]
    tokens, half = hidden_ref.shape
    slots, entries = values_ref.shape
    pair = entries // chips
    shard = pair // 2
    blocks = pair // BLOCK
    scales = jnp.concatenate([scales_ref[...]] * 2, axis=0)
    stacked = jnp.concatenate(
        [scales[:, blocks * chip : blocks * (chip + 1)] for chip in range(chips)], axis=0
    )
    block = lax.broadcasted_iota(jnp.int32, (blocks, pair), 0)
    entry = lax.broadcasted_iota(jnp.int32, (blocks, pair), 1)
    inside = (entry >= block * BLOCK) & (entry < block * BLOCK + BLOCK)
    spread = jnp.dot(
        stacked.astype(jnp.bfloat16),
        inside.astype(jnp.bfloat16),
        preferred_element_type=jnp.float32,
    )
    values = values_ref[...].astype(jnp.float32)
    values = jnp.concatenate([values, values], axis=0)
    for chip in range(chips):
        wide_ref[:, pair * chip : pair * (chip + 1)] = (
            values[:, pair * chip : pair * (chip + 1)]
            * spread[2 * slots * chip : 2 * slots * (chip + 1)]
        )
    wide_ref[:, entries:] = jnp.zeros((2 * slots, LANES), jnp.float32)

    hidden = hidden_ref[...].astype(jnp.float32)
    zeros = jnp.zeros((tokens, LANES // 2), jnp.float32)
    tiles = tiles_of(jnp.concatenate([hidden, zeros], axis=1), 3)
    turns = [turned(tile) for tile in tiles]
    low = low_lanes(tiles[0].shape)
    first = place_ref[0] % 2 == 0
    hidden = jnp.concatenate(
        [
            jnp.where(first, tiles[0], jnp.where(low, turns[0], turns[1])),
            jnp.where(first, tiles[1], jnp.where(low, turns[1], turns[2])),
            folded(first, jnp.where(first, tiles[2], turns[0])),
        ],
        axis=0,
    ).astype(jnp.bfloat16)
    hidden_rows = hidden.shape[0]
    upper = low_rows((2 * slots, LANES), slots)
    low = low_lanes((2 * slots, LANES))
    tile_pairs = (shard + LANES // 2) // LANES // 2
    for chip in range(chips):
        rows = []
        for core in range(2):
            start = pair * chip + (shard - LANES // 2) * core
            tiles = [
                wide_ref[:, start + LANES * i : start + LANES * (i + 1)]
                for i in range(2 * tile_pairs + core)
            ]
            if core == 1:
                tiles = [turned(tile) for tile in tiles]
                tiles = [
                    jnp.where(low, tiles[i], tiles[i + 1]) for i in range(2 * tile_pairs)
                ]
            rows += [
                jnp.where(upper, tiles[2 * i], tiles[2 * i + 1]) for i in range(tile_pairs)
            ]
        step = lax.rem(chip - place_ref[0] // 2 + chips, chips)
        packed_ref[step, :hidden_rows] = hidden
        packed_ref[step, hidden_rows:] = jnp.concatenate(rows, axis=0).astype(jnp.bfloat16)


def head_copy(head_ref, held_ref, sems, chip, step):
    width = held_ref.shape[2]
    columns = pl.ds(pl.multiple_of(chip * width, LANES), width)
    return pltpu.make_async_copy(head_ref.at[:, columns], held_ref.at[step], sems.at[step])


def stream(chip_at, count, ahead, head_ref, held_ref, sems, use):
    def copy(step):
        return head_copy(head_ref, held_ref, sems, chip_at(step), step)

    def body(step, _):
        copy(step).wait()
        if ahead < count:

            @pl.when(step + ahead < count)
            def _():
                copy(step + ahead).start()

        use(step)

    for step in range(min(ahead, count)):
        copy(step).start()
    return lambda: lax.fori_loop(0, count, body, None)


def source_chip(place_ref, chips, step):
    return lax.rem(place_ref[0] // 2 - step + chips, chips)


def preload_kernel(place_ref, head_ref, _, early_ref, sems, *, chips):
    copies = [
        head_copy(head_ref, early_ref, sems, source_chip(place_ref, chips, step), step)
        for step in range(EARLY)
    ]
    for copy in copies:
        copy.start()
    for copy in copies:
        copy.wait()


def logits_kernel(
    place_ref,
    first_ref,
    last_ref,
    first_far_ref,
    last_far_ref,
    owner_ref,
    tokens_ref,
    early_ref,
    head_ref,
    rows_ref,
    stats_ref,
    own_ref,
    held_ref,
    made_ref,
    hidden_ref,
    arrived_ref,
    teacher_ref,
    logits_ref,
    copies_ref,
    sems,
    made_sem,
    stats_sem,
):
    core = place_ref[0] % 2
    chips, tokens, width = hidden_ref.shape
    shard_rows = head_ref.shape[0]
    hidden_rows = 5 * tokens // 2
    slots = tokens // (2 * chips)
    low = low_lanes((tokens // 2, LANES))

    def product(step, columns):
        return lax.dot_general(
            columns, hidden_ref[step], (((1,), (1,)), ((), ())), preferred_element_type=jnp.float32
        )

    def add(step, columns):
        logits_ref[...] += product(step, columns)

    run = stream(
        lambda step: source_chip(place_ref, chips, step + EARLY),
        chips - EARLY,
        chips - EARLY,
        head_ref,
        held_ref,
        sems,
        lambda step: add(step + EARLY, held_ref[step]),
    )

    def unpack(near_ref, far_ref, base):
        for place in range(near_ref.shape[0]):
            step = place + base
            blocks = near_ref.at[place], far_ref.at[place]
            for block, parity in zip(blocks, (core, 1 - core)):
                for i in range(2):
                    column = LANES * i + (width - 2 * LANES) * parity
                    lanes = pl.ds(pl.multiple_of(column, LANES), LANES)
                    hidden_ref[step, :, lanes] = block[tokens * i : tokens * (i + 1)]
                teacher = block[hidden_rows:].astype(jnp.float32)
                share = teacher.shape[0] // 2
                teacher = jnp.where(core == 0, teacher[:share], teacher[share:])
                row = 2 * slots * (2 * source_chip(place_ref, chips, step) + parity)
                rows = pl.ds(pl.multiple_of(row, 2 * slots), 2 * slots)
                for i in range(share // (2 * slots)):
                    arrived_ref[rows, LANES * i : LANES * (i + 1)] = teacher[
                        2 * slots * i : 2 * slots * (i + 1)
                    ]
            own, other = [block[2 * tokens : hidden_rows].astype(jnp.float32) for block in blocks]
            one, two = jnp.where(core == 0, own, other), jnp.where(core == 0, other, own)
            tile = [jnp.where(low, one, two), turned(jnp.where(low, two, one))]
            tile = jnp.concatenate(tile, axis=0).astype(jnp.bfloat16)
            hidden_ref[step, :, 2 * LANES : 3 * LANES] = tile

    unpack(first_ref, first_far_ref, 0)
    logits_ref[...] = product(0, early_ref[0])
    for step in range(1, EARLY):
        add(step, early_ref[step])
    unpack(last_ref, last_far_ref, first_ref.shape[0])
    placed = jnp.dot(
        owner_ref[...], arrived_ref[...].astype(jnp.bfloat16), preferred_element_type=jnp.float32
    )
    pairs = arrived_ref.shape[1] // LANES
    even, odd = tiles_of(placed[:tokens], pairs), tiles_of(placed[tokens:], pairs)
    teacher = jnp.concatenate([tile for pair in zip(even, odd) for tile in pair], axis=1)
    teacher = teacher[:, :shard_rows]
    teacher_top = jnp.max(teacher, axis=1, keepdims=True)
    teacher_off = teacher - teacher_top
    teacher_total = jnp.sum(jnp.exp(teacher_off), axis=1, keepdims=True)
    teacher_ref[...] = teacher_off
    run()
    logits = logits_ref[...].T

    top = jnp.max(logits, axis=1, keepdims=True)
    off = logits - top
    exps = jnp.exp(off)
    total = jnp.sum(exps, axis=1, keepdims=True)
    gap = off - teacher_ref[...]
    cross = jnp.sum(exps * gap, axis=1, keepdims=True)
    centre = cross / total
    entry = lax.broadcasted_iota(jnp.int32, (tokens, shard_rows), 1)
    hit = entry == tokens_ref[:, :1].astype(jnp.int32)
    target = jnp.sum(jnp.where(hit, logits, 0.0), axis=1, keepdims=True)
    made_ref[:tokens] = (exps * (gap - centre)).astype(jnp.bfloat16)
    made_ref[tokens : 2 * tokens] = exps.astype(jnp.bfloat16)
    made_ref[2 * tokens :] = hit.astype(jnp.bfloat16)
    out = pltpu.make_async_copy(made_ref, rows_ref, made_sem)
    out.start()

    lane = lax.broadcasted_iota(jnp.int32, (tokens, LANES), 1)
    table = jnp.zeros((tokens, LANES), jnp.float32)
    for place, column in enumerate(
        (top, total, teacher_top, teacher_total, cross, target, centre)
    ):
        table = jnp.where(lane == place, column, table)
    stats = jnp.concatenate([table, jnp.zeros((own_ref.shape[1] - tokens, LANES), jnp.float32)])
    stats = stats.T[:STATS]
    own_ref[...] = stats
    copies_ref[...] = jnp.broadcast_to(stats[None], copies_ref.shape)
    out_stats = pltpu.make_async_copy(copies_ref, stats_ref, stats_sem)
    out_stats.start()
    out.wait()
    out_stats.wait()


def products_kernel(
    place_ref, rows_ref, head_ref, terms_ref, picks_ref, held_ref, made_ref, sems, made_sem
):
    into = pltpu.make_async_copy(rows_ref, made_ref, made_sem)
    into.start()
    chips = terms_ref.shape[0]
    tokens = made_ref.shape[0] // 3
    width = held_ref.shape[2]

    def multiply(step):
        products = jnp.dot(made_ref[...], held_ref[step], preferred_element_type=jnp.float32)
        for i, tile in enumerate(tiles_of(products, width // LANES)):
            terms_ref[step, i, 0] = tile[:tokens]
            terms_ref[step, i, 1] = tile[tokens : 2 * tokens]
            picks_ref[step, i] = tile[2 * tokens :].astype(jnp.bfloat16)

    run = stream(
        lambda step: lax.rem(place_ref[0] // 2 + step, chips),
        chips,
        AHEAD,
        head_ref,
        held_ref,
        sems,
        multiply,
    )
    into.wait()
    run()


def put_shares(parity, factors_ref, terms_ref, picks_ref, out_ref):
    tokens = terms_ref.shape[3]
    factor, level, weight = [factors_ref[i] for i in range(3)]
    for step in range(terms_ref.shape[0]):
        for i, tile in enumerate((3 * parity, 3 * parity + 1, 2)):
            sums = terms_ref[step, tile, 0] + level * terms_ref[step, tile, 1]
            share = factor * sums - weight * picks_ref[step, tile].astype(jnp.float32)
            if i == 2:
                share = folded(parity == 0, share)
            out_ref[step, tokens * i : tokens * i + share.shape[0]] = share.astype(out_ref.dtype)


def give_kernel(
    place_ref,
    scale_ref,
    stats_ref,
    own_ref,
    tokens_ref,
    terms_ref,
    picks_ref,
    give_ref,
    factors_ref,
    loss_ref,
):
    tokens = tokens_ref.shape[0]
    tops, sums, teacher_tops, teacher_sums, crosses, targets = [
        stats_ref[:, i, :tokens] for i in range(6)
    ]
    top, total, teacher_top, teacher_total, cross = [
        part[None] for part in merge_stats(tops, sums, teacher_tops, teacher_sums, crosses)
    ]
    target = jnp.sum(targets, axis=0, keepdims=True)
    student_log = jnp.log(total)
    teacher_log = jnp.log(teacher_total)
    divergence = cross / total - (student_log - teacher_log)
    student_lse = top + student_log
    per_token = divergence + sample_weight * (student_lse - target)
    student_shift = own_ref[0:1, :tokens] - top - student_log
    teacher_shift = own_ref[2:3, :tokens] - teacher_top - teacher_log
    factor = jnp.exp(student_shift)
    level = (
        own_ref[6:7, :tokens] + student_shift - teacher_shift - divergence + sample_weight
    )
    zeros = jnp.zeros((LANES - 3, tokens), jnp.float32)
    columns = jnp.concatenate([factor, level, per_token, zeros], axis=0).T
    share = tokens_ref[:, 1:2]
    weight = share * scale_ref[0]
    loss_ref[...] = jnp.sum(share * columns[:, 2:3], axis=0, keepdims=True)
    for i, column in enumerate(
        (weight * columns[:, 0:1], columns[:, 1:2], sample_weight * weight)
    ):
        factors_ref[i] = jnp.broadcast_to(column, (tokens, LANES))
    put_shares(1 - place_ref[0] % 2, factors_ref, terms_ref, picks_ref, give_ref)


def keep_kernel(place_ref, factors_ref, found_ref, terms_ref, picks_ref, keep_ref, loss_ref):
    loss_ref[...] = found_ref[...]
    put_shares(place_ref[0] % 2, factors_ref, terms_ref, picks_ref, keep_ref)


def sum_kernel(place_ref, own_ref, *refs):
    tokens, half = refs[-1].shape
    total = own_ref[...]
    for share_ref in refs[:-1]:
        total += share_ref[...].astype(jnp.float32)
    one, two, rest = total[:tokens], total[tokens : 2 * tokens], total[2 * tokens :]
    rest = jnp.concatenate([rest, turned(rest)], axis=0)
    turns = [turned(tile) for tile in (rest, one, two)]
    low = low_lanes(one.shape)
    first = place_ref[0] % 2 == 0
    tiles = [
        jnp.where(first, one, jnp.where(low, turns[0], turns[1])),
        jnp.where(first, two, jnp.where(low, turns[1], turns[2])),
        jnp.where(first, rest, turns[2]),
    ]
    total = jnp.concatenate(tiles, axis=1)[:, :half]
    refs[-1][...] = total.astype(refs[-1].dtype)


def paired_shards(
    hidden_states, head, teacher_values, teacher_scales, token_ids, lengths, row_map, loss_scale
):
    count = lax.axis_size("vocab")
    own_index = lax.axis_index("vocab")
    chips = count // 2
    tokens, half = hidden_states.shape
    width = 2 * half
    shard_rows = head.shape[0]
    place = jnp.reshape(own_index, (1,))
    vmem = pl.BlockSpec(memory_space=pltpu.VMEM)
    smem = pl.BlockSpec(memory_space=pltpu.SMEM)
    hbm = pl.BlockSpec(memory_space=pl.ANY)
    params = pltpu.CompilerParams(vmem_limit_bytes=VMEM_LIMIT)
    head = in_hbm(head)
    head_scratch = pltpu.VMEM((chips, shard_rows, width), head.dtype)
    head_sems = pltpu.SemaphoreType.DMA((chips,))
    rows_scratch = pltpu.VMEM((3 * tokens, shard_rows), jnp.bfloat16)
    rows_sem = pltpu.SemaphoreType.DMA
    slots, entries = teacher_values.shape
    hidden_rows = 5 * tokens // 2
    teacher_rows = 2 * slots * (shard_rows + LANES // 2) // LANES

    operands = (
        hidden_states,
        teacher_values,
        teacher_scales,
        token_ids[None, :],
        row_map[None, :],
        lengths[None, :],
    )
    packed, owner, table = pl.pallas_call(
        functools.partial(pack_kernel, shard_rows=shard_rows),
        out_shape=(
            vmem_array((chips, hidden_rows + teacher_rows, LANES), jnp.bfloat16),
            vmem_array((2 * tokens, 2 * tokens), jnp.bfloat16),
            vmem_array((tokens, LANES), jnp.float32),
        ),
        in_specs=[smem] + [hbm] * len(operands),
        out_specs=[vmem] * 3,
        scratch_shapes=[pltpu.VMEM(operand.shape, operand.dtype) for operand in operands]
        + [
            pltpu.VMEM((2 * slots, entries + LANES), jnp.float32),
            pltpu.SemaphoreType.DMA((len(operands),)),
        ],
        compiler_params=params,
        name="pack",
    )(place, *[in_hbm(operand) for operand in operands])
    steps = range(1, chips)
    near = [packed[0]] + [along_chips(packed[step], step) for step in steps]
    first, last = jnp.stack(near[: chips // 2 + 1]), jnp.stack(near[chips // 2 + 1 :])
    early = pl.pallas_call(
        functools.partial(preload_kernel, chips=chips),
        out_shape=vmem_array((EARLY, shard_rows, width), head.dtype),
        in_specs=[smem] + [hbm] * 2,
        out_specs=vmem,
        scratch_shapes=[pltpu.SemaphoreType.DMA((EARLY,))],
        compiler_params=params,
        cost_estimate=pl.CostEstimate(
            flops=0, bytes_accessed=4 * EARLY * shard_rows * width, transcendentals=0
        ),
        name="preload",
    )(place, head, near[3])
    last, early = lax.optimization_barrier((last, early))
    far = [swap_cores(last), swap_cores(first)]

    stats_shape = (count, STATS, pl.cdiv(tokens, LANES) * LANES)
    rows, stats, own_stats = pl.pallas_call(
        logits_kernel,
        out_shape=(
            hbm_array((3 * tokens, shard_rows), jnp.bfloat16),
            hbm_array(stats_shape, jnp.float32),
            vmem_array(stats_shape[1:], jnp.float32),
        ),
        in_specs=[smem] + [vmem] * 7 + [hbm],
        out_specs=[hbm, hbm, vmem],
        scratch_shapes=[
            pltpu.VMEM((chips - EARLY, shard_rows, width), head.dtype),
            rows_scratch,
            pltpu.VMEM((chips, tokens, width), jnp.bfloat16),
            pltpu.VMEM((2 * tokens, (shard_rows + LANES // 2) // 2), jnp.float32),
            pltpu.VMEM((tokens, shard_rows), jnp.float32),
            pltpu.VMEM((shard_rows, tokens), jnp.float32),
            pltpu.VMEM(stats_shape, jnp.float32),
            pltpu.SemaphoreType.DMA((chips - EARLY,)),
            rows_sem,
            rows_sem,
        ],
        compiler_params=params,
        cost_estimate=pl.CostEstimate(
            flops=2 * tokens * head.size, bytes_accessed=2 * head.size, transcendentals=0
        ),
        name="logits",
    )(
        place,
        *[in_vmem(blocks) for blocks in (first, last, far[1], far[0])],
        in_vmem(owner),
        in_vmem(table),
        in_vmem(early),
        head,
    )

    all_stats = lax.all_to_all(stats, "vocab", split_axis=0, concat_axis=0, tiled=True)

    terms, picks = pl.pallas_call(
        products_kernel,
        out_shape=(
            vmem_array((chips, width // LANES, 2, tokens, LANES), jnp.float32),
            vmem_array((chips, width // LANES, tokens, LANES), jnp.bfloat16),
        ),
        in_specs=[smem, hbm, hbm],
        out_specs=[vmem] * 2,
        scratch_shapes=[head_scratch, rows_scratch, head_sems, rows_sem],
        compiler_params=params,
        cost_estimate=pl.CostEstimate(
            flops=6 * tokens * head.size, bytes_accessed=2 * head.size, transcendentals=0
        ),
        name="products",
    )(place, in_hbm(rows), head)

    terms, picks = in_vmem(terms), in_vmem(picks)
    give, factors, loss = pl.pallas_call(
        give_kernel,
        out_shape=(
            vmem_array((chips, hidden_rows, LANES), jnp.bfloat16),
            vmem_array((3, tokens, LANES), jnp.float32),
            vmem_array((1, 1), jnp.float32),
        ),
        in_specs=[smem] * 2 + [vmem] * 5,
        out_specs=[vmem] * 3,
        compiler_params=params,
        name="give",
    )(place, loss_scale, in_vmem(all_stats), in_vmem(own_stats), in_vmem(table), terms, picks)
    taken = swap_cores(give)
    keep, loss = pl.pallas_call(
        keep_kernel,
        out_shape=(
            vmem_array((chips, hidden_rows, LANES), jnp.float32),
            jax.ShapeDtypeStruct((1, 1), jnp.float32),
        ),
        in_specs=[smem] + [vmem] * 4,
        out_specs=[vmem] * 2,
        compiler_params=params,
        cost_estimate=pl.CostEstimate(
            flops=4 * terms.size, bytes_accessed=4 * terms.size, transcendentals=0
        ),
        name="keep",
    )(place, in_vmem(factors), in_vmem(loss), terms, picks)
    sums = keep + taken.astype(jnp.float32)
    shares = [along_chips(sums[step].astype(jnp.bfloat16), step) for step in steps]
    total = pl.pallas_call(
        sum_kernel,
        out_shape=jax.ShapeDtypeStruct((tokens, half), jnp.bfloat16),
        in_specs=[smem] + [vmem] * chips,
        out_specs=vmem,
        compiler_params=params,
        name="total",
    )(place, *[in_vmem(share) for share in [sums[0]] + shares])
    return total, jnp.reshape(loss, (1,))


VMEM_LIMIT = 24 * 1024 * 1024


def shards(
    hidden_states, head, teacher_values, teacher_scales, token_ids, lengths, row_map, loss_scale
):
    count = lax.axis_size("vocab")
    own_index = lax.axis_index("vocab")
    tokens = hidden_states.shape[0]
    own_features = hidden_states.shape[1]
    shard_rows = head.shape[0]
    seq_length = tokens // lengths.shape[0]
    contract_last = (((1,), (1,)), ((), ()))

    scaled = scaled_teacher(teacher_values, teacher_scales, count, shard_rows)
    arrived = lax.all_to_all(scaled, "vocab", split_axis=0, concat_axis=0, tiled=True)
    arrived = arrived.reshape(tokens, shard_rows)
    gathered = to_all(hidden_states, count).transpose(1, 0, 2).reshape(tokens, -1)
    logits = lax.dot_general(gathered, head, contract_last, preferred_element_type=jnp.float32)

    positions = jnp.arange(tokens, dtype=jnp.int32)
    owner = row_map[None, :] == positions[:, None]
    slot_of = jnp.sum(jnp.where(owner, positions[None, :], 0), axis=1)
    teacher = jnp.take(arrived, slot_of, axis=0).astype(jnp.float32)

    seq_ids = jnp.arange(lengths.shape[0], dtype=jnp.int32)
    own_length = jnp.sum(
        jnp.where((positions // seq_length)[:, None] == seq_ids[None, :], lengths[None, :], 0),
        axis=1,
    )
    live_mask = (positions % seq_length < own_length).astype(jnp.float32)
    live_count = jnp.sum(live_mask)

    local_ids = token_ids - own_index * shard_rows
    target_hit = local_ids[:, None] == jnp.arange(shard_rows, dtype=jnp.int32)[None, :]
    target_part = jnp.sum(jnp.where(target_hit, logits, 0.0), axis=1)
    student_top = jnp.max(logits, axis=1)
    teacher_top = jnp.max(teacher, axis=1)
    student_off = logits - student_top[:, None]
    teacher_off = teacher - teacher_top[:, None]
    student_exp = jnp.exp(student_off)
    student_sum = jnp.sum(student_exp, axis=1)
    teacher_sum = jnp.sum(jnp.exp(teacher_off), axis=1)
    cross_sum = jnp.sum(student_exp * (student_off - teacher_off), axis=1)

    stats = to_all(
        jnp.stack(
            [student_top, student_sum, teacher_top, teacher_sum, cross_sum, target_part]
        ),
        count,
    )
    tops, sums, teacher_tops, teacher_sums, crosses, targets = [stats[:, i] for i in range(6)]
    student_max, student_total, teacher_max, teacher_total, cross_total = merge_stats(
        tops, sums, teacher_tops, teacher_sums, crosses
    )
    student_log = jnp.log(student_total)
    teacher_log = jnp.log(teacher_total)
    student_lse = student_max + student_log
    teacher_lse = teacher_max + teacher_log
    divergence = cross_total / student_total - (student_log - teacher_log)
    target = jnp.sum(targets, axis=0)

    per_token = divergence + sample_weight * (student_lse - target)
    loss = jnp.reshape(jnp.sum(live_mask * per_token) / live_count, (1,))
    token_weight = live_mask * loss_scale[0] / live_count
    log_student = logits - student_lse[:, None]
    log_teacher = teacher - teacher_lse[:, None]
    student_prob = jnp.exp(log_student)
    grad_logits = (
        token_weight[:, None]
        * (
            student_prob * (log_student - log_teacher - divergence[:, None])
            + sample_weight * (student_prob - target_hit.astype(jnp.float32))
        )
    ).astype(jnp.bfloat16)
    terms = jnp.dot(grad_logits, head, preferred_element_type=jnp.float32).astype(jnp.bfloat16)
    terms = terms.reshape(tokens, count, own_features).transpose(1, 0, 2)
    shares = lax.all_to_all(terms, "vocab", split_axis=0, concat_axis=0, tiled=True)
    grad_hidden = jnp.sum(shares.astype(jnp.float32), axis=0)
    return (grad_hidden.astype(jnp.bfloat16), loss)


def any_shards(*arrays):
    hidden_states, head, teacher_values = arrays[:3]
    count = lax.axis_size("vocab")
    fits = (
        count % 2 == 0
        and hidden_states.shape[1] == 5 * LANES // 2
        and hidden_states.shape[0] % 32 == 0
        and head.shape[0] % LANES == LANES // 2
        and (head.shape[0] + LANES // 2) // LANES % 2 == 0
        and teacher_values.shape[0] == 4
    )
    return paired_shards(*arrays) if fits else shards(*arrays)


def solution(mesh):
    in_specs = (
        P("dom", "vocab"),
        P("vocab", None),
        P(("dom", "vocab"), None),
        P(("dom", "vocab"), None),
        P("dom"),
        P("dom"),
        P("dom"),
        P(),
    )
    out_specs = (P("dom", "vocab"), P("dom"))
    return jax.shard_map(
        any_shards, mesh=mesh, in_specs=in_specs, out_specs=out_specs, check_vma=False
    )
```

```python
import functools

import jax
import jax.numpy as jnp
from jax import lax
from jax.experimental import pallas as pl
from jax.experimental.pallas import tpu as pltpu
from jax.sharding import PartitionSpec as P

BLOCK = 32
LANES = 128
STATS = 8
AHEAD = 3
EARLY = 2


sample_weight = 0.5


def to_all(piece, count):
    copies = jnp.broadcast_to(piece[None], (count,) + piece.shape)
    return lax.all_to_all(copies, "vocab", split_axis=0, concat_axis=0, tiled=True)


def scaled_teacher(teacher_values, teacher_scales, count, shard_rows):
    slot_rows = teacher_values.shape[0]
    scaled = (
        teacher_values.astype(jnp.float32).reshape(slot_rows, -1, BLOCK) * teacher_scales[:, :, None]
    ).astype(jnp.bfloat16)
    return scaled.reshape(slot_rows, count, shard_rows).transpose(1, 0, 2)


def merge_stats(tops, sums, teacher_tops, teacher_sums, crosses):
    top = jnp.max(tops, axis=0)
    teacher_top = jnp.max(teacher_tops, axis=0)
    shift = tops - top[None]
    teacher_shift = teacher_tops - teacher_top[None]
    weight = jnp.exp(shift)
    total = jnp.sum(sums * weight, axis=0)
    teacher_total = jnp.sum(teacher_sums * jnp.exp(teacher_shift), axis=0)
    cross = jnp.sum(weight * (crosses + sums * (shift - teacher_shift)), axis=0)
    return top, total, teacher_top, teacher_total, cross


def swap_cores(array):
    count = lax.axis_size("vocab")
    return lax.ppermute(array, "vocab", [(i, i ^ 1) for i in range(count)])


def along_chips(array, step):
    count = lax.axis_size("vocab")
    return lax.ppermute(array, "vocab", [(i, (i + 2 * step) % count) for i in range(count)])


def vmem_array(shape, dtype):
    return pltpu.VMEM(shape, dtype)


def in_vmem(array):
    return pltpu.with_memory_space_constraint(array, pltpu.VMEM)


def in_hbm(array):
    return pltpu.with_memory_space_constraint(array, pltpu.HBM)


def hbm_array(shape, dtype):
    return pltpu.HBM(shape, dtype)


def low_lanes(shape):
    return lax.broadcasted_iota(jnp.int32, shape, len(shape) - 1) < LANES // 2


def low_rows(shape, count):
    return lax.broadcasted_iota(jnp.int32, shape, 0) < count


def turned(array):
    return pltpu.roll(array, LANES // 2, 1)


def folded(first, tile):
    rows = tile.shape[0] // 2
    upper, lower = tile[:rows], turned(tile[rows:])
    low = low_lanes(upper.shape)
    return jnp.where(first, jnp.where(low, upper, lower), jnp.where(low, lower, upper))


def tiles_of(array, count):
    return [array[:, LANES * i : LANES * (i + 1)] for i in range(count)]


def column_of(row):
    size = row.shape[1]
    down = lax.broadcasted_iota(jnp.int32, (size, size), 0)
    along = lax.broadcasted_iota(jnp.int32, (size, size), 1)
    return jnp.sum(jnp.where(down == along, row, jnp.zeros_like(row)), axis=1, keepdims=True)


def token_facts(ids, row_map, lengths, first_entry, slots):
    tokens = row_map.shape[1]
    token = lax.broadcasted_iota(jnp.int32, (tokens, tokens), 0)
    slot = lax.broadcasted_iota(jnp.int32, (tokens, tokens), 1)
    owner = (row_map == token).astype(jnp.float32)
    named = jnp.max(owner, axis=1, keepdims=True)
    owner = jnp.where((slot == 0) & (named == 0.0), 1.0, owner)
    rows = 2 * tokens
    slot = lax.broadcasted_iota(jnp.int32, (tokens, rows), 0)
    row = lax.broadcasted_iota(jnp.int32, (tokens, rows), 1)
    source, within = row // (2 * slots), row % (2 * slots)
    chosen = (slot == source * slots + within % slots).astype(jnp.bfloat16)
    owner = jnp.dot(owner.astype(jnp.bfloat16), chosen, preferred_element_type=jnp.float32)
    odd = within >= slots
    owner = jnp.concatenate([jnp.where(odd, 0.0, owner), jnp.where(odd, owner, 0.0)], axis=0)

    seqs = lengths.shape[1]
    seq_length = tokens // seqs
    position = lax.broadcasted_iota(jnp.int32, (tokens, 1), 0)
    live_until = jnp.zeros((tokens, 1), jnp.int32)
    for seq in range(seqs):
        inside = (position >= seq * seq_length) & (position < (seq + 1) * seq_length)
        until = lengths[:, seq : seq + 1] + seq * seq_length
        live_until = jnp.where(inside, until, live_until)
    live = (position < live_until).astype(jnp.float32)
    count = jnp.sum(live, axis=0, keepdims=True)
    entry = (column_of(ids) - first_entry).astype(jnp.float32)
    lane = lax.broadcasted_iota(jnp.int32, (tokens, LANES), 1)
    return owner.astype(jnp.bfloat16), jnp.where(lane == 0, entry, live / count)


def pack_kernel(place_ref, *refs, shard_rows):
    outside, refs = refs[:6], refs[6:]
    packed_ref, owner_ref, table_ref = refs[:3]
    inside, wide_ref, sems = refs[3:9], refs[9], refs[10]
    copies = [
        pltpu.make_async_copy(source, target, sems.at[i])
        for i, (source, target) in enumerate(zip(outside, inside))
    ]
    for copy in copies:
        copy.start()
    for copy in copies:
        copy.wait()
    hidden_ref, values_ref, scales_ref, ids_ref, map_ref, lengths_ref = inside
    owner_ref[...], table_ref[...] = token_facts(
        ids_ref[...], map_ref[...], lengths_ref[...], place_ref[0] * shard_rows, values_ref.shape[0]
    )
    chips = packed_ref.shape[0]
    tokens, half = hidden_ref.shape
    slots, entries = values_ref.shape
    pair = entries // chips
    shard = pair // 2
    blocks = pair // BLOCK
    scales = jnp.concatenate([scales_ref[...]] * 2, axis=0)
    stacked = jnp.concatenate(
        [scales[:, blocks * chip : blocks * (chip + 1)] for chip in range(chips)], axis=0
    )
    block = lax.broadcasted_iota(jnp.int32, (blocks, pair), 0)
    entry = lax.broadcasted_iota(jnp.int32, (blocks, pair), 1)
    inside = (entry >= block * BLOCK) & (entry < block * BLOCK + BLOCK)
    spread = jnp.dot(
        stacked.astype(jnp.bfloat16),
        inside.astype(jnp.bfloat16),
        preferred_element_type=jnp.float32,
    )
    values = values_ref[...].astype(jnp.float32)
    values = jnp.concatenate([values, values], axis=0)
    for chip in range(chips):
        wide_ref[:, pair * chip : pair * (chip + 1)] = (
            values[:, pair * chip : pair * (chip + 1)]
            * spread[2 * slots * chip : 2 * slots * (chip + 1)]
        )
    wide_ref[:, entries:] = jnp.zeros((2 * slots, LANES), jnp.float32)

    hidden = hidden_ref[...].astype(jnp.float32)
    zeros = jnp.zeros((tokens, LANES // 2), jnp.float32)
    tiles = tiles_of(jnp.concatenate([hidden, zeros], axis=1), 3)
    turns = [turned(tile) for tile in tiles]
    low = low_lanes(tiles[0].shape)
    first = place_ref[0] % 2 == 0
    hidden = jnp.concatenate(
        [
            jnp.where(first, tiles[0], jnp.where(low, turns[0], turns[1])),
            jnp.where(first, tiles[1], jnp.where(low, turns[1], turns[2])),
            folded(first, jnp.where(first, tiles[2], turns[0])),
        ],
        axis=0,
    ).astype(jnp.bfloat16)
    hidden_rows = hidden.shape[0]
    upper = low_rows((2 * slots, LANES), slots)
    low = low_lanes((2 * slots, LANES))
    tile_pairs = (shard + LANES // 2) // LANES // 2
    for chip in range(chips):
        rows = []
        for core in range(2):
            start = pair * chip + (shard - LANES // 2) * core
            tiles = [
                wide_ref[:, start + LANES * i : start + LANES * (i + 1)]
                for i in range(2 * tile_pairs + core)
            ]
            if core == 1:
                tiles = [turned(tile) for tile in tiles]
                tiles = [
                    jnp.where(low, tiles[i], tiles[i + 1]) for i in range(2 * tile_pairs)
                ]
            rows += [
                jnp.where(upper, tiles[2 * i], tiles[2 * i + 1]) for i in range(tile_pairs)
            ]
        step = lax.rem(chip - place_ref[0] // 2 + chips, chips)
        packed_ref[step, :hidden_rows] = hidden
        packed_ref[step, hidden_rows:] = jnp.concatenate(rows, axis=0).astype(jnp.bfloat16)


def head_copy(head_ref, held_ref, sems, chip, step):
    width = held_ref.shape[2]
    columns = pl.ds(pl.multiple_of(chip * width, LANES), width)
    return pltpu.make_async_copy(head_ref.at[:, columns], held_ref.at[step], sems.at[step])


def stream(chip_at, count, ahead, head_ref, held_ref, sems, use):
    def copy(step):
        return head_copy(head_ref, held_ref, sems, chip_at(step), step)

    def body(step, _):
        copy(step).wait()
        if ahead < count:

            @pl.when(step + ahead < count)
            def _():
                copy(step + ahead).start()

        use(step)

    for step in range(min(ahead, count)):
        copy(step).start()
    return lambda: lax.fori_loop(0, count, body, None)


def source_chip(place_ref, chips, step):
    return lax.rem(place_ref[0] // 2 - step + chips, chips)


def preload_kernel(place_ref, head_ref, _, early_ref, sems, *, chips):
    copies = [
        head_copy(head_ref, early_ref, sems, source_chip(place_ref, chips, step), step)
        for step in range(EARLY)
    ]
    for copy in copies:
        copy.start()
    for copy in copies:
        copy.wait()


def logits_kernel(
    place_ref,
    first_ref,
    last_ref,
    first_far_ref,
    last_far_ref,
    owner_ref,
    tokens_ref,
    early_ref,
    head_ref,
    rows_ref,
    stats_ref,
    own_ref,
    held_ref,
    made_ref,
    hidden_ref,
    arrived_ref,
    teacher_ref,
    logits_ref,
    copies_ref,
    sems,
    made_sem,
    stats_sem,
):
    core = place_ref[0] % 2
    chips, tokens, width = hidden_ref.shape
    shard_rows = head_ref.shape[0]
    hidden_rows = 5 * tokens // 2
    slots = tokens // (2 * chips)
    low = low_lanes((tokens // 2, LANES))

    def add(step, columns):
        logits_ref[...] += lax.dot_general(
            columns, hidden_ref[step], (((1,), (1,)), ((), ())), preferred_element_type=jnp.float32
        )

    run = stream(
        lambda step: source_chip(place_ref, chips, step + EARLY),
        chips - EARLY,
        chips - EARLY,
        head_ref,
        held_ref,
        sems,
        lambda step: add(step + EARLY, held_ref[step]),
    )

    def unpack(near_ref, far_ref, base):
        for place in range(near_ref.shape[0]):
            step = place + base
            blocks = near_ref.at[place], far_ref.at[place]
            for block, parity in zip(blocks, (core, 1 - core)):
                for i in range(2):
                    column = LANES * i + (width - 2 * LANES) * parity
                    lanes = pl.ds(pl.multiple_of(column, LANES), LANES)
                    hidden_ref[step, :, lanes] = block[tokens * i : tokens * (i + 1)]
                teacher = block[hidden_rows:].astype(jnp.float32)
                share = teacher.shape[0] // 2
                teacher = jnp.where(core == 0, teacher[:share], teacher[share:])
                row = 2 * slots * (2 * source_chip(place_ref, chips, step) + parity)
                rows = pl.ds(pl.multiple_of(row, 2 * slots), 2 * slots)
                for i in range(share // (2 * slots)):
                    arrived_ref[rows, LANES * i : LANES * (i + 1)] = teacher[
                        2 * slots * i : 2 * slots * (i + 1)
                    ]
            own, other = [block[2 * tokens : hidden_rows].astype(jnp.float32) for block in blocks]
            one, two = jnp.where(core == 0, own, other), jnp.where(core == 0, other, own)
            tile = [jnp.where(low, one, two), turned(jnp.where(low, two, one))]
            tile = jnp.concatenate(tile, axis=0).astype(jnp.bfloat16)
            hidden_ref[step, :, 2 * LANES : 3 * LANES] = tile

    unpack(first_ref, first_far_ref, 0)
    unpack(last_ref, last_far_ref, first_ref.shape[0])
    logits_ref[...] = jnp.zeros_like(logits_ref)
    lax.fori_loop(0, EARLY, lambda step, _: add(step, early_ref[step]), None)
    placed = jnp.dot(
        owner_ref[...], arrived_ref[...].astype(jnp.bfloat16), preferred_element_type=jnp.float32
    )
    pairs = arrived_ref.shape[1] // LANES
    even, odd = tiles_of(placed[:tokens], pairs), tiles_of(placed[tokens:], pairs)
    teacher = jnp.concatenate([tile for pair in zip(even, odd) for tile in pair], axis=1)
    teacher = teacher[:, :shard_rows]
    teacher_top = jnp.max(teacher, axis=1, keepdims=True)
    teacher_off = teacher - teacher_top
    teacher_total = jnp.sum(jnp.exp(teacher_off), axis=1, keepdims=True)
    teacher_ref[...] = teacher_off
    run()
    logits = logits_ref[...].T

    top = jnp.max(logits, axis=1, keepdims=True)
    off = logits - top
    exps = jnp.exp(off)
    total = jnp.sum(exps, axis=1, keepdims=True)
    gap = off - teacher_ref[...]
    cross = jnp.sum(exps * gap, axis=1, keepdims=True)
    centre = cross / total
    entry = lax.broadcasted_iota(jnp.int32, (tokens, shard_rows), 1)
    hit = entry == tokens_ref[:, :1].astype(jnp.int32)
    target = jnp.sum(jnp.where(hit, logits, 0.0), axis=1, keepdims=True)
    made_ref[:tokens] = (exps * (gap - centre)).astype(jnp.bfloat16)
    made_ref[tokens : 2 * tokens] = exps.astype(jnp.bfloat16)
    made_ref[2 * tokens :] = hit.astype(jnp.bfloat16)
    out = pltpu.make_async_copy(made_ref, rows_ref, made_sem)
    out.start()

    lane = lax.broadcasted_iota(jnp.int32, (tokens, LANES), 1)
    table = jnp.zeros((tokens, LANES), jnp.float32)
    for place, column in enumerate(
        (top, total, teacher_top, teacher_total, cross, target, centre)
    ):
        table = jnp.where(lane == place, column, table)
    stats = jnp.concatenate([table, jnp.zeros((own_ref.shape[1] - tokens, LANES), jnp.float32)])
    stats = stats.T[:STATS]
    own_ref[...] = stats
    copies_ref[...] = jnp.broadcast_to(stats[None], copies_ref.shape)
    out_stats = pltpu.make_async_copy(copies_ref, stats_ref, stats_sem)
    out_stats.start()
    out.wait()
    out_stats.wait()


def products_kernel(
    place_ref, rows_ref, head_ref, terms_ref, picks_ref, held_ref, made_ref, sems, made_sem
):
    into = pltpu.make_async_copy(rows_ref, made_ref, made_sem)
    into.start()
    chips = terms_ref.shape[0]
    tokens = made_ref.shape[0] // 3
    width = held_ref.shape[2]

    def multiply(step):
        products = jnp.dot(made_ref[...], held_ref[step], preferred_element_type=jnp.float32)
        for i, tile in enumerate(tiles_of(products, width // LANES)):
            terms_ref[step, i, 0] = tile[:tokens]
            terms_ref[step, i, 1] = tile[tokens : 2 * tokens]
            picks_ref[step, i] = tile[2 * tokens :].astype(jnp.bfloat16)

    run = stream(
        lambda step: lax.rem(place_ref[0] // 2 + step, chips),
        chips,
        AHEAD,
        head_ref,
        held_ref,
        sems,
        multiply,
    )
    into.wait()
    run()


def put_shares(parity, factors_ref, terms_ref, picks_ref, out_ref):
    tokens = terms_ref.shape[3]
    factor, level, weight = [factors_ref[i] for i in range(3)]
    for step in range(terms_ref.shape[0]):
        for i, tile in enumerate((3 * parity, 3 * parity + 1, 2)):
            sums = terms_ref[step, tile, 0] + level * terms_ref[step, tile, 1]
            share = factor * sums - weight * picks_ref[step, tile].astype(jnp.float32)
            if i == 2:
                share = folded(parity == 0, share)
            out_ref[step, tokens * i : tokens * i + share.shape[0]] = share.astype(out_ref.dtype)


def give_kernel(
    place_ref,
    scale_ref,
    stats_ref,
    own_ref,
    tokens_ref,
    terms_ref,
    picks_ref,
    give_ref,
    factors_ref,
    loss_ref,
):
    tokens = tokens_ref.shape[0]
    tops, sums, teacher_tops, teacher_sums, crosses, targets = [
        stats_ref[:, i, :tokens] for i in range(6)
    ]
    top, total, teacher_top, teacher_total, cross = [
        part[None] for part in merge_stats(tops, sums, teacher_tops, teacher_sums, crosses)
    ]
    target = jnp.sum(targets, axis=0, keepdims=True)
    student_log = jnp.log(total)
    teacher_log = jnp.log(teacher_total)
    divergence = cross / total - (student_log - teacher_log)
    student_lse = top + student_log
    per_token = divergence + sample_weight * (student_lse - target)
    student_shift = own_ref[0:1, :tokens] - top - student_log
    teacher_shift = own_ref[2:3, :tokens] - teacher_top - teacher_log
    factor = jnp.exp(student_shift)
    level = (
        own_ref[6:7, :tokens] + student_shift - teacher_shift - divergence + sample_weight
    )
    zeros = jnp.zeros((LANES - 3, tokens), jnp.float32)
    columns = jnp.concatenate([factor, level, per_token, zeros], axis=0).T
    share = tokens_ref[:, 1:2]
    weight = share * scale_ref[0]
    loss_ref[...] = jnp.sum(share * columns[:, 2:3], axis=0, keepdims=True)
    for i, column in enumerate(
        (weight * columns[:, 0:1], columns[:, 1:2], sample_weight * weight)
    ):
        factors_ref[i] = jnp.broadcast_to(column, (tokens, LANES))
    put_shares(1 - place_ref[0] % 2, factors_ref, terms_ref, picks_ref, give_ref)


def keep_kernel(place_ref, factors_ref, found_ref, terms_ref, picks_ref, keep_ref, loss_ref):
    loss_ref[...] = found_ref[...]
    put_shares(place_ref[0] % 2, factors_ref, terms_ref, picks_ref, keep_ref)


def sum_kernel(place_ref, own_ref, *refs):
    tokens, half = refs[-1].shape
    total = own_ref[...]
    for share_ref in refs[:-1]:
        total += share_ref[...].astype(jnp.float32)
    one, two, rest = total[:tokens], total[tokens : 2 * tokens], total[2 * tokens :]
    rest = jnp.concatenate([rest, turned(rest)], axis=0)
    turns = [turned(tile) for tile in (rest, one, two)]
    low = low_lanes(one.shape)
    first = place_ref[0] % 2 == 0
    tiles = [
        jnp.where(first, one, jnp.where(low, turns[0], turns[1])),
        jnp.where(first, two, jnp.where(low, turns[1], turns[2])),
        jnp.where(first, rest, turns[2]),
    ]
    total = jnp.concatenate(tiles, axis=1)[:, :half]
    refs[-1][...] = total.astype(refs[-1].dtype)


def paired_shards(
    hidden_states, head, teacher_values, teacher_scales, token_ids, lengths, row_map, loss_scale
):
    count = lax.axis_size("vocab")
    own_index = lax.axis_index("vocab")
    chips = count // 2
    tokens, half = hidden_states.shape
    width = 2 * half
    shard_rows = head.shape[0]
    place = jnp.reshape(own_index, (1,))
    vmem = pl.BlockSpec(memory_space=pltpu.VMEM)
    smem = pl.BlockSpec(memory_space=pltpu.SMEM)
    hbm = pl.BlockSpec(memory_space=pl.ANY)
    params = pltpu.CompilerParams(vmem_limit_bytes=VMEM_LIMIT)
    head = in_hbm(head)
    head_scratch = pltpu.VMEM((chips, shard_rows, width), head.dtype)
    head_sems = pltpu.SemaphoreType.DMA((chips,))
    rows_scratch = pltpu.VMEM((3 * tokens, shard_rows), jnp.bfloat16)
    rows_sem = pltpu.SemaphoreType.DMA
    slots, entries = teacher_values.shape
    hidden_rows = 5 * tokens // 2
    teacher_rows = 2 * slots * (shard_rows + LANES // 2) // LANES

    operands = (
        hidden_states,
        teacher_values,
        teacher_scales,
        token_ids[None, :],
        row_map[None, :],
        lengths[None, :],
    )
    packed, owner, table = pl.pallas_call(
        functools.partial(pack_kernel, shard_rows=shard_rows),
        out_shape=(
            vmem_array((chips, hidden_rows + teacher_rows, LANES), jnp.bfloat16),
            vmem_array((2 * tokens, 2 * tokens), jnp.bfloat16),
            vmem_array((tokens, LANES), jnp.float32),
        ),
        in_specs=[smem] + [hbm] * len(operands),
        out_specs=[vmem] * 3,
        scratch_shapes=[pltpu.VMEM(operand.shape, operand.dtype) for operand in operands]
        + [
            pltpu.VMEM((2 * slots, entries + LANES), jnp.float32),
            pltpu.SemaphoreType.DMA((len(operands),)),
        ],
        compiler_params=params,
        name="pack",
    )(place, *[in_hbm(operand) for operand in operands])
    steps = range(1, chips)
    near = [packed[0]] + [along_chips(packed[step], step) for step in steps]
    first, last = jnp.stack(near[: chips // 2 + 1]), jnp.stack(near[chips // 2 + 1 :])
    early = pl.pallas_call(
        functools.partial(preload_kernel, chips=chips),
        out_shape=vmem_array((EARLY, shard_rows, width), head.dtype),
        in_specs=[smem] + [hbm] * 2,
        out_specs=vmem,
        scratch_shapes=[pltpu.SemaphoreType.DMA((EARLY,))],
        compiler_params=params,
        cost_estimate=pl.CostEstimate(
            flops=0, bytes_accessed=4 * EARLY * shard_rows * width, transcendentals=0
        ),
        name="preload",
    )(place, head, near[3])
    last, early = lax.optimization_barrier((last, early))
    far = [swap_cores(last), swap_cores(first)]

    stats_shape = (count, STATS, pl.cdiv(tokens, LANES) * LANES)
    rows, stats, own_stats = pl.pallas_call(
        logits_kernel,
        out_shape=(
            hbm_array((3 * tokens, shard_rows), jnp.bfloat16),
            hbm_array(stats_shape, jnp.float32),
            vmem_array(stats_shape[1:], jnp.float32),
        ),
        in_specs=[smem] + [vmem] * 7 + [hbm],
        out_specs=[hbm, hbm, vmem],
        scratch_shapes=[
            pltpu.VMEM((chips - EARLY, shard_rows, width), head.dtype),
            rows_scratch,
            pltpu.VMEM((chips, tokens, width), jnp.bfloat16),
            pltpu.VMEM((2 * tokens, (shard_rows + LANES // 2) // 2), jnp.float32),
            pltpu.VMEM((tokens, shard_rows), jnp.float32),
            pltpu.VMEM((shard_rows, tokens), jnp.float32),
            pltpu.VMEM(stats_shape, jnp.float32),
            pltpu.SemaphoreType.DMA((chips - EARLY,)),
            rows_sem,
            rows_sem,
        ],
        compiler_params=params,
        cost_estimate=pl.CostEstimate(
            flops=2 * tokens * head.size, bytes_accessed=2 * head.size, transcendentals=0
        ),
        name="logits",
    )(
        place,
        *[in_vmem(blocks) for blocks in (first, last, far[1], far[0])],
        in_vmem(owner),
        in_vmem(table),
        in_vmem(early),
        head,
    )

    all_stats = lax.all_to_all(stats, "vocab", split_axis=0, concat_axis=0, tiled=True)

    terms, picks = pl.pallas_call(
        products_kernel,
        out_shape=(
            vmem_array((chips, width // LANES, 2, tokens, LANES), jnp.float32),
            vmem_array((chips, width // LANES, tokens, LANES), jnp.bfloat16),
        ),
        in_specs=[smem, hbm, hbm],
        out_specs=[vmem] * 2,
        scratch_shapes=[head_scratch, rows_scratch, head_sems, rows_sem],
        compiler_params=params,
        cost_estimate=pl.CostEstimate(
            flops=6 * tokens * head.size, bytes_accessed=2 * head.size, transcendentals=0
        ),
        name="products",
    )(place, in_hbm(rows), head)

    terms, picks = in_vmem(terms), in_vmem(picks)
    give, factors, loss = pl.pallas_call(
        give_kernel,
        out_shape=(
            vmem_array((chips, hidden_rows, LANES), jnp.bfloat16),
            vmem_array((3, tokens, LANES), jnp.float32),
            vmem_array((1, 1), jnp.float32),
        ),
        in_specs=[smem] * 2 + [vmem] * 5,
        out_specs=[vmem] * 3,
        compiler_params=params,
        name="give",
    )(place, loss_scale, in_vmem(all_stats), in_vmem(own_stats), in_vmem(table), terms, picks)
    taken = swap_cores(give)
    keep, loss = pl.pallas_call(
        keep_kernel,
        out_shape=(
            vmem_array((chips, hidden_rows, LANES), jnp.float32),
            jax.ShapeDtypeStruct((1, 1), jnp.float32),
        ),
        in_specs=[smem] + [vmem] * 4,
        out_specs=[vmem] * 2,
        compiler_params=params,
        cost_estimate=pl.CostEstimate(
            flops=4 * terms.size, bytes_accessed=4 * terms.size, transcendentals=0
        ),
        name="keep",
    )(place, in_vmem(factors), in_vmem(loss), terms, picks)
    sums = keep + taken.astype(jnp.float32)
    shares = [along_chips(sums[step].astype(jnp.bfloat16), step) for step in steps]
    total = pl.pallas_call(
        sum_kernel,
        out_shape=jax.ShapeDtypeStruct((tokens, half), jnp.bfloat16),
        in_specs=[smem] + [vmem] * chips,
        out_specs=vmem,
        compiler_params=params,
        name="total",
    )(place, *[in_vmem(share) for share in [sums[0]] + shares])
    return total, jnp.reshape(loss, (1,))


VMEM_LIMIT = 24 * 1024 * 1024


def shards(
    hidden_states, head, teacher_values, teacher_scales, token_ids, lengths, row_map, loss_scale
):
    count = lax.axis_size("vocab")
    own_index = lax.axis_index("vocab")
    tokens = hidden_states.shape[0]
    own_features = hidden_states.shape[1]
    shard_rows = head.shape[0]
    seq_length = tokens // lengths.shape[0]
    contract_last = (((1,), (1,)), ((), ()))

    scaled = scaled_teacher(teacher_values, teacher_scales, count, shard_rows)
    arrived = lax.all_to_all(scaled, "vocab", split_axis=0, concat_axis=0, tiled=True)
    arrived = arrived.reshape(tokens, shard_rows)
    gathered = to_all(hidden_states, count).transpose(1, 0, 2).reshape(tokens, -1)
    logits = lax.dot_general(gathered, head, contract_last, preferred_element_type=jnp.float32)

    positions = jnp.arange(tokens, dtype=jnp.int32)
    owner = row_map[None, :] == positions[:, None]
    slot_of = jnp.sum(jnp.where(owner, positions[None, :], 0), axis=1)
    teacher = jnp.take(arrived, slot_of, axis=0).astype(jnp.float32)

    seq_ids = jnp.arange(lengths.shape[0], dtype=jnp.int32)
    own_length = jnp.sum(
        jnp.where((positions // seq_length)[:, None] == seq_ids[None, :], lengths[None, :], 0),
        axis=1,
    )
    live_mask = (positions % seq_length < own_length).astype(jnp.float32)
    live_count = jnp.sum(live_mask)

    local_ids = token_ids - own_index * shard_rows
    target_hit = local_ids[:, None] == jnp.arange(shard_rows, dtype=jnp.int32)[None, :]
    target_part = jnp.sum(jnp.where(target_hit, logits, 0.0), axis=1)
    student_top = jnp.max(logits, axis=1)
    teacher_top = jnp.max(teacher, axis=1)
    student_off = logits - student_top[:, None]
    teacher_off = teacher - teacher_top[:, None]
    student_exp = jnp.exp(student_off)
    student_sum = jnp.sum(student_exp, axis=1)
    teacher_sum = jnp.sum(jnp.exp(teacher_off), axis=1)
    cross_sum = jnp.sum(student_exp * (student_off - teacher_off), axis=1)

    stats = to_all(
        jnp.stack(
            [student_top, student_sum, teacher_top, teacher_sum, cross_sum, target_part]
        ),
        count,
    )
    tops, sums, teacher_tops, teacher_sums, crosses, targets = [stats[:, i] for i in range(6)]
    student_max, student_total, teacher_max, teacher_total, cross_total = merge_stats(
        tops, sums, teacher_tops, teacher_sums, crosses
    )
    student_log = jnp.log(student_total)
    teacher_log = jnp.log(teacher_total)
    student_lse = student_max + student_log
    teacher_lse = teacher_max + teacher_log
    divergence = cross_total / student_total - (student_log - teacher_log)
    target = jnp.sum(targets, axis=0)

    per_token = divergence + sample_weight * (student_lse - target)
    loss = jnp.reshape(jnp.sum(live_mask * per_token) / live_count, (1,))
    token_weight = live_mask * loss_scale[0] / live_count
    log_student = logits - student_lse[:, None]
    log_teacher = teacher - teacher_lse[:, None]
    student_prob = jnp.exp(log_student)
    grad_logits = (
        token_weight[:, None]
        * (
            student_prob * (log_student - log_teacher - divergence[:, None])
            + sample_weight * (student_prob - target_hit.astype(jnp.float32))
        )
    ).astype(jnp.bfloat16)
    terms = jnp.dot(grad_logits, head, preferred_element_type=jnp.float32).astype(jnp.bfloat16)
    terms = terms.reshape(tokens, count, own_features).transpose(1, 0, 2)
    shares = lax.all_to_all(terms, "vocab", split_axis=0, concat_axis=0, tiled=True)
    grad_hidden = jnp.sum(shares.astype(jnp.float32), axis=0)
    return (grad_hidden.astype(jnp.bfloat16), loss)


def any_shards(*arrays):
    hidden_states, head, teacher_values = arrays[:3]
    count = lax.axis_size("vocab")
    fits = (
        count % 2 == 0
        and hidden_states.shape[1] == 5 * LANES // 2
        and hidden_states.shape[0] % 32 == 0
        and head.shape[0] % LANES == LANES // 2
        and (head.shape[0] + LANES // 2) // LANES % 2 == 0
        and teacher_values.shape[0] == 4
    )
    return paired_shards(*arrays) if fits else shards(*arrays)


def solution(mesh):
    in_specs = (
        P("dom", "vocab"),
        P("vocab", None),
        P(("dom", "vocab"), None),
        P(("dom", "vocab"), None),
        P("dom"),
        P("dom"),
        P("dom"),
        P(),
    )
    out_specs = (P("dom", "vocab"), P("dom"))
    return jax.shard_map(
        any_shards, mesh=mesh, in_specs=in_specs, out_specs=out_specs, check_vma=False
    )
```
